32 devices in a mesh: grp: 1, row: 32 (over z, y, x, core), ka: 1.
Axes of the slice: x: 2, y: 2, z: 4, core: 2. Of those that a mesh axis runs over, the one named last changes fastest.
Arguments:
- pair_rep: bfloat16 [128, 128, 128], P(('grp', 'row'), 'ka'), may hold values from -6 to 6
- pair_mask: int32 [128, 128], P(('grp', 'row'), 'ka'), may hold values from 0 to 1, as said below
- proj_weight: bfloat16 [2, 128, 512], replicated, may hold values from -0.5 to 0.5
- proj_bias: float32 [2, 512], replicated, may hold values from -4 to 4
- gate_weight: bfloat16 [2, 128, 128], replicated, may hold values from -0.5 to 0.5
- gate_bias: float32 [2, 128], replicated, may hold values from -4 to 4
- out_weight: bfloat16 [2, 128, 128], replicated, may hold values from -0.5 to 0.5
- out_bias: float32 [2, 128], replicated, may hold values from -3 to 3
- norm_scale: float32 [2, 2, 128], replicated, may hold values from 0.1 to 1.9
- norm_offset: float32 [2, 2, 128], replicated, may hold values from -3 to 3
Outputs:
- pair_out: bfloat16 [128, 128, 128], P(('grp', 'row'), 'ka')
The draws below stay inside these ranges and needn't reach their ends.
Inputs may be any that keep to these rules, and one draw needn't show every extreme that they name: pair_mask[a, b] is 1 wherever the circular residue distance min(|a - b|, 128 - |a - b|) is under 2 * 4; elsewhere it is 0 or 1.
All inputs are finite; a program needn't handle non-finite values.
Results may differ from the reference program's by a relative error of at most 0.014.
Values may be sent and summed in bfloat16 or wider, within the bound.
No kernel may reach another device: no remote copies, remote signals or barrier semaphores. Data moves between devices by JAX's collectives and lax.ppermute only.
A program may use at most 128 MiB of HBM per device.

```python
import jax
import jax.numpy as jnp
from jax import lax

C = 128
H = 128
RES_DEV = 4
L = 128


def draw_pair_mask(key, part):
    key = jax.random.fold_in(key, 7)
    positions = jnp.arange(L, dtype=jnp.int32)
    distance = jnp.abs(positions[:, None] - positions[None, :])
    distance = jnp.minimum(distance, L - distance)
    inside = distance < 2 * RES_DEV
    scattered = jax.random.randint(key, (L, L), 0, 64) == 0
    return jnp.logical_or(inside, scattered).astype(jnp.int32)


def block_scale(own_key, dims, split, low, largest):
    def one(axis_at, shards_of):
        steps = jax.random.uniform(jax.random.fold_in(jax.random.fold_in(own_key, 6), axis_at), (shards_of,), jnp.float32, low / len(split), largest / len(split))
        return jnp.repeat(jnp.exp(steps), dims[axis_at] // shards_of).reshape((-1,) + (1,) * (len(dims) - axis_at - 1))

    gain = one(*split[0])
    for cut in split[1:]:
        gain = gain * one(*cut)
    return gain


def gaussian(key, shape, scale, limit, shards=(), held_as=jnp.bfloat16):
    drawn = jax.random.normal(key, shape, jnp.float32) * scale
    if len(shards) > 0:
        drawn = block_scale(key, shape, shards, -0.22, 0.18) * drawn
    return jnp.clip(drawn, min=-limit, max=limit).astype(held_as)


def setup_inputs(seed: int = 0, part: int = 0) -> dict:
    keys = jax.random.split(jax.random.key(seed), 11)
    part_splits = jax.random.split(jax.random.fold_in(keys[10], part), 11)
    pair_rep = gaussian(part_splits[0], (L, L, C), 1.0, 6.0, ((0, 32),))
    pair_mask = draw_pair_mask(jax.random.fold_in(jax.random.fold_in(keys[10], part), 71), part)
    proj_weight = gaussian(keys[2], (2, C, 4 * H), C ** -0.5, 0.5)
    proj_bias = gaussian(keys[3], (2, 4 * H), 1.0, 4.0, (), jnp.float32)
    gate_weight = gaussian(keys[4], (2, C, C), C ** -0.5, 0.5)
    gate_bias = gaussian(keys[5], (2, C), 1.0, 4.0, (), jnp.float32)
    out_weight = gaussian(keys[6], (2, H, C), H ** -0.5, 0.5)
    out_bias = gaussian(keys[7], (2, C), 0.5, 3.0, (), jnp.float32)
    norm_scale = jnp.clip(1.0 + 0.18 * jax.random.normal(keys[8], (2, 2, C), jnp.float32), 0.1, 1.9)
    norm_offset = gaussian(keys[9], (2, 2, C), 0.5, 3.0, (), jnp.float32)
    return {"pair_rep": pair_rep, "pair_mask": pair_mask, "proj_weight": proj_weight, "proj_bias": proj_bias, "gate_weight": gate_weight, "gate_bias": gate_bias, "out_weight": out_weight, "out_bias": out_bias, "norm_scale": norm_scale, "norm_offset": norm_offset}


def layer_norm(values, norm_gain, norm_bias):
    average = lax.optimization_barrier(jnp.mean(values, -1, keepdims=True))
    centred = values - average
    variance = lax.optimization_barrier(jnp.mean(centred * centred, -1, keepdims=True))
    return centred * lax.rsqrt(variance + 1e-05) * norm_gain + norm_bias

def project(pair_block, pair_mask, update_index, proj_weight, proj_bias, gate_weight, gate_bias, norm_scale, norm_offset):
    normed = layer_norm(pair_block.astype(jnp.float32), norm_scale[update_index, 0], norm_offset[update_index, 0]).astype(jnp.bfloat16)
    projected = jnp.dot(normed, proj_weight[update_index], preferred_element_type=jnp.float32) + proj_bias[update_index]
    hidden_width = proj_weight.shape[2] // 4
    weight_mask = pair_mask.astype(jnp.float32)[..., None]
    left_side = (weight_mask * jax.nn.sigmoid(projected[..., hidden_width:2 * hidden_width]) * projected[..., :hidden_width]).astype(jnp.bfloat16)
    right_side = (weight_mask * jax.nn.sigmoid(projected[..., 3 * hidden_width:]) * projected[..., 2 * hidden_width:3 * hidden_width]).astype(jnp.bfloat16)
    gating = jax.nn.sigmoid(jnp.dot(normed, gate_weight[update_index], preferred_element_type=jnp.float32) + gate_bias[update_index])
    return (left_side, right_side, gating)

def finish(pair_block, summed, gating, update_index, out_weight, out_bias, norm_scale, norm_offset):
    normed = layer_norm(summed, norm_scale[update_index, 1], norm_offset[update_index, 1]).astype(jnp.bfloat16)
    change = jnp.dot(normed, out_weight[update_index], preferred_element_type=jnp.float32) + out_bias[update_index]
    return (pair_block.astype(jnp.float32) + gating * change).astype(jnp.bfloat16)

def reference(pair_rep, pair_mask, proj_weight, proj_bias, gate_weight, gate_bias, out_weight, out_bias, norm_scale, norm_offset):
    left_side, right_side, gating = project(pair_rep, pair_mask, 0, proj_weight, proj_bias, gate_weight, gate_bias, norm_scale, norm_offset)
    summed = jnp.einsum('ikc,jkc->ijc', left_side.astype(jnp.float32), right_side.astype(jnp.float32), precision=lax.Precision.HIGHEST)
    first_pass = finish(pair_rep, summed, gating, 0, out_weight, out_bias, norm_scale, norm_offset)
    left_side, right_side, gating = project(first_pass, pair_mask, 1, proj_weight, proj_bias, gate_weight, gate_bias, norm_scale, norm_offset)
    summed = jnp.einsum('kic,kjc->ijc', left_side.astype(jnp.float32), right_side.astype(jnp.float32), precision=lax.Precision.HIGHEST)
    return finish(first_pass, summed, gating, 1, out_weight, out_bias, norm_scale, norm_offset)
```

```python
import jax
import jax.numpy as jnp
from jax import lax
from jax.sharding import PartitionSpec as P

PEERS = ("row", "ka")


def layer_norm(values, norm_gain, norm_bias, axis):
    average = jnp.mean(values, axis, keepdims=True)
    centred = values - average
    variance = jnp.mean(centred * centred, axis, keepdims=True)
    return centred * lax.rsqrt(variance + 1e-05) * norm_gain + norm_bias


def update(pair_t, pair_mask, u, incoming, peers, rows_of, proj_weight, proj_bias, gate_weight, gate_bias, out_weight, out_bias, norm_scale, norm_offset):
    channels, positions = pair_t.shape
    width = positions // rows_of
    hidden_width = proj_weight.shape[2] // 4
    own = hidden_width // (peers[0] * peers[1])
    normed = layer_norm(pair_t, norm_scale[u, 0][:, None], norm_offset[u, 0][:, None], 0).astype(jnp.bfloat16)
    weights = jnp.concatenate([proj_weight[u], gate_weight[u]], 1)
    biases = jnp.concatenate([proj_bias[u], gate_bias[u]], 0)
    projected = lax.dot_general(weights, normed, (((0,), (0,)), ((), ())), preferred_element_type=jnp.float32) + biases[:, None]
    parts = [projected[n * hidden_width : (n + 1) * hidden_width] for n in range(4)]
    gating = jax.nn.sigmoid(projected[4 * hidden_width :])
    mask = pair_mask.astype(jnp.float32).reshape(1, positions)
    left = (mask * jax.nn.sigmoid(parts[1]) * parts[0]).astype(jnp.bfloat16)
    right = (mask * jax.nn.sigmoid(parts[3]) * parts[2]).astype(jnp.bfloat16)
    count = peers[0] * peers[1]
    sides = jnp.stack([left.reshape(count, own, rows_of, width), right.reshape(count, own, rows_of, width)], 1)
    sides = lax.all_to_all(sides, PEERS, split_axis=0, concat_axis=0, tiled=True)
    sides = sides.reshape(peers[0], peers[1], 2, own, rows_of, width)
    sides = sides.transpose(2, 3, 0, 4, 1, 5).reshape(2, own, peers[0] * rows_of, peers[1] * width)
    form = "cki,ckj->cij" if incoming else "cik,cjk->cij"
    summed = jnp.einsum(form, sides[0], sides[1], preferred_element_type=jnp.float32).astype(jnp.bfloat16)
    summed = summed.reshape(own, peers[0], rows_of, peers[1], width).transpose(1, 3, 0, 2, 4)
    summed = summed.reshape(count, own, rows_of, width)
    summed = lax.all_to_all(summed, PEERS, split_axis=0, concat_axis=0, tiled=True)
    summed = summed.reshape(hidden_width, positions).astype(jnp.float32)
    hidden = layer_norm(summed, norm_scale[u, 1][:, None], norm_offset[u, 1][:, None], 0).astype(jnp.bfloat16)
    change = lax.dot_general(out_weight[u], hidden, (((0,), (0,)), ((), ())), preferred_element_type=jnp.float32) + out_bias[u][:, None]
    return (pair_t + gating * change).astype(jnp.bfloat16)


def solution(mesh):
    peers = (mesh.shape["row"], mesh.shape["ka"])

    def on_device(pair_rep, pair_mask, *params):
        rows_of, width, channels = pair_rep.shape
        pair_t = pair_rep.reshape(rows_of * width, channels).T
        first = update(pair_t.astype(jnp.float32), pair_mask, 0, False, peers, rows_of, *params)
        second = update(first.astype(jnp.float32), pair_mask, 1, True, peers, rows_of, *params)
        return second.T.reshape(rows_of, width, channels)

    split = P(("grp", "row"), "ka", None)
    in_specs = (split, P(("grp", "row"), "ka")) + (P(),) * 8
    return jax.shard_map(on_device, mesh=mesh, in_specs=in_specs, out_specs=split, check_vma=False)
```

```python
import functools

import jax
import jax.numpy as jnp
from jax import lax
from jax.experimental import pallas as pl
from jax.experimental.pallas import tpu as pltpu
from jax.sharding import PartitionSpec as P

PEERS = ("row", "ka")
OWN = 4
BF16, F32 = jnp.bfloat16, jnp.float32


def over_rows(a, b):
    return lax.dot_general(a, b, (((0,), (0,)), ((), ())), preferred_element_type=F32)


def over_columns(a, b):
    return lax.dot_general(a, b, (((1,), (1,)), ((), ())), preferred_element_type=F32)


def layer_norm(values, norm_gain, norm_bias):
    average = jnp.mean(values, 0, keepdims=True)
    centred = values - average
    variance = jnp.mean(centred * centred, 0, keepdims=True)
    return centred * lax.rsqrt(variance + 1e-05) * norm_gain + norm_bias


def pack(blocks):
    channels, width = blocks[0].shape
    tiles = [b.reshape(channels // 8, 8, width) for b in blocks]
    turned = [pltpu.roll(b, 4, axis=0).reshape(channels // 8, 8, width) for b in blocks]
    low = lax.broadcasted_iota(jnp.int32, tiles[0].shape, 1) < 4
    back = [pltpu.roll(b, channels - 4, axis=0).reshape(channels // 8, 8, width) for b in blocks]
    even = [jnp.where(low, tiles[n], turned[n + 1]) for n in (0, 2)]
    odd = [jnp.where(low, back[n], tiles[n + 1]) for n in (0, 2)]
    return jnp.stack([jnp.stack(even, 1), jnp.stack(odd, 1)], 1).reshape(channels // 4, 16, width)


def unpack(packed):
    count, _, width = packed.shape
    tiles = packed.reshape(count // 2, 2, 2, 8, width)
    low = lax.broadcasted_iota(jnp.int32, (count // 2, 8, width), 1) < 4
    blocks = []
    for n in range(2):
        even, odd = tiles[:, 0, n], tiles[:, 1, n]
        down = pltpu.roll(odd.reshape(count * 4, width), 4, axis=0).reshape(even.shape)
        up = pltpu.roll(even.reshape(count * 4, width), count * 4 - 4, axis=0).reshape(even.shape)
        blocks.append(jnp.where(low, even, down).reshape(count * 4, width))
        blocks.append(jnp.where(low, up, odd).reshape(count * 4, width))
    return blocks


def as_columns(rows, columns):
    for n, row in enumerate(rows):
        columns[n : n + 1, :] = row
    turned = columns[...].T
    return [turned[:, n : n + 1] for n in range(len(rows))]


def project(u, z, mask, proj_weight, proj_bias, gate_weight, gate_bias, norm_scale, norm_offset, columns, send, gate):
    width = z[0].shape[1]
    h = proj_weight.shape[2] // 4
    rows = [norm_scale[u, 0:1, :], norm_offset[u, 0:1, :]]
    rows += [proj_bias[u : u + 1, n * h : (n + 1) * h] for n in range(4)] + [gate_bias[u : u + 1, :]]
    gain, offset, *biases = as_columns(rows, columns)
    weight, out_gate = proj_weight[u], gate_weight[u]
    lefts, rights = [], []
    for i in range(OWN):
        normed = layer_norm(z[i], gain, offset).astype(BF16)
        projected = over_rows(weight, normed)
        parts = [projected[n * h : (n + 1) * h] + biases[n] for n in range(4)]
        keep = mask[i : i + 1, :].astype(F32)
        lefts.append(keep * jax.nn.sigmoid(parts[1]) * parts[0])
        rights.append(keep * jax.nn.sigmoid(parts[3]) * parts[2])
        gate[:, i * width : (i + 1) * width] = jax.nn.sigmoid(over_rows(out_gate, normed) + biases[4])
    send[:, 0:16, :] = pack(lefts).astype(BF16)
    send[:, 16:32, :] = pack(rights).astype(BF16)


def finish(u, z, summed, gate, out_weight, out_bias, norm_scale, norm_offset, columns):
    width = z[0].shape[1]
    gain, offset, bias = as_columns([norm_scale[u, 1:2, :], norm_offset[u, 1:2, :], out_bias[u : u + 1, :]], columns)
    weight = out_weight[u]
    results = []
    for i, block in enumerate(unpack(summed[...].astype(F32))):
        hidden = layer_norm(block, gain, offset).astype(BF16)
        change = over_rows(weight, hidden) + bias
        results.append(z[i] + gate[:, i * width : (i + 1) * width] * change)
    return results


def first_kernel(pair, mask, pw, pb, gw, gb, ns, no, send, gate, turned, columns):
    width = pair.shape[1]
    z = [pair[i].astype(F32).T for i in range(OWN)]
    for i in range(OWN):
        turned[:, i * width : (i + 1) * width] = z[i].astype(BF16)
    project(0, z, mask, pw, pb, gw, gb, ns, no, columns, send, gate)


def middle_kernel(summed, old, old_gate, mask, pw, pb, gw, gb, ow, ob, ns, no, send, gate, turned, columns, more):
    width = mask.shape[1]
    z = [old[:, i * width : (i + 1) * width].astype(F32) for i in range(OWN)]
    z = [v.astype(BF16) for v in finish(0, z, summed, old_gate, ow, ob, ns, no, columns)]
    for i in range(OWN):
        turned[:, i * width : (i + 1) * width] = z[i]
    project(1, [v.astype(F32) for v in z], mask, pw, pb, gw, gb, ns, no, more, send, gate)


def last_kernel(summed, old, old_gate, ow, ob, ns, no, out, columns):
    width = out.shape[1]
    z = [old[:, i * width : (i + 1) * width].astype(F32) for i in range(OWN)]
    for i, v in enumerate(finish(1, z, summed, old_gate, ow, ob, ns, no, columns)):
        out[i] = v.T.astype(BF16)


def triangle_kernel(incoming, sides, out):
    count, _, width = sides.shape
    rows = count * 16
    left, right = [sides[:, n : n + 16, :].reshape(rows, width) for n in (0, 16)]
    down = lax.broadcasted_iota(jnp.int32, (rows, width), 0)
    across = lax.broadcasted_iota(jnp.int32, (rows, width), 1)
    spread = jnp.where(down // OWN == across, 1.0, 0.0).astype(BF16)
    both = over_columns(spread, left) if incoming else over_columns(left, right)
    channel = [lax.broadcasted_iota(jnp.int32, (rows, rows), d) % OWN for d in (0, 1)]
    both = jnp.where(channel[0] == channel[1], both, 0.0).astype(BF16)
    summed = jnp.dot(both, right if incoming else spread, preferred_element_type=F32)
    out[...] = summed.astype(BF16).reshape(count, 16, width)


def call(kernel, outs, scratch, *args):
    in_vmem = pl.BlockSpec(memory_space=pltpu.VMEM)
    return pl.pallas_call(
        kernel,
        out_shape=[jax.ShapeDtypeStruct(*o) for o in outs],
        in_specs=[in_vmem] * len(args),
        out_specs=[in_vmem] * len(outs),
        scratch_shapes=[pltpu.VMEM((8, 128), F32)] * scratch,
        compiler_params=pltpu.CompilerParams(vmem_limit_bytes=24 * 2**20),
    )(*args)


def exchange(blocks):
    return lax.all_to_all(blocks, PEERS, split_axis=0, concat_axis=0, tiled=True)


def packed_updates(count, pair_rep, pair_mask, pw, pb, gw, gb, ow, ob, ns, no):
    rows_of, width, channels = pair_rep.shape
    flat = (channels, rows_of * width)
    projected = [((count, 32, width), BF16), (flat, F32), (flat, BF16)]
    summed = [((count, 16, width), BF16)]
    send, gate, turned = call(first_kernel, projected, 1, pair_rep, pair_mask, pw, pb, gw, gb, ns, no)
    (send,) = call(functools.partial(triangle_kernel, False), summed, 0, exchange(send))
    send, gate, turned = call(
        middle_kernel, projected, 2, exchange(send), turned, gate, pair_mask, pw, pb, gw, gb, ow, ob, ns, no
    )
    (send,) = call(functools.partial(triangle_kernel, True), summed, 0, exchange(send))
    (out,) = call(last_kernel, [(pair_rep.shape, BF16)], 1, exchange(send), turned, gate, ow, ob, ns, no)
    return out


def update(pair_t, pair_mask, u, incoming, peers, rows_of, pw, pb, gw, gb, ow, ob, ns, no):
    channels, positions = pair_t.shape
    width = positions // rows_of
    h = pw.shape[2] // 4
    count = peers[0] * peers[1]
    own = h // count
    normed = layer_norm(pair_t, ns[u, 0][:, None], no[u, 0][:, None]).astype(BF16)
    projected = over_rows(jnp.concatenate([pw[u], gw[u]], 1), normed) + jnp.concatenate([pb[u], gb[u]], 0)[:, None]
    parts = [projected[n * h : (n + 1) * h] for n in range(4)]
    gating = jax.nn.sigmoid(projected[4 * h :])
    mask = pair_mask.astype(F32).reshape(1, positions)
    left = (mask * jax.nn.sigmoid(parts[1]) * parts[0]).astype(BF16)
    right = (mask * jax.nn.sigmoid(parts[3]) * parts[2]).astype(BF16)
    sides = exchange(jnp.stack([v.reshape(count, own, rows_of, width) for v in (left, right)], 1))
    sides = sides.reshape(peers[0], peers[1], 2, own, rows_of, width)
    sides = sides.transpose(2, 3, 0, 4, 1, 5).reshape(2, own, peers[0] * rows_of, peers[1] * width)
    form = "cki,ckj->cij" if incoming else "cik,cjk->cij"
    summed = jnp.einsum(form, sides[0], sides[1], preferred_element_type=F32).astype(BF16)
    summed = summed.reshape(own, peers[0], rows_of, peers[1], width).transpose(1, 3, 0, 2, 4)
    summed = exchange(summed.reshape(count, own, rows_of, width)).reshape(h, positions).astype(F32)
    hidden = layer_norm(summed, ns[u, 1][:, None], no[u, 1][:, None]).astype(BF16)
    change = over_rows(ow[u], hidden) + ob[u][:, None]
    return (pair_t + gating * change).astype(BF16)


def plain_updates(peers, pair_rep, pair_mask, *params):
    rows_of, width, channels = pair_rep.shape
    pair_t = pair_rep.reshape(rows_of * width, channels).T
    for u in range(2):
        pair_t = update(pair_t.astype(F32), pair_mask, u, u == 1, peers, rows_of, *params)
    return pair_t.T.reshape(rows_of, width, channels)


def solution(mesh):
    peers = (mesh.shape["row"], mesh.shape["ka"])
    count = peers[0] * peers[1]

    def on_device(pair_rep, pair_mask, *params):
        rows_of, width, channels = pair_rep.shape
        hidden = params[0].shape[2] // 4
        fits = peers[1] == 1 and rows_of == OWN and hidden == OWN * count and count % 2 == 0
        if fits and channels == hidden == 128 and width % 128 == 0:
            return packed_updates(count, pair_rep, pair_mask, *params)
        return plain_updates(peers, pair_rep, pair_mask, *params)

    split = P(("grp", "row"), "ka", None)
    in_specs = (split, P(("grp", "row"), "ka")) + (P(),) * 8
    return jax.shard_map(on_device, mesh=mesh, in_specs=in_specs, out_specs=split, check_vma=False)
```

```python
import functools

import jax
import jax.numpy as jnp
from jax import lax
from jax.experimental import pallas as pl
from jax.experimental.pallas import tpu as pltpu
from jax.sharding import PartitionSpec as P

PEERS = ("row", "ka")
OWN = 4
EACH = 16
BF16, F32 = jnp.bfloat16, jnp.float32


def over_rows(a, b):
    return lax.dot_general(a, b, (((0,), (0,)), ((), ())), preferred_element_type=F32)


def over_columns(a, b):
    return lax.dot_general(a, b, (((1,), (1,)), ((), ())), preferred_element_type=F32)


def layer_norm(values, norm_gain, norm_bias):
    average = jnp.mean(values, 0, keepdims=True)
    centred = values - average
    variance = jnp.mean(centred * centred, 0, keepdims=True)
    return centred * lax.rsqrt(variance + 1e-05) * norm_gain + norm_bias


def pack(blocks):
    channels, width = blocks[0].shape
    tiles = [b.reshape(channels // 8, 8, width) for b in blocks]
    turned = [pltpu.roll(b, 4, axis=0).reshape(channels // 8, 8, width) for b in blocks]
    low = lax.broadcasted_iota(jnp.int32, tiles[0].shape, 1) < 4
    back = [pltpu.roll(b, channels - 4, axis=0).reshape(channels // 8, 8, width) for b in blocks]
    even = [jnp.where(low, tiles[n], turned[n + 1]) for n in (0, 2)]
    odd = [jnp.where(low, back[n], tiles[n + 1]) for n in (0, 2)]
    return jnp.stack([jnp.stack(even, 1), jnp.stack(odd, 1)], 1).reshape(channels // 4, 16, width)


def unpack(packed):
    count, _, width = packed.shape
    tiles = packed.reshape(count // 2, 2, 2, 8, width)
    low = lax.broadcasted_iota(jnp.int32, (count // 2, 8, width), 1) < 4
    blocks = []
    for n in range(2):
        even, odd = tiles[:, 0, n], tiles[:, 1, n]
        down = pltpu.roll(odd.reshape(count * 4, width), 4, axis=0).reshape(even.shape)
        up = pltpu.roll(even.reshape(count * 4, width), count * 4 - 4, axis=0).reshape(even.shape)
        blocks.append(jnp.where(low, even, down).reshape(count * 4, width))
        blocks.append(jnp.where(low, up, odd).reshape(count * 4, width))
    return blocks


def project(u, z, mask, proj_weight, gate_weight, columns, send, gate):
    width = z[0].shape[1]
    h = proj_weight.shape[1] // 4
    gain, offset, *biases = [columns[:, n : n + 1] for n in range(u * EACH, u * EACH + 7)]
    lefts, rights = [], []
    for i in range(OWN):
        normed = layer_norm(z[i], gain, offset).astype(BF16)
        projected = over_rows(proj_weight, normed)
        parts = [projected[n * h : (n + 1) * h] + biases[n] for n in range(4)]
        keep = mask[i : i + 1, :].astype(F32)
        lefts.append(keep * jax.nn.sigmoid(parts[1]) * parts[0])
        rights.append(keep * jax.nn.sigmoid(parts[3]) * parts[2])
        gate[:, i * width : (i + 1) * width] = jax.nn.sigmoid(over_rows(gate_weight, normed) + biases[4])
    send[:, 0:16, :] = pack(lefts).astype(BF16)
    send[:, 16:32, :] = pack(rights).astype(BF16)


def finish(u, i, z, block, gate, out_weight, columns):
    width = z.shape[1]
    gain, offset, bias = [columns[:, n : n + 1] for n in range(u * EACH + 7, u * EACH + 10)]
    hidden = layer_norm(block, gain, offset).astype(BF16)
    change = over_rows(out_weight, hidden) + bias
    return z + gate[:, i * width : (i + 1) * width] * change


def first_kernel(
    pair, mask, pw, gw, pb, gb, ob, ns, no, send, gate, turned, columns, pair_in, mask_in, pw_in, gw_in, pb_in, gb_in, ob_in, ns_in, no_in, rows, arrived
):
    moves = [(pb, pb_in), (gb, gb_in), (ob, ob_in), (ns, ns_in), (no, no_in)]
    moves += [(pair, pair_in), (pw.at[0], pw_in), (gw.at[0], gw_in), (mask, mask_in)]
    moves = [pltpu.make_async_copy(a, b, arrived.at[n]) for n, (a, b) in enumerate(moves)]
    for move in moves:
        move.start()
    for move in moves[:5]:
        move.wait()
    h = pw.shape[2] // 4
    for u in range(2):
        found = [ns_in[u, 0:1, :], no_in[u, 0:1, :]] + [pb_in[u : u + 1, n * h : (n + 1) * h] for n in range(4)]
        found += [gb_in[u : u + 1, :], ns_in[u, 1:2, :], no_in[u, 1:2, :], ob_in[u : u + 1, :]]
        for n, row in enumerate(found):
            rows[u * EACH + n : u * EACH + n + 1, :] = row
    columns[...] = rows[...].T
    moves[5].wait()
    width = pair.shape[1]
    z = [pair_in[i].astype(F32).T for i in range(OWN)]
    for i in range(OWN):
        turned[:, i * width : (i + 1) * width] = z[i].astype(BF16)
    for move in moves[6:]:
        move.wait()
    project(0, z, mask_in, pw_in[...], gw_in[...], columns, send, gate)


def middle_kernel(summed, old, old_gate, columns, mask, pw, gw, ow, send, gate, turned):
    width = mask.shape[1]
    z = []
    for i, block in enumerate(unpack(summed[...].astype(F32))):
        at = slice(i * width, (i + 1) * width)
        z.append(finish(0, i, old[:, at].astype(F32), block, old_gate, ow[0], columns).astype(BF16))
        turned[:, at] = z[i]
    project(1, [v.astype(F32) for v in z], mask, pw[1], gw[1], columns, send, gate)


def last_kernel(summed, old, old_gate, columns, ow, out, ready, left):
    width = out.shape[1]
    moves = []
    for i, block in enumerate(unpack(summed[...].astype(F32))):
        z = old[:, i * width : (i + 1) * width].astype(F32)
        ready[i] = finish(1, i, z, block, old_gate, ow[1], columns).T.astype(BF16)
        moves.append(pltpu.make_async_copy(ready.at[i], out.at[i], left.at[i]))
        moves[i].start()
    for move in moves:
        move.wait()


def triangle_kernel(incoming, sides, out):
    count, _, width = sides.shape
    rows = count * 16
    left, right = [sides[:, n : n + 16, :].reshape(rows, width) for n in (0, 16)]
    down = lax.broadcasted_iota(jnp.int32, (rows, width), 0)
    across = lax.broadcasted_iota(jnp.int32, (rows, width), 1)
    spread = jnp.where(down // OWN == across, 1.0, 0.0).astype(BF16)
    both = over_columns(spread, left) if incoming else over_columns(left, right)
    channel = [lax.broadcasted_iota(jnp.int32, (rows, rows), d) % OWN for d in (0, 1)]
    both = jnp.where(channel[0] == channel[1], both, 0.0).astype(BF16)
    summed = jnp.dot(both, right if incoming else spread, preferred_element_type=F32)
    out[...] = summed.astype(BF16).reshape(count, 16, width)


def call(kernel, outs, scratch, *args, from_hbm=False, to_hbm=False):
    in_vmem, in_hbm = [pl.BlockSpec(memory_space=m) for m in (pltpu.VMEM, pltpu.HBM)]
    return pl.pallas_call(
        kernel,
        out_shape=[jax.ShapeDtypeStruct(*o) for o in outs],
        in_specs=[in_hbm if from_hbm else in_vmem] * len(args),
        out_specs=[in_hbm if to_hbm else in_vmem] * len(outs),
        scratch_shapes=scratch,
        compiler_params=pltpu.CompilerParams(vmem_limit_bytes=24 * 2**20),
    )(*args)


def exchange(blocks):
    return lax.all_to_all(blocks, PEERS, split_axis=0, concat_axis=0, tiled=True)


def packed_updates(count, pair_rep, pair_mask, pw, pb, gw, gb, ow, ob, ns, no):
    rows_of, width, channels = pair_rep.shape
    flat = (channels, rows_of * width)
    projected = [((count, 32, width), BF16), (flat, F32), (flat, BF16)]
    summed = [((count, 16, width), BF16)]
    params = [pair_rep, pair_mask, pw, gw, pb, gb, ob, ns, no]
    params = [pltpu.with_memory_space_constraint(v, pltpu.HBM) for v in params]
    held = [pltpu.VMEM(v.shape[1:] if n in (2, 3) else v.shape, v.dtype) for n, v in enumerate(params)]
    held += [pltpu.VMEM((2 * EACH, channels), F32), pltpu.SemaphoreType.DMA((len(params),))]
    send, gate, turned, columns = call(
        first_kernel, projected + [((channels, 2 * EACH), F32)], held, *params, from_hbm=True
    )
    (send,) = call(functools.partial(triangle_kernel, False), summed, [], exchange(send))
    send, gate, turned = call(middle_kernel, projected, [], exchange(send), turned, gate, columns, pair_mask, pw, gw, ow)
    (send,) = call(functools.partial(triangle_kernel, True), summed, [], exchange(send))
    held = [pltpu.VMEM(pair_rep.shape, BF16), pltpu.SemaphoreType.DMA((rows_of,))]
    (out,) = call(last_kernel, [(pair_rep.shape, BF16)], held, exchange(send), turned, gate, columns, ow, to_hbm=True)
    return out


def update(pair_t, pair_mask, u, incoming, peers, rows_of, pw, pb, gw, gb, ow, ob, ns, no):
    channels, positions = pair_t.shape
    width = positions // rows_of
    h = pw.shape[2] // 4
    count = peers[0] * peers[1]
    own = h // count
    normed = layer_norm(pair_t, ns[u, 0][:, None], no[u, 0][:, None]).astype(BF16)
    projected = over_rows(jnp.concatenate([pw[u], gw[u]], 1), normed) + jnp.concatenate([pb[u], gb[u]], 0)[:, None]
    parts = [projected[n * h : (n + 1) * h] for n in range(4)]
    gating = jax.nn.sigmoid(projected[4 * h :])
    mask = pair_mask.astype(F32).reshape(1, positions)
    left = (mask * jax.nn.sigmoid(parts[1]) * parts[0]).astype(BF16)
    right = (mask * jax.nn.sigmoid(parts[3]) * parts[2]).astype(BF16)
    sides = exchange(jnp.stack([v.reshape(count, own, rows_of, width) for v in (left, right)], 1))
    sides = sides.reshape(peers[0], peers[1], 2, own, rows_of, width)
    sides = sides.transpose(2, 3, 0, 4, 1, 5).reshape(2, own, peers[0] * rows_of, peers[1] * width)
    form = "cki,ckj->cij" if incoming else "cik,cjk->cij"
    summed = jnp.einsum(form, sides[0], sides[1], preferred_element_type=F32).astype(BF16)
    summed = summed.reshape(own, peers[0], rows_of, peers[1], width).transpose(1, 3, 0, 2, 4)
    summed = exchange(summed.reshape(count, own, rows_of, width)).reshape(h, positions).astype(F32)
    hidden = layer_norm(summed, ns[u, 1][:, None], no[u, 1][:, None]).astype(BF16)
    change = over_rows(ow[u], hidden) + ob[u][:, None]
    return (pair_t + gating * change).astype(BF16)


def plain_updates(peers, pair_rep, pair_mask, *params):
    rows_of, width, channels = pair_rep.shape
    pair_t = pair_rep.reshape(rows_of * width, channels).T
    for u in range(2):
        pair_t = update(pair_t.astype(F32), pair_mask, u, u == 1, peers, rows_of, *params)
    return pair_t.T.reshape(rows_of, width, channels)


def solution(mesh):
    peers = (mesh.shape["row"], mesh.shape["ka"])
    count = peers[0] * peers[1]

    def on_device(pair_rep, pair_mask, *params):
        rows_of, width, channels = pair_rep.shape
        hidden = params[0].shape[2] // 4
        fits = peers[1] == 1 and rows_of == OWN and hidden == OWN * count and count % 2 == 0
        if fits and channels == hidden == 128 and width % 128 == 0:
            return packed_updates(count, pair_rep, pair_mask, *params)
        return plain_updates(peers, pair_rep, pair_mask, *params)

    split = P(("grp", "row"), "ka", None)
    in_specs = (split, P(("grp", "row"), "ka")) + (P(),) * 8
    return jax.shard_map(on_device, mesh=mesh, in_specs=in_specs, out_specs=split, check_vma=False)
```

```python
import functools

import jax
import jax.numpy as jnp
from jax import lax
from jax.experimental import pallas as pl
from jax.experimental.pallas import tpu as pltpu
from jax.sharding import PartitionSpec as P

PEERS = ("row", "ka")
ROWS = 4
OWN = 8
EACH = 16
BF16, F32 = jnp.bfloat16, jnp.float32


def over_rows(a, b):
    return lax.dot_general(a, b, (((0,), (0,)), ((), ())), preferred_element_type=F32)


def over_columns(a, b):
    return lax.dot_general(a, b, (((1,), (1,)), ((), ())), preferred_element_type=F32)


def layer_norm(values, norm_gain, norm_bias):
    average = jnp.mean(values, 0, keepdims=True)
    centred = values - average
    variance = jnp.mean(centred * centred, 0, keepdims=True)
    return centred * lax.rsqrt(variance + 1e-05) * norm_gain + norm_bias


def pack(blocks):
    channels, width = blocks[0].shape
    tiles = [b.reshape(channels // OWN, OWN, width) for b in blocks]
    return jnp.stack(tiles, 1).reshape(channels // OWN, ROWS * OWN, width)


def unpack(packed):
    count, _, width = packed.shape
    tiles = packed.reshape(count, ROWS, OWN, width)
    return [tiles[:, i].reshape(count * OWN, width) for i in range(ROWS)]


def project(u, z, mask, proj_weight, gate_weight, columns, send, gate):
    width = z[0].shape[1]
    h = proj_weight.shape[1] // 4
    gain, offset, *biases = [columns[:, n : n + 1] for n in range(u * EACH, u * EACH + 7)]
    lefts, rights = [], []
    for i in range(ROWS):
        normed = layer_norm(z[i], gain, offset).astype(BF16)
        projected = over_rows(proj_weight, normed)
        parts = [projected[n * h : (n + 1) * h] + biases[n] for n in range(4)]
        keep = mask[i : i + 1, :]
        lefts.append(keep * jax.nn.sigmoid(parts[1]) * parts[0])
        rights.append(keep * jax.nn.sigmoid(parts[3]) * parts[2])
        gate[:, i * width : (i + 1) * width] = jax.nn.sigmoid(over_rows(gate_weight, normed) + biases[4])
    send[:, : ROWS * OWN, :] = pack(lefts).astype(BF16)
    send[:, ROWS * OWN :, :] = pack(rights).astype(BF16)


def finish(u, i, z, block, gate, out_weight, columns):
    width = z.shape[1]
    gain, offset, bias = [columns[:, n : n + 1] for n in range(u * EACH + 7, u * EACH + 10)]
    hidden = layer_norm(block, gain, offset).astype(BF16)
    change = over_rows(out_weight, hidden) + bias
    return z + gate[:, i * width : (i + 1) * width] * change


def first_kernel(
    pair, mask, pw, gw, pb, gb, ob, ns, no, send, gate, turned, columns, keep, pair_in, mask_in, pw_in, gw_in, pb_in, gb_in, ob_in, ns_in, no_in, rows, arrived
):
    moves = [(pb, pb_in), (gb, gb_in), (ob, ob_in), (ns, ns_in), (no, no_in)]
    moves += [(pair, pair_in), (pw.at[0], pw_in), (gw.at[0], gw_in), (mask, mask_in)]
    moves = [pltpu.make_async_copy(a, b, arrived.at[n]) for n, (a, b) in enumerate(moves)]
    for move in moves:
        move.start()
    for move in moves[:5]:
        move.wait()
    h = pw.shape[2] // 4
    for u in range(2):
        found = [ns_in[u, 0:1, :], no_in[u, 0:1, :]] + [pb_in[u : u + 1, n * h : (n + 1) * h] for n in range(4)]
        found += [gb_in[u : u + 1, :], ns_in[u, 1:2, :], no_in[u, 1:2, :], ob_in[u : u + 1, :]]
        for n, row in enumerate(found):
            rows[u * EACH + n : u * EACH + n + 1, :] = row
    columns[...] = rows[...].T
    moves[5].wait()
    width = pair.shape[1]
    z = [pair_in[i].astype(F32).T for i in range(ROWS)]
    for i in range(ROWS):
        turned[:, i * width : (i + 1) * width] = z[i].astype(BF16)
    for move in moves[6:]:
        move.wait()
    keep[0:ROWS, :] = mask_in[...].astype(F32)
    project(0, z, keep, pw_in[...], gw_in[...], columns, send, gate)


def middle_kernel(summed, old, old_gate, columns, mask, pw, gw, ow, send, gate, turned):
    width = mask.shape[1]
    z = []
    for i, block in enumerate(unpack(summed[...].astype(F32))):
        at = slice(i * width, (i + 1) * width)
        z.append(finish(0, i, old[:, at].astype(F32), block, old_gate, ow[0], columns).astype(BF16))
        turned[:, at] = z[i]
    project(1, [v.astype(F32) for v in z], mask, pw[1], gw[1], columns, send, gate)


def last_kernel(summed, old, old_gate, columns, ow, out):
    width = out.shape[1]
    for i, block in enumerate(unpack(summed[...].astype(F32))):
        z = old[:, i * width : (i + 1) * width].astype(F32)
        out[i] = finish(1, i, z, block, old_gate, ow[1], columns).T.astype(BF16)


def halves(sides):
    count, depth, width = sides.shape
    rows = count * depth // 2
    return [sides[:, n : n + depth // 2, :].reshape(rows, width) for n in (0, depth // 2)]


def spread_of(core, rows, residues):
    down = lax.broadcasted_iota(jnp.int32, (rows, residues), 0) // OWN
    across = lax.broadcasted_iota(jnp.int32, (rows, residues), 1)
    return jnp.where(down // ROWS * (2 * ROWS) + core * ROWS + down % ROWS == across, 1.0, 0.0).astype(BF16)


def same_channel(both):
    channel = [lax.broadcasted_iota(jnp.int32, both.shape, d) % OWN for d in (0, 1)]
    return jnp.where(channel[0] == channel[1], both, 0.0).astype(BF16)


def outgoing_kernel(sides, other_right, out):
    core = lax.axis_index("row") % 2
    left, right = halves(sides[...])
    rows, width = left.shape
    summed = jnp.zeros((rows, width), F32)
    for at, side in ((core, right), (1 - core, other_right[...].reshape(rows, width))):
        both = same_channel(over_columns(left, side))
        summed += jnp.dot(both, spread_of(at, rows, width), preferred_element_type=F32)
    out[...] = summed.astype(BF16).reshape(out.shape)


def incoming(sides, core):
    left, right = halves(sides[...])
    both = same_channel(over_columns(spread_of(core, *left.shape), left))
    return jnp.dot(both, right, preferred_element_type=F32)


def other_kernel(sides, out):
    out[...] = incoming(sides, 1 - lax.axis_index("row") % 2).reshape(out.shape)


def incoming_kernel(sides, from_other, out):
    own = incoming(sides, lax.axis_index("row") % 2).reshape(out.shape)
    out[...] = (own + from_other[...]).astype(BF16)


def call(kernel, outs, scratch, *args, place=pltpu.VMEM):
    in_vmem = pl.BlockSpec(memory_space=pltpu.VMEM)
    return pl.pallas_call(
        kernel,
        out_shape=[jax.ShapeDtypeStruct(*o) for o in outs],
        in_specs=[pl.BlockSpec(memory_space=place)] * len(args),
        out_specs=[in_vmem] * len(outs),
        scratch_shapes=scratch,
        compiler_params=pltpu.CompilerParams(vmem_limit_bytes=24 * 2**20),
    )(*args)


def exchange(blocks):
    return lax.all_to_all(blocks, PEERS, split_axis=0, concat_axis=0, tiled=True)


def among_chips(blocks):
    chips = blocks.shape[0]
    groups = [[2 * chip + core for chip in range(chips)] for core in range(2)]
    return lax.all_to_all(blocks, "row", split_axis=0, concat_axis=0, axis_index_groups=groups, tiled=True)


def to_other_core(chips, values):
    return lax.ppermute(values, "row", [(2 * chip + core, 2 * chip + 1 - core) for chip in range(chips) for core in range(2)])


def packed_updates(count, pair_rep, pair_mask, pw, pb, gw, gb, ow, ob, ns, no):
    rows_of, width, channels = pair_rep.shape
    chips, depth = count // 2, ROWS * OWN
    flat = (channels, rows_of * width)
    projected = [((chips, 2 * depth, width), BF16), (flat, F32), (flat, BF16)]
    summed = [((chips, depth, width), BF16)]
    params = [pair_rep, pair_mask, pw, gw, pb, gb, ob, ns, no]
    params = [pltpu.with_memory_space_constraint(v, pltpu.HBM) for v in params]
    held = [pltpu.VMEM(v.shape[1:] if n in (2, 3) else v.shape, v.dtype) for n, v in enumerate(params)]
    held += [pltpu.VMEM((2 * EACH, channels), F32), pltpu.SemaphoreType.DMA((len(params),))]
    kept = [((channels, 2 * EACH), F32), ((2 * ROWS, width), F32)]
    send, gate, turned, columns, keep = call(first_kernel, projected + kept, held, *params, place=pltpu.HBM)
    sides = among_chips(send)
    (send,) = call(outgoing_kernel, summed, [], sides, to_other_core(chips, sides[:, depth:]))
    send, gate, turned = call(middle_kernel, projected, [], among_chips(send), turned, gate, columns, keep, pw, gw, ow)
    sides = among_chips(send)
    (other,) = call(other_kernel, [(summed[0][0], F32)], [], sides)
    (send,) = call(incoming_kernel, summed, [], sides, to_other_core(chips, other))
    (out,) = call(last_kernel, [(pair_rep.shape, BF16)], [], among_chips(send), turned, gate, columns, ow)
    return out


def update(pair_t, pair_mask, u, incoming, peers, rows_of, pw, pb, gw, gb, ow, ob, ns, no):
    channels, positions = pair_t.shape
    width = positions // rows_of
    h = pw.shape[2] // 4
    count = peers[0] * peers[1]
    own = h // count
    normed = layer_norm(pair_t, ns[u, 0][:, None], no[u, 0][:, None]).astype(BF16)
    projected = over_rows(jnp.concatenate([pw[u], gw[u]], 1), normed) + jnp.concatenate([pb[u], gb[u]], 0)[:, None]
    parts = [projected[n * h : (n + 1) * h] for n in range(4)]
    gating = jax.nn.sigmoid(projected[4 * h :])
    mask = pair_mask.astype(F32).reshape(1, positions)
    left = (mask * jax.nn.sigmoid(parts[1]) * parts[0]).astype(BF16)
    right = (mask * jax.nn.sigmoid(parts[3]) * parts[2]).astype(BF16)
    sides = exchange(jnp.stack([v.reshape(count, own, rows_of, width) for v in (left, right)], 1))
    sides = sides.reshape(peers[0], peers[1], 2, own, rows_of, width)
    sides = sides.transpose(2, 3, 0, 4, 1, 5).reshape(2, own, peers[0] * rows_of, peers[1] * width)
    form = "cki,ckj->cij" if incoming else "cik,cjk->cij"
    summed = jnp.einsum(form, sides[0], sides[1], preferred_element_type=F32).astype(BF16)
    summed = summed.reshape(own, peers[0], rows_of, peers[1], width).transpose(1, 3, 0, 2, 4)
    summed = exchange(summed.reshape(count, own, rows_of, width)).reshape(h, positions).astype(F32)
    hidden = layer_norm(summed, ns[u, 1][:, None], no[u, 1][:, None]).astype(BF16)
    change = over_rows(ow[u], hidden) + ob[u][:, None]
    return (pair_t + gating * change).astype(BF16)


def plain_updates(peers, pair_rep, pair_mask, *params):
    rows_of, width, channels = pair_rep.shape
    pair_t = pair_rep.reshape(rows_of * width, channels).T
    for u in range(2):
        pair_t = update(pair_t.astype(F32), pair_mask, u, u == 1, peers, rows_of, *params)
    return pair_t.T.reshape(rows_of, width, channels)


def solution(mesh):
    peers = (mesh.shape["row"], mesh.shape["ka"])
    count = peers[0] * peers[1]

    def on_device(pair_rep, pair_mask, *params):
        rows_of, width, channels = pair_rep.shape
        hidden = params[0].shape[2] // 4
        fits = mesh.shape["grp"] == peers[1] == 1 and rows_of == ROWS and 2 * hidden == OWN * count
        if fits and channels == hidden == 128 and width % 128 == 0:
            return packed_updates(count, pair_rep, pair_mask, *params)
        return plain_updates(peers, pair_rep, pair_mask, *params)

    split = P(("grp", "row"), "ka", None)
    in_specs = (split, P(("grp", "row"), "ka")) + (P(),) * 8
    return jax.shard_map(on_device, mesh=mesh, in_specs=in_specs, out_specs=split, check_vma=False)
```

```python
import functools

import jax
import jax.numpy as jnp
from jax import lax
from jax.experimental import pallas as pl
from jax.experimental.pallas import tpu as pltpu
from jax.sharding import PartitionSpec as P

PEERS = ("row", "ka")
OWN = 4
PLANE = 8
EACH = 16
BF16, F32 = jnp.bfloat16, jnp.float32


def over_rows(a, b):
    return lax.dot_general(a, b, (((0,), (0,)), ((), ())), preferred_element_type=F32)


def over_columns(a, b):
    return lax.dot_general(a, b, (((1,), (1,)), ((), ())), preferred_element_type=F32)


def layer_norm(values, norm_gain, norm_bias):
    average = jnp.mean(values, 0, keepdims=True)
    centred = values - average
    variance = jnp.mean(centred * centred, 0, keepdims=True)
    return centred * lax.rsqrt(variance + 1e-05) * norm_gain + norm_bias


def pack(blocks):
    channels, width = blocks[0].shape
    tiles = [b.reshape(channels // 8, 8, width) for b in blocks]
    turned = [pltpu.roll(b, 4, axis=0).reshape(channels // 8, 8, width) for b in blocks]
    low = lax.broadcasted_iota(jnp.int32, tiles[0].shape, 1) < 4
    back = [pltpu.roll(b, channels - 4, axis=0).reshape(channels // 8, 8, width) for b in blocks]
    even = [jnp.where(low, tiles[n], turned[n + 1]) for n in (0, 2)]
    odd = [jnp.where(low, back[n], tiles[n + 1]) for n in (0, 2)]
    return jnp.stack([jnp.stack(even, 1), jnp.stack(odd, 1)], 1).reshape(channels // 4, 16, width)


def unpack(packed):
    count, _, width = packed.shape
    tiles = packed.reshape(count // 2, 2, 2, 8, width)
    low = lax.broadcasted_iota(jnp.int32, (count // 2, 8, width), 1) < 4
    blocks = []
    for n in range(2):
        even, odd = tiles[:, 0, n], tiles[:, 1, n]
        down = pltpu.roll(odd.reshape(count * 4, width), 4, axis=0).reshape(even.shape)
        up = pltpu.roll(even.reshape(count * 4, width), count * 4 - 4, axis=0).reshape(even.shape)
        blocks.append(jnp.where(low, even, down).reshape(count * 4, width))
        blocks.append(jnp.where(low, up, odd).reshape(count * 4, width))
    return blocks


def project(u, z, mask, proj_weight, gate_weight, columns, send, gate):
    width = z[0].shape[1]
    h = proj_weight.shape[1] // 4
    gain, offset, *biases = [columns[:, n : n + 1] for n in range(u * EACH, u * EACH + 7)]
    lefts, rights = [], []
    for i in range(OWN):
        normed = layer_norm(z[i], gain, offset).astype(BF16)
        projected = over_rows(proj_weight, normed)
        parts = [projected[n * h : (n + 1) * h] + biases[n] for n in range(4)]
        keep = mask[i : i + 1, :]
        lefts.append(keep * jax.nn.sigmoid(parts[1]) * parts[0])
        rights.append(keep * jax.nn.sigmoid(parts[3]) * parts[2])
        gate[:, i * width : (i + 1) * width] = jax.nn.sigmoid(over_rows(gate_weight, normed) + biases[4])
    send[:, 0:16, :] = pack(lefts).astype(BF16)
    send[:, 16:32, :] = pack(rights).astype(BF16)


def finish(u, i, z, block, gate, out_weight, columns):
    width = z.shape[1]
    gain, offset, bias = [columns[:, n : n + 1] for n in range(u * EACH + 7, u * EACH + 10)]
    hidden = layer_norm(block, gain, offset).astype(BF16)
    change = over_rows(out_weight, hidden) + bias
    return z + gate[:, i * width : (i + 1) * width] * change


def first_kernel(
    pair, mask, pw, gw, pb, gb, ob, ns, no, send, gate, turned, columns, keep, pair_in, mask_in, pw_in, gw_in, pb_in, gb_in, ob_in, ns_in, no_in, rows, arrived
):
    moves = [(pb, pb_in), (gb, gb_in), (ob, ob_in), (ns, ns_in), (no, no_in)]
    moves += [(pair, pair_in), (pw.at[0], pw_in), (gw.at[0], gw_in), (mask, mask_in)]
    moves = [pltpu.make_async_copy(a, b, arrived.at[n]) for n, (a, b) in enumerate(moves)]
    for move in moves:
        move.start()
    for move in moves[:5]:
        move.wait()
    h = pw.shape[2] // 4
    for u in range(2):
        found = [ns_in[u, 0:1, :], no_in[u, 0:1, :]] + [pb_in[u : u + 1, n * h : (n + 1) * h] for n in range(4)]
        found += [gb_in[u : u + 1, :], ns_in[u, 1:2, :], no_in[u, 1:2, :], ob_in[u : u + 1, :]]
        for n, row in enumerate(found):
            rows[u * EACH + n : u * EACH + n + 1, :] = row
    columns[...] = rows[...].T
    moves[5].wait()
    width = pair.shape[1]
    z = [pair_in[i].astype(F32).T for i in range(OWN)]
    for i in range(OWN):
        turned[:, i * width : (i + 1) * width] = z[i].astype(BF16)
    for move in moves[6:]:
        move.wait()
    keep[0:OWN, :] = mask_in[...].astype(F32)
    project(0, z, keep, pw_in[...], gw_in[...], columns, send, gate)


def middle_kernel(summed, old, old_gate, columns, mask, pw, gw, ow, send, gate, turned):
    width = mask.shape[1]
    z = []
    for i, block in enumerate(unpack(summed[...].astype(F32))):
        at = slice(i * width, (i + 1) * width)
        z.append(finish(0, i, old[:, at].astype(F32), block, old_gate, ow[0], columns).astype(BF16))
        turned[:, at] = z[i]
    project(1, [v.astype(F32) for v in z], mask, pw[1], gw[1], columns, send, gate)


def last_kernel(summed, old, old_gate, columns, ow, out):
    width = out.shape[1]
    for i, block in enumerate(unpack(summed[...].astype(F32))):
        z = old[:, i * width : (i + 1) * width].astype(F32)
        out[i] = finish(1, i, z, block, old_gate, ow[1], columns).T.astype(BF16)


def triangle_kernel(incoming, sides, out):
    count, _, width = sides.shape
    rows = count * 16
    left, right = [sides[:, n : n + 16, :].reshape(rows, width) for n in (0, 16)]
    down = lax.broadcasted_iota(jnp.int32, (rows, width), 0)
    across = lax.broadcasted_iota(jnp.int32, (rows, width), 1)
    device, residue = down // (OWN * OWN), down // OWN % OWN
    planes = count // PLANE
    device = device % planes * PLANE + device // planes
    spread = jnp.where(device * OWN + residue == across, 1.0, 0.0).astype(BF16)
    both = over_columns(spread, left) if incoming else over_columns(left, right)
    channel = [lax.broadcasted_iota(jnp.int32, (rows, rows), d) % OWN for d in (0, 1)]
    both = jnp.where(channel[0] == channel[1], both, 0.0).astype(BF16)
    summed = jnp.dot(both, right if incoming else spread, preferred_element_type=F32)
    out[...] = summed.astype(BF16).reshape(count, 16, width)


def call(kernel, outs, scratch, *args, place=pltpu.VMEM):
    in_vmem = pl.BlockSpec(memory_space=pltpu.VMEM)
    return pl.pallas_call(
        kernel,
        out_shape=[jax.ShapeDtypeStruct(*o) for o in outs],
        in_specs=[pl.BlockSpec(memory_space=place)] * len(args),
        out_specs=[in_vmem] * len(outs),
        scratch_shapes=scratch,
        compiler_params=pltpu.CompilerParams(vmem_limit_bytes=24 * 2**20),
    )(*args)


def exchange(blocks):
    return lax.all_to_all(blocks, PEERS, split_axis=0, concat_axis=0, tiled=True)


def swap(blocks, outer):
    count = blocks.shape[0]
    return blocks.reshape(outer, count // outer, *blocks.shape[1:]).swapaxes(0, 1).reshape(blocks.shape)


def along_z(blocks):
    planes = blocks.shape[0] // PLANE
    groups = [[PLANE * z + p for z in range(planes)] for p in range(PLANE)]
    return among(blocks, groups)


def in_plane(blocks):
    planes = blocks.shape[0] // PLANE
    return among(blocks, [[PLANE * z + p for p in range(PLANE)] for z in range(planes)])


def among(blocks, groups):
    joined = blocks.reshape(len(groups[0]), -1, blocks.shape[2])
    joined = lax.all_to_all(joined, "row", split_axis=0, concat_axis=0, axis_index_groups=groups, tiled=True)
    return joined.reshape(blocks.shape)


def to_channels(blocks):
    return in_plane(swap(along_z(blocks), blocks.shape[0] // PLANE))


def to_rows(blocks):
    return along_z(swap(in_plane(blocks), PLANE))


def packed_updates(count, pair_rep, pair_mask, pw, pb, gw, gb, ow, ob, ns, no):
    rows_of, width, channels = pair_rep.shape
    flat = (channels, rows_of * width)
    projected = [((count, 32, width), BF16), (flat, F32), (flat, BF16)]
    summed = [((count, 16, width), BF16)]
    params = [pair_rep, pair_mask, pw, gw, pb, gb, ob, ns, no]
    params = [pltpu.with_memory_space_constraint(v, pltpu.HBM) for v in params]
    held = [pltpu.VMEM(v.shape[1:] if n in (2, 3) else v.shape, v.dtype) for n, v in enumerate(params)]
    held += [pltpu.VMEM((2 * EACH, channels), F32), pltpu.SemaphoreType.DMA((len(params),))]
    kept = [((channels, 2 * EACH), F32), ((2 * OWN, width), F32)]
    send, gate, turned, columns, keep = call(first_kernel, projected + kept, held, *params, place=pltpu.HBM)
    (send,) = call(functools.partial(triangle_kernel, False), summed, [], to_channels(send))
    send, gate, turned = call(middle_kernel, projected, [], to_rows(send), turned, gate, columns, keep, pw, gw, ow)
    (send,) = call(functools.partial(triangle_kernel, True), summed, [], to_channels(send))
    (out,) = call(last_kernel, [(pair_rep.shape, BF16)], [], to_rows(send), turned, gate, columns, ow)
    return out


def update(pair_t, pair_mask, u, incoming, peers, rows_of, pw, pb, gw, gb, ow, ob, ns, no):
    channels, positions = pair_t.shape
    width = positions // rows_of
    h = pw.shape[2] // 4
    count = peers[0] * peers[1]
    own = h // count
    normed = layer_norm(pair_t, ns[u, 0][:, None], no[u, 0][:, None]).astype(BF16)
    projected = over_rows(jnp.concatenate([pw[u], gw[u]], 1), normed) + jnp.concatenate([pb[u], gb[u]], 0)[:, None]
    parts = [projected[n * h : (n + 1) * h] for n in range(4)]
    gating = jax.nn.sigmoid(projected[4 * h :])
    mask = pair_mask.astype(F32).reshape(1, positions)
    left = (mask * jax.nn.sigmoid(parts[1]) * parts[0]).astype(BF16)
    right = (mask * jax.nn.sigmoid(parts[3]) * parts[2]).astype(BF16)
    sides = exchange(jnp.stack([v.reshape(count, own, rows_of, width) for v in (left, right)], 1))
    sides = sides.reshape(peers[0], peers[1], 2, own, rows_of, width)
    sides = sides.transpose(2, 3, 0, 4, 1, 5).reshape(2, own, peers[0] * rows_of, peers[1] * width)
    form = "cki,ckj->cij" if incoming else "cik,cjk->cij"
    summed = jnp.einsum(form, sides[0], sides[1], preferred_element_type=F32).astype(BF16)
    summed = summed.reshape(own, peers[0], rows_of, peers[1], width).transpose(1, 3, 0, 2, 4)
    summed = exchange(summed.reshape(count, own, rows_of, width)).reshape(h, positions).astype(F32)
    hidden = layer_norm(summed, ns[u, 1][:, None], no[u, 1][:, None]).astype(BF16)
    change = over_rows(ow[u], hidden) + ob[u][:, None]
    return (pair_t + gating * change).astype(BF16)


def plain_updates(peers, pair_rep, pair_mask, *params):
    rows_of, width, channels = pair_rep.shape
    pair_t = pair_rep.reshape(rows_of * width, channels).T
    for u in range(2):
        pair_t = update(pair_t.astype(F32), pair_mask, u, u == 1, peers, rows_of, *params)
    return pair_t.T.reshape(rows_of, width, channels)


def solution(mesh):
    peers = (mesh.shape["row"], mesh.shape["ka"])
    count = peers[0] * peers[1]

    def on_device(pair_rep, pair_mask, *params):
        rows_of, width, channels = pair_rep.shape
        hidden = params[0].shape[2] // 4
        fits = peers[1] == 1 and rows_of == OWN and hidden == OWN * count and count % PLANE == 0
        if fits and channels == hidden == 128 and width % 128 == 0:
            return packed_updates(count, pair_rep, pair_mask, *params)
        return plain_updates(peers, pair_rep, pair_mask, *params)

    split = P(("grp", "row"), "ka", None)
    in_specs = (split, P(("grp", "row"), "ka")) + (P(),) * 8
    return jax.shard_map(on_device, mesh=mesh, in_specs=in_specs, out_specs=split, check_vma=False)
```

```python
import functools

import jax
import jax.numpy as jnp
from jax import lax
from jax.experimental import pallas as pl
from jax.experimental.pallas import tpu as pltpu
from jax.sharding import PartitionSpec as P

PEERS = ("row", "ka")
OWN = 4
EACH = 16
BF16, F32 = jnp.bfloat16, jnp.float32


def over_rows(a, b):
    return lax.dot_general(a, b, (((0,), (0,)), ((), ())), preferred_element_type=F32)


def over_columns(a, b):
    return lax.dot_general(a, b, (((1,), (1,)), ((), ())), preferred_element_type=F32)


def layer_norm(values, norm_gain, norm_bias):
    average = jnp.mean(values, 0, keepdims=True)
    centred = values - average
    variance = jnp.mean(centred * centred, 0, keepdims=True)
    return centred * lax.rsqrt(variance + 1e-05) * norm_gain + norm_bias


def pack(blocks):
    channels, width = blocks[0].shape
    tiles = [b.reshape(channels // 8, 8, width) for b in blocks]
    turned = [pltpu.roll(b, 4, axis=0).reshape(channels // 8, 8, width) for b in blocks]
    low = lax.broadcasted_iota(jnp.int32, tiles[0].shape, 1) < 4
    back = [pltpu.roll(b, channels - 4, axis=0).reshape(channels // 8, 8, width) for b in blocks]
    even = [jnp.where(low, tiles[n], turned[n + 1]) for n in (0, 2)]
    odd = [jnp.where(low, back[n], tiles[n + 1]) for n in (0, 2)]
    return jnp.stack([jnp.stack(even, 1), jnp.stack(odd, 1)], 1).reshape(channels // 4, 16, width)


def unpack(packed):
    count, _, width = packed.shape
    tiles = packed.reshape(count // 2, 2, 2, 8, width)
    low = lax.broadcasted_iota(jnp.int32, (count // 2, 8, width), 1) < 4
    blocks = []
    for n in range(2):
        even, odd = tiles[:, 0, n], tiles[:, 1, n]
        down = pltpu.roll(odd.reshape(count * 4, width), 4, axis=0).reshape(even.shape)
        up = pltpu.roll(even.reshape(count * 4, width), count * 4 - 4, axis=0).reshape(even.shape)
        blocks.append(jnp.where(low, even, down).reshape(count * 4, width))
        blocks.append(jnp.where(low, up, odd).reshape(count * 4, width))
    return blocks


def sigmoid(x):
    return 0.5 * jnp.tanh(0.5 * x) + 0.5


def broadcast_columns(columns, first, many, width):
    held = columns[...]
    return [jnp.broadcast_to(held[:, n : n + 1], (held.shape[0], width)) for n in range(first, first + many)]


def project(u, z, mask, proj_weight, gate_weight, columns, send, gate):
    width = z[0].shape[1]
    h = proj_weight.shape[1] // 4
    gain, offset, *biases = broadcast_columns(columns, u * EACH, 7, width)
    turned = [proj_weight[:, n * h : (n + 1) * h].T for n in range(4)] + [gate_weight.T]
    lefts, rights = [], []
    for i in range(OWN):
        normed = layer_norm(z[i], gain, offset).astype(BF16)
        parts = [jnp.dot(w, normed, preferred_element_type=F32) + b for w, b in zip(turned, biases)]
        keep = mask[i : i + 1, :]
        lefts.append(keep * sigmoid(parts[1]) * parts[0])
        rights.append(keep * sigmoid(parts[3]) * parts[2])
        gate[:, i * width : (i + 1) * width] = sigmoid(parts[4])
    send[:, 0:16, :] = pack(lefts).astype(BF16)
    send[:, 16:32, :] = pack(rights).astype(BF16)


def finish(u, z, summed, gate, out_weight, columns):
    width = z[0].shape[1]
    gain, offset, bias = broadcast_columns(columns, u * EACH + 7, 3, width)
    turned = out_weight.T
    results = []
    for i, block in enumerate(unpack(summed[...].astype(F32))):
        hidden = layer_norm(block, gain, offset).astype(BF16)
        change = jnp.dot(turned, hidden, preferred_element_type=F32) + bias
        results.append((z[i].astype(F32) + gate[:, i * width : (i + 1) * width] * change).astype(BF16))
    return results


def first_kernel(
    pair, mask, pw, gw, pb, gb, ob, ns, no, send, gate, turned, columns, keep, pair_in, mask_in, pw_in, gw_in, pb_in, gb_in, ob_in, ns_in, no_in, rows, arrived
):
    moves = [(pair, pair_in), (pb, pb_in), (gb, gb_in), (ob, ob_in), (ns, ns_in), (no, no_in)]
    moves += [(pw.at[0], pw_in), (gw.at[0], gw_in), (mask, mask_in)]
    moves = [pltpu.make_async_copy(a, b, arrived.at[n]) for n, (a, b) in enumerate(moves)]
    for move in moves:
        move.start()
    moves[0].wait()
    width = pair.shape[1]
    z = [pair_in[i].T for i in range(OWN)]
    for i in range(OWN):
        turned[:, i * width : (i + 1) * width] = z[i]
    for move in moves[1:6]:
        move.wait()
    h = pw.shape[2] // 4
    for u in range(2):
        found = [ns_in[u, 0:1, :], no_in[u, 0:1, :]] + [pb_in[u : u + 1, n * h : (n + 1) * h] for n in range(4)]
        found += [gb_in[u : u + 1, :], ns_in[u, 1:2, :], no_in[u, 1:2, :], ob_in[u : u + 1, :]]
        for n, row in enumerate(found):
            rows[u * EACH + n : u * EACH + n + 1, :] = row
    columns[...] = rows[...].T
    for move in moves[6:]:
        move.wait()
    keep[0:OWN, :] = mask_in[...].astype(F32)
    project(0, [v.astype(F32) for v in z], keep, pw_in[...], gw_in[...], columns, send, gate)


def middle_kernel(summed, old, old_gate, columns, keep, pw, gw, ow, send, gate, turned):
    width = keep.shape[1]
    z = finish(0, [old[:, i * width : (i + 1) * width] for i in range(OWN)], summed, old_gate, ow[0], columns)
    for i in range(OWN):
        turned[:, i * width : (i + 1) * width] = z[i]
    project(1, [v.astype(F32) for v in z], keep, pw[1], gw[1], columns, send, gate)


def last_kernel(summed, old, old_gate, columns, ow, out):
    width = out.shape[1]
    z = finish(1, [old[:, i * width : (i + 1) * width] for i in range(OWN)], summed, old_gate, ow[1], columns)
    for i in range(OWN):
        out[i] = z[i].T


def triangle_kernel(incoming, sides, out):
    count, _, width = sides.shape
    rows = count * 16
    left, right = [sides[:, n : n + 16, :].reshape(rows, width) for n in (0, 16)]
    down = lax.broadcasted_iota(jnp.int32, (rows, width), 0)
    across = lax.broadcasted_iota(jnp.int32, (rows, width), 1)
    spread = jnp.where((down >> 2) == across, 1.0, 0.0).astype(BF16)
    both = over_columns(spread, left) if incoming else over_columns(left, right)
    down = lax.broadcasted_iota(jnp.int32, (8, rows), 0)
    across = lax.broadcasted_iota(jnp.int32, (8, rows), 1)
    same = ((down ^ across) & 3) == 0
    both = jnp.where(same[None], both.reshape(rows // 8, 8, rows), 0.0).reshape(rows, rows).astype(BF16)
    summed = jnp.dot(both, right if incoming else spread, preferred_element_type=F32)
    out[...] = summed.astype(BF16).reshape(count, 16, width)


def call(kernel, outs, scratch, *args, place=pltpu.VMEM):
    in_vmem = pl.BlockSpec(memory_space=pltpu.VMEM)
    return pl.pallas_call(
        kernel,
        out_shape=[jax.ShapeDtypeStruct(*o) for o in outs],
        in_specs=[pl.BlockSpec(memory_space=place)] * len(args),
        out_specs=[in_vmem] * len(outs),
        scratch_shapes=scratch,
        compiler_params=pltpu.CompilerParams(vmem_limit_bytes=24 * 2**20),
    )(*args)


def exchange(blocks):
    return lax.all_to_all(blocks, PEERS, split_axis=0, concat_axis=0, tiled=True)


def packed_updates(count, pair_rep, pair_mask, pw, pb, gw, gb, ow, ob, ns, no):
    rows_of, width, channels = pair_rep.shape
    flat = (channels, rows_of * width)
    projected = [((count, 32, width), BF16), (flat, F32), (flat, BF16)]
    summed = [((count, 16, width), BF16)]
    params = [pair_rep, pair_mask, pw, gw, pb, gb, ob, ns, no]
    params = [pltpu.with_memory_space_constraint(v, pltpu.HBM) for v in params]
    held = [pltpu.VMEM(v.shape[1:] if n in (2, 3) else v.shape, v.dtype) for n, v in enumerate(params)]
    held += [pltpu.VMEM((2 * EACH, channels), F32), pltpu.SemaphoreType.DMA((len(params),))]
    kept = [((channels, 2 * EACH), F32), ((2 * OWN, width), F32)]
    send, gate, turned, columns, keep = call(first_kernel, projected + kept, held, *params, place=pltpu.HBM)
    (send,) = call(functools.partial(triangle_kernel, False), summed, [], exchange(send))
    send, gate, turned = call(middle_kernel, projected, [], exchange(send), turned, gate, columns, keep, pw, gw, ow)
    (send,) = call(functools.partial(triangle_kernel, True), summed, [], exchange(send))
    (out,) = call(last_kernel, [(pair_rep.shape, BF16)], [], exchange(send), turned, gate, columns, ow)
    return out


def update(pair_t, pair_mask, u, incoming, peers, rows_of, pw, pb, gw, gb, ow, ob, ns, no):
    channels, positions = pair_t.shape
    width = positions // rows_of
    h = pw.shape[2] // 4
    count = peers[0] * peers[1]
    own = h // count
    normed = layer_norm(pair_t, ns[u, 0][:, None], no[u, 0][:, None]).astype(BF16)
    projected = over_rows(jnp.concatenate([pw[u], gw[u]], 1), normed) + jnp.concatenate([pb[u], gb[u]], 0)[:, None]
    parts = [projected[n * h : (n + 1) * h] for n in range(4)]
    gating = jax.nn.sigmoid(projected[4 * h :])
    mask = pair_mask.astype(F32).reshape(1, positions)
    left = (mask * jax.nn.sigmoid(parts[1]) * parts[0]).astype(BF16)
    right = (mask * jax.nn.sigmoid(parts[3]) * parts[2]).astype(BF16)
    sides = exchange(jnp.stack([v.reshape(count, own, rows_of, width) for v in (left, right)], 1))
    sides = sides.reshape(peers[0], peers[1], 2, own, rows_of, width)
    sides = sides.transpose(2, 3, 0, 4, 1, 5).reshape(2, own, peers[0] * rows_of, peers[1] * width)
    form = "cki,ckj->cij" if incoming else "cik,cjk->cij"
    summed = jnp.einsum(form, sides[0], sides[1], preferred_element_type=F32).astype(BF16)
    summed = summed.reshape(own, peers[0], rows_of, peers[1], width).transpose(1, 3, 0, 2, 4)
    summed = exchange(summed.reshape(count, own, rows_of, width)).reshape(h, positions).astype(F32)
    hidden = layer_norm(summed, ns[u, 1][:, None], no[u, 1][:, None]).astype(BF16)
    change = over_rows(ow[u], hidden) + ob[u][:, None]
    return (pair_t + gating * change).astype(BF16)


def plain_updates(peers, pair_rep, pair_mask, *params):
    rows_of, width, channels = pair_rep.shape
    pair_t = pair_rep.reshape(rows_of * width, channels).T
    for u in range(2):
        pair_t = update(pair_t.astype(F32), pair_mask, u, u == 1, peers, rows_of, *params)
    return pair_t.T.reshape(rows_of, width, channels)


def solution(mesh):
    peers = (mesh.shape["row"], mesh.shape["ka"])
    count = peers[0] * peers[1]

    def on_device(pair_rep, pair_mask, *params):
        rows_of, width, channels = pair_rep.shape
        hidden = params[0].shape[2] // 4
        fits = peers[1] == 1 and rows_of == OWN and hidden == OWN * count and count % 2 == 0
        if fits and channels == hidden == 128 and width % 128 == 0:
            return packed_updates(count, pair_rep, pair_mask, *params)
        return plain_updates(peers, pair_rep, pair_mask, *params)

    split = P(("grp", "row"), "ka", None)
    in_specs = (split, P(("grp", "row"), "ka")) + (P(),) * 8
    return jax.shard_map(on_device, mesh=mesh, in_specs=in_specs, out_specs=split, check_vma=False)
```

```python
import functools

import jax
import jax.numpy as jnp
from jax import lax
from jax.experimental import pallas as pl
from jax.experimental.pallas import tpu as pltpu
from jax.sharding import PartitionSpec as P

PEERS = ("row", "ka")
OWN = 4
EACH = 16
BF16, F32 = jnp.bfloat16, jnp.float32


def over_rows(a, b):
    return lax.dot_general(a, b, (((0,), (0,)), ((), ())), preferred_element_type=F32)


def over_columns(a, b):
    return lax.dot_general(a, b, (((1,), (1,)), ((), ())), preferred_element_type=F32)


def layer_norm(values, norm_gain, norm_bias):
    average = jnp.mean(values, 0, keepdims=True)
    centred = values - average
    variance = jnp.mean(centred * centred, 0, keepdims=True)
    return centred * lax.rsqrt(variance + 1e-05) * norm_gain + norm_bias


def pack(blocks):
    channels, width = blocks[0].shape
    tiles = [b.reshape(channels // 8, 8, width) for b in blocks]
    turned = [pltpu.roll(b, 4, axis=0).reshape(channels // 8, 8, width) for b in blocks]
    low = lax.broadcasted_iota(jnp.int32, tiles[0].shape, 1) < 4
    back = [pltpu.roll(b, channels - 4, axis=0).reshape(channels // 8, 8, width) for b in blocks]
    even = [jnp.where(low, tiles[n], turned[n + 1]) for n in (0, 2)]
    odd = [jnp.where(low, back[n], tiles[n + 1]) for n in (0, 2)]
    return jnp.stack([jnp.stack(even, 1), jnp.stack(odd, 1)], 1).reshape(channels // 4, 16, width)


def unpack(packed):
    count, _, width = packed.shape
    tiles = packed.reshape(count // 2, 2, 2, 8, width)
    low = lax.broadcasted_iota(jnp.int32, (count // 2, 8, width), 1) < 4
    blocks = []
    for n in range(2):
        even, odd = tiles[:, 0, n], tiles[:, 1, n]
        down = pltpu.roll(odd.reshape(count * 4, width), 4, axis=0).reshape(even.shape)
        up = pltpu.roll(even.reshape(count * 4, width), count * 4 - 4, axis=0).reshape(even.shape)
        blocks.append(jnp.where(low, even, down).reshape(count * 4, width))
        blocks.append(jnp.where(low, up, odd).reshape(count * 4, width))
    return blocks


def sigmoid(x):
    return 0.5 * jnp.tanh(0.5 * x) + 0.5


def broadcast_columns(columns, first, many, width):
    held = columns[...]
    return [jnp.broadcast_to(held[:, n : n + 1], (held.shape[0], width)) for n in range(first, first + many)]


def project(u, z, mask, proj_weight, gate_weight, columns, send, gate, mixed):
    width = z[0].shape[1]
    h = proj_weight.shape[1] // 4
    rows = mixed.shape[1]
    gain, offset, *biases = broadcast_columns(columns, u * EACH, 7, width)
    turned = [proj_weight[:, n * h : (n + 1) * h].T for n in range(4)] + [gate_weight.T]
    for pair in range(0, OWN, 2):
        normed = [layer_norm(z[i], gain, offset).astype(BF16) for i in (pair, pair + 1)]
        normed = jnp.concatenate(normed, 1)
        both = [jnp.dot(w, normed, preferred_element_type=F32) for w in turned]
        for n in range(2):
            i = pair + n
            parts = [v[:, n * width : (n + 1) * width] + b for v, b in zip(both, biases)]
            keep = mask[i : i + 1, :]
            mixed[0, pl.ds(i, h, stride=OWN), :] = keep * sigmoid(parts[1]) * parts[0]
            mixed[1, pl.ds(i, h, stride=OWN), :] = keep * sigmoid(parts[3]) * parts[2]
            gate[:, i * width : (i + 1) * width] = sigmoid(parts[4])
    send[:, 0:16, :] = mixed[0].reshape(rows // 16, 16, width).astype(BF16)
    send[:, 16:32, :] = mixed[1].reshape(rows // 16, 16, width).astype(BF16)


def finish(u, z, summed, gate, out_weight, columns, mixed):
    width = z[0].shape[1]
    gain, offset, bias = broadcast_columns(columns, u * EACH + 7, 3, width)
    turned = out_weight.T
    mixed[...] = summed[...].astype(F32).reshape(mixed.shape)
    results = []
    for pair in range(0, OWN, 2):
        blocks = [mixed[pl.ds(i, mixed.shape[0] // OWN, stride=OWN), :] for i in (pair, pair + 1)]
        hidden = jnp.concatenate([layer_norm(v, gain, offset).astype(BF16) for v in blocks], 1)
        both = jnp.dot(turned, hidden, preferred_element_type=F32)
        for n in range(2):
            change = both[:, n * width : (n + 1) * width] + bias
            at = slice((pair + n) * width, (pair + n + 1) * width)
            results.append((z[pair + n].astype(F32) + gate[:, at] * change).astype(BF16))
    return results


def first_kernel(
    pair, mask, pw, gw, pb, gb, ob, ns, no, send, gate, turned, columns, keep, pair_in, mask_in, pw_in, gw_in, pb_in, gb_in, ob_in, ns_in, no_in, rows, arrived, mixed
):
    moves = [(pair, pair_in), (pb, pb_in), (gb, gb_in), (ob, ob_in), (ns, ns_in), (no, no_in)]
    moves += [(pw.at[0], pw_in), (gw.at[0], gw_in), (mask, mask_in)]
    moves = [pltpu.make_async_copy(a, b, arrived.at[n]) for n, (a, b) in enumerate(moves)]
    for move in moves:
        move.start()
    moves[0].wait()
    width = pair.shape[1]
    z = [pair_in[i].T for i in range(OWN)]
    for i in range(OWN):
        turned[:, i * width : (i + 1) * width] = z[i]
    for move in moves[1:6]:
        move.wait()
    h = pw.shape[2] // 4
    for u in range(2):
        found = [ns_in[u, 0:1, :], no_in[u, 0:1, :]] + [pb_in[u : u + 1, n * h : (n + 1) * h] for n in range(4)]
        found += [gb_in[u : u + 1, :], ns_in[u, 1:2, :], no_in[u, 1:2, :], ob_in[u : u + 1, :]]
        for n, row in enumerate(found):
            rows[u * EACH + n : u * EACH + n + 1, :] = row
    columns[...] = rows[...].T
    for move in moves[6:]:
        move.wait()
    keep[0:OWN, :] = mask_in[...].astype(F32)
    project(0, [v.astype(F32) for v in z], keep, pw_in[...], gw_in[...], columns, send, gate, mixed)


def middle_kernel(summed, old, old_gate, columns, keep, pw, gw, ow, send, gate, turned, mixed, mixed_back):
    width = keep.shape[1]
    z = finish(0, [old[:, i * width : (i + 1) * width] for i in range(OWN)], summed, old_gate, ow[0], columns, mixed_back)
    for i in range(OWN):
        turned[:, i * width : (i + 1) * width] = z[i]
    project(1, [v.astype(F32) for v in z], keep, pw[1], gw[1], columns, send, gate, mixed)


def last_kernel(summed, old, old_gate, columns, ow, out, mixed_back):
    width = out.shape[1]
    z = finish(1, [old[:, i * width : (i + 1) * width] for i in range(OWN)], summed, old_gate, ow[1], columns, mixed_back)
    for i in range(OWN):
        out[i] = z[i].T


def triangle_kernel(incoming, sides, out):
    left, right = [unpack(sides[:, n : n + 16, :].astype(F32)) for n in (0, 16)]
    product = over_rows if incoming else over_columns
    out[...] = pack([product(a.astype(BF16), b.astype(BF16)) for a, b in zip(left, right)]).astype(BF16)


def call(kernel, outs, scratch, *args, place=pltpu.VMEM):
    in_vmem = pl.BlockSpec(memory_space=pltpu.VMEM)
    return pl.pallas_call(
        kernel,
        out_shape=[jax.ShapeDtypeStruct(*o) for o in outs],
        in_specs=[pl.BlockSpec(memory_space=place)] * len(args),
        out_specs=[in_vmem] * len(outs),
        scratch_shapes=scratch,
        compiler_params=pltpu.CompilerParams(vmem_limit_bytes=24 * 2**20),
    )(*args)


def exchange(blocks):
    return lax.all_to_all(blocks, PEERS, split_axis=0, concat_axis=0, tiled=True)


def packed_updates(count, pair_rep, pair_mask, pw, pb, gw, gb, ow, ob, ns, no):
    rows_of, width, channels = pair_rep.shape
    flat = (channels, rows_of * width)
    projected = [((count, 32, width), BF16), (flat, F32), (flat, BF16)]
    summed = [((count, 16, width), BF16)]
    params = [pair_rep, pair_mask, pw, gw, pb, gb, ob, ns, no]
    params = [pltpu.with_memory_space_constraint(v, pltpu.HBM) for v in params]
    held = [pltpu.VMEM(v.shape[1:] if n in (2, 3) else v.shape, v.dtype) for n, v in enumerate(params)]
    held += [pltpu.VMEM((2 * EACH, channels), F32), pltpu.SemaphoreType.DMA((len(params),))]
    back = pltpu.VMEM((OWN * channels, width), F32)
    mixed = pltpu.VMEM((2, OWN * channels, width), F32)
    kept = [((channels, 2 * EACH), F32), ((2 * OWN, width), F32)]
    send, gate, turned, columns, keep = call(first_kernel, projected + kept, held + [mixed], *params, place=pltpu.HBM)
    (send,) = call(functools.partial(triangle_kernel, False), summed, [], exchange(send))
    send, gate, turned = call(middle_kernel, projected, [mixed, back], exchange(send), turned, gate, columns, keep, pw, gw, ow)
    (send,) = call(functools.partial(triangle_kernel, True), summed, [], exchange(send))
    (out,) = call(last_kernel, [(pair_rep.shape, BF16)], [back], exchange(send), turned, gate, columns, ow)
    return out


def update(pair_t, pair_mask, u, incoming, peers, rows_of, pw, pb, gw, gb, ow, ob, ns, no):
    channels, positions = pair_t.shape
    width = positions // rows_of
    h = pw.shape[2] // 4
    count = peers[0] * peers[1]
    own = h // count
    normed = layer_norm(pair_t, ns[u, 0][:, None], no[u, 0][:, None]).astype(BF16)
    projected = over_rows(jnp.concatenate([pw[u], gw[u]], 1), normed) + jnp.concatenate([pb[u], gb[u]], 0)[:, None]
    parts = [projected[n * h : (n + 1) * h] for n in range(4)]
    gating = jax.nn.sigmoid(projected[4 * h :])
    mask = pair_mask.astype(F32).reshape(1, positions)
    left = (mask * jax.nn.sigmoid(parts[1]) * parts[0]).astype(BF16)
    right = (mask * jax.nn.sigmoid(parts[3]) * parts[2]).astype(BF16)
    sides = exchange(jnp.stack([v.reshape(count, own, rows_of, width) for v in (left, right)], 1))
    sides = sides.reshape(peers[0], peers[1], 2, own, rows_of, width)
    sides = sides.transpose(2, 3, 0, 4, 1, 5).reshape(2, own, peers[0] * rows_of, peers[1] * width)
    form = "cki,ckj->cij" if incoming else "cik,cjk->cij"
    summed = jnp.einsum(form, sides[0], sides[1], preferred_element_type=F32).astype(BF16)
    summed = summed.reshape(own, peers[0], rows_of, peers[1], width).transpose(1, 3, 0, 2, 4)
    summed = exchange(summed.reshape(count, own, rows_of, width)).reshape(h, positions).astype(F32)
    hidden = layer_norm(summed, ns[u, 1][:, None], no[u, 1][:, None]).astype(BF16)
    change = over_rows(ow[u], hidden) + ob[u][:, None]
    return (pair_t + gating * change).astype(BF16)


def plain_updates(peers, pair_rep, pair_mask, *params):
    rows_of, width, channels = pair_rep.shape
    pair_t = pair_rep.reshape(rows_of * width, channels).T
    for u in range(2):
        pair_t = update(pair_t.astype(F32), pair_mask, u, u == 1, peers, rows_of, *params)
    return pair_t.T.reshape(rows_of, width, channels)


def solution(mesh):
    peers = (mesh.shape["row"], mesh.shape["ka"])
    count = peers[0] * peers[1]

    def on_device(pair_rep, pair_mask, *params):
        rows_of, width, channels = pair_rep.shape
        hidden = params[0].shape[2] // 4
        fits = peers[1] == 1 and rows_of == OWN and hidden == OWN * count and count % 2 == 0
        if fits and channels == hidden == 128 and width % 128 == 0:
            return packed_updates(count, pair_rep, pair_mask, *params)
        return plain_updates(peers, pair_rep, pair_mask, *params)

    split = P(("grp", "row"), "ka", None)
    in_specs = (split, P(("grp", "row"), "ka")) + (P(),) * 8
    return jax.shard_map(on_device, mesh=mesh, in_specs=in_specs, out_specs=split, check_vma=False)
```

```python
import functools

import jax
import jax.numpy as jnp
from jax import lax
from jax.experimental import pallas as pl
from jax.experimental.pallas import tpu as pltpu
from jax.sharding import PartitionSpec as P

PEERS = ("row", "ka")
OWN = 4
EACH = 16
BF16, F32 = jnp.bfloat16, jnp.float32


def over_rows(a, b):
    return lax.dot_general(a, b, (((0,), (0,)), ((), ())), preferred_element_type=F32)


def over_columns(a, b):
    return lax.dot_general(a, b, (((1,), (1,)), ((), ())), preferred_element_type=F32)


def layer_norm(values, norm_gain, norm_bias):
    average = jnp.mean(values, 0, keepdims=True)
    centred = values - average
    variance = jnp.mean(centred * centred, 0, keepdims=True)
    return centred * lax.rsqrt(variance + 1e-05) * norm_gain + norm_bias


def pack(blocks):
    channels, width = blocks[0].shape
    tiles = [b.reshape(channels // 8, 8, width) for b in blocks]
    turned = [pltpu.roll(b, 4, axis=0).reshape(channels // 8, 8, width) for b in blocks]
    low = lax.broadcasted_iota(jnp.int32, tiles[0].shape, 1) < 4
    back = [pltpu.roll(b, channels - 4, axis=0).reshape(channels // 8, 8, width) for b in blocks]
    even = [jnp.where(low, tiles[n], turned[n + 1]) for n in (0, 2)]
    odd = [jnp.where(low, back[n], tiles[n + 1]) for n in (0, 2)]
    return jnp.stack([jnp.stack(even, 1), jnp.stack(odd, 1)], 1).reshape(channels // 4, 16, width)


def unpack(packed):
    count, _, width = packed.shape
    tiles = packed.reshape(count // 2, 2, 2, 8, width)
    low = lax.broadcasted_iota(jnp.int32, (count // 2, 8, width), 1) < 4
    blocks = []
    for n in range(2):
        even, odd = tiles[:, 0, n], tiles[:, 1, n]
        down = pltpu.roll(odd.reshape(count * 4, width), 4, axis=0).reshape(even.shape)
        up = pltpu.roll(even.reshape(count * 4, width), count * 4 - 4, axis=0).reshape(even.shape)
        blocks.append(jnp.where(low, even, down).reshape(count * 4, width))
        blocks.append(jnp.where(low, up, odd).reshape(count * 4, width))
    return blocks


def place():
    index = lax.axis_index("row")
    return index >> 3, (index >> 1) & 3, index & 1


def device(z, chip, core):
    return z * 8 + chip * 2 + core


def arrived_blocks(me, near, far):
    z, chip, core = me
    for m in range(4):
        for n in range(4):
            yield (z ^ n, chip ^ m, core), near[m][core, n]
            yield (z ^ n, chip ^ m, core ^ 1), far[m, n]


def to_planes(blocks, outs):
    z, _, _ = place()
    for m in range(4):
        outs[m][...] = blocks[pl.ds(pl.multiple_of((z ^ m) * 8, 8), 8)]


def to_chips_kernel(z0, z1, z2, z3, *outs):
    _, chip, _ = place()
    for m in range(4):
        for n, came in enumerate((z0, z1, z2, z3)):
            for core in range(2):
                outs[m][core, n] = came[(chip ^ m) * 2 + core]


def to_core_kernel(c0, c1, c2, c3, out):
    _, _, core = place()
    for m, came in enumerate((c0, c1, c2, c3)):
        out[m] = came[core ^ 1]


def sigmoid(x):
    return 0.5 * jnp.tanh(0.5 * x) + 0.5


def broadcast_columns(columns, first, many, width):
    held = columns[...]
    return [jnp.broadcast_to(held[:, n : n + 1], (held.shape[0], width)) for n in range(first, first + many)]


def project(u, z, mask, proj_weight, gate_weight, columns, send, gate, mixed):
    width = z[0].shape[1]
    h = proj_weight.shape[1] // 4
    rows = mixed.shape[1]
    gain, offset, *biases = broadcast_columns(columns, u * EACH, 7, width)
    turned = [proj_weight[:, n * h : (n + 1) * h].T for n in range(4)] + [gate_weight.T]
    for pair in range(0, OWN, 2):
        normed = [layer_norm(z[i], gain, offset).astype(BF16) for i in (pair, pair + 1)]
        normed = jnp.concatenate(normed, 1)
        both = [jnp.dot(w, normed, preferred_element_type=F32) for w in turned]
        for n in range(2):
            i = pair + n
            parts = [v[:, n * width : (n + 1) * width] + b for v, b in zip(both, biases)]
            keep = mask[i : i + 1, :]
            mixed[0, pl.ds(i, h, stride=OWN), :] = keep * sigmoid(parts[1]) * parts[0]
            mixed[1, pl.ds(i, h, stride=OWN), :] = keep * sigmoid(parts[3]) * parts[2]
            gate[:, i * width : (i + 1) * width] = sigmoid(parts[4])
    send[:, 0:16, :] = mixed[0].reshape(rows // 16, 16, width).astype(BF16)
    send[:, 16:32, :] = mixed[1].reshape(rows // 16, 16, width).astype(BF16)


def finish(u, z, near, far, gate, out_weight, columns, mixed):
    width = z[0].shape[1]
    gain, offset, bias = broadcast_columns(columns, u * EACH + 7, 3, width)
    turned = out_weight.T
    me = place()
    for at, block in arrived_blocks(me, near, far):
        mixed[pl.ds(pl.multiple_of(device(*at) * 16, 16), 16), :] = block.astype(F32)
    results = []
    for pair in range(0, OWN, 2):
        blocks = [mixed[pl.ds(i, mixed.shape[0] // OWN, stride=OWN), :] for i in (pair, pair + 1)]
        hidden = jnp.concatenate([layer_norm(v, gain, offset).astype(BF16) for v in blocks], 1)
        both = jnp.dot(turned, hidden, preferred_element_type=F32)
        for n in range(2):
            change = both[:, n * width : (n + 1) * width] + bias
            at = slice((pair + n) * width, (pair + n + 1) * width)
            results.append((z[pair + n].astype(F32) + gate[:, at] * change).astype(BF16))
    return results


def first_kernel(
    pair, mask, pw, gw, pb, gb, ob, ns, no, send, gate, turned, columns, keep, pair_in, mask_in, pw_in, gw_in, pb_in, gb_in, ob_in, ns_in, no_in, rows, arrived, mixed
):
    moves = [(pair, pair_in), (pb, pb_in), (gb, gb_in), (ob, ob_in), (ns, ns_in), (no, no_in)]
    moves += [(pw.at[0], pw_in), (gw.at[0], gw_in), (mask, mask_in)]
    moves = [pltpu.make_async_copy(a, b, arrived.at[n]) for n, (a, b) in enumerate(moves)]
    for move in moves:
        move.start()
    moves[0].wait()
    width = pair.shape[1]
    z = [pair_in[i].T for i in range(OWN)]
    for i in range(OWN):
        turned[:, i * width : (i + 1) * width] = z[i]
    for move in moves[1:6]:
        move.wait()
    h = pw.shape[2] // 4
    for u in range(2):
        found = [ns_in[u, 0:1, :], no_in[u, 0:1, :]] + [pb_in[u : u + 1, n * h : (n + 1) * h] for n in range(4)]
        found += [gb_in[u : u + 1, :], ns_in[u, 1:2, :], no_in[u, 1:2, :], ob_in[u : u + 1, :]]
        for n, row in enumerate(found):
            rows[u * EACH + n : u * EACH + n + 1, :] = row
    columns[...] = rows[...].T
    for move in moves[6:]:
        move.wait()
    keep[0:OWN, :] = mask_in[...].astype(F32)
    project(0, [v.astype(F32) for v in z], keep, pw_in[...], gw_in[...], columns, send, gate, mixed)


def middle_kernel(c0, c1, c2, c3, far, old, old_gate, columns, keep, pw, gw, ow, send, gate, turned, mixed, mixed_back):
    width = keep.shape[1]
    z = finish(0, [old[:, i * width : (i + 1) * width] for i in range(OWN)], (c0, c1, c2, c3), far, old_gate, ow[0], columns, mixed_back)
    for i in range(OWN):
        turned[:, i * width : (i + 1) * width] = z[i]
    project(1, [v.astype(F32) for v in z], keep, pw[1], gw[1], columns, send, gate, mixed)


def last_kernel(c0, c1, c2, c3, far, old, old_gate, columns, ow, out, mixed_back):
    width = out.shape[1]
    z = finish(1, [old[:, i * width : (i + 1) * width] for i in range(OWN)], (c0, c1, c2, c3), far, old_gate, ow[1], columns, mixed_back)
    for i in range(OWN):
        out[i] = z[i].T


def triangle_kernel(incoming, sides, p0, p1, p2, p3, summed):
    left, right = [unpack(sides[:, n : n + 16, :].astype(F32)) for n in (0, 16)]
    product = over_rows if incoming else over_columns
    summed[...] = pack([product(a.astype(BF16), b.astype(BF16)) for a, b in zip(left, right)]).astype(BF16)
    to_planes(summed, (p0, p1, p2, p3))


def call(kernel, outs, scratch, *args, place=pltpu.VMEM):
    in_vmem = pl.BlockSpec(memory_space=pltpu.VMEM)
    return pl.pallas_call(
        kernel,
        out_shape=[jax.ShapeDtypeStruct(*o) for o in outs],
        in_specs=[pl.BlockSpec(memory_space=place)] * len(args),
        out_specs=[in_vmem] * len(outs),
        scratch_shapes=scratch,
        compiler_params=pltpu.CompilerParams(vmem_limit_bytes=24 * 2**20),
    )(*args)


def exchange(blocks):
    return lax.all_to_all(blocks, PEERS, split_axis=0, concat_axis=0, tiled=True)


def permute(values, change):
    return lax.ppermute(values, "row", [(d, d ^ change) for d in range(32)])


def triangle(incoming, sides):
    width = sides.shape[2]
    whole = pltpu.VMEM((32, 16, width), BF16)
    planes = call(functools.partial(triangle_kernel, incoming), [((8, 16, width), BF16)] * 4, [whole], sides)
    planes = [permute(v, n << 3) if n else v for n, v in enumerate(planes)]
    chips = call(to_chips_kernel, [((2, 4, 16, width), BF16)] * 4, [], *planes)
    chips = [permute(v, n << 1) if n else v for n, v in enumerate(chips)]
    (cores,) = call(to_core_kernel, [((4, 4, 16, width), BF16)], [], *chips)
    return *chips, permute(cores, 1)


def packed_updates(count, pair_rep, pair_mask, pw, pb, gw, gb, ow, ob, ns, no):
    rows_of, width, channels = pair_rep.shape
    flat = (channels, rows_of * width)
    projected = [((count, 32, width), BF16), (flat, F32), (flat, BF16)]
    params = [pair_rep, pair_mask, pw, gw, pb, gb, ob, ns, no]
    params = [pltpu.with_memory_space_constraint(v, pltpu.HBM) for v in params]
    held = [pltpu.VMEM(v.shape[1:] if n in (2, 3) else v.shape, v.dtype) for n, v in enumerate(params)]
    held += [pltpu.VMEM((2 * EACH, channels), F32), pltpu.SemaphoreType.DMA((len(params),))]
    back = pltpu.VMEM((OWN * channels, width), F32)
    mixed = pltpu.VMEM((2, OWN * channels, width), F32)
    kept = [((channels, 2 * EACH), F32), ((2 * OWN, width), F32)]
    send, gate, turned, columns, keep = call(first_kernel, projected + kept, held + [mixed], *params, place=pltpu.HBM)
    sums = triangle(False, exchange(send))
    send, gate, turned = call(middle_kernel, projected, [mixed, back], *sums, turned, gate, columns, keep, pw, gw, ow)
    sums = triangle(True, exchange(send))
    (out,) = call(last_kernel, [(pair_rep.shape, BF16)], [back], *sums, turned, gate, columns, ow)
    return out


def update(pair_t, pair_mask, u, incoming, peers, rows_of, pw, pb, gw, gb, ow, ob, ns, no):
    channels, positions = pair_t.shape
    width = positions // rows_of
    h = pw.shape[2] // 4
    count = peers[0] * peers[1]
    own = h // count
    normed = layer_norm(pair_t, ns[u, 0][:, None], no[u, 0][:, None]).astype(BF16)
    projected = over_rows(jnp.concatenate([pw[u], gw[u]], 1), normed) + jnp.concatenate([pb[u], gb[u]], 0)[:, None]
    parts = [projected[n * h : (n + 1) * h] for n in range(4)]
    gating = jax.nn.sigmoid(projected[4 * h :])
    mask = pair_mask.astype(F32).reshape(1, positions)
    left = (mask * jax.nn.sigmoid(parts[1]) * parts[0]).astype(BF16)
    right = (mask * jax.nn.sigmoid(parts[3]) * parts[2]).astype(BF16)
    sides = exchange(jnp.stack([v.reshape(count, own, rows_of, width) for v in (left, right)], 1))
    sides = sides.reshape(peers[0], peers[1], 2, own, rows_of, width)
    sides = sides.transpose(2, 3, 0, 4, 1, 5).reshape(2, own, peers[0] * rows_of, peers[1] * width)
    form = "cki,ckj->cij" if incoming else "cik,cjk->cij"
    summed = jnp.einsum(form, sides[0], sides[1], preferred_element_type=F32).astype(BF16)
    summed = summed.reshape(own, peers[0], rows_of, peers[1], width).transpose(1, 3, 0, 2, 4)
    summed = exchange(summed.reshape(count, own, rows_of, width)).reshape(h, positions).astype(F32)
    hidden = layer_norm(summed, ns[u, 1][:, None], no[u, 1][:, None]).astype(BF16)
    change = over_rows(ow[u], hidden) + ob[u][:, None]
    return (pair_t + gating * change).astype(BF16)


def plain_updates(peers, pair_rep, pair_mask, *params):
    rows_of, width, channels = pair_rep.shape
    pair_t = pair_rep.reshape(rows_of * width, channels).T
    for u in range(2):
        pair_t = update(pair_t.astype(F32), pair_mask, u, u == 1, peers, rows_of, *params)
    return pair_t.T.reshape(rows_of, width, channels)


def solution(mesh):
    peers = (mesh.shape["row"], mesh.shape["ka"])
    count = peers[0] * peers[1]

    def on_device(pair_rep, pair_mask, *params):
        rows_of, width, channels = pair_rep.shape
        hidden = params[0].shape[2] // 4
        fits = peers[1] == 1 and rows_of == OWN and hidden == OWN * count and count == 32
        if fits and channels == hidden == 128 and width % 128 == 0:
            return packed_updates(count, pair_rep, pair_mask, *params)
        return plain_updates(peers, pair_rep, pair_mask, *params)

    split = P(("grp", "row"), "ka", None)
    in_specs = (split, P(("grp", "row"), "ka")) + (P(),) * 8
    return jax.shard_map(on_device, mesh=mesh, in_specs=in_specs, out_specs=split, check_vma=False)
```

```python
import functools

import jax
import jax.numpy as jnp
from jax import lax
from jax.experimental import pallas as pl
from jax.experimental.pallas import tpu as pltpu
from jax.sharding import PartitionSpec as P

PEERS = ("row", "ka")
OWN = 4
CHIPS = (12, 14, 13, 15, 9, 11, 7, 5, 3, 1, 2, 0, 6, 4, 8, 10)
EACH = 16
BF16, F32 = jnp.bfloat16, jnp.float32


def over_rows(a, b):
    return lax.dot_general(a, b, (((0,), (0,)), ((), ())), preferred_element_type=F32)


def over_columns(a, b):
    return lax.dot_general(a, b, (((1,), (1,)), ((), ())), preferred_element_type=F32)


def layer_norm(values, norm_gain, norm_bias):
    average = jnp.mean(values, 0, keepdims=True)
    centred = values - average
    variance = jnp.mean(centred * centred, 0, keepdims=True)
    return centred * lax.rsqrt(variance + 1e-05) * norm_gain + norm_bias


def pack(blocks):
    channels, width = blocks[0].shape
    tiles = [b.reshape(channels // 8, 8, width) for b in blocks]
    turned = [pltpu.roll(b, 4, axis=0).reshape(channels // 8, 8, width) for b in blocks]
    low = lax.broadcasted_iota(jnp.int32, tiles[0].shape, 1) < 4
    back = [pltpu.roll(b, channels - 4, axis=0).reshape(channels // 8, 8, width) for b in blocks]
    even = [jnp.where(low, tiles[n], turned[n + 1]) for n in (0, 2)]
    odd = [jnp.where(low, back[n], tiles[n + 1]) for n in (0, 2)]
    return jnp.stack([jnp.stack(even, 1), jnp.stack(odd, 1)], 1).reshape(channels // 4, 16, width)


def unpack(packed):
    count, _, width = packed.shape
    tiles = packed.reshape(count // 2, 2, 2, 8, width)
    low = lax.broadcasted_iota(jnp.int32, (count // 2, 8, width), 1) < 4
    blocks = []
    for n in range(2):
        even, odd = tiles[:, 0, n], tiles[:, 1, n]
        down = pltpu.roll(odd.reshape(count * 4, width), 4, axis=0).reshape(even.shape)
        up = pltpu.roll(even.reshape(count * 4, width), count * 4 - 4, axis=0).reshape(even.shape)
        blocks.append(jnp.where(low, even, down).reshape(count * 4, width))
        blocks.append(jnp.where(low, up, odd).reshape(count * 4, width))
    return blocks


def sigmoid(x):
    return 0.5 * jnp.tanh(0.5 * x) + 0.5


def broadcast_columns(columns, first, many, width):
    held = columns[...]
    return [jnp.broadcast_to(held[:, n : n + 1], (held.shape[0], width)) for n in range(first, first + many)]


def project(u, z, mask, proj_weight, gate_weight, columns, send, gate, mixed):
    width = z[0].shape[1]
    h = proj_weight.shape[1] // 4
    rows = mixed.shape[1]
    gain, offset, *biases = broadcast_columns(columns, u * EACH, 7, width)
    turned = [proj_weight[:, n * h : (n + 1) * h].T for n in range(4)] + [gate_weight.T]
    for pair in range(0, OWN, 2):
        normed = [layer_norm(z[i], gain, offset).astype(BF16) for i in (pair, pair + 1)]
        normed = jnp.concatenate(normed, 1)
        both = [jnp.dot(w, normed, preferred_element_type=F32) for w in turned]
        for n in range(2):
            i = pair + n
            parts = [v[:, n * width : (n + 1) * width] + b for v, b in zip(both, biases)]
            keep = mask[i : i + 1, :]
            mixed[0, pl.ds(i, h, stride=OWN), :] = keep * sigmoid(parts[1]) * parts[0]
            mixed[1, pl.ds(i, h, stride=OWN), :] = keep * sigmoid(parts[3]) * parts[2]
            gate[:, i * width : (i + 1) * width] = sigmoid(parts[4])
    send[:, 0:16, :] = mixed[0].reshape(rows // 16, 16, width).astype(BF16)
    send[:, 16:32, :] = mixed[1].reshape(rows // 16, 16, width).astype(BF16)


def finish(u, z, summed, gate, out_weight, columns, mixed):
    width = z[0].shape[1]
    gain, offset, bias = broadcast_columns(columns, u * EACH + 7, 3, width)
    turned = out_weight.T
    mixed[...] = summed[...].astype(F32).reshape(mixed.shape)
    results = []
    for pair in range(0, OWN, 2):
        blocks = [mixed[pl.ds(i, mixed.shape[0] // OWN, stride=OWN), :] for i in (pair, pair + 1)]
        hidden = jnp.concatenate([layer_norm(v, gain, offset).astype(BF16) for v in blocks], 1)
        both = jnp.dot(turned, hidden, preferred_element_type=F32)
        for n in range(2):
            change = both[:, n * width : (n + 1) * width] + bias
            at = slice((pair + n) * width, (pair + n + 1) * width)
            results.append((z[pair + n].astype(F32) + gate[:, at] * change).astype(BF16))
    return results


def first_kernel(
    pair, mask, pw, gw, pb, gb, ob, ns, no, send, gate, turned, columns, keep, pair_in, mask_in, pw_in, gw_in, pb_in, gb_in, ob_in, ns_in, no_in, rows, arrived, mixed
):
    moves = [(pair, pair_in), (pb, pb_in), (gb, gb_in), (ob, ob_in), (ns, ns_in), (no, no_in)]
    moves += [(pw.at[0], pw_in), (gw.at[0], gw_in), (mask, mask_in)]
    moves = [pltpu.make_async_copy(a, b, arrived.at[n]) for n, (a, b) in enumerate(moves)]
    for move in moves:
        move.start()
    moves[0].wait()
    width = pair.shape[1]
    z = [pair_in[i].T for i in range(OWN)]
    for i in range(OWN):
        turned[:, i * width : (i + 1) * width] = z[i]
    for move in moves[1:6]:
        move.wait()
    h = pw.shape[2] // 4
    for u in range(2):
        found = [ns_in[u, 0:1, :], no_in[u, 0:1, :]] + [pb_in[u : u + 1, n * h : (n + 1) * h] for n in range(4)]
        found += [gb_in[u : u + 1, :], ns_in[u, 1:2, :], no_in[u, 1:2, :], ob_in[u : u + 1, :]]
        for n, row in enumerate(found):
            rows[u * EACH + n : u * EACH + n + 1, :] = row
    columns[...] = rows[...].T
    for move in moves[6:]:
        move.wait()
    keep[0:OWN, :] = mask_in[...].astype(F32)
    project(0, [v.astype(F32) for v in z], keep, pw_in[...], gw_in[...], columns, send, gate, mixed)


def middle_kernel(summed, old, old_gate, columns, keep, pw, gw, ow, send, gate, turned, mixed, mixed_back):
    width = keep.shape[1]
    z = finish(0, [old[:, i * width : (i + 1) * width] for i in range(OWN)], summed, old_gate, ow[0], columns, mixed_back)
    for i in range(OWN):
        turned[:, i * width : (i + 1) * width] = z[i]
    project(1, [v.astype(F32) for v in z], keep, pw[1], gw[1], columns, send, gate, mixed)


def last_kernel(summed, old, old_gate, columns, ow, out, mixed_back):
    width = out.shape[1]
    z = finish(1, [old[:, i * width : (i + 1) * width] for i in range(OWN)], summed, old_gate, ow[1], columns, mixed_back)
    for i in range(OWN):
        out[i] = z[i].T


def reorder(values, order):
    tiles = values.reshape(len(order), 2 * OWN, values.shape[1])
    return jnp.concatenate([tiles[n : n + 1] for n in order]).reshape(values.shape)


def triangle_kernel(incoming, sides, out):
    left, right = [unpack(sides[:, n : n + 16, :].astype(F32)) for n in (0, 16)]
    if incoming:
        summed = [reorder(over_rows(a.astype(BF16), b.astype(BF16)), CHIPS) for a, b in zip(left, right)]
    else:
        back = [CHIPS.index(n) for n in range(len(CHIPS))]
        right = [reorder(b, back) for b in right]
        summed = [over_columns(a.astype(BF16), b.astype(BF16)) for a, b in zip(left, right)]
    out[...] = pack(summed).astype(BF16)


def call(kernel, outs, scratch, *args, place=pltpu.VMEM):
    in_vmem = pl.BlockSpec(memory_space=pltpu.VMEM)
    return pl.pallas_call(
        kernel,
        out_shape=[jax.ShapeDtypeStruct(*o) for o in outs],
        in_specs=[pl.BlockSpec(memory_space=place)] * len(args),
        out_specs=[in_vmem] * len(outs),
        scratch_shapes=scratch,
        compiler_params=pltpu.CompilerParams(vmem_limit_bytes=24 * 2**20),
    )(*args)


def exchange(blocks):
    return lax.all_to_all(blocks, PEERS, split_axis=0, concat_axis=0, tiled=True)


def exchange_in_order(blocks):
    listed = [[2 * chip + core for chip in CHIPS for core in range(2)]]
    return lax.all_to_all(blocks, "row", split_axis=0, concat_axis=0, axis_index_groups=listed, tiled=True)


def packed_updates(count, pair_rep, pair_mask, pw, pb, gw, gb, ow, ob, ns, no):
    rows_of, width, channels = pair_rep.shape
    flat = (channels, rows_of * width)
    projected = [((count, 32, width), BF16), (flat, F32), (flat, BF16)]
    summed = [((count, 16, width), BF16)]
    params = [pair_rep, pair_mask, pw, gw, pb, gb, ob, ns, no]
    params = [pltpu.with_memory_space_constraint(v, pltpu.HBM) for v in params]
    held = [pltpu.VMEM(v.shape[1:] if n in (2, 3) else v.shape, v.dtype) for n, v in enumerate(params)]
    held += [pltpu.VMEM((2 * EACH, channels), F32), pltpu.SemaphoreType.DMA((len(params),))]
    back = pltpu.VMEM((OWN * channels, width), F32)
    mixed = pltpu.VMEM((2, OWN * channels, width), F32)
    kept = [((channels, 2 * EACH), F32), ((2 * OWN, width), F32)]
    send, gate, turned, columns, keep = call(first_kernel, projected + kept, held + [mixed], *params, place=pltpu.HBM)
    (send,) = call(functools.partial(triangle_kernel, False), summed, [], exchange_in_order(send))
    send, gate, turned = call(middle_kernel, projected, [mixed, back], exchange_in_order(send), turned, gate, columns, keep, pw, gw, ow)
    (send,) = call(functools.partial(triangle_kernel, True), summed, [], exchange_in_order(send))
    (out,) = call(last_kernel, [(pair_rep.shape, BF16)], [back], exchange_in_order(send), turned, gate, columns, ow)
    return out


def update(pair_t, pair_mask, u, incoming, peers, rows_of, pw, pb, gw, gb, ow, ob, ns, no):
    channels, positions = pair_t.shape
    width = positions // rows_of
    h = pw.shape[2] // 4
    count = peers[0] * peers[1]
    own = h // count
    normed = layer_norm(pair_t, ns[u, 0][:, None], no[u, 0][:, None]).astype(BF16)
    projected = over_rows(jnp.concatenate([pw[u], gw[u]], 1), normed) + jnp.concatenate([pb[u], gb[u]], 0)[:, None]
    parts = [projected[n * h : (n + 1) * h] for n in range(4)]
    gating = jax.nn.sigmoid(projected[4 * h :])
    mask = pair_mask.astype(F32).reshape(1, positions)
    left = (mask * jax.nn.sigmoid(parts[1]) * parts[0]).astype(BF16)
    right = (mask * jax.nn.sigmoid(parts[3]) * parts[2]).astype(BF16)
    sides = exchange(jnp.stack([v.reshape(count, own, rows_of, width) for v in (left, right)], 1))
    sides = sides.reshape(peers[0], peers[1], 2, own, rows_of, width)
    sides = sides.transpose(2, 3, 0, 4, 1, 5).reshape(2, own, peers[0] * rows_of, peers[1] * width)
    form = "cki,ckj->cij" if incoming else "cik,cjk->cij"
    summed = jnp.einsum(form, sides[0], sides[1], preferred_element_type=F32).astype(BF16)
    summed = summed.reshape(own, peers[0], rows_of, peers[1], width).transpose(1, 3, 0, 2, 4)
    summed = exchange(summed.reshape(count, own, rows_of, width)).reshape(h, positions).astype(F32)
    hidden = layer_norm(summed, ns[u, 1][:, None], no[u, 1][:, None]).astype(BF16)
    change = over_rows(ow[u], hidden) + ob[u][:, None]
    return (pair_t + gating * change).astype(BF16)


def plain_updates(peers, pair_rep, pair_mask, *params):
    rows_of, width, channels = pair_rep.shape
    pair_t = pair_rep.reshape(rows_of * width, channels).T
    for u in range(2):
        pair_t = update(pair_t.astype(F32), pair_mask, u, u == 1, peers, rows_of, *params)
    return pair_t.T.reshape(rows_of, width, channels)


def solution(mesh):
    peers = (mesh.shape["row"], mesh.shape["ka"])
    count = peers[0] * peers[1]

    def on_device(pair_rep, pair_mask, *params):
        rows_of, width, channels = pair_rep.shape
        hidden = params[0].shape[2] // 4
        fits = peers[1] == 1 and rows_of == OWN and hidden == OWN * count and count == 2 * len(CHIPS)
        if fits and channels == hidden == 128 and width % 128 == 0:
            return packed_updates(count, pair_rep, pair_mask, *params)
        return plain_updates(peers, pair_rep, pair_mask, *params)

    split = P(("grp", "row"), "ka", None)
    in_specs = (split, P(("grp", "row"), "ka")) + (P(),) * 8
    return jax.shard_map(on_device, mesh=mesh, in_specs=in_specs, out_specs=split, check_vma=False)
```

```python
import functools

import jax
import jax.numpy as jnp
from jax import lax
from jax.experimental import pallas as pl
from jax.experimental.pallas import tpu as pltpu
from jax.sharding import PartitionSpec as P

PEERS = ("row", "ka")
OWN = 4
ORDERS = (
    ((0, 4, 8, 12, 1, 5, 9, 13, 2, 6, 10, 14, 3, 7, 11, 15), (0, 4, 8, 12, 13, 9, 5, 1, 3, 7, 11, 15, 14, 10, 6, 2)),
    ((0, 4, 8, 12, 13, 9, 5, 1, 3, 7, 11, 15, 14, 10, 6, 2), (0, 4, 8, 12, 1, 5, 9, 13, 2, 6, 10, 14, 3, 7, 11, 15)),
)
EACH = 16
BF16, F32 = jnp.bfloat16, jnp.float32


def over_rows(a, b):
    return lax.dot_general(a, b, (((0,), (0,)), ((), ())), preferred_element_type=F32)


def over_columns(a, b):
    return lax.dot_general(a, b, (((1,), (1,)), ((), ())), preferred_element_type=F32)


def layer_norm(values, norm_gain, norm_bias):
    average = jnp.mean(values, 0, keepdims=True)
    centred = values - average
    variance = jnp.mean(centred * centred, 0, keepdims=True)
    return centred * lax.rsqrt(variance + 1e-05) * norm_gain + norm_bias


def pack(blocks):
    channels, width = blocks[0].shape
    tiles = [b.reshape(channels // 8, 8, width) for b in blocks]
    turned = [pltpu.roll(b, 4, axis=0).reshape(channels // 8, 8, width) for b in blocks]
    low = lax.broadcasted_iota(jnp.int32, tiles[0].shape, 1) < 4
    back = [pltpu.roll(b, channels - 4, axis=0).reshape(channels // 8, 8, width) for b in blocks]
    even = [jnp.where(low, tiles[n], turned[n + 1]) for n in (0, 2)]
    odd = [jnp.where(low, back[n], tiles[n + 1]) for n in (0, 2)]
    return jnp.stack([jnp.stack(even, 1), jnp.stack(odd, 1)], 1).reshape(channels // 4, 16, width)


def unpack(packed):
    count, _, width = packed.shape
    tiles = packed.reshape(count // 2, 2, 2, 8, width)
    low = lax.broadcasted_iota(jnp.int32, (count // 2, 8, width), 1) < 4
    blocks = []
    for n in range(2):
        even, odd = tiles[:, 0, n], tiles[:, 1, n]
        down = pltpu.roll(odd.reshape(count * 4, width), 4, axis=0).reshape(even.shape)
        up = pltpu.roll(even.reshape(count * 4, width), count * 4 - 4, axis=0).reshape(even.shape)
        blocks.append(jnp.where(low, even, down).reshape(count * 4, width))
        blocks.append(jnp.where(low, up, odd).reshape(count * 4, width))
    return blocks


def sigmoid(x):
    return 0.5 * jnp.tanh(0.5 * x) + 0.5


def broadcast_columns(columns, first, many, width):
    held = columns[...]
    return [jnp.broadcast_to(held[:, n : n + 1], (held.shape[0], width)) for n in range(first, first + many)]


def project(u, z, mask, proj_weight, gate_weight, columns, send, gate, mixed):
    width = z[0].shape[1]
    h = proj_weight.shape[1] // 4
    rows = mixed.shape[1]
    gain, offset, *biases = broadcast_columns(columns, u * EACH, 7, width)
    turned = [proj_weight[:, n * h : (n + 1) * h].T for n in range(4)] + [gate_weight.T]
    for pair in range(0, OWN, 2):
        normed = [layer_norm(z[i], gain, offset).astype(BF16) for i in (pair, pair + 1)]
        normed = jnp.concatenate(normed, 1)
        both = [jnp.dot(w, normed, preferred_element_type=F32) for w in turned]
        for n in range(2):
            i = pair + n
            parts = [v[:, n * width : (n + 1) * width] + b for v, b in zip(both, biases)]
            keep = mask[i : i + 1, :]
            mixed[0, pl.ds(i, h, stride=OWN), :] = keep * sigmoid(parts[1]) * parts[0]
            mixed[1, pl.ds(i, h, stride=OWN), :] = keep * sigmoid(parts[3]) * parts[2]
            gate[:, i * width : (i + 1) * width] = sigmoid(parts[4])
    send[:, 0:16, :] = mixed[0].reshape(rows // 16, 16, width).astype(BF16)
    send[:, 16:32, :] = mixed[1].reshape(rows // 16, 16, width).astype(BF16)


def finish(u, z, summed, gate, out_weight, columns, mixed):
    width = z[0].shape[1]
    gain, offset, bias = broadcast_columns(columns, u * EACH + 7, 3, width)
    turned = out_weight.T
    mixed[...] = summed[...].astype(F32).reshape(mixed.shape)
    results = []
    for pair in range(0, OWN, 2):
        blocks = [mixed[pl.ds(i, mixed.shape[0] // OWN, stride=OWN), :] for i in (pair, pair + 1)]
        blocks = [reorder(v, ORDERS[u][1], ORDERS[u][0]) for v in blocks]
        hidden = jnp.concatenate([layer_norm(v, gain, offset).astype(BF16) for v in blocks], 1)
        both = jnp.dot(turned, hidden, preferred_element_type=F32)
        for n in range(2):
            change = both[:, n * width : (n + 1) * width] + bias
            at = slice((pair + n) * width, (pair + n + 1) * width)
            results.append((z[pair + n].astype(F32) + gate[:, at] * change).astype(BF16))
    return results


def first_kernel(
    pair, mask, pw, gw, pb, gb, ob, ns, no, send, gate, turned, columns, keep, pair_in, mask_in, pw_in, gw_in, pb_in, gb_in, ob_in, ns_in, no_in, rows, arrived, mixed
):
    moves = [(pair, pair_in), (pb, pb_in), (gb, gb_in), (ob, ob_in), (ns, ns_in), (no, no_in)]
    moves += [(pw.at[0], pw_in), (gw.at[0], gw_in), (mask, mask_in)]
    moves = [pltpu.make_async_copy(a, b, arrived.at[n]) for n, (a, b) in enumerate(moves)]
    for move in moves:
        move.start()
    moves[0].wait()
    width = pair.shape[1]
    z = [pair_in[i].T for i in range(OWN)]
    for i in range(OWN):
        turned[:, i * width : (i + 1) * width] = z[i]
    for move in moves[1:6]:
        move.wait()
    h = pw.shape[2] // 4
    for u in range(2):
        found = [ns_in[u, 0:1, :], no_in[u, 0:1, :]] + [pb_in[u : u + 1, n * h : (n + 1) * h] for n in range(4)]
        found += [gb_in[u : u + 1, :], ns_in[u, 1:2, :], no_in[u, 1:2, :], ob_in[u : u + 1, :]]
        for n, row in enumerate(found):
            rows[u * EACH + n : u * EACH + n + 1, :] = row
    columns[...] = rows[...].T
    for move in moves[6:]:
        move.wait()
    keep[0:OWN, :] = mask_in[...].astype(F32)
    project(0, [v.astype(F32) for v in z], keep, pw_in[...], gw_in[...], columns, send, gate, mixed)


def middle_kernel(summed, old, old_gate, columns, keep, pw, gw, ow, send, gate, turned, mixed, mixed_back):
    width = keep.shape[1]
    z = finish(0, [old[:, i * width : (i + 1) * width] for i in range(OWN)], summed, old_gate, ow[0], columns, mixed_back)
    for i in range(OWN):
        turned[:, i * width : (i + 1) * width] = z[i]
    project(1, [v.astype(F32) for v in z], keep, pw[1], gw[1], columns, send, gate, mixed)


def last_kernel(summed, old, old_gate, columns, ow, out, mixed_back):
    width = out.shape[1]
    z = finish(1, [old[:, i * width : (i + 1) * width] for i in range(OWN)], summed, old_gate, ow[1], columns, mixed_back)
    for i in range(OWN):
        out[i] = z[i].T


def reorder(values, have, want):
    tiles = values.reshape(len(have), 2 * OWN, values.shape[1])
    places = [have.index(chip) for chip in want]
    return jnp.concatenate([tiles[n : n + 1] for n in places]).reshape(values.shape)


def triangle_kernel(incoming, sides, out):
    come, go = ORDERS[1 if incoming else 0]
    in_mesh = tuple(range(len(come)))
    left, right = [unpack(sides[:, n : n + 16, :].astype(F32)) for n in (0, 16)]
    if incoming:
        summed = [over_rows(a.astype(BF16), b.astype(BF16)) for a, b in zip(left, right)]
        summed = [reorder(v, in_mesh, go) for v in summed]
    else:
        left = [reorder(v, come, go) for v in left]
        right = [reorder(v, come, in_mesh) for v in right]
        summed = [over_columns(a.astype(BF16), b.astype(BF16)) for a, b in zip(left, right)]
    out[...] = pack(summed).astype(BF16)


def call(kernel, outs, scratch, *args, place=pltpu.VMEM):
    in_vmem = pl.BlockSpec(memory_space=pltpu.VMEM)
    return pl.pallas_call(
        kernel,
        out_shape=[jax.ShapeDtypeStruct(*o) for o in outs],
        in_specs=[pl.BlockSpec(memory_space=place)] * len(args),
        out_specs=[in_vmem] * len(outs),
        scratch_shapes=scratch,
        compiler_params=pltpu.CompilerParams(vmem_limit_bytes=24 * 2**20),
    )(*args)


def exchange(blocks):
    return lax.all_to_all(blocks, PEERS, split_axis=0, concat_axis=0, tiled=True)


def exchange_in_order(blocks, chips):
    listed = [[2 * chip + core for chip in chips for core in range(2)]]
    return lax.all_to_all(blocks, "row", split_axis=0, concat_axis=0, axis_index_groups=listed, tiled=True)


def packed_updates(count, pair_rep, pair_mask, pw, pb, gw, gb, ow, ob, ns, no):
    rows_of, width, channels = pair_rep.shape
    flat = (channels, rows_of * width)
    projected = [((count, 32, width), BF16), (flat, F32), (flat, BF16)]
    summed = [((count, 16, width), BF16)]
    params = [pair_rep, pair_mask, pw, gw, pb, gb, ob, ns, no]
    params = [pltpu.with_memory_space_constraint(v, pltpu.HBM) for v in params]
    held = [pltpu.VMEM(v.shape[1:] if n in (2, 3) else v.shape, v.dtype) for n, v in enumerate(params)]
    held += [pltpu.VMEM((2 * EACH, channels), F32), pltpu.SemaphoreType.DMA((len(params),))]
    back = pltpu.VMEM((OWN * channels, width), F32)
    mixed = pltpu.VMEM((2, OWN * channels, width), F32)
    kept = [((channels, 2 * EACH), F32), ((2 * OWN, width), F32)]
    send, gate, turned, columns, keep = call(first_kernel, projected + kept, held + [mixed], *params, place=pltpu.HBM)
    (send,) = call(functools.partial(triangle_kernel, False), summed, [], exchange_in_order(send, ORDERS[0][0]))
    send, gate, turned = call(middle_kernel, projected, [mixed, back], exchange_in_order(send, ORDERS[0][1]), turned, gate, columns, keep, pw, gw, ow)
    (send,) = call(functools.partial(triangle_kernel, True), summed, [], exchange_in_order(send, ORDERS[1][0]))
    (out,) = call(last_kernel, [(pair_rep.shape, BF16)], [back], exchange_in_order(send, ORDERS[1][1]), turned, gate, columns, ow)
    return out


def update(pair_t, pair_mask, u, incoming, peers, rows_of, pw, pb, gw, gb, ow, ob, ns, no):
    channels, positions = pair_t.shape
    width = positions // rows_of
    h = pw.shape[2] // 4
    count = peers[0] * peers[1]
    own = h // count
    normed = layer_norm(pair_t, ns[u, 0][:, None], no[u, 0][:, None]).astype(BF16)
    projected = over_rows(jnp.concatenate([pw[u], gw[u]], 1), normed) + jnp.concatenate([pb[u], gb[u]], 0)[:, None]
    parts = [projected[n * h : (n + 1) * h] for n in range(4)]
    gating = jax.nn.sigmoid(projected[4 * h :])
    mask = pair_mask.astype(F32).reshape(1, positions)
    left = (mask * jax.nn.sigmoid(parts[1]) * parts[0]).astype(BF16)
    right = (mask * jax.nn.sigmoid(parts[3]) * parts[2]).astype(BF16)
    sides = exchange(jnp.stack([v.reshape(count, own, rows_of, width) for v in (left, right)], 1))
    sides = sides.reshape(peers[0], peers[1], 2, own, rows_of, width)
    sides = sides.transpose(2, 3, 0, 4, 1, 5).reshape(2, own, peers[0] * rows_of, peers[1] * width)
    form = "cki,ckj->cij" if incoming else "cik,cjk->cij"
    summed = jnp.einsum(form, sides[0], sides[1], preferred_element_type=F32).astype(BF16)
    summed = summed.reshape(own, peers[0], rows_of, peers[1], width).transpose(1, 3, 0, 2, 4)
    summed = exchange(summed.reshape(count, own, rows_of, width)).reshape(h, positions).astype(F32)
    hidden = layer_norm(summed, ns[u, 1][:, None], no[u, 1][:, None]).astype(BF16)
    change = over_rows(ow[u], hidden) + ob[u][:, None]
    return (pair_t + gating * change).astype(BF16)


def plain_updates(peers, pair_rep, pair_mask, *params):
    rows_of, width, channels = pair_rep.shape
    pair_t = pair_rep.reshape(rows_of * width, channels).T
    for u in range(2):
        pair_t = update(pair_t.astype(F32), pair_mask, u, u == 1, peers, rows_of, *params)
    return pair_t.T.reshape(rows_of, width, channels)


def solution(mesh):
    peers = (mesh.shape["row"], mesh.shape["ka"])
    count = peers[0] * peers[1]

    def on_device(pair_rep, pair_mask, *params):
        rows_of, width, channels = pair_rep.shape
        hidden = params[0].shape[2] // 4
        fits = peers[1] == 1 and rows_of == OWN and hidden == OWN * count and count == 2 * len(ORDERS[0][0])
        if fits and channels == hidden == 128 and width % 128 == 0:
            return packed_updates(count, pair_rep, pair_mask, *params)
        return plain_updates(peers, pair_rep, pair_mask, *params)

    split = P(("grp", "row"), "ka", None)
    in_specs = (split, P(("grp", "row"), "ka")) + (P(),) * 8
    return jax.shard_map(on_device, mesh=mesh, in_specs=in_specs, out_specs=split, check_vma=False)
```

```python
import functools

import jax
import jax.numpy as jnp
from jax import lax
from jax.experimental import pallas as pl
from jax.experimental.pallas import tpu as pltpu
from jax.sharding import PartitionSpec as P

PEERS = ("row", "ka")
OWN = 4
ORDERS = (
    ((0, 4, 8, 12, 1, 5, 9, 13, 2, 6, 10, 14, 3, 7, 11, 15), (12, 14, 13, 15, 9, 11, 7, 5, 3, 1, 2, 0, 6, 4, 8, 10)),
    ((0, 1, 2, 3, 4, 5, 6, 7, 8, 9, 10, 11, 12, 13, 14, 15), (12, 14, 13, 15, 9, 11, 7, 5, 3, 1, 2, 0, 6, 4, 8, 10)),
)
EACH = 16
BF16, F32 = jnp.bfloat16, jnp.float32


def over_rows(a, b):
    return lax.dot_general(a, b, (((0,), (0,)), ((), ())), preferred_element_type=F32)


def over_columns(a, b):
    return lax.dot_general(a, b, (((1,), (1,)), ((), ())), preferred_element_type=F32)


def standardised(values):
    average = jnp.mean(values, 0, keepdims=True)
    centred = values - average
    variance = jnp.mean(centred * centred, 0, keepdims=True)
    return centred * lax.rsqrt(variance + 1e-05)


def layer_norm(values, norm_gain, norm_bias):
    return standardised(values) * norm_gain + norm_bias


def pack(blocks):
    channels, width = blocks[0].shape
    tiles = [b.reshape(channels // 8, 8, width) for b in blocks]
    turned = [pltpu.roll(b, 4, axis=0).reshape(channels // 8, 8, width) for b in blocks]
    low = lax.broadcasted_iota(jnp.int32, tiles[0].shape, 1) < 4
    back = [pltpu.roll(b, channels - 4, axis=0).reshape(channels // 8, 8, width) for b in blocks]
    even = [jnp.where(low, tiles[n], turned[n + 1]) for n in (0, 2)]
    odd = [jnp.where(low, back[n], tiles[n + 1]) for n in (0, 2)]
    return jnp.stack([jnp.stack(even, 1), jnp.stack(odd, 1)], 1).reshape(channels // 4, 16, width)


def unpack(packed):
    count, _, width = packed.shape
    tiles = packed.reshape(count // 2, 2, 2, 8, width)
    low = lax.broadcasted_iota(jnp.int32, (count // 2, 8, width), 1) < 4
    blocks = []
    for n in range(2):
        even, odd = tiles[:, 0, n], tiles[:, 1, n]
        down = pltpu.roll(odd.reshape(count * 4, width), 4, axis=0).reshape(even.shape)
        up = pltpu.roll(even.reshape(count * 4, width), count * 4 - 4, axis=0).reshape(even.shape)
        blocks.append(jnp.where(low, even, down).reshape(count * 4, width))
        blocks.append(jnp.where(low, up, odd).reshape(count * 4, width))
    return blocks


def sigmoid(x):
    return 0.5 * jnp.tanh(0.5 * x) + 0.5


def broadcast_columns(columns, first, many, width):
    held = columns[...]
    return [jnp.broadcast_to(held[:, n : n + 1], (held.shape[0], width)) for n in range(first, first + many)]


def project(u, normed, mask, proj_weight, gate_weight, columns, send, gate, mixed):
    width = normed[0].shape[1]
    h = proj_weight.shape[1] // 4
    rows = mixed.shape[1]
    biases = broadcast_columns(columns, u * EACH + 2, 5, width)
    turned = [proj_weight[:, n * h : (n + 1) * h].T for n in range(4)] + [gate_weight.T]
    halves = [mask[i : i + 1, :] * 0.5 for i in range(OWN)]
    joined = [jnp.concatenate(normed[pair : pair + 2], 1) for pair in range(0, OWN, 2)]
    for side in range(2):
        for pair in range(0, OWN, 2):
            value, gating = [jnp.dot(turned[2 * side + n], joined[pair // 2], preferred_element_type=F32) for n in (0, 1)]
            for n in range(2):
                i, at = pair + n, slice(n * width, (n + 1) * width)
                weight = halves[i] + halves[i] * jnp.tanh(0.5 * (gating[:, at] + biases[2 * side + 1]))
                mixed[side, pl.ds(i, h, stride=OWN), :] = weight * (value[:, at] + biases[2 * side])
        send[:, side * 16 : (side + 1) * 16, :] = mixed[side].reshape(rows // 16, 16, width).astype(BF16)
    for pair in range(0, OWN, 2):
        gating = jnp.dot(turned[4], joined[pair // 2], preferred_element_type=F32)
        for n in range(2):
            at = slice((pair + n) * width, (pair + n + 1) * width)
            gate[:, at] = sigmoid(gating[:, n * width : (n + 1) * width] + biases[4])


def finish(u, z, summed, gate, out_weight, columns, mixed):
    width = z[0].shape[1]
    gain, offset, bias = broadcast_columns(columns, u * EACH + 7, 3, width)
    turned = out_weight.T
    mixed[...] = summed[...].astype(F32).reshape(mixed.shape)
    results = []
    for pair in range(0, OWN, 2):
        blocks = [mixed[pl.ds(i, mixed.shape[0] // OWN, stride=OWN), :] for i in (pair, pair + 1)]
        blocks = [reorder(v, ORDERS[u][1], ORDERS[u][0]) for v in blocks]
        hidden = jnp.concatenate([layer_norm(v, gain, offset).astype(BF16) for v in blocks], 1)
        both = jnp.dot(turned, hidden, preferred_element_type=F32)
        for n in range(2):
            change = both[:, n * width : (n + 1) * width] + bias
            at = slice((pair + n) * width, (pair + n + 1) * width)
            results.append((z[pair + n].astype(F32) + gate[:, at] * change).astype(BF16))
    return results


def first_kernel(
    pair, mask, pw, gw, pb, gb, ob, ns, no, send, gate, turned, columns, keep, pair_in, mask_in, pw_in, gw_in, pb_in, gb_in, ob_in, ns_in, no_in, rows, arrived, mixed
):
    moves = [(pair, pair_in), (ns, ns_in), (no, no_in), (pb, pb_in), (gb, gb_in), (ob, ob_in)]
    moves += [(pw.at[0], pw_in), (gw.at[0], gw_in), (mask, mask_in)]
    moves = [pltpu.make_async_copy(a, b, arrived.at[n]) for n, (a, b) in enumerate(moves)]
    for move in moves:
        move.start()
    moves[0].wait()
    width = pair.shape[1]
    z = [pair_in[i].T for i in range(OWN)]
    for i in range(OWN):
        turned[:, i * width : (i + 1) * width] = z[i]
    z = [standardised(v.astype(F32)) for v in z]
    for move in moves[1:6]:
        move.wait()
    h = pw.shape[2] // 4
    for u in range(2):
        found = [ns_in[u, 0:1, :], no_in[u, 0:1, :]] + [pb_in[u : u + 1, n * h : (n + 1) * h] for n in range(4)]
        found += [gb_in[u : u + 1, :], ns_in[u, 1:2, :], no_in[u, 1:2, :], ob_in[u : u + 1, :]]
        for n, row in enumerate(found):
            rows[u * EACH + n : u * EACH + n + 1, :] = row
    columns[...] = rows[...].T
    gain, offset = broadcast_columns(columns, 0, 2, width)
    normed = [(v * gain + offset).astype(BF16) for v in z]
    for move in moves[6:]:
        move.wait()
    keep[0:OWN, :] = mask_in[...].astype(F32)
    project(0, normed, keep, pw_in[...], gw_in[...], columns, send, gate, mixed)


def middle_kernel(summed, old, old_gate, columns, keep, pw, gw, ow, send, gate, turned, mixed, mixed_back):
    width = keep.shape[1]
    z = finish(0, [old[:, i * width : (i + 1) * width] for i in range(OWN)], summed, old_gate, ow[0], columns, mixed_back)
    for i in range(OWN):
        turned[:, i * width : (i + 1) * width] = z[i]
    gain, offset = broadcast_columns(columns, EACH, 2, width)
    normed = [layer_norm(v.astype(F32), gain, offset).astype(BF16) for v in z]
    project(1, normed, keep, pw[1], gw[1], columns, send, gate, mixed)


def last_kernel(summed, old, old_gate, columns, ow, out, mixed_back):
    width = out.shape[1]
    z = finish(1, [old[:, i * width : (i + 1) * width] for i in range(OWN)], summed, old_gate, ow[1], columns, mixed_back)
    for i in range(OWN):
        out[i] = z[i].T


def reorder(values, have, want):
    tiles = values.reshape(len(have), 2 * OWN, values.shape[1])
    places = [have.index(chip) for chip in want]
    return jnp.concatenate([tiles[n : n + 1] for n in places]).reshape(values.shape)


def triangle_kernel(incoming, sides, out):
    come, go = ORDERS[1 if incoming else 0]
    in_mesh = tuple(range(len(come)))
    left, right = [unpack(sides[:, n : n + 16, :].astype(F32)) for n in (0, 16)]
    if incoming:
        summed = [over_rows(a.astype(BF16), b.astype(BF16)) for a, b in zip(left, right)]
        summed = [reorder(v, in_mesh, go) for v in summed]
    else:
        left = [reorder(v, come, go) for v in left]
        right = [reorder(v, come, in_mesh) for v in right]
        summed = [over_columns(a.astype(BF16), b.astype(BF16)) for a, b in zip(left, right)]
    out[...] = pack(summed).astype(BF16)


def call(kernel, outs, scratch, *args, place=pltpu.VMEM):
    in_vmem = pl.BlockSpec(memory_space=pltpu.VMEM)
    return pl.pallas_call(
        kernel,
        out_shape=[jax.ShapeDtypeStruct(*o) for o in outs],
        in_specs=[pl.BlockSpec(memory_space=place)] * len(args),
        out_specs=[in_vmem] * len(outs),
        scratch_shapes=scratch,
        compiler_params=pltpu.CompilerParams(vmem_limit_bytes=24 * 2**20),
    )(*args)


def exchange(blocks):
    return lax.all_to_all(blocks, PEERS, split_axis=0, concat_axis=0, tiled=True)


def exchange_in_order(blocks, chips):
    listed = [[2 * chip + core for chip in chips for core in range(2)]]
    return lax.all_to_all(blocks, "row", split_axis=0, concat_axis=0, axis_index_groups=listed, tiled=True)


def packed_updates(count, pair_rep, pair_mask, pw, pb, gw, gb, ow, ob, ns, no):
    rows_of, width, channels = pair_rep.shape
    flat = (channels, rows_of * width)
    projected = [((count, 32, width), BF16), (flat, F32), (flat, BF16)]
    summed = [((count, 16, width), BF16)]
    params = [pair_rep, pair_mask, pw, gw, pb, gb, ob, ns, no]
    params = [pltpu.with_memory_space_constraint(v, pltpu.HBM) for v in params]
    held = [pltpu.VMEM(v.shape[1:] if n in (2, 3) else v.shape, v.dtype) for n, v in enumerate(params)]
    held += [pltpu.VMEM((2 * EACH, channels), F32), pltpu.SemaphoreType.DMA((len(params),))]
    back = pltpu.VMEM((OWN * channels, width), F32)
    mixed = pltpu.VMEM((2, OWN * channels, width), F32)
    kept = [((channels, 2 * EACH), F32), ((2 * OWN, width), F32)]
    send, gate, turned, columns, keep = call(first_kernel, projected + kept, held + [mixed], *params, place=pltpu.HBM)
    (send,) = call(functools.partial(triangle_kernel, False), summed, [], exchange_in_order(send, ORDERS[0][0]))
    send, gate, turned = call(middle_kernel, projected, [mixed, back], exchange_in_order(send, ORDERS[0][1]), turned, gate, columns, keep, pw, gw, ow)
    (send,) = call(functools.partial(triangle_kernel, True), summed, [], exchange_in_order(send, ORDERS[1][0]))
    (out,) = call(last_kernel, [(pair_rep.shape, BF16)], [back], exchange_in_order(send, ORDERS[1][1]), turned, gate, columns, ow)
    return out


def update(pair_t, pair_mask, u, incoming, peers, rows_of, pw, pb, gw, gb, ow, ob, ns, no):
    channels, positions = pair_t.shape
    width = positions // rows_of
    h = pw.shape[2] // 4
    count = peers[0] * peers[1]
    own = h // count
    normed = layer_norm(pair_t, ns[u, 0][:, None], no[u, 0][:, None]).astype(BF16)
    projected = over_rows(jnp.concatenate([pw[u], gw[u]], 1), normed) + jnp.concatenate([pb[u], gb[u]], 0)[:, None]
    parts = [projected[n * h : (n + 1) * h] for n in range(4)]
    gating = jax.nn.sigmoid(projected[4 * h :])
    mask = pair_mask.astype(F32).reshape(1, positions)
    left = (mask * jax.nn.sigmoid(parts[1]) * parts[0]).astype(BF16)
    right = (mask * jax.nn.sigmoid(parts[3]) * parts[2]).astype(BF16)
    sides = exchange(jnp.stack([v.reshape(count, own, rows_of, width) for v in (left, right)], 1))
    sides = sides.reshape(peers[0], peers[1], 2, own, rows_of, width)
    sides = sides.transpose(2, 3, 0, 4, 1, 5).reshape(2, own, peers[0] * rows_of, peers[1] * width)
    form = "cki,ckj->cij" if incoming else "cik,cjk->cij"
    summed = jnp.einsum(form, sides[0], sides[1], preferred_element_type=F32).astype(BF16)
    summed = summed.reshape(own, peers[0], rows_of, peers[1], width).transpose(1, 3, 0, 2, 4)
    summed = exchange(summed.reshape(count, own, rows_of, width)).reshape(h, positions).astype(F32)
    hidden = layer_norm(summed, ns[u, 1][:, None], no[u, 1][:, None]).astype(BF16)
    change = over_rows(ow[u], hidden) + ob[u][:, None]
    return (pair_t + gating * change).astype(BF16)


def plain_updates(peers, pair_rep, pair_mask, *params):
    rows_of, width, channels = pair_rep.shape
    pair_t = pair_rep.reshape(rows_of * width, channels).T
    for u in range(2):
        pair_t = update(pair_t.astype(F32), pair_mask, u, u == 1, peers, rows_of, *params)
    return pair_t.T.reshape(rows_of, width, channels)


def solution(mesh):
    peers = (mesh.shape["row"], mesh.shape["ka"])
    count = peers[0] * peers[1]

    def on_device(pair_rep, pair_mask, *params):
        rows_of, width, channels = pair_rep.shape
        hidden = params[0].shape[2] // 4
        fits = peers[1] == 1 and rows_of == OWN and hidden == OWN * count and count == 2 * len(ORDERS[0][0])
        if fits and channels == hidden == 128 and width % 128 == 0:
            return packed_updates(count, pair_rep, pair_mask, *params)
        return plain_updates(peers, pair_rep, pair_mask, *params)

    split = P(("grp", "row"), "ka", None)
    in_specs = (split, P(("grp", "row"), "ka")) + (P(),) * 8
    return jax.shard_map(on_device, mesh=mesh, in_specs=in_specs, out_specs=split, check_vma=False)
```

```python
import functools

import jax
import jax.numpy as jnp
from jax import lax
from jax.experimental import pallas as pl
from jax.experimental.pallas import tpu as pltpu
from jax.sharding import PartitionSpec as P

PEERS = ("row", "ka")
OWN = 4
EACH = 16
BF16, F32 = jnp.bfloat16, jnp.float32


def over_rows(a, b):
    return lax.dot_general(a, b, (((0,), (0,)), ((), ())), preferred_element_type=F32)


def over_columns(a, b):
    return lax.dot_general(a, b, (((1,), (1,)), ((), ())), preferred_element_type=F32)


def standardised(values):
    average = jnp.mean(values, 0, keepdims=True)
    centred = values - average
    variance = jnp.mean(centred * centred, 0, keepdims=True)
    return centred * lax.rsqrt(variance + 1e-05)


def layer_norm(values, norm_gain, norm_bias):
    return standardised(values) * norm_gain + norm_bias


def pack(blocks):
    channels, width = blocks[0].shape
    tiles = [b.reshape(channels // 8, 8, width) for b in blocks]
    turned = [pltpu.roll(b, 4, axis=0).reshape(channels // 8, 8, width) for b in blocks]
    low = lax.broadcasted_iota(jnp.int32, tiles[0].shape, 1) < 4
    back = [pltpu.roll(b, channels - 4, axis=0).reshape(channels // 8, 8, width) for b in blocks]
    even = [jnp.where(low, tiles[n], turned[n + 1]) for n in (0, 2)]
    odd = [jnp.where(low, back[n], tiles[n + 1]) for n in (0, 2)]
    return jnp.stack([jnp.stack(even, 1), jnp.stack(odd, 1)], 1).reshape(channels // 4, 16, width)


def unpack(packed):
    count, _, width = packed.shape
    tiles = packed.reshape(count // 2, 2, 2, 8, width)
    low = lax.broadcasted_iota(jnp.int32, (count // 2, 8, width), 1) < 4
    blocks = []
    for n in range(2):
        even, odd = tiles[:, 0, n], tiles[:, 1, n]
        down = pltpu.roll(odd.reshape(count * 4, width), 4, axis=0).reshape(even.shape)
        up = pltpu.roll(even.reshape(count * 4, width), count * 4 - 4, axis=0).reshape(even.shape)
        blocks.append(jnp.where(low, even, down).reshape(count * 4, width))
        blocks.append(jnp.where(low, up, odd).reshape(count * 4, width))
    return blocks


def sigmoid(x):
    return 0.5 * jnp.tanh(0.5 * x) + 0.5


def broadcast_columns(columns, first, many, width):
    held = columns[...]
    return [jnp.broadcast_to(held[:, n : n + 1], (held.shape[0], width)) for n in range(first, first + many)]


def project(u, norm, mask, proj_weight, columns, send, mixed):
    width = norm.shape[1] // OWN
    h = proj_weight.shape[1] // 4
    rows = mixed.shape[1]
    biases = broadcast_columns(columns, u * EACH + 2, 4, width)
    turned = [proj_weight[:, n * h : (n + 1) * h].T for n in range(4)]
    halves = [mask[i : i + 1, :] * 0.5 for i in range(OWN)]
    joined = [norm[:, pair * width : (pair + 2) * width] for pair in range(0, OWN, 2)]
    for side in range(2):
        for pair in range(0, OWN, 2):
            value, gating = [jnp.dot(turned[2 * side + n], joined[pair // 2], preferred_element_type=F32) for n in (0, 1)]
            for n in range(2):
                i, at = pair + n, slice(n * width, (n + 1) * width)
                weight = halves[i] + halves[i] * jnp.tanh(0.5 * (gating[:, at] + biases[2 * side + 1]))
                mixed[side, pl.ds(i, h, stride=OWN), :] = weight * (value[:, at] + biases[2 * side])
        send[:, side * 16 : (side + 1) * 16, :] = mixed[side].reshape(rows // 16, 16, width).astype(BF16)


def finish(u, z, summed, gate, turned, columns, mixed):
    width = z[0].shape[1]
    gain, offset, bias = broadcast_columns(columns, u * EACH + 7, 3, width)
    mixed[...] = summed[...].astype(F32).reshape(mixed.shape)
    results = []
    for pair in range(0, OWN, 2):
        blocks = [mixed[pl.ds(i, mixed.shape[0] // OWN, stride=OWN), :] for i in (pair, pair + 1)]
        hidden = jnp.concatenate([layer_norm(v, gain, offset).astype(BF16) for v in blocks], 1)
        both = jnp.dot(turned, hidden, preferred_element_type=F32)
        for n in range(2):
            change = both[:, n * width : (n + 1) * width] + bias
            at = slice((pair + n) * width, (pair + n + 1) * width)
            results.append((z[pair + n].astype(F32) + gate[:, at] * change).astype(BF16))
    return results


def first_kernel(
    pair, mask, pw, gw, pb, gb, ob, ns, no, send, norm, turned, columns, keep, gw_in, pair_in, mask_in, pw_in, pb_in, gb_in, ob_in, ns_in, no_in, rows, arrived, mixed
):
    moves = [(pair, pair_in), (pw.at[0], pw_in), (ns, ns_in), (no, no_in), (pb, pb_in), (gb, gb_in), (ob, ob_in)]
    moves += [(mask, mask_in), (gw.at[0], gw_in)]
    moves = [pltpu.make_async_copy(a, b, arrived.at[n]) for n, (a, b) in enumerate(moves)]
    for move in moves:
        move.start()
    for move in moves:
        move.wait()
    width = pair.shape[1]
    z = [pair_in[i].T for i in range(OWN)]
    h = pw.shape[2] // 4
    for u in range(2):
        found = [ns_in[u, 0:1, :], no_in[u, 0:1, :]] + [pb_in[u : u + 1, n * h : (n + 1) * h] for n in range(4)]
        found += [gb_in[u : u + 1, :], ns_in[u, 1:2, :], no_in[u, 1:2, :], ob_in[u : u + 1, :]]
        for n, row in enumerate(found):
            rows[u * EACH + n : u * EACH + n + 1, :] = row
    columns[...] = rows[...].T
    keep[0:OWN, :] = mask_in[...].astype(F32)
    normalise(0, z, columns, norm, turned, width)
    project(0, norm, keep, pw_in[...], columns, send, mixed)


def normalise(u, z, columns, norm, turned, width):
    gain, offset = broadcast_columns(columns, u * EACH, 2, width)
    for i in range(OWN):
        at = slice(i * width, (i + 1) * width)
        turned[:, at] = z[i]
        norm[:, at] = layer_norm(z[i].astype(F32), gain, offset).astype(BF16)


def middle_kernel(summed, old, old_gate, columns, keep, pw, ow, send, norm, turned, mixed, mixed_back):
    width = keep.shape[1]
    z = [old[:, i * width : (i + 1) * width] for i in range(OWN)]
    z = finish(0, z, summed, old_gate, ow[0].T, columns, mixed_back)
    normalise(1, z, columns, norm, turned, width)
    project(1, norm, keep, pw[1], columns, send, mixed)


def last_kernel(summed, old, old_gate, columns, weight, out, mixed_back):
    width = out.shape[1]
    z = [old[:, i * width : (i + 1) * width] for i in range(OWN)]
    z = finish(1, z, summed, old_gate, weight[...], columns, mixed_back)
    for i in range(OWN):
        out[i] = z[i].T


def triangle(incoming, sides, out):
    left, right = [[v.astype(BF16) for v in unpack(sides[:, n : n + 16, :].astype(F32))] for n in (0, 16)]
    product = over_rows if incoming else over_columns
    out[...] = pack([product(a, b) for a, b in zip(left, right)]).astype(BF16)


def output_gate(u, normed, gate_weight, columns, gate):
    gating = jnp.dot(gate_weight.T, normed[...], preferred_element_type=F32)
    gate[...] = sigmoid(gating + columns[:, u * EACH + 6 : u * EACH + 7])


def outgoing_kernel(sides, normed, gw, columns, out, gate):
    triangle(False, sides, out)
    output_gate(0, normed, gw[...], columns, gate)


def incoming_kernel(sides, normed, gw, columns, ow, out, gate, turned):
    triangle(True, sides, out)
    output_gate(1, normed, gw[1], columns, gate)
    turned[...] = ow[1].T


def call(kernel, outs, scratch, *args, place=pltpu.VMEM):
    in_vmem = pl.BlockSpec(memory_space=pltpu.VMEM)
    return pl.pallas_call(
        kernel,
        out_shape=[jax.ShapeDtypeStruct(*o) for o in outs],
        in_specs=[pl.BlockSpec(memory_space=place)] * len(args),
        out_specs=[in_vmem] * len(outs),
        scratch_shapes=scratch,
        compiler_params=pltpu.CompilerParams(vmem_limit_bytes=24 * 2**20),
    )(*args)


def exchange(blocks):
    return lax.all_to_all(blocks, PEERS, split_axis=0, concat_axis=0, tiled=True)


def packed_updates(count, pair_rep, pair_mask, pw, pb, gw, gb, ow, ob, ns, no):
    rows_of, width, channels = pair_rep.shape
    flat = (channels, rows_of * width)
    square = ((channels, channels), BF16)
    projected = [((count, 32, width), BF16), (flat, BF16), (flat, BF16)]
    summed = [((count, 16, width), BF16), (flat, F32)]
    params = [pair_rep, pair_mask, pw, gw, pb, gb, ob, ns, no]
    params = [pltpu.with_memory_space_constraint(v, pltpu.HBM) for v in params]
    held = [pltpu.VMEM(v.shape[1:] if n == 2 else v.shape, v.dtype) for n, v in enumerate(params) if n != 3]
    held += [pltpu.VMEM((2 * EACH, channels), F32), pltpu.SemaphoreType.DMA((len(params),))]
    back = pltpu.VMEM((OWN * channels, width), F32)
    mixed = pltpu.VMEM((2, OWN * channels, width), F32)
    kept = [((channels, 2 * EACH), F32), ((2 * OWN, width), F32), square]
    send, norm, turned, columns, keep, gw0 = call(
        first_kernel, projected + kept, held + [mixed], *params, place=pltpu.HBM
    )
    send, gate = call(outgoing_kernel, summed, [], exchange(send), norm, gw0, columns)
    send, norm, turned = call(
        middle_kernel, projected, [mixed, back], exchange(send), turned, gate, columns, keep, pw, ow
    )
    send, gate, weight = call(incoming_kernel, summed + [square], [], exchange(send), norm, gw, columns, ow)
    (out,) = call(last_kernel, [(pair_rep.shape, BF16)], [back], exchange(send), turned, gate, columns, weight)
    return out


def update(pair_t, pair_mask, u, incoming, peers, rows_of, pw, pb, gw, gb, ow, ob, ns, no):
    channels, positions = pair_t.shape
    width = positions // rows_of
    h = pw.shape[2] // 4
    count = peers[0] * peers[1]
    own = h // count
    normed = layer_norm(pair_t, ns[u, 0][:, None], no[u, 0][:, None]).astype(BF16)
    projected = over_rows(jnp.concatenate([pw[u], gw[u]], 1), normed) + jnp.concatenate([pb[u], gb[u]], 0)[:, None]
    parts = [projected[n * h : (n + 1) * h] for n in range(4)]
    gating = jax.nn.sigmoid(projected[4 * h :])
    mask = pair_mask.astype(F32).reshape(1, positions)
    left = (mask * jax.nn.sigmoid(parts[1]) * parts[0]).astype(BF16)
    right = (mask * jax.nn.sigmoid(parts[3]) * parts[2]).astype(BF16)
    sides = exchange(jnp.stack([v.reshape(count, own, rows_of, width) for v in (left, right)], 1))
    sides = sides.reshape(peers[0], peers[1], 2, own, rows_of, width)
    sides = sides.transpose(2, 3, 0, 4, 1, 5).reshape(2, own, peers[0] * rows_of, peers[1] * width)
    form = "cki,ckj->cij" if incoming else "cik,cjk->cij"
    summed = jnp.einsum(form, sides[0], sides[1], preferred_element_type=F32).astype(BF16)
    summed = summed.reshape(own, peers[0], rows_of, peers[1], width).transpose(1, 3, 0, 2, 4)
    summed = exchange(summed.reshape(count, own, rows_of, width)).reshape(h, positions).astype(F32)
    hidden = layer_norm(summed, ns[u, 1][:, None], no[u, 1][:, None]).astype(BF16)
    change = over_rows(ow[u], hidden) + ob[u][:, None]
    return (pair_t + gating * change).astype(BF16)


def plain_updates(peers, pair_rep, pair_mask, *params):
    rows_of, width, channels = pair_rep.shape
    pair_t = pair_rep.reshape(rows_of * width, channels).T
    for u in range(2):
        pair_t = update(pair_t.astype(F32), pair_mask, u, u == 1, peers, rows_of, *params)
    return pair_t.T.reshape(rows_of, width, channels)


def solution(mesh):
    peers = (mesh.shape["row"], mesh.shape["ka"])
    count = peers[0] * peers[1]

    def on_device(pair_rep, pair_mask, *params):
        rows_of, width, channels = pair_rep.shape
        hidden = params[0].shape[2] // 4
        fits = peers[1] == 1 and rows_of == OWN and hidden == OWN * count and count % 2 == 0
        if fits and channels == hidden == 128 and width % 128 == 0:
            return packed_updates(count, pair_rep, pair_mask, *params)
        return plain_updates(peers, pair_rep, pair_mask, *params)

    split = P(("grp", "row"), "ka", None)
    in_specs = (split, P(("grp", "row"), "ka")) + (P(),) * 8
    return jax.shard_map(on_device, mesh=mesh, in_specs=in_specs, out_specs=split, check_vma=False)
```

```python
import functools

import jax
import jax.numpy as jnp
from jax import lax
from jax.experimental import pallas as pl
from jax.experimental.pallas import tpu as pltpu
from jax.sharding import PartitionSpec as P

PEERS = ("row", "ka")
OWN = 4
ORDERS = (
    ((0, 1, 2, 3, 4, 6, 8, 5, 12, 7, 9, 10, 13, 14, 11, 15), (0, 1, 2, 3, 4, 6, 8, 5, 12, 7, 9, 10, 13, 14, 11, 15)),
    ((0, 15, 11, 14, 13, 10, 9, 7, 12, 5, 8, 6, 4, 3, 2, 1), (0, 15, 11, 14, 13, 10, 9, 7, 12, 5, 8, 6, 4, 3, 2, 1)),
)
EACH = 16
BF16, F32 = jnp.bfloat16, jnp.float32


def over_rows(a, b):
    return lax.dot_general(a, b, (((0,), (0,)), ((), ())), preferred_element_type=F32)


def over_columns(a, b):
    return lax.dot_general(a, b, (((1,), (1,)), ((), ())), preferred_element_type=F32)


def layer_norm(values, norm_gain, norm_bias):
    average = jnp.mean(values, 0, keepdims=True)
    centred = values - average
    variance = jnp.mean(centred * centred, 0, keepdims=True)
    return centred * lax.rsqrt(variance + 1e-05) * norm_gain + norm_bias


def pack(blocks):
    channels, width = blocks[0].shape
    tiles = [b.reshape(channels // 8, 8, width) for b in blocks]
    turned = [pltpu.roll(b, 4, axis=0).reshape(channels // 8, 8, width) for b in blocks]
    low = lax.broadcasted_iota(jnp.int32, tiles[0].shape, 1) < 4
    back = [pltpu.roll(b, channels - 4, axis=0).reshape(channels // 8, 8, width) for b in blocks]
    even = [jnp.where(low, tiles[n], turned[n + 1]) for n in (0, 2)]
    odd = [jnp.where(low, back[n], tiles[n + 1]) for n in (0, 2)]
    return jnp.stack([jnp.stack(even, 1), jnp.stack(odd, 1)], 1).reshape(channels // 4, 16, width)


def unpack(packed):
    count, _, width = packed.shape
    tiles = packed.reshape(count // 2, 2, 2, 8, width)
    low = lax.broadcasted_iota(jnp.int32, (count // 2, 8, width), 1) < 4
    blocks = []
    for n in range(2):
        even, odd = tiles[:, 0, n], tiles[:, 1, n]
        down = pltpu.roll(odd.reshape(count * 4, width), 4, axis=0).reshape(even.shape)
        up = pltpu.roll(even.reshape(count * 4, width), count * 4 - 4, axis=0).reshape(even.shape)
        blocks.append(jnp.where(low, even, down).reshape(count * 4, width))
        blocks.append(jnp.where(low, up, odd).reshape(count * 4, width))
    return blocks


def sigmoid(x):
    return 0.5 * jnp.tanh(0.5 * x) + 0.5


def broadcast_columns(columns, first, many, width):
    held = columns[...]
    return [jnp.broadcast_to(held[:, n : n + 1], (held.shape[0], width)) for n in range(first, first + many)]


def project(u, z, mask, proj_weight, gate_weight, columns, send, gate, mixed):
    width = z[0].shape[1]
    h = proj_weight.shape[1] // 4
    rows = mixed.shape[1]
    gain, offset, *biases = broadcast_columns(columns, u * EACH, 7, width)
    turned = [proj_weight[:, n * h : (n + 1) * h].T for n in range(4)] + [gate_weight.T]
    for pair in range(0, OWN, 2):
        normed = [layer_norm(z[i], gain, offset).astype(BF16) for i in (pair, pair + 1)]
        normed = jnp.concatenate(normed, 1)
        both = [jnp.dot(w, normed, preferred_element_type=F32) for w in turned]
        for n in range(2):
            i = pair + n
            parts = [v[:, n * width : (n + 1) * width] + b for v, b in zip(both, biases)]
            keep = mask[i : i + 1, :]
            mixed[0, pl.ds(i, h, stride=OWN), :] = keep * sigmoid(parts[1]) * parts[0]
            mixed[1, pl.ds(i, h, stride=OWN), :] = keep * sigmoid(parts[3]) * parts[2]
            gate[:, i * width : (i + 1) * width] = sigmoid(parts[4])
    send[:, 0:16, :] = mixed[0].reshape(rows // 16, 16, width).astype(BF16)
    send[:, 16:32, :] = mixed[1].reshape(rows // 16, 16, width).astype(BF16)


def finish(u, z, summed, gate, out_weight, columns, mixed):
    width = z[0].shape[1]
    gain, offset, bias = broadcast_columns(columns, u * EACH + 7, 3, width)
    turned = out_weight.T
    mixed[...] = summed[...].astype(F32).reshape(mixed.shape)
    results = []
    for pair in range(0, OWN, 2):
        blocks = [mixed[pl.ds(i, mixed.shape[0] // OWN, stride=OWN), :] for i in (pair, pair + 1)]
        blocks = [reorder(v, ORDERS[u][1], ORDERS[u][0]) for v in blocks]
        hidden = jnp.concatenate([layer_norm(v, gain, offset).astype(BF16) for v in blocks], 1)
        both = jnp.dot(turned, hidden, preferred_element_type=F32)
        for n in range(2):
            change = both[:, n * width : (n + 1) * width] + bias
            at = slice((pair + n) * width, (pair + n + 1) * width)
            results.append((z[pair + n].astype(F32) + gate[:, at] * change).astype(BF16))
    return results


def first_kernel(
    pair, mask, pw, gw, pb, gb, ob, ns, no, send, gate, turned, columns, keep, pair_in, mask_in, pw_in, gw_in, pb_in, gb_in, ob_in, ns_in, no_in, rows, arrived, mixed
):
    moves = [(pair, pair_in), (pb, pb_in), (gb, gb_in), (ob, ob_in), (ns, ns_in), (no, no_in)]
    moves += [(pw.at[0], pw_in), (gw.at[0], gw_in), (mask, mask_in)]
    moves = [pltpu.make_async_copy(a, b, arrived.at[n]) for n, (a, b) in enumerate(moves)]
    for move in moves:
        move.start()
    moves[0].wait()
    width = pair.shape[1]
    z = [pair_in[i].T for i in range(OWN)]
    for i in range(OWN):
        turned[:, i * width : (i + 1) * width] = z[i]
    for move in moves[1:6]:
        move.wait()
    h = pw.shape[2] // 4
    for u in range(2):
        found = [ns_in[u, 0:1, :], no_in[u, 0:1, :]] + [pb_in[u : u + 1, n * h : (n + 1) * h] for n in range(4)]
        found += [gb_in[u : u + 1, :], ns_in[u, 1:2, :], no_in[u, 1:2, :], ob_in[u : u + 1, :]]
        for n, row in enumerate(found):
            rows[u * EACH + n : u * EACH + n + 1, :] = row
    columns[...] = rows[...].T
    for move in moves[6:]:
        move.wait()
    keep[0:OWN, :] = mask_in[...].astype(F32)
    project(0, [v.astype(F32) for v in z], keep, pw_in[...], gw_in[...], columns, send, gate, mixed)


def middle_kernel(summed, old, old_gate, columns, keep, pw, gw, ow, send, gate, turned, mixed, mixed_back):
    width = keep.shape[1]
    z = finish(0, [old[:, i * width : (i + 1) * width] for i in range(OWN)], summed, old_gate, ow[0], columns, mixed_back)
    for i in range(OWN):
        turned[:, i * width : (i + 1) * width] = z[i]
    project(1, [v.astype(F32) for v in z], keep, pw[1], gw[1], columns, send, gate, mixed)


def last_kernel(summed, old, old_gate, columns, ow, out, mixed_back):
    width = out.shape[1]
    z = finish(1, [old[:, i * width : (i + 1) * width] for i in range(OWN)], summed, old_gate, ow[1], columns, mixed_back)
    for i in range(OWN):
        out[i] = z[i].T


def reorder(values, have, want):
    tiles = values.reshape(len(have), 2 * OWN, values.shape[1])
    places = [have.index(chip) for chip in want]
    return jnp.concatenate([tiles[n : n + 1] for n in places]).reshape(values.shape)


def triangle_kernel(incoming, sides, out):
    come, go = ORDERS[1 if incoming else 0]
    in_mesh = tuple(range(len(come)))
    left, right = [unpack(sides[:, n : n + 16, :].astype(F32)) for n in (0, 16)]
    if incoming:
        summed = [over_rows(a.astype(BF16), b.astype(BF16)) for a, b in zip(left, right)]
        summed = [reorder(v, in_mesh, go) for v in summed]
    else:
        left = [reorder(v, come, go) for v in left]
        right = [reorder(v, come, in_mesh) for v in right]
        summed = [over_columns(a.astype(BF16), b.astype(BF16)) for a, b in zip(left, right)]
    out[...] = pack(summed).astype(BF16)


def call(kernel, outs, scratch, *args, place=pltpu.VMEM):
    in_vmem = pl.BlockSpec(memory_space=pltpu.VMEM)
    return pl.pallas_call(
        kernel,
        out_shape=[jax.ShapeDtypeStruct(*o) for o in outs],
        in_specs=[pl.BlockSpec(memory_space=place)] * len(args),
        out_specs=[in_vmem] * len(outs),
        scratch_shapes=scratch,
        compiler_params=pltpu.CompilerParams(vmem_limit_bytes=24 * 2**20),
    )(*args)


def exchange(blocks):
    return lax.all_to_all(blocks, PEERS, split_axis=0, concat_axis=0, tiled=True)


def exchange_in_order(blocks, chips):
    listed = [[2 * chip + core for chip in chips for core in range(2)]]
    return lax.all_to_all(blocks, "row", split_axis=0, concat_axis=0, axis_index_groups=listed, tiled=True)


def packed_updates(count, pair_rep, pair_mask, pw, pb, gw, gb, ow, ob, ns, no):
    rows_of, width, channels = pair_rep.shape
    flat = (channels, rows_of * width)
    projected = [((count, 32, width), BF16), (flat, F32), (flat, BF16)]
    summed = [((count, 16, width), BF16)]
    params = [pair_rep, pair_mask, pw, gw, pb, gb, ob, ns, no]
    params = [pltpu.with_memory_space_constraint(v, pltpu.HBM) for v in params]
    held = [pltpu.VMEM(v.shape[1:] if n in (2, 3) else v.shape, v.dtype) for n, v in enumerate(params)]
    held += [pltpu.VMEM((2 * EACH, channels), F32), pltpu.SemaphoreType.DMA((len(params),))]
    back = pltpu.VMEM((OWN * channels, width), F32)
    mixed = pltpu.VMEM((2, OWN * channels, width), F32)
    kept = [((channels, 2 * EACH), F32), ((2 * OWN, width), F32)]
    send, gate, turned, columns, keep = call(first_kernel, projected + kept, held + [mixed], *params, place=pltpu.HBM)
    (send,) = call(functools.partial(triangle_kernel, False), summed, [], exchange_in_order(send, ORDERS[0][0]))
    send, gate, turned = call(middle_kernel, projected, [mixed, back], exchange_in_order(send, ORDERS[0][1]), turned, gate, columns, keep, pw, gw, ow)
    (send,) = call(functools.partial(triangle_kernel, True), summed, [], exchange_in_order(send, ORDERS[1][0]))
    (out,) = call(last_kernel, [(pair_rep.shape, BF16)], [back], exchange_in_order(send, ORDERS[1][1]), turned, gate, columns, ow)
    return out


def update(pair_t, pair_mask, u, incoming, peers, rows_of, pw, pb, gw, gb, ow, ob, ns, no):
    channels, positions = pair_t.shape
    width = positions // rows_of
    h = pw.shape[2] // 4
    count = peers[0] * peers[1]
    own = h // count
    normed = layer_norm(pair_t, ns[u, 0][:, None], no[u, 0][:, None]).astype(BF16)
    projected = over_rows(jnp.concatenate([pw[u], gw[u]], 1), normed) + jnp.concatenate([pb[u], gb[u]], 0)[:, None]
    parts = [projected[n * h : (n + 1) * h] for n in range(4)]
    gating = jax.nn.sigmoid(projected[4 * h :])
    mask = pair_mask.astype(F32).reshape(1, positions)
    left = (mask * jax.nn.sigmoid(parts[1]) * parts[0]).astype(BF16)
    right = (mask * jax.nn.sigmoid(parts[3]) * parts[2]).astype(BF16)
    sides = exchange(jnp.stack([v.reshape(count, own, rows_of, width) for v in (left, right)], 1))
    sides = sides.reshape(peers[0], peers[1], 2, own, rows_of, width)
    sides = sides.transpose(2, 3, 0, 4, 1, 5).reshape(2, own, peers[0] * rows_of, peers[1] * width)
    form = "cki,ckj->cij" if incoming else "cik,cjk->cij"
    summed = jnp.einsum(form, sides[0], sides[1], preferred_element_type=F32).astype(BF16)
    summed = summed.reshape(own, peers[0], rows_of, peers[1], width).transpose(1, 3, 0, 2, 4)
    summed = exchange(summed.reshape(count, own, rows_of, width)).reshape(h, positions).astype(F32)
    hidden = layer_norm(summed, ns[u, 1][:, None], no[u, 1][:, None]).astype(BF16)
    change = over_rows(ow[u], hidden) + ob[u][:, None]
    return (pair_t + gating * change).astype(BF16)


def plain_updates(peers, pair_rep, pair_mask, *params):
    rows_of, width, channels = pair_rep.shape
    pair_t = pair_rep.reshape(rows_of * width, channels).T
    for u in range(2):
        pair_t = update(pair_t.astype(F32), pair_mask, u, u == 1, peers, rows_of, *params)
    return pair_t.T.reshape(rows_of, width, channels)


def solution(mesh):
    peers = (mesh.shape["row"], mesh.shape["ka"])
    count = peers[0] * peers[1]

    def on_device(pair_rep, pair_mask, *params):
        rows_of, width, channels = pair_rep.shape
        hidden = params[0].shape[2] // 4
        fits = peers[1] == 1 and rows_of == OWN and hidden == OWN * count and count == 2 * len(ORDERS[0][0])
        if fits and channels == hidden == 128 and width % 128 == 0:
            return packed_updates(count, pair_rep, pair_mask, *params)
        return plain_updates(peers, pair_rep, pair_mask, *params)

    split = P(("grp", "row"), "ka", None)
    in_specs = (split, P(("grp", "row"), "ka")) + (P(),) * 8
    return jax.shard_map(on_device, mesh=mesh, in_specs=in_specs, out_specs=split, check_vma=False)
```

```python
import functools

import jax
import jax.numpy as jnp
from jax import lax
from jax.experimental import pallas as pl
from jax.experimental.pallas import tpu as pltpu
from jax.sharding import PartitionSpec as P

PEERS = ("row", "ka")
OWN = 4
ORDERS = (
    ((0, 15, 11, 14, 13, 10, 9, 7, 12, 5, 8, 6, 4, 3, 2, 1), (0, 15, 11, 14, 13, 10, 9, 7, 12, 5, 8, 6, 4, 3, 2, 1)),
    ((0, 15, 11, 14, 13, 10, 9, 7, 12, 5, 8, 6, 4, 3, 2, 1), (0, 15, 11, 14, 13, 10, 9, 7, 12, 5, 8, 6, 4, 3, 2, 1)),
)
EACH = 16
BF16, F32 = jnp.bfloat16, jnp.float32


def over_rows(a, b):
    return lax.dot_general(a, b, (((0,), (0,)), ((), ())), preferred_element_type=F32)


def over_columns(a, b):
    return lax.dot_general(a, b, (((1,), (1,)), ((), ())), preferred_element_type=F32)


def layer_norm(values, norm_gain, norm_bias):
    average = jnp.mean(values, 0, keepdims=True)
    centred = values - average
    variance = jnp.mean(centred * centred, 0, keepdims=True)
    return centred * lax.rsqrt(variance + 1e-05) * norm_gain + norm_bias


def pack(blocks):
    channels, width = blocks[0].shape
    tiles = [b.reshape(channels // 8, 8, width) for b in blocks]
    turned = [pltpu.roll(b, 4, axis=0).reshape(channels // 8, 8, width) for b in blocks]
    low = lax.broadcasted_iota(jnp.int32, tiles[0].shape, 1) < 4
    back = [pltpu.roll(b, channels - 4, axis=0).reshape(channels // 8, 8, width) for b in blocks]
    even = [jnp.where(low, tiles[n], turned[n + 1]) for n in (0, 2)]
    odd = [jnp.where(low, back[n], tiles[n + 1]) for n in (0, 2)]
    return jnp.stack([jnp.stack(even, 1), jnp.stack(odd, 1)], 1).reshape(channels // 4, 16, width)


def unpack(packed):
    count, _, width = packed.shape
    tiles = packed.reshape(count // 2, 2, 2, 8, width)
    low = lax.broadcasted_iota(jnp.int32, (count // 2, 8, width), 1) < 4
    blocks = []
    for n in range(2):
        even, odd = tiles[:, 0, n], tiles[:, 1, n]
        down = pltpu.roll(odd.reshape(count * 4, width), 4, axis=0).reshape(even.shape)
        up = pltpu.roll(even.reshape(count * 4, width), count * 4 - 4, axis=0).reshape(even.shape)
        blocks.append(jnp.where(low, even, down).reshape(count * 4, width))
        blocks.append(jnp.where(low, up, odd).reshape(count * 4, width))
    return blocks


def sigmoid(x):
    return 0.5 * jnp.tanh(0.5 * x) + 0.5


def broadcast_columns(columns, first, many, width):
    held = columns[...]
    return [jnp.broadcast_to(held[:, n : n + 1], (held.shape[0], width)) for n in range(first, first + many)]


def project(u, z, mask, proj_weight, gate_weight, columns, send, gate, mixed):
    width = z[0].shape[1]
    h = proj_weight.shape[1] // 4
    rows = mixed.shape[1]
    gain, offset, *biases = broadcast_columns(columns, u * EACH, 7, width)
    turned = [proj_weight[:, n * h : (n + 1) * h].T for n in range(4)] + [gate_weight.T]
    for pair in range(0, OWN, 2):
        normed = [layer_norm(z[i], gain, offset).astype(BF16) for i in (pair, pair + 1)]
        normed = jnp.concatenate(normed, 1)
        both = [jnp.dot(w, normed, preferred_element_type=F32) for w in turned]
        for n in range(2):
            i = pair + n
            parts = [v[:, n * width : (n + 1) * width] + b for v, b in zip(both, biases)]
            keep = mask[i : i + 1, :]
            mixed[0, pl.ds(i, h, stride=OWN), :] = keep * sigmoid(parts[1]) * parts[0]
            mixed[1, pl.ds(i, h, stride=OWN), :] = keep * sigmoid(parts[3]) * parts[2]
            gate[:, i * width : (i + 1) * width] = sigmoid(parts[4])
    send[:, 0:16, :] = mixed[0].reshape(rows // 16, 16, width).astype(BF16)
    send[:, 16:32, :] = mixed[1].reshape(rows // 16, 16, width).astype(BF16)


def finish(u, z, summed, gate, out_weight, columns, mixed):
    width = z[0].shape[1]
    gain, offset, bias = broadcast_columns(columns, u * EACH + 7, 3, width)
    turned = out_weight.T
    mixed[...] = summed[...].astype(F32).reshape(mixed.shape)
    results = []
    for pair in range(0, OWN, 2):
        blocks = [mixed[pl.ds(i, mixed.shape[0] // OWN, stride=OWN), :] for i in (pair, pair + 1)]
        blocks = [reorder(v, ORDERS[u][1], ORDERS[u][0]) for v in blocks]
        hidden = jnp.concatenate([layer_norm(v, gain, offset).astype(BF16) for v in blocks], 1)
        both = jnp.dot(turned, hidden, preferred_element_type=F32)
        for n in range(2):
            change = both[:, n * width : (n + 1) * width] + bias
            at = slice((pair + n) * width, (pair + n + 1) * width)
            results.append((z[pair + n].astype(F32) + gate[:, at] * change).astype(BF16))
    return results


def first_kernel(
    pair, mask, pw, gw, pb, gb, ob, ns, no, send, gate, turned, columns, keep, pair_in, mask_in, pw_in, gw_in, pb_in, gb_in, ob_in, ns_in, no_in, rows, arrived, mixed
):
    moves = [(pair, pair_in), (pb, pb_in), (gb, gb_in), (ob, ob_in), (ns, ns_in), (no, no_in)]
    moves += [(pw.at[0], pw_in), (gw.at[0], gw_in), (mask, mask_in)]
    moves = [pltpu.make_async_copy(a, b, arrived.at[n]) for n, (a, b) in enumerate(moves)]
    for move in moves:
        move.start()
    moves[0].wait()
    width = pair.shape[1]
    z = [pair_in[i].T for i in range(OWN)]
    for i in range(OWN):
        turned[:, i * width : (i + 1) * width] = z[i]
    for move in moves[1:6]:
        move.wait()
    h = pw.shape[2] // 4
    for u in range(2):
        found = [ns_in[u, 0:1, :], no_in[u, 0:1, :]] + [pb_in[u : u + 1, n * h : (n + 1) * h] for n in range(4)]
        found += [gb_in[u : u + 1, :], ns_in[u, 1:2, :], no_in[u, 1:2, :], ob_in[u : u + 1, :]]
        for n, row in enumerate(found):
            rows[u * EACH + n : u * EACH + n + 1, :] = row
    columns[...] = rows[...].T
    for move in moves[6:]:
        move.wait()
    keep[0:OWN, :] = mask_in[...].astype(F32)
    project(0, [v.astype(F32) for v in z], keep, pw_in[...], gw_in[...], columns, send, gate, mixed)


def middle_kernel(summed, old, old_gate, columns, keep, pw, gw, ow, send, gate, turned, mixed, mixed_back):
    width = keep.shape[1]
    z = finish(0, [old[:, i * width : (i + 1) * width] for i in range(OWN)], summed, old_gate, ow[0], columns, mixed_back)
    for i in range(OWN):
        turned[:, i * width : (i + 1) * width] = z[i]
    project(1, [v.astype(F32) for v in z], keep, pw[1], gw[1], columns, send, gate, mixed)


def last_kernel(summed, old, old_gate, columns, ow, out, mixed_back):
    width = out.shape[1]
    z = finish(1, [old[:, i * width : (i + 1) * width] for i in range(OWN)], summed, old_gate, ow[1], columns, mixed_back)
    for i in range(OWN):
        out[i] = z[i].T


def reorder(values, have, want):
    tiles = values.reshape(len(have), 2 * OWN, values.shape[1])
    places = [have.index(chip) for chip in want]
    return jnp.concatenate([tiles[n : n + 1] for n in places]).reshape(values.shape)


def triangle_kernel(incoming, sides, out):
    come, go = ORDERS[1 if incoming else 0]
    in_mesh = tuple(range(len(come)))
    left, right = [unpack(sides[:, n : n + 16, :].astype(F32)) for n in (0, 16)]
    if incoming:
        summed = [over_rows(a.astype(BF16), b.astype(BF16)) for a, b in zip(left, right)]
        summed = [reorder(v, in_mesh, go) for v in summed]
    else:
        left = [reorder(v, come, go) for v in left]
        right = [reorder(v, come, in_mesh) for v in right]
        summed = [over_columns(a.astype(BF16), b.astype(BF16)) for a, b in zip(left, right)]
    out[...] = pack(summed).astype(BF16)


def call(kernel, outs, scratch, *args, place=pltpu.VMEM):
    in_vmem = pl.BlockSpec(memory_space=pltpu.VMEM)
    return pl.pallas_call(
        kernel,
        out_shape=[jax.ShapeDtypeStruct(*o) for o in outs],
        in_specs=[pl.BlockSpec(memory_space=place)] * len(args),
        out_specs=[in_vmem] * len(outs),
        scratch_shapes=scratch,
        compiler_params=pltpu.CompilerParams(vmem_limit_bytes=24 * 2**20),
    )(*args)


def exchange(blocks):
    return lax.all_to_all(blocks, PEERS, split_axis=0, concat_axis=0, tiled=True)


def exchange_in_order(blocks, chips):
    listed = [[2 * chip + core for chip in chips for core in range(2)]]
    return lax.all_to_all(blocks, "row", split_axis=0, concat_axis=0, axis_index_groups=listed, tiled=True)


def packed_updates(count, pair_rep, pair_mask, pw, pb, gw, gb, ow, ob, ns, no):
    rows_of, width, channels = pair_rep.shape
    flat = (channels, rows_of * width)
    projected = [((count, 32, width), BF16), (flat, F32), (flat, BF16)]
    summed = [((count, 16, width), BF16)]
    params = [pair_rep, pair_mask, pw, gw, pb, gb, ob, ns, no]
    params = [pltpu.with_memory_space_constraint(v, pltpu.HBM) for v in params]
    held = [pltpu.VMEM(v.shape[1:] if n in (2, 3) else v.shape, v.dtype) for n, v in enumerate(params)]
    held += [pltpu.VMEM((2 * EACH, channels), F32), pltpu.SemaphoreType.DMA((len(params),))]
    back = pltpu.VMEM((OWN * channels, width), F32)
    mixed = pltpu.VMEM((2, OWN * channels, width), F32)
    kept = [((channels, 2 * EACH), F32), ((2 * OWN, width), F32)]
    send, gate, turned, columns, keep = call(first_kernel, projected + kept, held + [mixed], *params, place=pltpu.HBM)
    (send,) = call(functools.partial(triangle_kernel, False), summed, [], exchange_in_order(send, ORDERS[0][0]))
    send, gate, turned = call(middle_kernel, projected, [mixed, back], exchange_in_order(send, ORDERS[0][1]), turned, gate, columns, keep, pw, gw, ow)
    (send,) = call(functools.partial(triangle_kernel, True), summed, [], exchange_in_order(send, ORDERS[1][0]))
    (out,) = call(last_kernel, [(pair_rep.shape, BF16)], [back], exchange_in_order(send, ORDERS[1][1]), turned, gate, columns, ow)
    return out


def update(pair_t, pair_mask, u, incoming, peers, rows_of, pw, pb, gw, gb, ow, ob, ns, no):
    channels, positions = pair_t.shape
    width = positions // rows_of
    h = pw.shape[2] // 4
    count = peers[0] * peers[1]
    own = h // count
    normed = layer_norm(pair_t, ns[u, 0][:, None], no[u, 0][:, None]).astype(BF16)
    projected = over_rows(jnp.concatenate([pw[u], gw[u]], 1), normed) + jnp.concatenate([pb[u], gb[u]], 0)[:, None]
    parts = [projected[n * h : (n + 1) * h] for n in range(4)]
    gating = jax.nn.sigmoid(projected[4 * h :])
    mask = pair_mask.astype(F32).reshape(1, positions)
    left = (mask * jax.nn.sigmoid(parts[1]) * parts[0]).astype(BF16)
    right = (mask * jax.nn.sigmoid(parts[3]) * parts[2]).astype(BF16)
    sides = exchange(jnp.stack([v.reshape(count, own, rows_of, width) for v in (left, right)], 1))
    sides = sides.reshape(peers[0], peers[1], 2, own, rows_of, width)
    sides = sides.transpose(2, 3, 0, 4, 1, 5).reshape(2, own, peers[0] * rows_of, peers[1] * width)
    form = "cki,ckj->cij" if incoming else "cik,cjk->cij"
    summed = jnp.einsum(form, sides[0], sides[1], preferred_element_type=F32).astype(BF16)
    summed = summed.reshape(own, peers[0], rows_of, peers[1], width).transpose(1, 3, 0, 2, 4)
    summed = exchange(summed.reshape(count, own, rows_of, width)).reshape(h, positions).astype(F32)
    hidden = layer_norm(summed, ns[u, 1][:, None], no[u, 1][:, None]).astype(BF16)
    change = over_rows(ow[u], hidden) + ob[u][:, None]
    return (pair_t + gating * change).astype(BF16)


def plain_updates(peers, pair_rep, pair_mask, *params):
    rows_of, width, channels = pair_rep.shape
    pair_t = pair_rep.reshape(rows_of * width, channels).T
    for u in range(2):
        pair_t = update(pair_t.astype(F32), pair_mask, u, u == 1, peers, rows_of, *params)
    return pair_t.T.reshape(rows_of, width, channels)


def solution(mesh):
    peers = (mesh.shape["row"], mesh.shape["ka"])
    count = peers[0] * peers[1]

    def on_device(pair_rep, pair_mask, *params):
        rows_of, width, channels = pair_rep.shape
        hidden = params[0].shape[2] // 4
        fits = peers[1] == 1 and rows_of == OWN and hidden == OWN * count and count == 2 * len(ORDERS[0][0])
        if fits and channels == hidden == 128 and width % 128 == 0:
            return packed_updates(count, pair_rep, pair_mask, *params)
        return plain_updates(peers, pair_rep, pair_mask, *params)

    split = P(("grp", "row"), "ka", None)
    in_specs = (split, P(("grp", "row"), "ka")) + (P(),) * 8
    return jax.shard_map(on_device, mesh=mesh, in_specs=in_specs, out_specs=split, check_vma=False)
```

```python
import functools

import jax
import jax.numpy as jnp
from jax import lax
from jax.experimental import pallas as pl
from jax.experimental.pallas import tpu as pltpu
from jax.sharding import PartitionSpec as P

PEERS = ("row", "ka")
OWN = 4
ORDERS = (
    ((0, 1, 2, 3, 4, 5, 6, 7, 8, 9, 10, 11, 12, 13, 14, 15), (0, 15, 11, 14, 13, 10, 9, 7, 12, 5, 8, 6, 4, 3, 2, 1)),
    ((0, 1, 2, 3, 4, 5, 6, 7, 8, 9, 10, 11, 12, 13, 14, 15), (0, 15, 11, 14, 13, 10, 9, 7, 12, 5, 8, 6, 4, 3, 2, 1)),
)
EACH = 16
BF16, F32 = jnp.bfloat16, jnp.float32


def over_rows(a, b):
    return lax.dot_general(a, b, (((0,), (0,)), ((), ())), preferred_element_type=F32)


def over_columns(a, b):
    return lax.dot_general(a, b, (((1,), (1,)), ((), ())), preferred_element_type=F32)


def layer_norm(values, norm_gain, norm_bias):
    average = jnp.mean(values, 0, keepdims=True)
    centred = values - average
    variance = jnp.mean(centred * centred, 0, keepdims=True)
    return centred * lax.rsqrt(variance + 1e-05) * norm_gain + norm_bias


def pack(blocks):
    channels, width = blocks[0].shape
    tiles = [b.reshape(channels // 8, 8, width) for b in blocks]
    turned = [pltpu.roll(b, 4, axis=0).reshape(channels // 8, 8, width) for b in blocks]
    low = lax.broadcasted_iota(jnp.int32, tiles[0].shape, 1) < 4
    back = [pltpu.roll(b, channels - 4, axis=0).reshape(channels // 8, 8, width) for b in blocks]
    even = [jnp.where(low, tiles[n], turned[n + 1]) for n in (0, 2)]
    odd = [jnp.where(low, back[n], tiles[n + 1]) for n in (0, 2)]
    return jnp.stack([jnp.stack(even, 1), jnp.stack(odd, 1)], 1).reshape(channels // 4, 16, width)


def unpack(packed):
    count, _, width = packed.shape
    tiles = packed.reshape(count // 2, 2, 2, 8, width)
    low = lax.broadcasted_iota(jnp.int32, (count // 2, 8, width), 1) < 4
    blocks = []
    for n in range(2):
        even, odd = tiles[:, 0, n], tiles[:, 1, n]
        down = pltpu.roll(odd.reshape(count * 4, width), 4, axis=0).reshape(even.shape)
        up = pltpu.roll(even.reshape(count * 4, width), count * 4 - 4, axis=0).reshape(even.shape)
        blocks.append(jnp.where(low, even, down).reshape(count * 4, width))
        blocks.append(jnp.where(low, up, odd).reshape(count * 4, width))
    return blocks


def sigmoid(x):
    return 0.5 * jnp.tanh(0.5 * x) + 0.5


def broadcast_columns(columns, first, many, width):
    held = columns[...]
    return [jnp.broadcast_to(held[:, n : n + 1], (held.shape[0], width)) for n in range(first, first + many)]


def project(u, z, mask, proj_weight, gate_weight, columns, send, gate, mixed):
    width = z[0].shape[1]
    h = proj_weight.shape[1] // 4
    rows = mixed.shape[1]
    gain, offset, *biases = broadcast_columns(columns, u * EACH, 7, width)
    turned = [proj_weight[:, n * h : (n + 1) * h].T for n in range(4)] + [gate_weight.T]
    for pair in range(0, OWN, 2):
        normed = [layer_norm(z[i], gain, offset).astype(BF16) for i in (pair, pair + 1)]
        normed = jnp.concatenate(normed, 1)
        both = [jnp.dot(w, normed, preferred_element_type=F32) for w in turned]
        for n in range(2):
            i = pair + n
            parts = [v[:, n * width : (n + 1) * width] + b for v, b in zip(both, biases)]
            keep = mask[i : i + 1, :]
            mixed[0, pl.ds(i, h, stride=OWN), :] = keep * sigmoid(parts[1]) * parts[0]
            mixed[1, pl.ds(i, h, stride=OWN), :] = keep * sigmoid(parts[3]) * parts[2]
            gate[:, i * width : (i + 1) * width] = sigmoid(parts[4])
    send[:, 0:16, :] = mixed[0].reshape(rows // 16, 16, width).astype(BF16)
    send[:, 16:32, :] = mixed[1].reshape(rows // 16, 16, width).astype(BF16)


def finish(u, z, summed, gate, out_weight, columns, mixed):
    width = z[0].shape[1]
    gain, offset, bias = broadcast_columns(columns, u * EACH + 7, 3, width)
    turned = out_weight.T
    mixed[...] = summed[...].astype(F32).reshape(mixed.shape)
    results = []
    for pair in range(0, OWN, 2):
        blocks = [mixed[pl.ds(i, mixed.shape[0] // OWN, stride=OWN), :] for i in (pair, pair + 1)]
        blocks = [reorder(v, ORDERS[u][1], ORDERS[u][0]) for v in blocks]
        hidden = jnp.concatenate([layer_norm(v, gain, offset).astype(BF16) for v in blocks], 1)
        both = jnp.dot(turned, hidden, preferred_element_type=F32)
        for n in range(2):
            change = both[:, n * width : (n + 1) * width] + bias
            at = slice((pair + n) * width, (pair + n + 1) * width)
            results.append((z[pair + n].astype(F32) + gate[:, at] * change).astype(BF16))
    return results


def first_kernel(
    pair, mask, pw, gw, pb, gb, ob, ns, no, send, gate, turned, columns, keep, pair_in, mask_in, pw_in, gw_in, pb_in, gb_in, ob_in, ns_in, no_in, rows, arrived, mixed
):
    moves = [(pair, pair_in), (pb, pb_in), (gb, gb_in), (ob, ob_in), (ns, ns_in), (no, no_in)]
    moves += [(pw.at[0], pw_in), (gw.at[0], gw_in), (mask, mask_in)]
    moves = [pltpu.make_async_copy(a, b, arrived.at[n]) for n, (a, b) in enumerate(moves)]
    for move in moves:
        move.start()
    moves[0].wait()
    width = pair.shape[1]
    z = [pair_in[i].T for i in range(OWN)]
    for i in range(OWN):
        turned[:, i * width : (i + 1) * width] = z[i]
    for move in moves[1:6]:
        move.wait()
    h = pw.shape[2] // 4
    for u in range(2):
        found = [ns_in[u, 0:1, :], no_in[u, 0:1, :]] + [pb_in[u : u + 1, n * h : (n + 1) * h] for n in range(4)]
        found += [gb_in[u : u + 1, :], ns_in[u, 1:2, :], no_in[u, 1:2, :], ob_in[u : u + 1, :]]
        for n, row in enumerate(found):
            rows[u * EACH + n : u * EACH + n + 1, :] = row
    columns[...] = rows[...].T
    for move in moves[6:]:
        move.wait()
    keep[0:OWN, :] = mask_in[...].astype(F32)
    project(0, [v.astype(F32) for v in z], keep, pw_in[...], gw_in[...], columns, send, gate, mixed)


def middle_kernel(summed, old, old_gate, columns, keep, pw, gw, ow, send, gate, turned, mixed, mixed_back):
    width = keep.shape[1]
    z = finish(0, [old[:, i * width : (i + 1) * width] for i in range(OWN)], summed, old_gate, ow[0], columns, mixed_back)
    for i in range(OWN):
        turned[:, i * width : (i + 1) * width] = z[i]
    project(1, [v.astype(F32) for v in z], keep, pw[1], gw[1], columns, send, gate, mixed)


def last_kernel(summed, old, old_gate, columns, ow, out, mixed_back):
    width = out.shape[1]
    z = finish(1, [old[:, i * width : (i + 1) * width] for i in range(OWN)], summed, old_gate, ow[1], columns, mixed_back)
    for i in range(OWN):
        out[i] = z[i].T


def reorder(values, have, want):
    tiles = values.reshape(len(have), 2 * OWN, values.shape[1])
    places = [have.index(chip) for chip in want]
    return jnp.concatenate([tiles[n : n + 1] for n in places]).reshape(values.shape)


def triangle_kernel(incoming, sides, out):
    come, go = ORDERS[1 if incoming else 0]
    in_mesh = tuple(range(len(come)))
    left, right = [unpack(sides[:, n : n + 16, :].astype(F32)) for n in (0, 16)]
    if incoming:
        summed = [over_rows(a.astype(BF16), b.astype(BF16)) for a, b in zip(left, right)]
        summed = [reorder(v, in_mesh, go) for v in summed]
    else:
        left = [reorder(v, come, go) for v in left]
        right = [reorder(v, come, in_mesh) for v in right]
        summed = [over_columns(a.astype(BF16), b.astype(BF16)) for a, b in zip(left, right)]
    out[...] = pack(summed).astype(BF16)


def call(kernel, outs, scratch, *args, place=pltpu.VMEM):
    in_vmem = pl.BlockSpec(memory_space=pltpu.VMEM)
    return pl.pallas_call(
        kernel,
        out_shape=[jax.ShapeDtypeStruct(*o) for o in outs],
        in_specs=[pl.BlockSpec(memory_space=place)] * len(args),
        out_specs=[in_vmem] * len(outs),
        scratch_shapes=scratch,
        compiler_params=pltpu.CompilerParams(vmem_limit_bytes=24 * 2**20),
    )(*args)


def exchange(blocks):
    return lax.all_to_all(blocks, PEERS, split_axis=0, concat_axis=0, tiled=True)


def exchange_in_order(blocks, chips):
    listed = [[2 * chip + core for chip in chips for core in range(2)]]
    return lax.all_to_all(blocks, "row", split_axis=0, concat_axis=0, axis_index_groups=listed, tiled=True)


def packed_updates(count, pair_rep, pair_mask, pw, pb, gw, gb, ow, ob, ns, no):
    rows_of, width, channels = pair_rep.shape
    flat = (channels, rows_of * width)
    projected = [((count, 32, width), BF16), (flat, F32), (flat, BF16)]
    summed = [((count, 16, width), BF16)]
    params = [pair_rep, pair_mask, pw, gw, pb, gb, ob, ns, no]
    params = [pltpu.with_memory_space_constraint(v, pltpu.HBM) for v in params]
    held = [pltpu.VMEM(v.shape[1:] if n in (2, 3) else v.shape, v.dtype) for n, v in enumerate(params)]
    held += [pltpu.VMEM((2 * EACH, channels), F32), pltpu.SemaphoreType.DMA((len(params),))]
    back = pltpu.VMEM((OWN * channels, width), F32)
    mixed = pltpu.VMEM((2, OWN * channels, width), F32)
    kept = [((channels, 2 * EACH), F32), ((2 * OWN, width), F32)]
    send, gate, turned, columns, keep = call(first_kernel, projected + kept, held + [mixed], *params, place=pltpu.HBM)
    (send,) = call(functools.partial(triangle_kernel, False), summed, [], exchange_in_order(send, ORDERS[0][0]))
    send, gate, turned = call(middle_kernel, projected, [mixed, back], exchange_in_order(send, ORDERS[0][1]), turned, gate, columns, keep, pw, gw, ow)
    (send,) = call(functools.partial(triangle_kernel, True), summed, [], exchange_in_order(send, ORDERS[1][0]))
    (out,) = call(last_kernel, [(pair_rep.shape, BF16)], [back], exchange_in_order(send, ORDERS[1][1]), turned, gate, columns, ow)
    return out


def update(pair_t, pair_mask, u, incoming, peers, rows_of, pw, pb, gw, gb, ow, ob, ns, no):
    channels, positions = pair_t.shape
    width = positions // rows_of
    h = pw.shape[2] // 4
    count = peers[0] * peers[1]
    own = h // count
    normed = layer_norm(pair_t, ns[u, 0][:, None], no[u, 0][:, None]).astype(BF16)
    projected = over_rows(jnp.concatenate([pw[u], gw[u]], 1), normed) + jnp.concatenate([pb[u], gb[u]], 0)[:, None]
    parts = [projected[n * h : (n + 1) * h] for n in range(4)]
    gating = jax.nn.sigmoid(projected[4 * h :])
    mask = pair_mask.astype(F32).reshape(1, positions)
    left = (mask * jax.nn.sigmoid(parts[1]) * parts[0]).astype(BF16)
    right = (mask * jax.nn.sigmoid(parts[3]) * parts[2]).astype(BF16)
    sides = exchange(jnp.stack([v.reshape(count, own, rows_of, width) for v in (left, right)], 1))
    sides = sides.reshape(peers[0], peers[1], 2, own, rows_of, width)
    sides = sides.transpose(2, 3, 0, 4, 1, 5).reshape(2, own, peers[0] * rows_of, peers[1] * width)
    form = "cki,ckj->cij" if incoming else "cik,cjk->cij"
    summed = jnp.einsum(form, sides[0], sides[1], preferred_element_type=F32).astype(BF16)
    summed = summed.reshape(own, peers[0], rows_of, peers[1], width).transpose(1, 3, 0, 2, 4)
    summed = exchange(summed.reshape(count, own, rows_of, width)).reshape(h, positions).astype(F32)
    hidden = layer_norm(summed, ns[u, 1][:, None], no[u, 1][:, None]).astype(BF16)
    change = over_rows(ow[u], hidden) + ob[u][:, None]
    return (pair_t + gating * change).astype(BF16)


def plain_updates(peers, pair_rep, pair_mask, *params):
    rows_of, width, channels = pair_rep.shape
    pair_t = pair_rep.reshape(rows_of * width, channels).T
    for u in range(2):
        pair_t = update(pair_t.astype(F32), pair_mask, u, u == 1, peers, rows_of, *params)
    return pair_t.T.reshape(rows_of, width, channels)


def solution(mesh):
    peers = (mesh.shape["row"], mesh.shape["ka"])
    count = peers[0] * peers[1]

    def on_device(pair_rep, pair_mask, *params):
        rows_of, width, channels = pair_rep.shape
        hidden = params[0].shape[2] // 4
        fits = peers[1] == 1 and rows_of == OWN and hidden == OWN * count and count == 2 * len(ORDERS[0][0])
        if fits and channels == hidden == 128 and width % 128 == 0:
            return packed_updates(count, pair_rep, pair_mask, *params)
        return plain_updates(peers, pair_rep, pair_mask, *params)

    split = P(("grp", "row"), "ka", None)
    in_specs = (split, P(("grp", "row"), "ka")) + (P(),) * 8
    return jax.shard_map(on_device, mesh=mesh, in_specs=in_specs, out_specs=split, check_vma=False)
```

```python
import functools

import jax
import jax.numpy as jnp
from jax import lax
from jax.experimental import pallas as pl
from jax.experimental.pallas import tpu as pltpu
from jax.sharding import PartitionSpec as P

PEERS = ("row", "ka")
OWN = 4
CHIPS = (0, 15, 11, 14, 13, 10, 9, 7, 12, 5, 8, 6, 4, 3, 2, 1)
EACH = 16
BF16, F32 = jnp.bfloat16, jnp.float32


def over_rows(a, b):
    return lax.dot_general(a, b, (((0,), (0,)), ((), ())), preferred_element_type=F32)


def over_columns(a, b):
    return lax.dot_general(a, b, (((1,), (1,)), ((), ())), preferred_element_type=F32)


def standardised(values):
    average = jnp.mean(values, 0, keepdims=True)
    centred = values - average
    variance = jnp.mean(centred * centred, 0, keepdims=True)
    return centred * lax.rsqrt(variance + 1e-05)


def layer_norm(values, norm_gain, norm_bias):
    return standardised(values) * norm_gain + norm_bias


def pack(blocks):
    channels, width = blocks[0].shape
    tiles = [b.reshape(channels // 8, 8, width) for b in blocks]
    turned = [pltpu.roll(b, 4, axis=0).reshape(channels // 8, 8, width) for b in blocks]
    low = lax.broadcasted_iota(jnp.int32, tiles[0].shape, 1) < 4
    back = [pltpu.roll(b, channels - 4, axis=0).reshape(channels // 8, 8, width) for b in blocks]
    even = [jnp.where(low, tiles[n], turned[n + 1]) for n in (0, 2)]
    odd = [jnp.where(low, back[n], tiles[n + 1]) for n in (0, 2)]
    return jnp.stack([jnp.stack(even, 1), jnp.stack(odd, 1)], 1).reshape(channels // 4, 16, width)


def unpack(packed):
    count, _, width = packed.shape
    tiles = packed.reshape(count // 2, 2, 2, 8, width)
    low = lax.broadcasted_iota(jnp.int32, (count // 2, 8, width), 1) < 4
    blocks = []
    for n in range(2):
        even, odd = tiles[:, 0, n], tiles[:, 1, n]
        down = pltpu.roll(odd.reshape(count * 4, width), 4, axis=0).reshape(even.shape)
        up = pltpu.roll(even.reshape(count * 4, width), count * 4 - 4, axis=0).reshape(even.shape)
        blocks.append(jnp.where(low, even, down).reshape(count * 4, width))
        blocks.append(jnp.where(low, up, odd).reshape(count * 4, width))
    return blocks


def sigmoid(x):
    return 0.5 * jnp.tanh(0.5 * x) + 0.5


def broadcast_columns(columns, first, many, width):
    held = columns[...]
    return [jnp.broadcast_to(held[:, n : n + 1], (held.shape[0], width)) for n in range(first, first + many)]


def project(u, norm, mask, proj_weight, columns, send, mixed):
    width = norm.shape[1] // OWN
    h = proj_weight.shape[1] // 4
    rows = mixed.shape[1]
    biases = broadcast_columns(columns, u * EACH + 2, 4, width)
    turned = [proj_weight[:, n * h : (n + 1) * h].T for n in range(4)]
    halves = [mask[i : i + 1, :] * 0.5 for i in range(OWN)]
    joined = [norm[:, pair * width : (pair + 2) * width] for pair in range(0, OWN, 2)]
    for side in range(2):
        for pair in range(0, OWN, 2):
            value, gating = [jnp.dot(turned[2 * side + n], joined[pair // 2], preferred_element_type=F32) for n in (0, 1)]
            for n in range(2):
                i, at = pair + n, slice(n * width, (n + 1) * width)
                weight = halves[i] + halves[i] * jnp.tanh(0.5 * (gating[:, at] + biases[2 * side + 1]))
                mixed[side, pl.ds(i, h, stride=OWN), :] = weight * (value[:, at] + biases[2 * side])
        send[:, side * 16 : (side + 1) * 16, :] = mixed[side].reshape(rows // 16, 16, width).astype(BF16)


def finish(u, z, summed, gate, turned, columns, mixed):
    width = z[0].shape[1]
    gain, offset, bias = broadcast_columns(columns, u * EACH + 7, 3, width)
    mixed[...] = summed[...].astype(F32).reshape(mixed.shape)
    results = []
    for pair in range(0, OWN, 2):
        blocks = [mixed[pl.ds(i, mixed.shape[0] // OWN, stride=OWN), :] for i in (pair, pair + 1)]
        hidden = jnp.concatenate([layer_norm(v, gain, offset).astype(BF16) for v in blocks], 1)
        both = jnp.dot(turned, hidden, preferred_element_type=F32)
        for n in range(2):
            change = both[:, n * width : (n + 1) * width] + bias
            at = slice((pair + n) * width, (pair + n + 1) * width)
            results.append((z[pair + n].astype(F32) + gate[:, at] * change).astype(BF16))
    return results


def first_kernel(
    pair, mask, pw, gw, pb, gb, ob, ns, no, send, norm, turned, columns, keep, gw_in, pair_in, mask_in, pw_in, pb_in, gb_in, ob_in, ns_in, no_in, rows, arrived, mixed
):
    moves = [(pair, pair_in), (pw.at[0], pw_in), (ns, ns_in), (no, no_in), (pb, pb_in), (gb, gb_in), (ob, ob_in)]
    moves += [(mask, mask_in), (gw.at[0], gw_in)]
    moves = [pltpu.make_async_copy(a, b, arrived.at[n]) for n, (a, b) in enumerate(moves)]
    for move in moves:
        move.start()
    for move in moves:
        move.wait()
    width = pair.shape[1]
    z = [pair_in[i].T for i in range(OWN)]
    h = pw.shape[2] // 4
    for u in range(2):
        found = [ns_in[u, 0:1, :], no_in[u, 0:1, :]] + [pb_in[u : u + 1, n * h : (n + 1) * h] for n in range(4)]
        found += [gb_in[u : u + 1, :], ns_in[u, 1:2, :], no_in[u, 1:2, :], ob_in[u : u + 1, :]]
        for n, row in enumerate(found):
            rows[u * EACH + n : u * EACH + n + 1, :] = row
    columns[...] = rows[...].T
    keep[0:OWN, :] = mask_in[...].astype(F32)
    normalise(0, z, columns, norm, turned, width)
    project(0, norm, keep, pw_in[...], columns, send, mixed)


def normalise(u, z, columns, norm, turned, width):
    gain, offset = broadcast_columns(columns, u * EACH, 2, width)
    for i in range(OWN):
        at = slice(i * width, (i + 1) * width)
        turned[:, at] = z[i]
        norm[:, at] = layer_norm(z[i].astype(F32), gain, offset).astype(BF16)


def middle_kernel(summed, old, old_gate, columns, keep, pw, ow, send, norm, turned, mixed, mixed_back):
    width = keep.shape[1]
    z = [old[:, i * width : (i + 1) * width] for i in range(OWN)]
    z = finish(0, z, summed, old_gate, ow[0].T, columns, mixed_back)
    normalise(1, z, columns, norm, turned, width)
    project(1, norm, keep, pw[1], columns, send, mixed)


def last_kernel(summed, old, old_gate, columns, ow, out, mixed_back):
    width = out.shape[1]
    z = [old[:, i * width : (i + 1) * width] for i in range(OWN)]
    z = finish(1, z, summed, old_gate, ow[1].T, columns, mixed_back)
    for i in range(OWN):
        out[i] = z[i].T


def reorder(values, have, want):
    tiles = values.reshape(len(have), 2 * OWN, values.shape[1])
    places = [have.index(chip) for chip in want]
    return jnp.concatenate([tiles[n : n + 1] for n in places]).reshape(values.shape)


def triangle(incoming, sides, out):
    in_mesh = tuple(range(len(CHIPS)))
    left, right = [unpack(sides[:, n : n + 16, :].astype(F32)) for n in (0, 16)]
    if incoming:
        summed = [over_rows(a.astype(BF16), b.astype(BF16)) for a, b in zip(left, right)]
        summed = [reorder(v, in_mesh, CHIPS) for v in summed]
    else:
        right = [reorder(v, CHIPS, in_mesh) for v in right]
        summed = [over_columns(a.astype(BF16), b.astype(BF16)) for a, b in zip(left, right)]
    out[...] = pack(summed).astype(BF16)


def output_gate(u, normed, gate_weight, columns, gate):
    gating = jnp.dot(gate_weight.T, normed[...], preferred_element_type=F32)
    gate[...] = sigmoid(gating + columns[:, u * EACH + 6 : u * EACH + 7])


def outgoing_kernel(sides, normed, gw, columns, out, gate):
    triangle(False, sides, out)
    output_gate(0, normed, gw[...], columns, gate)


def incoming_kernel(sides, normed, gw, columns, out, gate):
    triangle(True, sides, out)
    output_gate(1, normed, gw[1], columns, gate)


def call(kernel, outs, scratch, *args, place=pltpu.VMEM):
    in_vmem = pl.BlockSpec(memory_space=pltpu.VMEM)
    return pl.pallas_call(
        kernel,
        out_shape=[jax.ShapeDtypeStruct(*o) for o in outs],
        in_specs=[pl.BlockSpec(memory_space=place)] * len(args),
        out_specs=[in_vmem] * len(outs),
        scratch_shapes=scratch,
        compiler_params=pltpu.CompilerParams(vmem_limit_bytes=24 * 2**20),
    )(*args)


def exchange(blocks):
    return lax.all_to_all(blocks, PEERS, split_axis=0, concat_axis=0, tiled=True)


def exchange_in_order(blocks):
    listed = [[2 * chip + core for chip in CHIPS for core in range(2)]]
    return lax.all_to_all(blocks, "row", split_axis=0, concat_axis=0, axis_index_groups=listed, tiled=True)


def packed_updates(count, pair_rep, pair_mask, pw, pb, gw, gb, ow, ob, ns, no):
    rows_of, width, channels = pair_rep.shape
    flat = (channels, rows_of * width)
    square = ((channels, channels), BF16)
    projected = [((count, 32, width), BF16), (flat, BF16), (flat, BF16)]
    summed = [((count, 16, width), BF16), (flat, F32)]
    params = [pair_rep, pair_mask, pw, gw, pb, gb, ob, ns, no]
    params = [pltpu.with_memory_space_constraint(v, pltpu.HBM) for v in params]
    held = [pltpu.VMEM(v.shape[1:] if n == 2 else v.shape, v.dtype) for n, v in enumerate(params) if n != 3]
    held += [pltpu.VMEM((2 * EACH, channels), F32), pltpu.SemaphoreType.DMA((len(params),))]
    back = pltpu.VMEM((OWN * channels, width), F32)
    mixed = pltpu.VMEM((2, OWN * channels, width), F32)
    kept = [((channels, 2 * EACH), F32), ((2 * OWN, width), F32), square]
    send, norm, turned, columns, keep, gw0 = call(
        first_kernel, projected + kept, held + [mixed], *params, place=pltpu.HBM
    )
    send, gate = call(outgoing_kernel, summed, [], exchange_in_order(send), norm, gw0, columns)
    send, norm, turned = call(
        middle_kernel, projected, [mixed, back], exchange_in_order(send), turned, gate, columns, keep, pw, ow
    )
    send, gate = call(incoming_kernel, summed, [], exchange_in_order(send), norm, gw, columns)
    (out,) = call(last_kernel, [(pair_rep.shape, BF16)], [back], exchange_in_order(send), turned, gate, columns, ow)
    return out


def update(pair_t, pair_mask, u, incoming, peers, rows_of, pw, pb, gw, gb, ow, ob, ns, no):
    channels, positions = pair_t.shape
    width = positions // rows_of
    h = pw.shape[2] // 4
    count = peers[0] * peers[1]
    own = h // count
    normed = layer_norm(pair_t, ns[u, 0][:, None], no[u, 0][:, None]).astype(BF16)
    projected = over_rows(jnp.concatenate([pw[u], gw[u]], 1), normed) + jnp.concatenate([pb[u], gb[u]], 0)[:, None]
    parts = [projected[n * h : (n + 1) * h] for n in range(4)]
    gating = jax.nn.sigmoid(projected[4 * h :])
    mask = pair_mask.astype(F32).reshape(1, positions)
    left = (mask * jax.nn.sigmoid(parts[1]) * parts[0]).astype(BF16)
    right = (mask * jax.nn.sigmoid(parts[3]) * parts[2]).astype(BF16)
    sides = exchange(jnp.stack([v.reshape(count, own, rows_of, width) for v in (left, right)], 1))
    sides = sides.reshape(peers[0], peers[1], 2, own, rows_of, width)
    sides = sides.transpose(2, 3, 0, 4, 1, 5).reshape(2, own, peers[0] * rows_of, peers[1] * width)
    form = "cki,ckj->cij" if incoming else "cik,cjk->cij"
    summed = jnp.einsum(form, sides[0], sides[1], preferred_element_type=F32).astype(BF16)
    summed = summed.reshape(own, peers[0], rows_of, peers[1], width).transpose(1, 3, 0, 2, 4)
    summed = exchange(summed.reshape(count, own, rows_of, width)).reshape(h, positions).astype(F32)
    hidden = layer_norm(summed, ns[u, 1][:, None], no[u, 1][:, None]).astype(BF16)
    change = over_rows(ow[u], hidden) + ob[u][:, None]
    return (pair_t + gating * change).astype(BF16)


def plain_updates(peers, pair_rep, pair_mask, *params):
    rows_of, width, channels = pair_rep.shape
    pair_t = pair_rep.reshape(rows_of * width, channels).T
    for u in range(2):
        pair_t = update(pair_t.astype(F32), pair_mask, u, u == 1, peers, rows_of, *params)
    return pair_t.T.reshape(rows_of, width, channels)


def solution(mesh):
    peers = (mesh.shape["row"], mesh.shape["ka"])
    count = peers[0] * peers[1]

    def on_device(pair_rep, pair_mask, *params):
        rows_of, width, channels = pair_rep.shape
        hidden = params[0].shape[2] // 4
        fits = peers[1] == 1 and rows_of == OWN and hidden == OWN * count and count == 2 * len(CHIPS)
        if fits and channels == hidden == 128 and width % 128 == 0:
            return packed_updates(count, pair_rep, pair_mask, *params)
        return plain_updates(peers, pair_rep, pair_mask, *params)

    split = P(("grp", "row"), "ka", None)
    in_specs = (split, P(("grp", "row"), "ka")) + (P(),) * 8
    return jax.shard_map(on_device, mesh=mesh, in_specs=in_specs, out_specs=split, check_vma=False)
```

```python
import functools

import jax
import jax.numpy as jnp
from jax import lax
from jax.experimental import pallas as pl
from jax.experimental.pallas import tpu as pltpu
from jax.sharding import PartitionSpec as P

PEERS = ("row", "ka")
OWN = 4
ORDERS = (
    ((0, 15, 11, 14, 13, 10, 9, 7, 12, 5, 8, 6, 4, 3, 2, 1), (0, 15, 11, 14, 13, 10, 9, 7, 12, 5, 8, 6, 4, 3, 2, 1)),
    ((0, 15, 11, 14, 13, 10, 9, 7, 12, 5, 8, 6, 4, 3, 2, 1), (0, 15, 11, 14, 13, 10, 9, 7, 12, 5, 8, 6, 4, 3, 2, 1)),
)
EACH = 16
BF16, F32 = jnp.bfloat16, jnp.float32


def over_rows(a, b):
    return lax.dot_general(a, b, (((0,), (0,)), ((), ())), preferred_element_type=F32)


def over_columns(a, b):
    return lax.dot_general(a, b, (((1,), (1,)), ((), ())), preferred_element_type=F32)


def layer_norm(values, norm_gain, norm_bias):
    average = jnp.mean(values, 0, keepdims=True)
    centred = values - average
    variance = jnp.mean(centred * centred, 0, keepdims=True)
    return centred * lax.rsqrt(variance + 1e-05) * norm_gain + norm_bias


def pack(blocks):
    channels, width = blocks[0].shape
    tiles = [b.reshape(channels // 8, 8, width) for b in blocks]
    turned = [pltpu.roll(b, 4, axis=0).reshape(channels // 8, 8, width) for b in blocks]
    low = lax.broadcasted_iota(jnp.int32, tiles[0].shape, 1) < 4
    back = [pltpu.roll(b, channels - 4, axis=0).reshape(channels // 8, 8, width) for b in blocks]
    even = [jnp.where(low, tiles[n], turned[n + 1]) for n in (0, 2)]
    odd = [jnp.where(low, back[n], tiles[n + 1]) for n in (0, 2)]
    return jnp.stack([jnp.stack(even, 1), jnp.stack(odd, 1)], 1).reshape(channels // 4, 16, width)


def unpack(packed):
    count, _, width = packed.shape
    tiles = packed.reshape(count // 2, 2, 2, 8, width)
    low = lax.broadcasted_iota(jnp.int32, (count // 2, 8, width), 1) < 4
    blocks = []
    for n in range(2):
        even, odd = tiles[:, 0, n], tiles[:, 1, n]
        down = pltpu.roll(odd.reshape(count * 4, width), 4, axis=0).reshape(even.shape)
        up = pltpu.roll(even.reshape(count * 4, width), count * 4 - 4, axis=0).reshape(even.shape)
        blocks.append(jnp.where(low, even, down).reshape(count * 4, width))
        blocks.append(jnp.where(low, up, odd).reshape(count * 4, width))
    return blocks


def sigmoid(x):
    return 0.5 * jnp.tanh(0.5 * x) + 0.5


def broadcast_columns(columns, first, many, width):
    held = columns[...]
    return [jnp.broadcast_to(held[:, n : n + 1], (held.shape[0], width)) for n in range(first, first + many)]


def project(u, z, mask, proj_weight, gate_weight, columns, send, gate, mixed):
    width = z[0].shape[1]
    h = proj_weight.shape[1] // 4
    rows = mixed.shape[1]
    gain, offset, *biases = broadcast_columns(columns, u * EACH, 7, width)
    turned = [proj_weight[:, n * h : (n + 1) * h].T for n in range(4)] + [gate_weight.T]
    for pair in range(0, OWN, 2):
        normed = [layer_norm(z[i], gain, offset).astype(BF16) for i in (pair, pair + 1)]
        normed = jnp.concatenate(normed, 1)
        both = [jnp.dot(w, normed, preferred_element_type=F32) for w in turned]
        for n in range(2):
            i = pair + n
            parts = [v[:, n * width : (n + 1) * width] + b for v, b in zip(both, biases)]
            keep = mask[i : i + 1, :]
            mixed[0, pl.ds(i, h, stride=OWN), :] = keep * sigmoid(parts[1]) * parts[0]
            mixed[1, pl.ds(i, h, stride=OWN), :] = keep * sigmoid(parts[3]) * parts[2]
            gate[:, i * width : (i + 1) * width] = sigmoid(parts[4])
    send[:, 0:16, :] = mixed[0].reshape(rows // 16, 16, width).astype(BF16)
    send[:, 16:32, :] = mixed[1].reshape(rows // 16, 16, width).astype(BF16)


def finish(u, z, summed, gate, out_weight, columns, mixed):
    width = z[0].shape[1]
    gain, offset, bias = broadcast_columns(columns, u * EACH + 7, 3, width)
    turned = out_weight.T
    mixed[...] = summed[...].astype(F32).reshape(mixed.shape)
    results = []
    for pair in range(0, OWN, 2):
        blocks = [mixed[pl.ds(i, mixed.shape[0] // OWN, stride=OWN), :] for i in (pair, pair + 1)]
        blocks = [reorder(v, ORDERS[u][1], ORDERS[u][0]) for v in blocks]
        hidden = jnp.concatenate([layer_norm(v, gain, offset).astype(BF16) for v in blocks], 1)
        both = jnp.dot(turned, hidden, preferred_element_type=F32)
        for n in range(2):
            change = both[:, n * width : (n + 1) * width] + bias
            at = slice((pair + n) * width, (pair + n + 1) * width)
            results.append((z[pair + n].astype(F32) + gate[:, at] * change).astype(BF16))
    return results


def first_kernel(
    pair, mask, pw, gw, pb, gb, ob, ns, no, send, gate, turned, columns, keep, pair_in, mask_in, pw_in, gw_in, pb_in, gb_in, ob_in, ns_in, no_in, rows, arrived, mixed
):
    halves = [pl.ds(0, OWN // 2), pl.ds(OWN // 2, OWN // 2)]
    depth = pw.shape[1] // 2
    moves = [(pair.at[n], pair_in.at[n]) for n in halves]
    moves += [(pw.at[0, pl.ds(n * depth, depth)], pw_in.at[pl.ds(n * depth, depth)]) for n in range(2)]
    moves += [(pb, pb_in), (gb, gb_in), (ob, ob_in), (ns, ns_in), (no, no_in), (mask, mask_in), (gw.at[0], gw_in)]
    moves = [pltpu.make_async_copy(a, b, arrived.at[n]) for n, (a, b) in enumerate(moves)]
    for move in moves:
        move.start()
    for move in moves:
        move.wait()
    width = pair.shape[1]
    z = [pair_in[i].T for i in range(OWN)]
    for i in range(OWN):
        turned[:, i * width : (i + 1) * width] = z[i]
    h = pw.shape[2] // 4
    for u in range(2):
        found = [ns_in[u, 0:1, :], no_in[u, 0:1, :]] + [pb_in[u : u + 1, n * h : (n + 1) * h] for n in range(4)]
        found += [gb_in[u : u + 1, :], ns_in[u, 1:2, :], no_in[u, 1:2, :], ob_in[u : u + 1, :]]
        for n, row in enumerate(found):
            rows[u * EACH + n : u * EACH + n + 1, :] = row
    columns[...] = rows[...].T
    keep[0:OWN, :] = mask_in[...].astype(F32)
    project(0, [v.astype(F32) for v in z], keep, pw_in[...], gw_in[...], columns, send, gate, mixed)


def middle_kernel(summed, old, old_gate, columns, keep, pw, gw, ow, send, gate, turned, mixed, mixed_back):
    width = keep.shape[1]
    z = finish(0, [old[:, i * width : (i + 1) * width] for i in range(OWN)], summed, old_gate, ow[0], columns, mixed_back)
    for i in range(OWN):
        turned[:, i * width : (i + 1) * width] = z[i]
    project(1, [v.astype(F32) for v in z], keep, pw[1], gw[1], columns, send, gate, mixed)


def last_kernel(summed, old, old_gate, columns, ow, out, ready, left, mixed_back):
    width = out.shape[1]
    z = [old[:, i * width : (i + 1) * width] for i in range(OWN)]
    z = finish(1, z, summed, old_gate, ow[1], columns, mixed_back)
    moves = [pltpu.make_async_copy(ready.at[i], out.at[i], left.at[i]) for i in range(OWN)]
    for i in range(OWN):
        ready[i] = z[i].T
        moves[i].start()
    for move in moves:
        move.wait()


def reorder(values, have, want):
    tiles = values.reshape(len(have), 2 * OWN, values.shape[1])
    places = [have.index(chip) for chip in want]
    return jnp.concatenate([tiles[n : n + 1] for n in places]).reshape(values.shape)


def triangle_kernel(incoming, sides, out):
    come, go = ORDERS[1 if incoming else 0]
    in_mesh = tuple(range(len(come)))
    left, right = [unpack(sides[:, n : n + 16, :].astype(F32)) for n in (0, 16)]
    if incoming:
        summed = [over_rows(a.astype(BF16), b.astype(BF16)) for a, b in zip(left, right)]
        summed = [reorder(v, in_mesh, go) for v in summed]
    else:
        left = [reorder(v, come, go) for v in left]
        right = [reorder(v, come, in_mesh) for v in right]
        summed = [over_columns(a.astype(BF16), b.astype(BF16)) for a, b in zip(left, right)]
    out[...] = pack(summed).astype(BF16)


def call(kernel, outs, scratch, *args, place=pltpu.VMEM, result=pltpu.VMEM):
    return pl.pallas_call(
        kernel,
        out_shape=[jax.ShapeDtypeStruct(*o) for o in outs],
        in_specs=[pl.BlockSpec(memory_space=place)] * len(args),
        out_specs=[pl.BlockSpec(memory_space=result)] * len(outs),
        scratch_shapes=scratch,
        compiler_params=pltpu.CompilerParams(vmem_limit_bytes=24 * 2**20),
    )(*args)


def exchange(blocks):
    return lax.all_to_all(blocks, PEERS, split_axis=0, concat_axis=0, tiled=True)


def exchange_in_order(blocks, chips):
    listed = [[2 * chip + core for chip in chips for core in range(2)]]
    return lax.all_to_all(blocks, "row", split_axis=0, concat_axis=0, axis_index_groups=listed, tiled=True)


def packed_updates(count, pair_rep, pair_mask, pw, pb, gw, gb, ow, ob, ns, no):
    rows_of, width, channels = pair_rep.shape
    flat = (channels, rows_of * width)
    projected = [((count, 32, width), BF16), (flat, F32), (flat, BF16)]
    summed = [((count, 16, width), BF16)]
    params = [pair_rep, pair_mask, pw, gw, pb, gb, ob, ns, no]
    params = [pltpu.with_memory_space_constraint(v, pltpu.HBM) for v in params]
    held = [pltpu.VMEM(v.shape[1:] if n in (2, 3) else v.shape, v.dtype) for n, v in enumerate(params)]
    held += [pltpu.VMEM((2 * EACH, channels), F32), pltpu.SemaphoreType.DMA((len(params) + 2,))]
    back = pltpu.VMEM((OWN * channels, width), F32)
    mixed = pltpu.VMEM((2, OWN * channels, width), F32)
    kept = [((channels, 2 * EACH), F32), ((2 * OWN, width), F32)]
    send, gate, turned, columns, keep = call(first_kernel, projected + kept, held + [mixed], *params, place=pltpu.HBM)
    (send,) = call(functools.partial(triangle_kernel, False), summed, [], exchange_in_order(send, ORDERS[0][0]))
    send, gate, turned = call(middle_kernel, projected, [mixed, back], exchange_in_order(send, ORDERS[0][1]), turned, gate, columns, keep, pw, gw, ow)
    (send,) = call(functools.partial(triangle_kernel, True), summed, [], exchange_in_order(send, ORDERS[1][0]))
    held = [pltpu.VMEM(pair_rep.shape, BF16), pltpu.SemaphoreType.DMA((rows_of,)), back]
    send = exchange_in_order(send, ORDERS[1][1])
    (out,) = call(last_kernel, [(pair_rep.shape, BF16)], held, send, turned, gate, columns, ow, result=pltpu.HBM)
    return out


def update(pair_t, pair_mask, u, incoming, peers, rows_of, pw, pb, gw, gb, ow, ob, ns, no):
    channels, positions = pair_t.shape
    width = positions // rows_of
    h = pw.shape[2] // 4
    count = peers[0] * peers[1]
    own = h // count
    normed = layer_norm(pair_t, ns[u, 0][:, None], no[u, 0][:, None]).astype(BF16)
    projected = over_rows(jnp.concatenate([pw[u], gw[u]], 1), normed) + jnp.concatenate([pb[u], gb[u]], 0)[:, None]
    parts = [projected[n * h : (n + 1) * h] for n in range(4)]
    gating = jax.nn.sigmoid(projected[4 * h :])
    mask = pair_mask.astype(F32).reshape(1, positions)
    left = (mask * jax.nn.sigmoid(parts[1]) * parts[0]).astype(BF16)
    right = (mask * jax.nn.sigmoid(parts[3]) * parts[2]).astype(BF16)
    sides = exchange(jnp.stack([v.reshape(count, own, rows_of, width) for v in (left, right)], 1))
    sides = sides.reshape(peers[0], peers[1], 2, own, rows_of, width)
    sides = sides.transpose(2, 3, 0, 4, 1, 5).reshape(2, own, peers[0] * rows_of, peers[1] * width)
    form = "cki,ckj->cij" if incoming else "cik,cjk->cij"
    summed = jnp.einsum(form, sides[0], sides[1], preferred_element_type=F32).astype(BF16)
    summed = summed.reshape(own, peers[0], rows_of, peers[1], width).transpose(1, 3, 0, 2, 4)
    summed = exchange(summed.reshape(count, own, rows_of, width)).reshape(h, positions).astype(F32)
    hidden = layer_norm(summed, ns[u, 1][:, None], no[u, 1][:, None]).astype(BF16)
    change = over_rows(ow[u], hidden) + ob[u][:, None]
    return (pair_t + gating * change).astype(BF16)


def plain_updates(peers, pair_rep, pair_mask, *params):
    rows_of, width, channels = pair_rep.shape
    pair_t = pair_rep.reshape(rows_of * width, channels).T
    for u in range(2):
        pair_t = update(pair_t.astype(F32), pair_mask, u, u == 1, peers, rows_of, *params)
    return pair_t.T.reshape(rows_of, width, channels)


def solution(mesh):
    peers = (mesh.shape["row"], mesh.shape["ka"])
    count = peers[0] * peers[1]

    def on_device(pair_rep, pair_mask, *params):
        rows_of, width, channels = pair_rep.shape
        hidden = params[0].shape[2] // 4
        fits = peers[1] == 1 and rows_of == OWN and hidden == OWN * count and count == 2 * len(ORDERS[0][0])
        if fits and channels == hidden == 128 and width % 128 == 0:
            return packed_updates(count, pair_rep, pair_mask, *params)
        return plain_updates(peers, pair_rep, pair_mask, *params)

    split = P(("grp", "row"), "ka", None)
    in_specs = (split, P(("grp", "row"), "ka")) + (P(),) * 8
    return jax.shard_map(on_device, mesh=mesh, in_specs=in_specs, out_specs=split, check_vma=False)
```

```python
import functools

import jax
import jax.numpy as jnp
from jax import lax
from jax.experimental import pallas as pl
from jax.experimental.pallas import tpu as pltpu
from jax.sharding import PartitionSpec as P

PEERS = ("row", "ka")
OWN = 4
CHIPS = (0, 15, 11, 14, 13, 10, 9, 7, 12, 5, 8, 6, 4, 3, 2, 1)
EACH = 16
BF16, F32 = jnp.bfloat16, jnp.float32


def over_rows(a, b):
    return lax.dot_general(a, b, (((0,), (0,)), ((), ())), preferred_element_type=F32)


def over_columns(a, b):
    return lax.dot_general(a, b, (((1,), (1,)), ((), ())), preferred_element_type=F32)


def standardised(values):
    average = jnp.mean(values, 0, keepdims=True)
    centred = values - average
    variance = jnp.mean(centred * centred, 0, keepdims=True)
    return centred * lax.rsqrt(variance + 1e-05)


def layer_norm(values, norm_gain, norm_bias):
    return standardised(values) * norm_gain + norm_bias


def pack(blocks):
    channels, width = blocks[0].shape
    tiles = [b.reshape(channels // 8, 8, width) for b in blocks]
    turned = [pltpu.roll(b, 4, axis=0).reshape(channels // 8, 8, width) for b in blocks]
    low = lax.broadcasted_iota(jnp.int32, tiles[0].shape, 1) < 4
    back = [pltpu.roll(b, channels - 4, axis=0).reshape(channels // 8, 8, width) for b in blocks]
    even = [jnp.where(low, tiles[n], turned[n + 1]) for n in (0, 2)]
    odd = [jnp.where(low, back[n], tiles[n + 1]) for n in (0, 2)]
    return jnp.stack([jnp.stack(even, 1), jnp.stack(odd, 1)], 1).reshape(channels // 4, 16, width)


def unpack(packed):
    count, _, width = packed.shape
    tiles = packed.reshape(count // 2, 2, 2, 8, width)
    low = lax.broadcasted_iota(jnp.int32, (count // 2, 8, width), 1) < 4
    blocks = []
    for n in range(2):
        even, odd = tiles[:, 0, n], tiles[:, 1, n]
        down = pltpu.roll(odd.reshape(count * 4, width), 4, axis=0).reshape(even.shape)
        up = pltpu.roll(even.reshape(count * 4, width), count * 4 - 4, axis=0).reshape(even.shape)
        blocks.append(jnp.where(low, even, down).reshape(count * 4, width))
        blocks.append(jnp.where(low, up, odd).reshape(count * 4, width))
    return blocks


def sigmoid(x):
    return 0.5 * jnp.tanh(0.5 * x) + 0.5


def broadcast_columns(columns, first, many, width):
    held = columns[...]
    return [jnp.broadcast_to(held[:, n : n + 1], (held.shape[0], width)) for n in range(first, first + many)]


def project(u, norm, mask, proj_weight, columns, send, mixed):
    width = norm.shape[1] // OWN
    h = proj_weight.shape[1] // 4
    rows = mixed.shape[1]
    biases = broadcast_columns(columns, u * EACH + 2, 4, width)
    turned = [proj_weight[:, n * h : (n + 1) * h].T for n in range(4)]
    halves = [mask[i : i + 1, :] * 0.5 for i in range(OWN)]
    joined = [norm[:, pair * width : (pair + 2) * width] for pair in range(0, OWN, 2)]
    for side in range(2):
        for pair in range(0, OWN, 2):
            value, gating = [jnp.dot(turned[2 * side + n], joined[pair // 2], preferred_element_type=F32) for n in (0, 1)]
            for n in range(2):
                i, at = pair + n, slice(n * width, (n + 1) * width)
                weight = halves[i] + halves[i] * jnp.tanh(0.5 * (gating[:, at] + biases[2 * side + 1]))
                mixed[side, pl.ds(i, h, stride=OWN), :] = weight * (value[:, at] + biases[2 * side])
        send[:, side * 16 : (side + 1) * 16, :] = mixed[side].reshape(rows // 16, 16, width).astype(BF16)


def finish(u, z, summed, gate, turned, columns, mixed):
    width = z[0].shape[1]
    gain, offset, bias = broadcast_columns(columns, u * EACH + 7, 3, width)
    mixed[...] = summed[...].astype(F32).reshape(mixed.shape)
    results = []
    for pair in range(0, OWN, 2):
        blocks = [mixed[pl.ds(i, mixed.shape[0] // OWN, stride=OWN), :] for i in (pair, pair + 1)]
        hidden = jnp.concatenate([layer_norm(v, gain, offset).astype(BF16) for v in blocks], 1)
        both = jnp.dot(turned, hidden, preferred_element_type=F32)
        for n in range(2):
            change = both[:, n * width : (n + 1) * width] + bias
            at = slice((pair + n) * width, (pair + n + 1) * width)
            results.append((z[pair + n].astype(F32) + gate[:, at] * change).astype(BF16))
    return results


def first_kernel(
    pair, mask, pw, pb, gb, ob, ns, no, send, norm, turned, columns, keep, pair_in, mask_in, pw_in, pb_in, gb_in, ob_in, ns_in, no_in, rows, arrived, mixed
):
    moves = [(pair, pair_in), (pw.at[0], pw_in), (ns, ns_in), (no, no_in), (pb, pb_in), (gb, gb_in), (ob, ob_in)]
    moves += [(mask, mask_in)]
    moves = [pltpu.make_async_copy(a, b, arrived.at[n]) for n, (a, b) in enumerate(moves)]
    for move in moves:
        move.start()
    for move in moves:
        move.wait()
    width = pair.shape[1]
    z = [pair_in[i].T for i in range(OWN)]
    h = pw.shape[2] // 4
    for u in range(2):
        found = [ns_in[u, 0:1, :], no_in[u, 0:1, :]] + [pb_in[u : u + 1, n * h : (n + 1) * h] for n in range(4)]
        found += [gb_in[u : u + 1, :], ns_in[u, 1:2, :], no_in[u, 1:2, :], ob_in[u : u + 1, :]]
        for n, row in enumerate(found):
            rows[u * EACH + n : u * EACH + n + 1, :] = row
    columns[...] = rows[...].T
    keep[0:OWN, :] = mask_in[...].astype(F32)
    normalise(0, z, columns, norm, turned, width)
    project(0, norm, keep, pw_in[...], columns, send, mixed)


def normalise(u, z, columns, norm, turned, width):
    gain, offset = broadcast_columns(columns, u * EACH, 2, width)
    for i in range(OWN):
        at = slice(i * width, (i + 1) * width)
        turned[:, at] = z[i]
        norm[:, at] = layer_norm(z[i].astype(F32), gain, offset).astype(BF16)


def middle_kernel(summed, old, old_gate, columns, keep, pw, ow, send, norm, turned, mixed, mixed_back):
    width = keep.shape[1]
    z = [old[:, i * width : (i + 1) * width] for i in range(OWN)]
    z = finish(0, z, summed, old_gate, ow[0].T, columns, mixed_back)
    normalise(1, z, columns, norm, turned, width)
    project(1, norm, keep, pw[1], columns, send, mixed)


def last_kernel(summed, old, old_gate, columns, ow, out, mixed_back):
    width = out.shape[1]
    z = [old[:, i * width : (i + 1) * width] for i in range(OWN)]
    z = finish(1, z, summed, old_gate, ow[1].T, columns, mixed_back)
    for i in range(OWN):
        out[i] = z[i].T


def reorder(values, have, want):
    tiles = values.reshape(len(have), 2 * OWN, values.shape[1])
    places = [have.index(chip) for chip in want]
    return jnp.concatenate([tiles[n : n + 1] for n in places]).reshape(values.shape)


def triangle(incoming, sides, out):
    in_mesh = tuple(range(len(CHIPS)))
    left, right = [unpack(sides[:, n : n + 16, :].astype(F32)) for n in (0, 16)]
    if incoming:
        summed = [over_rows(a.astype(BF16), b.astype(BF16)) for a, b in zip(left, right)]
        summed = [reorder(v, in_mesh, CHIPS) for v in summed]
    else:
        right = [reorder(v, CHIPS, in_mesh) for v in right]
        summed = [over_columns(a.astype(BF16), b.astype(BF16)) for a, b in zip(left, right)]
    out[...] = pack(summed).astype(BF16)


def output_gate(u, normed, gate_weight, columns, gate):
    gating = jnp.dot(gate_weight.T, normed[...], preferred_element_type=F32)
    gate[...] = sigmoid(gating + columns[:, u * EACH + 6 : u * EACH + 7])


def outgoing_kernel(sides, out):
    triangle(False, sides, out)


def incoming_kernel(sides, out):
    triangle(True, sides, out)


def gate_kernel(u, normed, gw, columns, gate):
    output_gate(u, normed, gw[u], columns, gate)


def call(kernel, outs, scratch, *args, place=pltpu.VMEM, cost=None):
    in_vmem = pl.BlockSpec(memory_space=pltpu.VMEM)
    return pl.pallas_call(
        kernel,
        out_shape=[jax.ShapeDtypeStruct(*o) for o in outs],
        in_specs=[pl.BlockSpec(memory_space=place)] * len(args),
        out_specs=[in_vmem] * len(outs),
        scratch_shapes=scratch,
        cost_estimate=cost,
        compiler_params=pltpu.CompilerParams(vmem_limit_bytes=24 * 2**20),
    )(*args)


def exchange(blocks):
    return lax.all_to_all(blocks, PEERS, split_axis=0, concat_axis=0, tiled=True)


def exchange_in_order(blocks):
    listed = [[2 * chip + core for chip in CHIPS for core in range(2)]]
    return lax.all_to_all(blocks, "row", split_axis=0, concat_axis=0, axis_index_groups=listed, tiled=True)


def packed_updates(count, pair_rep, pair_mask, pw, pb, gw, gb, ow, ob, ns, no):
    rows_of, width, channels = pair_rep.shape
    flat = (channels, rows_of * width)
    projected = [((count, 32, width), BF16), (flat, BF16), (flat, BF16)]
    summed = [((count, 16, width), BF16)]
    params = [pair_rep, pair_mask, pw, pb, gb, ob, ns, no]
    params = [pltpu.with_memory_space_constraint(v, pltpu.HBM) for v in params]
    held = [pltpu.VMEM(v.shape[1:] if n == 2 else v.shape, v.dtype) for n, v in enumerate(params)]
    held += [pltpu.VMEM((2 * EACH, channels), F32), pltpu.SemaphoreType.DMA((len(params),))]
    back = pltpu.VMEM((OWN * channels, width), F32)
    mixed = pltpu.VMEM((2, OWN * channels, width), F32)
    kept = [((channels, 2 * EACH), F32), ((2 * OWN, width), F32)]
    send, norm, turned, columns, keep = call(
        first_kernel, projected + kept, held + [mixed], *params, place=pltpu.HBM
    )
    cost = pl.CostEstimate(flops=2 * channels * channels * rows_of * width, bytes_accessed=2**20, transcendentals=2**16)
    (gate,) = call(functools.partial(gate_kernel, 0), [(flat, F32)], [], norm, gw, columns, cost=cost)
    (send,) = call(outgoing_kernel, summed, [], exchange_in_order(send))
    send, norm, turned = call(
        middle_kernel, projected, [mixed, back], exchange_in_order(send), turned, gate, columns, keep, pw, ow
    )
    (gate,) = call(functools.partial(gate_kernel, 1), [(flat, F32)], [], norm, gw, columns, cost=cost)
    (send,) = call(incoming_kernel, summed, [], exchange_in_order(send))
    (out,) = call(last_kernel, [(pair_rep.shape, BF16)], [back], exchange_in_order(send), turned, gate, columns, ow)
    return out


def update(pair_t, pair_mask, u, incoming, peers, rows_of, pw, pb, gw, gb, ow, ob, ns, no):
    channels, positions = pair_t.shape
    width = positions // rows_of
    h = pw.shape[2] // 4
    count = peers[0] * peers[1]
    own = h // count
    normed = layer_norm(pair_t, ns[u, 0][:, None], no[u, 0][:, None]).astype(BF16)
    projected = over_rows(jnp.concatenate([pw[u], gw[u]], 1), normed) + jnp.concatenate([pb[u], gb[u]], 0)[:, None]
    parts = [projected[n * h : (n + 1) * h] for n in range(4)]
    gating = jax.nn.sigmoid(projected[4 * h :])
    mask = pair_mask.astype(F32).reshape(1, positions)
    left = (mask * jax.nn.sigmoid(parts[1]) * parts[0]).astype(BF16)
    right = (mask * jax.nn.sigmoid(parts[3]) * parts[2]).astype(BF16)
    sides = exchange(jnp.stack([v.reshape(count, own, rows_of, width) for v in (left, right)], 1))
    sides = sides.reshape(peers[0], peers[1], 2, own, rows_of, width)
    sides = sides.transpose(2, 3, 0, 4, 1, 5).reshape(2, own, peers[0] * rows_of, peers[1] * width)
    form = "cki,ckj->cij" if incoming else "cik,cjk->cij"
    summed = jnp.einsum(form, sides[0], sides[1], preferred_element_type=F32).astype(BF16)
    summed = summed.reshape(own, peers[0], rows_of, peers[1], width).transpose(1, 3, 0, 2, 4)
    summed = exchange(summed.reshape(count, own, rows_of, width)).reshape(h, positions).astype(F32)
    hidden = layer_norm(summed, ns[u, 1][:, None], no[u, 1][:, None]).astype(BF16)
    change = over_rows(ow[u], hidden) + ob[u][:, None]
    return (pair_t + gating * change).astype(BF16)


def plain_updates(peers, pair_rep, pair_mask, *params):
    rows_of, width, channels = pair_rep.shape
    pair_t = pair_rep.reshape(rows_of * width, channels).T
    for u in range(2):
        pair_t = update(pair_t.astype(F32), pair_mask, u, u == 1, peers, rows_of, *params)
    return pair_t.T.reshape(rows_of, width, channels)


def solution(mesh):
    peers = (mesh.shape["row"], mesh.shape["ka"])
    count = peers[0] * peers[1]

    def on_device(pair_rep, pair_mask, *params):
        rows_of, width, channels = pair_rep.shape
        hidden = params[0].shape[2] // 4
        fits = peers[1] == 1 and rows_of == OWN and hidden == OWN * count and count == 2 * len(CHIPS)
        if fits and channels == hidden == 128 and width % 128 == 0:
            return packed_updates(count, pair_rep, pair_mask, *params)
        return plain_updates(peers, pair_rep, pair_mask, *params)

    split = P(("grp", "row"), "ka", None)
    in_specs = (split, P(("grp", "row"), "ka")) + (P(),) * 8
    return jax.shard_map(on_device, mesh=mesh, in_specs=in_specs, out_specs=split, check_vma=False)
```

```python
import functools

import jax
import jax.numpy as jnp
from jax import lax
from jax.experimental import pallas as pl
from jax.experimental.pallas import tpu as pltpu
from jax.sharding import PartitionSpec as P

PEERS = ("row", "ka")
ROWS = 4
OWN = 8
CHIPS = (15, 14, 13, 12, 11, 10, 9, 8, 7, 6, 5, 4, 3, 2, 1, 0)
EACH = 16
BF16, F32 = jnp.bfloat16, jnp.float32


def over_rows(a, b):
    return lax.dot_general(a, b, (((0,), (0,)), ((), ())), preferred_element_type=F32)


def over_columns(a, b):
    return lax.dot_general(a, b, (((1,), (1,)), ((), ())), preferred_element_type=F32)


def layer_norm(values, norm_gain, norm_bias):
    average = jnp.mean(values, 0, keepdims=True)
    centred = values - average
    variance = jnp.mean(centred * centred, 0, keepdims=True)
    return centred * lax.rsqrt(variance + 1e-05) * norm_gain + norm_bias


def pack(blocks):
    channels, width = blocks[0].shape
    tiles = [b.reshape(channels // OWN, OWN, width) for b in blocks]
    return jnp.stack(tiles, 1).reshape(channels // OWN, ROWS * OWN, width)


def unpack(packed):
    count, _, width = packed.shape
    tiles = packed.reshape(count, ROWS, OWN, width)
    return [tiles[:, i].reshape(count * OWN, width) for i in range(ROWS)]


def sigmoid(x):
    return 0.5 * jnp.tanh(0.5 * x) + 0.5


def broadcast_columns(columns, first, many, width):
    held = columns[...]
    return [jnp.broadcast_to(held[:, n : n + 1], (held.shape[0], width)) for n in range(first, first + many)]


def project(u, z, mask, proj_weight, gate_weight, columns, send, gate):
    width = z[0].shape[1]
    h = proj_weight.shape[1] // 4
    gain, offset, *biases = broadcast_columns(columns, u * EACH, 7, width)
    turned = [proj_weight[:, n * h : (n + 1) * h].T for n in range(4)] + [gate_weight.T]
    lefts, rights = [], []
    for pair in range(0, ROWS, 2):
        normed = [layer_norm(z[i], gain, offset).astype(BF16) for i in (pair, pair + 1)]
        normed = jnp.concatenate(normed, 1)
        both = [jnp.dot(w, normed, preferred_element_type=F32) for w in turned]
        for n in range(2):
            i = pair + n
            parts = [v[:, n * width : (n + 1) * width] + b for v, b in zip(both, biases)]
            keep = mask[i : i + 1, :]
            lefts.append((keep * sigmoid(parts[1]) * parts[0]).astype(BF16))
            rights.append((keep * sigmoid(parts[3]) * parts[2]).astype(BF16))
            gate[:, i * width : (i + 1) * width] = sigmoid(parts[4])
    for n, side in enumerate((lefts, rights)):
        send[:, n * ROWS * OWN : (n + 1) * ROWS * OWN, :] = pack([v.astype(F32) for v in side]).astype(BF16)


def finish(u, z, summed, gate, out_weight, columns):
    width = z[0].shape[1]
    gain, offset, bias = broadcast_columns(columns, u * EACH + 7, 3, width)
    turned = out_weight.T
    results = []
    blocks = unpack(summed[...].astype(F32))
    for pair in range(0, ROWS, 2):
        hidden = [layer_norm(blocks[i], gain, offset).astype(BF16) for i in (pair, pair + 1)]
        both = jnp.dot(turned, jnp.concatenate(hidden, 1), preferred_element_type=F32)
        for n in range(2):
            change = both[:, n * width : (n + 1) * width] + bias
            at = slice((pair + n) * width, (pair + n + 1) * width)
            results.append((z[pair + n].astype(F32) + gate[:, at] * change).astype(BF16))
    return results


def first_kernel(
    pair, mask, pw, gw, pb, gb, ob, ns, no, send, gate, turned, columns, keep, pair_in, mask_in, pw_in, gw_in, pb_in, gb_in, ob_in, ns_in, no_in, rows, arrived
):
    moves = [(pair, pair_in), (pb, pb_in), (gb, gb_in), (ob, ob_in), (ns, ns_in), (no, no_in)]
    moves += [(pw.at[0], pw_in), (gw.at[0], gw_in), (mask, mask_in)]
    moves = [pltpu.make_async_copy(a, b, arrived.at[n]) for n, (a, b) in enumerate(moves)]
    for move in moves:
        move.start()
    moves[0].wait()
    width = pair.shape[1]
    z = [pair_in[i].T for i in range(ROWS)]
    for i in range(ROWS):
        turned[:, i * width : (i + 1) * width] = z[i]
    for move in moves[1:6]:
        move.wait()
    h = pw.shape[2] // 4
    for u in range(2):
        found = [ns_in[u, 0:1, :], no_in[u, 0:1, :]] + [pb_in[u : u + 1, n * h : (n + 1) * h] for n in range(4)]
        found += [gb_in[u : u + 1, :], ns_in[u, 1:2, :], no_in[u, 1:2, :], ob_in[u : u + 1, :]]
        for n, row in enumerate(found):
            rows[u * EACH + n : u * EACH + n + 1, :] = row
    columns[...] = rows[...].T
    for move in moves[6:]:
        move.wait()
    keep[0:ROWS, :] = mask_in[...].astype(F32)
    project(0, [v.astype(F32) for v in z], keep, pw_in[...], gw_in[...], columns, send, gate)


def middle_kernel(summed, old, old_gate, columns, keep, pw, gw, ow, send, gate, turned):
    width = keep.shape[1]
    z = finish(0, [old[:, i * width : (i + 1) * width] for i in range(ROWS)], summed, old_gate, ow[0], columns)
    for i in range(ROWS):
        turned[:, i * width : (i + 1) * width] = z[i]
    project(1, [v.astype(F32) for v in z], keep, pw[1], gw[1], columns, send, gate)


def last_kernel(summed, old, old_gate, columns, ow, out):
    width = out.shape[1]
    z = finish(1, [old[:, i * width : (i + 1) * width] for i in range(ROWS)], summed, old_gate, ow[1], columns)
    for i in range(ROWS):
        out[i] = z[i].T


def rows_at(chip, core):
    return pl.ds(pl.multiple_of((2 * chip + core) * ROWS * OWN, ROWS * OWN), ROWS * OWN)


def outgoing_kernel(sides, other_right, out, left, right, sums):
    core = lax.axis_index("row") & 1
    depth, count = ROWS * OWN, left.shape[0]
    left[...] = sides[:, :depth, :].astype(F32).reshape(left.shape)
    for n, chip in enumerate(CHIPS):
        right[rows_at(chip, core), :] = sides[n, depth:, :].astype(F32)
        right[rows_at(chip, 1 - core), :] = other_right[n].astype(F32)
    for c in range(OWN):
        a = left[pl.ds(c, count // OWN, stride=OWN), :].astype(BF16)
        b = right[pl.ds(c, 2 * count // OWN, stride=OWN), :].astype(BF16)
        sums[pl.ds(c, count // OWN, stride=OWN), :] = over_columns(a, b)
    out[...] = sums[...].astype(BF16).reshape(out.shape)


def incoming_kernel(sides, own, other, left, right, sums):
    core = lax.axis_index("row") & 1
    depth, count = ROWS * OWN, left.shape[0]
    left[...] = sides[:, :depth, :].astype(F32).reshape(left.shape)
    right[...] = sides[:, depth:, :].astype(F32).reshape(right.shape)
    for c in range(OWN):
        a, b = [v[pl.ds(c, count // OWN, stride=OWN), :].astype(BF16) for v in (left, right)]
        sums[pl.ds(c, 2 * count // OWN, stride=OWN), :] = over_rows(a, b)
    for n, chip in enumerate(CHIPS):
        own[n] = sums[rows_at(chip, core), :]
        other[n] = sums[rows_at(chip, 1 - core), :]


def add_kernel(own, from_other, out):
    out[...] = (own[...] + from_other[...]).astype(BF16)


def call(kernel, outs, scratch, *args, place=pltpu.VMEM):
    in_vmem = pl.BlockSpec(memory_space=pltpu.VMEM)
    return pl.pallas_call(
        kernel,
        out_shape=[jax.ShapeDtypeStruct(*o) for o in outs],
        in_specs=[pl.BlockSpec(memory_space=place)] * len(args),
        out_specs=[in_vmem] * len(outs),
        scratch_shapes=scratch,
        compiler_params=pltpu.CompilerParams(vmem_limit_bytes=24 * 2**20),
    )(*args)


def exchange(blocks):
    return lax.all_to_all(blocks, PEERS, split_axis=0, concat_axis=0, tiled=True)


def among_chips(blocks):
    groups = [[2 * chip + core for chip in CHIPS] for core in range(2)]
    return lax.all_to_all(blocks, "row", split_axis=0, concat_axis=0, axis_index_groups=groups, tiled=True)


def to_other_core(values):
    return lax.ppermute(values, "row", [(n, n ^ 1) for n in range(2 * len(CHIPS))])


def packed_updates(count, pair_rep, pair_mask, pw, pb, gw, gb, ow, ob, ns, no):
    rows_of, width, channels = pair_rep.shape
    chips, depth = count // 2, ROWS * OWN
    flat = (channels, rows_of * width)
    projected = [((chips, 2 * depth, width), BF16), (flat, F32), (flat, BF16)]
    summed = (chips, depth, width)
    params = [pair_rep, pair_mask, pw, gw, pb, gb, ob, ns, no]
    params = [pltpu.with_memory_space_constraint(v, pltpu.HBM) for v in params]
    held = [pltpu.VMEM(v.shape[1:] if n in (2, 3) else v.shape, v.dtype) for n, v in enumerate(params)]
    held += [pltpu.VMEM((2 * EACH, channels), F32), pltpu.SemaphoreType.DMA((len(params),))]
    half, whole = [pltpu.VMEM((n * chips * depth, width), F32) for n in (1, 2)]
    kept = [((channels, 2 * EACH), F32), ((2 * ROWS, width), F32)]
    send, gate, turned, columns, keep = call(first_kernel, projected + kept, held, *params, place=pltpu.HBM)
    sides = among_chips(send)
    other = to_other_core(sides[:, depth:])
    (send,) = call(outgoing_kernel, [(summed, BF16)], [half, whole, half], sides, other)
    send, gate, turned = call(middle_kernel, projected, [], among_chips(send), turned, gate, columns, keep, pw, gw, ow)
    own, other = call(incoming_kernel, [(summed, F32)] * 2, [half, half, whole], among_chips(send))
    (send,) = call(add_kernel, [(summed, BF16)], [], own, to_other_core(other))
    (out,) = call(last_kernel, [(pair_rep.shape, BF16)], [], among_chips(send), turned, gate, columns, ow)
    return out


def update(pair_t, pair_mask, u, incoming, peers, rows_of, pw, pb, gw, gb, ow, ob, ns, no):
    channels, positions = pair_t.shape
    width = positions // rows_of
    h = pw.shape[2] // 4
    count = peers[0] * peers[1]
    own = h // count
    normed = layer_norm(pair_t, ns[u, 0][:, None], no[u, 0][:, None]).astype(BF16)
    projected = over_rows(jnp.concatenate([pw[u], gw[u]], 1), normed) + jnp.concatenate([pb[u], gb[u]], 0)[:, None]
    parts = [projected[n * h : (n + 1) * h] for n in range(4)]
    gating = jax.nn.sigmoid(projected[4 * h :])
    mask = pair_mask.astype(F32).reshape(1, positions)
    left = (mask * jax.nn.sigmoid(parts[1]) * parts[0]).astype(BF16)
    right = (mask * jax.nn.sigmoid(parts[3]) * parts[2]).astype(BF16)
    sides = exchange(jnp.stack([v.reshape(count, own, rows_of, width) for v in (left, right)], 1))
    sides = sides.reshape(peers[0], peers[1], 2, own, rows_of, width)
    sides = sides.transpose(2, 3, 0, 4, 1, 5).reshape(2, own, peers[0] * rows_of, peers[1] * width)
    form = "cki,ckj->cij" if incoming else "cik,cjk->cij"
    summed = jnp.einsum(form, sides[0], sides[1], preferred_element_type=F32).astype(BF16)
    summed = summed.reshape(own, peers[0], rows_of, peers[1], width).transpose(1, 3, 0, 2, 4)
    summed = exchange(summed.reshape(count, own, rows_of, width)).reshape(h, positions).astype(F32)
    hidden = layer_norm(summed, ns[u, 1][:, None], no[u, 1][:, None]).astype(BF16)
    change = over_rows(ow[u], hidden) + ob[u][:, None]
    return (pair_t + gating * change).astype(BF16)


def plain_updates(peers, pair_rep, pair_mask, *params):
    rows_of, width, channels = pair_rep.shape
    pair_t = pair_rep.reshape(rows_of * width, channels).T
    for u in range(2):
        pair_t = update(pair_t.astype(F32), pair_mask, u, u == 1, peers, rows_of, *params)
    return pair_t.T.reshape(rows_of, width, channels)


def solution(mesh):
    peers = (mesh.shape["row"], mesh.shape["ka"])
    count = peers[0] * peers[1]

    def on_device(pair_rep, pair_mask, *params):
        rows_of, width, channels = pair_rep.shape
        hidden = params[0].shape[2] // 4
        fits = peers[1] == 1 and rows_of == ROWS and 2 * hidden == OWN * count and count == 2 * len(CHIPS)
        if fits and channels == hidden == 128 and width == 2 * len(CHIPS) * ROWS:
            return packed_updates(count, pair_rep, pair_mask, *params)
        return plain_updates(peers, pair_rep, pair_mask, *params)

    split = P(("grp", "row"), "ka", None)
    in_specs = (split, P(("grp", "row"), "ka")) + (P(),) * 8
    return jax.shard_map(on_device, mesh=mesh, in_specs=in_specs, out_specs=split, check_vma=False)
```

```python
import jax
import jax.numpy as jnp
from jax import lax
from jax.experimental import pallas as pl
from jax.experimental.pallas import tpu as pltpu
from jax.sharding import PartitionSpec as P

PEERS = ("row", "ka")
OWN = 4
ORDERS = (
    ((15, 14, 13, 12, 11, 10, 9, 8, 7, 6, 5, 4, 3, 2, 1, 0), (0, 15, 11, 14, 13, 10, 9, 7, 12, 5, 8, 6, 4, 3, 2, 1)),
    ((0, 15, 11, 14, 13, 10, 9, 7, 12, 5, 8, 6, 4, 3, 2, 1), (0, 15, 11, 14, 13, 10, 9, 7, 12, 5, 8, 6, 4, 3, 2, 1)),
)
EACH = 16
BF16, F32 = jnp.bfloat16, jnp.float32


def over_rows(a, b):
    return lax.dot_general(a, b, (((0,), (0,)), ((), ())), preferred_element_type=F32)


def over_columns(a, b):
    return lax.dot_general(a, b, (((1,), (1,)), ((), ())), preferred_element_type=F32)


def layer_norm(values, norm_gain, norm_bias):
    average = jnp.mean(values, 0, keepdims=True)
    centred = values - average
    variance = jnp.mean(centred * centred, 0, keepdims=True)
    return centred * lax.rsqrt(variance + 1e-05) * norm_gain + norm_bias


def pack(blocks):
    channels, width = blocks[0].shape
    tiles = [b.reshape(channels // 8, 8, width) for b in blocks]
    turned = [pltpu.roll(b, 4, axis=0).reshape(channels // 8, 8, width) for b in blocks]
    low = lax.broadcasted_iota(jnp.int32, tiles[0].shape, 1) < 4
    back = [pltpu.roll(b, channels - 4, axis=0).reshape(channels // 8, 8, width) for b in blocks]
    even = [jnp.where(low, tiles[n], turned[n + 1]) for n in (0, 2)]
    odd = [jnp.where(low, back[n], tiles[n + 1]) for n in (0, 2)]
    return jnp.stack([jnp.stack(even, 1), jnp.stack(odd, 1)], 1).reshape(channels // 4, 16, width)


def unpack(packed):
    count, _, width = packed.shape
    tiles = packed.reshape(count // 2, 2, 2, 8, width)
    low = lax.broadcasted_iota(jnp.int32, (count // 2, 8, width), 1) < 4
    blocks = []
    for n in range(2):
        even, odd = tiles[:, 0, n], tiles[:, 1, n]
        down = pltpu.roll(odd.reshape(count * 4, width), 4, axis=0).reshape(even.shape)
        up = pltpu.roll(even.reshape(count * 4, width), count * 4 - 4, axis=0).reshape(even.shape)
        blocks.append(jnp.where(low, even, down).reshape(count * 4, width))
        blocks.append(jnp.where(low, up, odd).reshape(count * 4, width))
    return blocks


def sigmoid(x):
    return 0.5 * jnp.tanh(0.5 * x) + 0.5


def broadcast_columns(columns, first, many, width):
    held = columns[...]
    return [jnp.broadcast_to(held[:, n : n + 1], (held.shape[0], width)) for n in range(first, first + many)]


def project(u, z, mask, proj_weight, gate_weight, columns, send, gate, mixed):
    width = z[0].shape[1]
    h = proj_weight.shape[1] // 4
    rows = mixed.shape[1]
    gain, offset, *biases = broadcast_columns(columns, u * EACH, 7, width)
    turned = [proj_weight[:, n * h : (n + 1) * h].T for n in range(4)] + [gate_weight.T]
    for pair in range(0, OWN, 2):
        normed = [layer_norm(z[i], gain, offset).astype(BF16) for i in (pair, pair + 1)]
        normed = jnp.concatenate(normed, 1)
        both = [jnp.dot(w, normed, preferred_element_type=F32) for w in turned]
        for n in range(2):
            i = pair + n
            parts = [v[:, n * width : (n + 1) * width] + b for v, b in zip(both, biases)]
            keep = mask[i : i + 1, :]
            mixed[0, pl.ds(i, h, stride=OWN), :] = keep * sigmoid(parts[1]) * parts[0]
            mixed[1, pl.ds(i, h, stride=OWN), :] = keep * sigmoid(parts[3]) * parts[2]
            gate[:, i * width : (i + 1) * width] = sigmoid(parts[4])
    send[:, 0:16, :] = mixed[0].reshape(rows // 16, 16, width).astype(BF16)
    send[:, 16:32, :] = mixed[1].reshape(rows // 16, 16, width).astype(BF16)


def finish(u, z, summed, gate, out_weight, columns, mixed):
    width = z[0].shape[1]
    gain, offset, bias = broadcast_columns(columns, u * EACH + 7, 3, width)
    turned = out_weight.T
    mixed[...] = summed[...].astype(F32).reshape(mixed.shape)
    results = []
    for pair in range(0, OWN, 2):
        blocks = [mixed[pl.ds(i, mixed.shape[0] // OWN, stride=OWN), :] for i in (pair, pair + 1)]
        blocks = [reorder(v, ORDERS[u][1], ORDERS[u][0]) for v in blocks]
        hidden = jnp.concatenate([layer_norm(v, gain, offset).astype(BF16) for v in blocks], 1)
        both = jnp.dot(turned, hidden, preferred_element_type=F32)
        for n in range(2):
            change = both[:, n * width : (n + 1) * width] + bias
            at = slice((pair + n) * width, (pair + n + 1) * width)
            results.append((z[pair + n].astype(F32) + gate[:, at] * change).astype(BF16))
    return results


def first_kernel(
    pair, mask, pw, gw, pb, gb, ob, ns, no, send, gate, turned, columns, keep, pair_in, mask_in, pw_in, gw_in, pb_in, gb_in, ob_in, ns_in, no_in, rows, arrived, mixed
):
    moves = [(pair, pair_in), (pb, pb_in), (gb, gb_in), (ob, ob_in), (ns, ns_in), (no, no_in)]
    moves += [(pw.at[0], pw_in), (gw.at[0], gw_in), (mask, mask_in)]
    moves = [pltpu.make_async_copy(a, b, arrived.at[n]) for n, (a, b) in enumerate(moves)]
    for move in moves:
        move.start()
    moves[0].wait()
    width = pair.shape[1]
    z = [pair_in[i].T for i in range(OWN)]
    for i in range(OWN):
        turned[:, i * width : (i + 1) * width] = z[i]
    for move in moves[1:6]:
        move.wait()
    h = pw.shape[2] // 4
    for u in range(2):
        found = [ns_in[u, 0:1, :], no_in[u, 0:1, :]] + [pb_in[u : u + 1, n * h : (n + 1) * h] for n in range(4)]
        found += [gb_in[u : u + 1, :], ns_in[u, 1:2, :], no_in[u, 1:2, :], ob_in[u : u + 1, :]]
        for n, row in enumerate(found):
            rows[u * EACH + n : u * EACH + n + 1, :] = row
    columns[...] = rows[...].T
    for move in moves[6:]:
        move.wait()
    keep[0:OWN, :] = mask_in[...].astype(F32)
    project(0, [v.astype(F32) for v in z], keep, pw_in[...], gw_in[...], columns, send, gate, mixed)


def middle_kernel(summed, old, old_gate, columns, keep, pw, gw, ow, send, gate, turned, mixed, mixed_back):
    width = keep.shape[1]
    z = finish(0, [old[:, i * width : (i + 1) * width] for i in range(OWN)], summed, old_gate, ow[0], columns, mixed_back)
    for i in range(OWN):
        turned[:, i * width : (i + 1) * width] = z[i]
    project(1, [v.astype(F32) for v in z], keep, pw[1], gw[1], columns, send, gate, mixed)


def last_kernel(summed, old, old_gate, columns, ow, out, mixed_back):
    width = out.shape[1]
    z = finish(1, [old[:, i * width : (i + 1) * width] for i in range(OWN)], summed, old_gate, ow[1], columns, mixed_back)
    for i in range(OWN):
        out[i] = z[i].T


def reorder(values, have, want):
    tiles = values.reshape(len(have), 2 * OWN, values.shape[1])
    places = [have.index(chip) for chip in want]
    return jnp.concatenate([tiles[n : n + 1] for n in places]).reshape(values.shape)


def triangle(incoming, sides, out):
    come, go = ORDERS[1 if incoming else 0]
    in_mesh = tuple(range(len(come)))
    left, right = [unpack(sides[:, n : n + 16, :].astype(F32)) for n in (0, 16)]
    if incoming:
        summed = [over_rows(a.astype(BF16), b.astype(BF16)) for a, b in zip(left, right)]
        summed = [reorder(v, in_mesh, go) for v in summed]
    else:
        left = [reorder(v, come, go) for v in left]
        right = [reorder(v, come, in_mesh) for v in right]
        summed = [over_columns(a.astype(BF16), b.astype(BF16)) for a, b in zip(left, right)]
    out[...] = pack(summed).astype(BF16)


def theirs_kernel(sides, theirs):
    theirs[...] = sides[:, 1 - (lax.axis_index("row") & 1)]


def outgoing_kernel(sides, others, out, both):
    core = lax.axis_index("row") & 1
    both[:, core] = sides[:, core]
    both[:, 1 - core] = others[...]
    triangle(False, both[...].reshape(2 * both.shape[0], *both.shape[2:]), out)


def incoming_kernel(sides, out):
    triangle(True, sides, out)


def call(kernel, outs, scratch, *args, place=pltpu.VMEM):
    in_vmem = pl.BlockSpec(memory_space=pltpu.VMEM)
    return pl.pallas_call(
        kernel,
        out_shape=[jax.ShapeDtypeStruct(*o) for o in outs],
        in_specs=[pl.BlockSpec(memory_space=place)] * len(args),
        out_specs=[in_vmem] * len(outs),
        scratch_shapes=scratch,
        compiler_params=pltpu.CompilerParams(vmem_limit_bytes=24 * 2**20),
    )(*args)


def exchange(blocks):
    return lax.all_to_all(blocks, PEERS, split_axis=0, concat_axis=0, tiled=True)


def exchange_in_order(blocks, chips):
    listed = [[2 * chip + core for chip in chips for core in range(2)]]
    return lax.all_to_all(blocks, "row", split_axis=0, concat_axis=0, axis_index_groups=listed, tiled=True)


def first_exchange(blocks, chips):
    groups = [[2 * chip + core for chip in chips] for core in range(2)]
    joined = blocks.reshape(len(chips), -1, blocks.shape[2])
    joined = lax.all_to_all(joined, "row", split_axis=0, concat_axis=0, axis_index_groups=groups, tiled=True)
    sides = joined.reshape(len(chips), 2, *blocks.shape[1:])
    (theirs,) = call(theirs_kernel, [((len(chips), *blocks.shape[1:]), BF16)], [], sides)
    return sides, lax.ppermute(theirs, "row", [(n, n ^ 1) for n in range(2 * len(chips))])


def packed_updates(count, pair_rep, pair_mask, pw, pb, gw, gb, ow, ob, ns, no):
    rows_of, width, channels = pair_rep.shape
    flat = (channels, rows_of * width)
    projected = [((count, 32, width), BF16), (flat, F32), (flat, BF16)]
    summed = [((count, 16, width), BF16)]
    params = [pair_rep, pair_mask, pw, gw, pb, gb, ob, ns, no]
    params = [pltpu.with_memory_space_constraint(v, pltpu.HBM) for v in params]
    held = [pltpu.VMEM(v.shape[1:] if n in (2, 3) else v.shape, v.dtype) for n, v in enumerate(params)]
    held += [pltpu.VMEM((2 * EACH, channels), F32), pltpu.SemaphoreType.DMA((len(params),))]
    back = pltpu.VMEM((OWN * channels, width), F32)
    mixed = pltpu.VMEM((2, OWN * channels, width), F32)
    kept = [((channels, 2 * EACH), F32), ((2 * OWN, width), F32)]
    send, gate, turned, columns, keep = call(first_kernel, projected + kept, held + [mixed], *params, place=pltpu.HBM)
    both = pltpu.VMEM((count // 2, 2, 32, width), BF16)
    (send,) = call(outgoing_kernel, summed, [both], *first_exchange(send, ORDERS[0][0]))
    send, gate, turned = call(middle_kernel, projected, [mixed, back], exchange_in_order(send, ORDERS[0][1]), turned, gate, columns, keep, pw, gw, ow)
    (send,) = call(incoming_kernel, summed, [], exchange_in_order(send, ORDERS[1][0]))
    (out,) = call(last_kernel, [(pair_rep.shape, BF16)], [back], exchange_in_order(send, ORDERS[1][1]), turned, gate, columns, ow)
    return out


def update(pair_t, pair_mask, u, incoming, peers, rows_of, pw, pb, gw, gb, ow, ob, ns, no):
    channels, positions = pair_t.shape
    width = positions // rows_of
    h = pw.shape[2] // 4
    count = peers[0] * peers[1]
    own = h // count
    normed = layer_norm(pair_t, ns[u, 0][:, None], no[u, 0][:, None]).astype(BF16)
    projected = over_rows(jnp.concatenate([pw[u], gw[u]], 1), normed) + jnp.concatenate([pb[u], gb[u]], 0)[:, None]
    parts = [projected[n * h : (n + 1) * h] for n in range(4)]
    gating = jax.nn.sigmoid(projected[4 * h :])
    mask = pair_mask.astype(F32).reshape(1, positions)
    left = (mask * jax.nn.sigmoid(parts[1]) * parts[0]).astype(BF16)
    right = (mask * jax.nn.sigmoid(parts[3]) * parts[2]).astype(BF16)
    sides = exchange(jnp.stack([v.reshape(count, own, rows_of, width) for v in (left, right)], 1))
    sides = sides.reshape(peers[0], peers[1], 2, own, rows_of, width)
    sides = sides.transpose(2, 3, 0, 4, 1, 5).reshape(2, own, peers[0] * rows_of, peers[1] * width)
    form = "cki,ckj->cij" if incoming else "cik,cjk->cij"
    summed = jnp.einsum(form, sides[0], sides[1], preferred_element_type=F32).astype(BF16)
    summed = summed.reshape(own, peers[0], rows_of, peers[1], width).transpose(1, 3, 0, 2, 4)
    summed = exchange(summed.reshape(count, own, rows_of, width)).reshape(h, positions).astype(F32)
    hidden = layer_norm(summed, ns[u, 1][:, None], no[u, 1][:, None]).astype(BF16)
    change = over_rows(ow[u], hidden) + ob[u][:, None]
    return (pair_t + gating * change).astype(BF16)


def plain_updates(peers, pair_rep, pair_mask, *params):
    rows_of, width, channels = pair_rep.shape
    pair_t = pair_rep.reshape(rows_of * width, channels).T
    for u in range(2):
        pair_t = update(pair_t.astype(F32), pair_mask, u, u == 1, peers, rows_of, *params)
    return pair_t.T.reshape(rows_of, width, channels)


def solution(mesh):
    peers = (mesh.shape["row"], mesh.shape["ka"])
    count = peers[0] * peers[1]

    def on_device(pair_rep, pair_mask, *params):
        rows_of, width, channels = pair_rep.shape
        hidden = params[0].shape[2] // 4
        fits = peers[1] == 1 and rows_of == OWN and hidden == OWN * count and count == 2 * len(ORDERS[0][0])
        if fits and channels == hidden == 128 and width % 128 == 0:
            return packed_updates(count, pair_rep, pair_mask, *params)
        return plain_updates(peers, pair_rep, pair_mask, *params)

    split = P(("grp", "row"), "ka", None)
    in_specs = (split, P(("grp", "row"), "ka")) + (P(),) * 8
    return jax.shard_map(on_device, mesh=mesh, in_specs=in_specs, out_specs=split, check_vma=False)
```

```python
import functools

import jax
import jax.numpy as jnp
from jax import lax
from jax.experimental import pallas as pl
from jax.experimental.pallas import tpu as pltpu
from jax.sharding import PartitionSpec as P

PEERS = ("row", "ka")
OWN = 4
ORDERS = (
    ((0, 15, 11, 14, 13, 10, 9, 7, 12, 5, 8, 6, 4, 3, 2, 1), (0, 15, 11, 14, 13, 10, 9, 7, 12, 5, 8, 6, 4, 3, 2, 1)),
    ((0, 15, 11, 14, 13, 10, 9, 7, 12, 5, 8, 6, 4, 3, 2, 1), (0, 15, 11, 14, 13, 10, 9, 7, 12, 5, 8, 6, 4, 3, 2, 1)),
)
EACH = 16
BF16, F32 = jnp.bfloat16, jnp.float32


def over_rows(a, b):
    return lax.dot_general(a, b, (((0,), (0,)), ((), ())), preferred_element_type=F32)


def over_columns(a, b):
    return lax.dot_general(a, b, (((1,), (1,)), ((), ())), preferred_element_type=F32)


def layer_norm(values, norm_gain, norm_bias):
    average = jnp.mean(values, 0, keepdims=True)
    centred = values - average
    variance = jnp.mean(centred * centred, 0, keepdims=True)
    return centred * lax.rsqrt(variance + 1e-05) * norm_gain + norm_bias


def pack(blocks):
    rows, width = blocks[0].shape
    tiles = [b.reshape(rows // 8, 8, width) for b in blocks]
    turned = [pltpu.roll(b, 4, axis=0).reshape(rows // 8, 8, width) for b in blocks]
    low = lax.broadcasted_iota(jnp.int32, tiles[0].shape, 1) < 4
    back = [pltpu.roll(b, rows - 4, axis=0).reshape(rows // 8, 8, width) for b in blocks]
    first = [jnp.where(low, tiles[n], turned[n + 1]) for n in (0, 2)]
    second = [jnp.where(low, back[n], tiles[n + 1]) for n in (0, 2)]
    return jnp.stack([jnp.stack(first, 1), jnp.stack(second, 1)]).reshape(rows // 4, 16, width)


def unpack(packed):
    count, _, width = packed.shape
    tiles = packed.reshape(2, count // 2, 2, 8, width)
    low = lax.broadcasted_iota(jnp.int32, (count // 2, 8, width), 1) < 4
    blocks = []
    for n in range(2):
        first, second = tiles[0, :, n], tiles[1, :, n]
        down = pltpu.roll(second.reshape(count * 4, width), 4, axis=0).reshape(first.shape)
        up = pltpu.roll(first.reshape(count * 4, width), count * 4 - 4, axis=0).reshape(first.shape)
        blocks.append(jnp.where(low, first, down).reshape(count * 4, width))
        blocks.append(jnp.where(low, up, second).reshape(count * 4, width))
    return blocks


def sigmoid(x):
    return 0.5 * jnp.tanh(0.5 * x) + 0.5


def broadcast_columns(columns, first, many, width):
    held = columns[...]
    return [jnp.broadcast_to(held[:, n : n + 1], (held.shape[0], width)) for n in range(first, first + many)]


def project(u, z, mask, proj_weight, gate_weight, columns, send, gate, mixed):
    width = z[0].shape[1]
    h = proj_weight.shape[1] // 4
    rows = mixed.shape[1]
    gain, offset, *biases = broadcast_columns(columns, u * EACH, 7, width)
    turned = [proj_weight[:, n * h : (n + 1) * h].T for n in range(4)] + [gate_weight.T]
    for pair in range(0, OWN, 2):
        normed = [layer_norm(z[i], gain, offset).astype(BF16) for i in (pair, pair + 1)]
        normed = jnp.concatenate(normed, 1)
        both = [jnp.dot(w, normed, preferred_element_type=F32) for w in turned]
        for n in range(2):
            i = pair + n
            parts = [v[:, n * width : (n + 1) * width] + b for v, b in zip(both, biases)]
            keep = mask[i : i + 1, :]
            mixed[0, pl.ds(i, h, stride=OWN), :] = keep * sigmoid(parts[1]) * parts[0]
            mixed[1, pl.ds(i, h, stride=OWN), :] = keep * sigmoid(parts[3]) * parts[2]
            gate[:, i * width : (i + 1) * width] = sigmoid(parts[4])
    send[:, 0:16, :] = mixed[0].reshape(rows // 16, 16, width).astype(BF16)
    send[:, 16:32, :] = mixed[1].reshape(rows // 16, 16, width).astype(BF16)


def finish(u, z, summed, gate, out_weight, columns, mixed):
    width = z[0].shape[1]
    gain, offset, bias = broadcast_columns(columns, u * EACH + 7, 3, width)
    turned = out_weight.T
    mixed[...] = summed[...].astype(F32).reshape(mixed.shape)
    results = []
    for pair in range(0, OWN, 2):
        blocks = [mixed[pl.ds(i, mixed.shape[0] // OWN, stride=OWN), :] for i in (pair, pair + 1)]
        blocks = [reorder(v, ORDERS[u][1], ORDERS[u][0]) for v in blocks]
        hidden = jnp.concatenate([layer_norm(v, gain, offset).astype(BF16) for v in blocks], 1)
        both = jnp.dot(turned, hidden, preferred_element_type=F32)
        for n in range(2):
            change = both[:, n * width : (n + 1) * width] + bias
            at = slice((pair + n) * width, (pair + n + 1) * width)
            results.append((z[pair + n].astype(F32) + gate[:, at] * change).astype(BF16))
    return results


def first_kernel(
    pair, mask, pw, gw, pb, gb, ob, ns, no, send, gate, turned, columns, keep, pair_in, mask_in, pw_in, gw_in, pb_in, gb_in, ob_in, ns_in, no_in, rows, arrived, mixed
):
    moves = [(pair, pair_in), (pb, pb_in), (gb, gb_in), (ob, ob_in), (ns, ns_in), (no, no_in)]
    moves += [(pw.at[0], pw_in), (gw.at[0], gw_in), (mask, mask_in)]
    moves = [pltpu.make_async_copy(a, b, arrived.at[n]) for n, (a, b) in enumerate(moves)]
    for move in moves:
        move.start()
    moves[0].wait()
    width = pair.shape[1]
    z = [pair_in[i].T for i in range(OWN)]
    for i in range(OWN):
        turned[:, i * width : (i + 1) * width] = z[i]
    for move in moves[1:6]:
        move.wait()
    h = pw.shape[2] // 4
    for u in range(2):
        found = [ns_in[u, 0:1, :], no_in[u, 0:1, :]] + [pb_in[u : u + 1, n * h : (n + 1) * h] for n in range(4)]
        found += [gb_in[u : u + 1, :], ns_in[u, 1:2, :], no_in[u, 1:2, :], ob_in[u : u + 1, :]]
        for n, row in enumerate(found):
            rows[u * EACH + n : u * EACH + n + 1, :] = row
    columns[...] = rows[...].T
    for move in moves[6:]:
        move.wait()
    keep[0:OWN, :] = mask_in[...].astype(F32)
    project(0, [v.astype(F32) for v in z], keep, pw_in[...], gw_in[...], columns, send, gate, mixed)


def middle_kernel(summed, old, old_gate, columns, keep, pw, gw, ow, send, gate, turned, mixed, mixed_back):
    width = keep.shape[1]
    z = finish(0, [old[:, i * width : (i + 1) * width] for i in range(OWN)], summed, old_gate, ow[0], columns, mixed_back)
    for i in range(OWN):
        turned[:, i * width : (i + 1) * width] = z[i]
    project(1, [v.astype(F32) for v in z], keep, pw[1], gw[1], columns, send, gate, mixed)


def last_kernel(summed, old, old_gate, columns, ow, out, mixed_back):
    width = out.shape[1]
    z = finish(1, [old[:, i * width : (i + 1) * width] for i in range(OWN)], summed, old_gate, ow[1], columns, mixed_back)
    for i in range(OWN):
        out[i] = z[i].T


def reorder(values, have, want):
    tiles = values.reshape(len(have), 2 * OWN, values.shape[1])
    places = [have.index(chip) for chip in want]
    return jnp.concatenate([tiles[n : n + 1] for n in places]).reshape(values.shape)


def triangle_kernel(incoming, sides, out):
    come, go = ORDERS[1 if incoming else 0]
    in_mesh = tuple(range(len(come)))
    left, right = [unpack(sides[:, n : n + 16, :].astype(F32)) for n in (0, 16)]
    if incoming:
        summed = [over_rows(a.astype(BF16), b.astype(BF16)) for a, b in zip(left, right)]
        summed = [reorder(v, in_mesh, go) for v in summed]
    else:
        left = [reorder(v, come, go) for v in left]
        right = [reorder(v, come, in_mesh) for v in right]
        summed = [over_columns(a.astype(BF16), b.astype(BF16)) for a, b in zip(left, right)]
    out[...] = pack(summed).astype(BF16)


def call(kernel, outs, scratch, *args, place=pltpu.VMEM):
    in_vmem = pl.BlockSpec(memory_space=pltpu.VMEM)
    return pl.pallas_call(
        kernel,
        out_shape=[jax.ShapeDtypeStruct(*o) for o in outs],
        in_specs=[pl.BlockSpec(memory_space=place)] * len(args),
        out_specs=[in_vmem] * len(outs),
        scratch_shapes=scratch,
        compiler_params=pltpu.CompilerParams(vmem_limit_bytes=24 * 2**20),
    )(*args)


def exchange(blocks):
    return lax.all_to_all(blocks, PEERS, split_axis=0, concat_axis=0, tiled=True)


def exchange_in_order(blocks, chips):
    listed = [[2 * chip + core for core in range(2) for chip in chips]]
    return lax.all_to_all(blocks, "row", split_axis=0, concat_axis=0, axis_index_groups=listed, tiled=True)


def packed_updates(count, pair_rep, pair_mask, pw, pb, gw, gb, ow, ob, ns, no):
    rows_of, width, channels = pair_rep.shape
    flat = (channels, rows_of * width)
    projected = [((count, 32, width), BF16), (flat, F32), (flat, BF16)]
    summed = [((count, 16, width), BF16)]
    params = [pair_rep, pair_mask, pw, gw, pb, gb, ob, ns, no]
    params = [pltpu.with_memory_space_constraint(v, pltpu.HBM) for v in params]
    held = [pltpu.VMEM(v.shape[1:] if n in (2, 3) else v.shape, v.dtype) for n, v in enumerate(params)]
    held += [pltpu.VMEM((2 * EACH, channels), F32), pltpu.SemaphoreType.DMA((len(params),))]
    back = pltpu.VMEM((OWN * channels, width), F32)
    mixed = pltpu.VMEM((2, OWN * channels, width), F32)
    kept = [((channels, 2 * EACH), F32), ((2 * OWN, width), F32)]
    send, gate, turned, columns, keep = call(first_kernel, projected + kept, held + [mixed], *params, place=pltpu.HBM)
    (send,) = call(functools.partial(triangle_kernel, False), summed, [], exchange_in_order(send, ORDERS[0][0]))
    send, gate, turned = call(middle_kernel, projected, [mixed, back], exchange_in_order(send, ORDERS[0][1]), turned, gate, columns, keep, pw, gw, ow)
    (send,) = call(functools.partial(triangle_kernel, True), summed, [], exchange_in_order(send, ORDERS[1][0]))
    (out,) = call(last_kernel, [(pair_rep.shape, BF16)], [back], exchange_in_order(send, ORDERS[1][1]), turned, gate, columns, ow)
    return out


def update(pair_t, pair_mask, u, incoming, peers, rows_of, pw, pb, gw, gb, ow, ob, ns, no):
    channels, positions = pair_t.shape
    width = positions // rows_of
    h = pw.shape[2] // 4
    count = peers[0] * peers[1]
    own = h // count
    normed = layer_norm(pair_t, ns[u, 0][:, None], no[u, 0][:, None]).astype(BF16)
    projected = over_rows(jnp.concatenate([pw[u], gw[u]], 1), normed) + jnp.concatenate([pb[u], gb[u]], 0)[:, None]
    parts = [projected[n * h : (n + 1) * h] for n in range(4)]
    gating = jax.nn.sigmoid(projected[4 * h :])
    mask = pair_mask.astype(F32).reshape(1, positions)
    left = (mask * jax.nn.sigmoid(parts[1]) * parts[0]).astype(BF16)
    right = (mask * jax.nn.sigmoid(parts[3]) * parts[2]).astype(BF16)
    sides = exchange(jnp.stack([v.reshape(count, own, rows_of, width) for v in (left, right)], 1))
    sides = sides.reshape(peers[0], peers[1], 2, own, rows_of, width)
    sides = sides.transpose(2, 3, 0, 4, 1, 5).reshape(2, own, peers[0] * rows_of, peers[1] * width)
    form = "cki,ckj->cij" if incoming else "cik,cjk->cij"
    summed = jnp.einsum(form, sides[0], sides[1], preferred_element_type=F32).astype(BF16)
    summed = summed.reshape(own, peers[0], rows_of, peers[1], width).transpose(1, 3, 0, 2, 4)
    summed = exchange(summed.reshape(count, own, rows_of, width)).reshape(h, positions).astype(F32)
    hidden = layer_norm(summed, ns[u, 1][:, None], no[u, 1][:, None]).astype(BF16)
    change = over_rows(ow[u], hidden) + ob[u][:, None]
    return (pair_t + gating * change).astype(BF16)


def plain_updates(peers, pair_rep, pair_mask, *params):
    rows_of, width, channels = pair_rep.shape
    pair_t = pair_rep.reshape(rows_of * width, channels).T
    for u in range(2):
        pair_t = update(pair_t.astype(F32), pair_mask, u, u == 1, peers, rows_of, *params)
    return pair_t.T.reshape(rows_of, width, channels)


def solution(mesh):
    peers = (mesh.shape["row"], mesh.shape["ka"])
    count = peers[0] * peers[1]

    def on_device(pair_rep, pair_mask, *params):
        rows_of, width, channels = pair_rep.shape
        hidden = params[0].shape[2] // 4
        fits = peers[1] == 1 and rows_of == OWN and hidden == OWN * count and count == 2 * len(ORDERS[0][0])
        if fits and channels == hidden == 128 and width % 128 == 0:
            return packed_updates(count, pair_rep, pair_mask, *params)
        return plain_updates(peers, pair_rep, pair_mask, *params)

    split = P(("grp", "row"), "ka", None)
    in_specs = (split, P(("grp", "row"), "ka")) + (P(),) * 8
    return jax.shard_map(on_device, mesh=mesh, in_specs=in_specs, out_specs=split, check_vma=False)
```

```python
import functools

import jax
import jax.numpy as jnp
from jax import lax
from jax.experimental import pallas as pl
from jax.experimental.pallas import tpu as pltpu
from jax.sharding import PartitionSpec as P

PEERS = ("row", "ka")
OWN = 4
ORDERS = (
    ((0, 15, 11, 14, 13, 10, 9, 7, 12, 5, 8, 6, 4, 3, 2, 1), (0, 15, 11, 14, 13, 10, 9, 7, 12, 5, 8, 6, 4, 3, 2, 1)),
    ((0, 15, 11, 14, 13, 10, 9, 7, 12, 5, 8, 6, 4, 3, 2, 1), (0, 15, 11, 14, 13, 10, 9, 7, 12, 5, 8, 6, 4, 3, 2, 1)),
)
EACH = 16
BF16, F32 = jnp.bfloat16, jnp.float32


def over_rows(a, b):
    return lax.dot_general(a, b, (((0,), (0,)), ((), ())), preferred_element_type=F32)


def over_columns(a, b):
    return lax.dot_general(a, b, (((1,), (1,)), ((), ())), preferred_element_type=F32)


def layer_norm(values, norm_gain, norm_bias):
    average = jnp.mean(values, 0, keepdims=True)
    centred = values - average
    variance = jnp.mean(centred * centred, 0, keepdims=True)
    return centred * lax.rsqrt(variance + 1e-05) * norm_gain + norm_bias


def pack(blocks):
    channels, width = blocks[0].shape
    tiles = [b.reshape(channels // 8, 8, width) for b in blocks]
    turned = [pltpu.roll(b, 4, axis=0).reshape(channels // 8, 8, width) for b in blocks]
    low = lax.broadcasted_iota(jnp.int32, tiles[0].shape, 1) < 4
    back = [pltpu.roll(b, channels - 4, axis=0).reshape(channels // 8, 8, width) for b in blocks]
    even = [jnp.where(low, tiles[n], turned[n + 1]) for n in (0, 2)]
    odd = [jnp.where(low, back[n], tiles[n + 1]) for n in (0, 2)]
    return jnp.stack([jnp.stack(even, 1), jnp.stack(odd, 1)], 1).reshape(channels // 4, 16, width)


def unpack(packed):
    count, _, width = packed.shape
    tiles = packed.reshape(count // 2, 2, 2, 8, width)
    low = lax.broadcasted_iota(jnp.int32, (count // 2, 8, width), 1) < 4
    blocks = []
    for n in range(2):
        even, odd = tiles[:, 0, n], tiles[:, 1, n]
        down = pltpu.roll(odd.reshape(count * 4, width), 4, axis=0).reshape(even.shape)
        up = pltpu.roll(even.reshape(count * 4, width), count * 4 - 4, axis=0).reshape(even.shape)
        blocks.append(jnp.where(low, even, down).reshape(count * 4, width))
        blocks.append(jnp.where(low, up, odd).reshape(count * 4, width))
    return blocks


def broadcast_columns(columns, first, many, width):
    held = columns[...]
    return [jnp.broadcast_to(held[:, n : n + 1], (held.shape[0], width)) for n in range(first, first + many)]


def project(u, z, mask, proj_weight, gate_weight, columns, send, gate, mixed):
    width = z[0].shape[1]
    h = proj_weight.shape[1] // 4
    rows = mixed.shape[1]
    gain, offset, *biases = broadcast_columns(columns, u * EACH, 7, width)
    scales = (1.0, 0.5, 1.0, 0.5, 0.5)
    biases = [b * k for b, k in zip(biases, scales)]
    turned = [proj_weight[:, n * h : (n + 1) * h] for n in range(4)] + [gate_weight]
    turned = [(w * jnp.asarray(k, BF16)).T if k != 1.0 else w.T for w, k in zip(turned, scales)]
    pairs = []
    for pair in range(0, OWN, 2):
        normed = [layer_norm(z[i], gain, offset).astype(BF16) for i in (pair, pair + 1)]
        pairs.append(jnp.concatenate(normed, 1))
    for side in range(2):
        for pair, normed in enumerate(pairs):
            value, gating = [jnp.dot(turned[2 * side + n], normed, preferred_element_type=F32) for n in range(2)]
            for n in range(2):
                i, at = 2 * pair + n, slice(n * width, (n + 1) * width)
                half = mask[i : i + 1, :] * 0.5
                weight = jnp.tanh(gating[:, at] + biases[2 * side + 1]) * half + half
                mixed[side, pl.ds(i, h, stride=OWN), :] = weight * (value[:, at] + biases[2 * side])
    for side in range(2):
        send[:, side * 16 : (side + 1) * 16, :] = mixed[side].reshape(rows // 16, 16, width).astype(BF16)
    for pair, normed in enumerate(pairs):
        gating = jnp.dot(turned[4], normed, preferred_element_type=F32)
        for n in range(2):
            i = 2 * pair + n
            gate[:, i * width : (i + 1) * width] = 0.5 * jnp.tanh(gating[:, n * width : (n + 1) * width] + biases[4]) + 0.5


def finish(u, z, summed, gate, out_weight, columns, mixed):
    width = z[0].shape[1]
    gain, offset, bias = broadcast_columns(columns, u * EACH + 7, 3, width)
    turned = out_weight.T
    mixed[...] = summed[...].astype(F32).reshape(mixed.shape)
    results = []
    for pair in range(0, OWN, 2):
        blocks = [mixed[pl.ds(i, mixed.shape[0] // OWN, stride=OWN), :] for i in (pair, pair + 1)]
        blocks = [reorder(v, ORDERS[u][1], ORDERS[u][0]) for v in blocks]
        hidden = jnp.concatenate([layer_norm(v, gain, offset).astype(BF16) for v in blocks], 1)
        both = jnp.dot(turned, hidden, preferred_element_type=F32)
        for n in range(2):
            change = both[:, n * width : (n + 1) * width] + bias
            at = slice((pair + n) * width, (pair + n + 1) * width)
            results.append((z[pair + n].astype(F32) + gate[:, at] * change).astype(BF16))
    return results


def first_kernel(
    pair, mask, pw, gw, pb, gb, ob, ns, no, send, gate, turned, columns, keep, pair_in, mask_in, pw_in, gw_in, pb_in, gb_in, ob_in, ns_in, no_in, rows, arrived, mixed
):
    moves = [(pair, pair_in), (pb, pb_in), (gb, gb_in), (ob, ob_in), (ns, ns_in), (no, no_in)]
    moves += [(pw.at[0], pw_in), (gw.at[0], gw_in), (mask, mask_in)]
    moves = [pltpu.make_async_copy(a, b, arrived.at[n]) for n, (a, b) in enumerate(moves)]
    for move in moves:
        move.start()
    for move in moves:
        move.wait()
    width = pair.shape[1]
    z = [pair_in[i].T for i in range(OWN)]
    for i in range(OWN):
        turned[:, i * width : (i + 1) * width] = z[i]
    h = pw.shape[2] // 4
    for u in range(2):
        found = [ns_in[u, 0:1, :], no_in[u, 0:1, :]] + [pb_in[u : u + 1, n * h : (n + 1) * h] for n in range(4)]
        found += [gb_in[u : u + 1, :], ns_in[u, 1:2, :], no_in[u, 1:2, :], ob_in[u : u + 1, :]]
        for n, row in enumerate(found):
            rows[u * EACH + n : u * EACH + n + 1, :] = row
    columns[...] = rows[...].T
    keep[0:OWN, :] = mask_in[...].astype(F32)
    project(0, [v.astype(F32) for v in z], keep, pw_in[...], gw_in[...], columns, send, gate, mixed)


def middle_kernel(summed, old, old_gate, columns, keep, pw, gw, ow, send, gate, turned, mixed, mixed_back):
    width = keep.shape[1]
    z = finish(0, [old[:, i * width : (i + 1) * width] for i in range(OWN)], summed, old_gate, ow[0], columns, mixed_back)
    for i in range(OWN):
        turned[:, i * width : (i + 1) * width] = z[i]
    project(1, [v.astype(F32) for v in z], keep, pw[1], gw[1], columns, send, gate, mixed)


def last_kernel(summed, old, old_gate, columns, ow, out, mixed_back):
    width = out.shape[1]
    z = finish(1, [old[:, i * width : (i + 1) * width] for i in range(OWN)], summed, old_gate, ow[1], columns, mixed_back)
    for i in range(OWN):
        out[i] = z[i].T


def reorder(values, have, want):
    tiles = values.reshape(len(have), 2 * OWN, values.shape[1])
    places = [have.index(chip) for chip in want]
    return jnp.concatenate([tiles[n : n + 1] for n in places]).reshape(values.shape)


def triangle_kernel(incoming, sides, out):
    come, go = ORDERS[1 if incoming else 0]
    in_mesh = tuple(range(len(come)))
    left, right = [unpack(sides[:, n : n + 16, :].astype(F32)) for n in (0, 16)]
    if incoming:
        summed = [over_rows(a.astype(BF16), b.astype(BF16)) for a, b in zip(left, right)]
        summed = [reorder(v, in_mesh, go) for v in summed]
    else:
        left = [reorder(v, come, go) for v in left]
        right = [reorder(v, come, in_mesh) for v in right]
        summed = [over_columns(a.astype(BF16), b.astype(BF16)) for a, b in zip(left, right)]
    out[...] = pack(summed).astype(BF16)


def call(kernel, outs, scratch, *args, place=pltpu.VMEM):
    in_vmem = pl.BlockSpec(memory_space=pltpu.VMEM)
    return pl.pallas_call(
        kernel,
        out_shape=[jax.ShapeDtypeStruct(*o) for o in outs],
        in_specs=[pl.BlockSpec(memory_space=place)] * len(args),
        out_specs=[in_vmem] * len(outs),
        scratch_shapes=scratch,
        compiler_params=pltpu.CompilerParams(vmem_limit_bytes=24 * 2**20),
    )(*args)


def exchange(blocks):
    return lax.all_to_all(blocks, PEERS, split_axis=0, concat_axis=0, tiled=True)


def exchange_in_order(blocks, chips):
    listed = [[2 * chip + core for chip in chips for core in range(2)]]
    return lax.all_to_all(blocks, "row", split_axis=0, concat_axis=0, axis_index_groups=listed, tiled=True)


def packed_updates(count, pair_rep, pair_mask, pw, pb, gw, gb, ow, ob, ns, no):
    rows_of, width, channels = pair_rep.shape
    flat = (channels, rows_of * width)
    projected = [((count, 32, width), BF16), (flat, F32), (flat, BF16)]
    summed = [((count, 16, width), BF16)]
    params = [pair_rep, pair_mask, pw, gw, pb, gb, ob, ns, no]
    params = [pltpu.with_memory_space_constraint(v, pltpu.HBM) for v in params]
    held = [pltpu.VMEM(v.shape[1:] if n in (2, 3) else v.shape, v.dtype) for n, v in enumerate(params)]
    held += [pltpu.VMEM((2 * EACH, channels), F32), pltpu.SemaphoreType.DMA((len(params),))]
    back = pltpu.VMEM((OWN * channels, width), F32)
    mixed = pltpu.VMEM((2, OWN * channels, width), F32)
    kept = [((channels, 2 * EACH), F32), ((2 * OWN, width), F32)]
    send, gate, turned, columns, keep = call(first_kernel, projected + kept, held + [mixed], *params, place=pltpu.HBM)
    (send,) = call(functools.partial(triangle_kernel, False), summed, [], exchange_in_order(send, ORDERS[0][0]))
    send, gate, turned = call(middle_kernel, projected, [mixed, back], exchange_in_order(send, ORDERS[0][1]), turned, gate, columns, keep, pw, gw, ow)
    (send,) = call(functools.partial(triangle_kernel, True), summed, [], exchange_in_order(send, ORDERS[1][0]))
    (out,) = call(last_kernel, [(pair_rep.shape, BF16)], [back], exchange_in_order(send, ORDERS[1][1]), turned, gate, columns, ow)
    return out


def update(pair_t, pair_mask, u, incoming, peers, rows_of, pw, pb, gw, gb, ow, ob, ns, no):
    channels, positions = pair_t.shape
    width = positions // rows_of
    h = pw.shape[2] // 4
    count = peers[0] * peers[1]
    own = h // count
    normed = layer_norm(pair_t, ns[u, 0][:, None], no[u, 0][:, None]).astype(BF16)
    projected = over_rows(jnp.concatenate([pw[u], gw[u]], 1), normed) + jnp.concatenate([pb[u], gb[u]], 0)[:, None]
    parts = [projected[n * h : (n + 1) * h] for n in range(4)]
    gating = jax.nn.sigmoid(projected[4 * h :])
    mask = pair_mask.astype(F32).reshape(1, positions)
    left = (mask * jax.nn.sigmoid(parts[1]) * parts[0]).astype(BF16)
    right = (mask * jax.nn.sigmoid(parts[3]) * parts[2]).astype(BF16)
    sides = exchange(jnp.stack([v.reshape(count, own, rows_of, width) for v in (left, right)], 1))
    sides = sides.reshape(peers[0], peers[1], 2, own, rows_of, width)
    sides = sides.transpose(2, 3, 0, 4, 1, 5).reshape(2, own, peers[0] * rows_of, peers[1] * width)
    form = "cki,ckj->cij" if incoming else "cik,cjk->cij"
    summed = jnp.einsum(form, sides[0], sides[1], preferred_element_type=F32).astype(BF16)
    summed = summed.reshape(own, peers[0], rows_of, peers[1], width).transpose(1, 3, 0, 2, 4)
    summed = exchange(summed.reshape(count, own, rows_of, width)).reshape(h, positions).astype(F32)
    hidden = layer_norm(summed, ns[u, 1][:, None], no[u, 1][:, None]).astype(BF16)
    change = over_rows(ow[u], hidden) + ob[u][:, None]
    return (pair_t + gating * change).astype(BF16)


def plain_updates(peers, pair_rep, pair_mask, *params):
    rows_of, width, channels = pair_rep.shape
    pair_t = pair_rep.reshape(rows_of * width, channels).T
    for u in range(2):
        pair_t = update(pair_t.astype(F32), pair_mask, u, u == 1, peers, rows_of, *params)
    return pair_t.T.reshape(rows_of, width, channels)


def solution(mesh):
    peers = (mesh.shape["row"], mesh.shape["ka"])
    count = peers[0] * peers[1]

    def on_device(pair_rep, pair_mask, *params):
        rows_of, width, channels = pair_rep.shape
        hidden = params[0].shape[2] // 4
        fits = peers[1] == 1 and rows_of == OWN and hidden == OWN * count and count == 2 * len(ORDERS[0][0])
        if fits and channels == hidden == 128 and width % 128 == 0:
            return packed_updates(count, pair_rep, pair_mask, *params)
        return plain_updates(peers, pair_rep, pair_mask, *params)

    split = P(("grp", "row"), "ka", None)
    in_specs = (split, P(("grp", "row"), "ka")) + (P(),) * 8
    return jax.shard_map(on_device, mesh=mesh, in_specs=in_specs, out_specs=split, check_vma=False)
```

```python
import functools

import jax
import jax.numpy as jnp
from jax import lax
from jax.experimental import pallas as pl
from jax.experimental.pallas import tpu as pltpu
from jax.sharding import PartitionSpec as P

PEERS = ("row", "ka")
OWN = 4
ORDERS = (
    ((0, 15, 11, 14, 13, 10, 9, 7, 12, 5, 8, 6, 4, 3, 2, 1), (0, 15, 11, 14, 13, 10, 9, 7, 12, 5, 8, 6, 4, 3, 2, 1)),
    ((0, 15, 11, 14, 13, 10, 9, 7, 12, 5, 8, 6, 4, 3, 2, 1), (0, 15, 11, 14, 13, 10, 9, 7, 12, 5, 8, 6, 4, 3, 2, 1)),
)
EACH = 16
BF16, F32 = jnp.bfloat16, jnp.float32


def over_rows(a, b):
    return lax.dot_general(a, b, (((0,), (0,)), ((), ())), preferred_element_type=F32)


def over_columns(a, b):
    return lax.dot_general(a, b, (((1,), (1,)), ((), ())), preferred_element_type=F32)


def layer_norm(values, norm_gain, norm_bias):
    average = jnp.mean(values, 0, keepdims=True)
    centred = values - average
    variance = jnp.mean(centred * centred, 0, keepdims=True)
    return centred * lax.rsqrt(variance + 1e-05) * norm_gain + norm_bias


def pack(blocks):
    channels, width = blocks[0].shape
    tiles = [b.reshape(channels // 8, 8, width) for b in blocks]
    turned = [pltpu.roll(b, 4, axis=0).reshape(channels // 8, 8, width) for b in blocks]
    low = lax.broadcasted_iota(jnp.int32, tiles[0].shape, 1) < 4
    back = [pltpu.roll(b, channels - 4, axis=0).reshape(channels // 8, 8, width) for b in blocks]
    even = [jnp.where(low, tiles[n], turned[n + 1]) for n in (0, 2)]
    odd = [jnp.where(low, back[n], tiles[n + 1]) for n in (0, 2)]
    return jnp.stack([jnp.stack(even, 1), jnp.stack(odd, 1)], 1).reshape(channels // 4, 16, width)


def unpack(packed):
    count, _, width = packed.shape
    tiles = packed.reshape(count // 2, 2, 2, 8, width)
    low = lax.broadcasted_iota(jnp.int32, (count // 2, 8, width), 1) < 4
    blocks = []
    for n in range(2):
        even, odd = tiles[:, 0, n], tiles[:, 1, n]
        down = pltpu.roll(odd.reshape(count * 4, width), 4, axis=0).reshape(even.shape)
        up = pltpu.roll(even.reshape(count * 4, width), count * 4 - 4, axis=0).reshape(even.shape)
        blocks.append(jnp.where(low, even, down).reshape(count * 4, width))
        blocks.append(jnp.where(low, up, odd).reshape(count * 4, width))
    return blocks


def broadcast_columns(columns, first, many, width):
    held = columns[...]
    return [jnp.broadcast_to(held[:, n : n + 1], (held.shape[0], width)) for n in range(first, first + many)]


def project(u, z, mask, proj_weight, gate_weight, columns, send, gate, mixed):
    width = z[0].shape[1]
    h = proj_weight.shape[1] // 4
    rows = mixed.shape[1]
    gain, offset, *biases = broadcast_columns(columns, u * EACH, 7, width)
    scales = (1.0, 0.5, 1.0, 0.5, 0.5)
    biases = [b * k for b, k in zip(biases, scales)]
    turned = [proj_weight[:, n * h : (n + 1) * h] for n in range(4)] + [gate_weight]
    turned = [(w * jnp.asarray(k, BF16)).T if k != 1.0 else w.T for w, k in zip(turned, scales)]
    pairs = []
    for pair in range(0, OWN, 2):
        normed = [layer_norm(z[i], gain, offset).astype(BF16) for i in (pair, pair + 1)]
        pairs.append(jnp.concatenate(normed, 1))
    for side in range(2):
        for pair, normed in enumerate(pairs):
            value, gating = [jnp.dot(turned[2 * side + n], normed, preferred_element_type=F32) for n in range(2)]
            for n in range(2):
                i, at = 2 * pair + n, slice(n * width, (n + 1) * width)
                half = mask[i : i + 1, :] * 0.5
                weight = jnp.tanh(gating[:, at] + biases[2 * side + 1]) * half + half
                mixed[side, pl.ds(i, h, stride=OWN), :] = weight * (value[:, at] + biases[2 * side])
    for side in range(2):
        send[:, side * 16 : (side + 1) * 16, :] = mixed[side].reshape(rows // 16, 16, width).astype(BF16)
    for pair, normed in enumerate(pairs):
        gating = jnp.dot(turned[4], normed, preferred_element_type=F32)
        for n in range(2):
            i = 2 * pair + n
            gate[:, i * width : (i + 1) * width] = 0.5 * jnp.tanh(gating[:, n * width : (n + 1) * width] + biases[4]) + 0.5


def finish(u, z, summed, gate, out_weight, columns, mixed):
    width = z[0].shape[1]
    gain, offset, bias = broadcast_columns(columns, u * EACH + 7, 3, width)
    turned = out_weight.T
    mixed[...] = summed[...].astype(F32).reshape(mixed.shape)
    results = []
    for pair in range(0, OWN, 2):
        blocks = [mixed[pl.ds(i, mixed.shape[0] // OWN, stride=OWN), :] for i in (pair, pair + 1)]
        blocks = [reorder(v, ORDERS[u][1], ORDERS[u][0]) for v in blocks]
        hidden = jnp.concatenate([layer_norm(v, gain, offset).astype(BF16) for v in blocks], 1)
        both = jnp.dot(turned, hidden, preferred_element_type=F32)
        for n in range(2):
            change = both[:, n * width : (n + 1) * width] + bias
            at = slice((pair + n) * width, (pair + n + 1) * width)
            results.append((z[pair + n].astype(F32) + gate[:, at] * change).astype(BF16))
    return results


def first_kernel(
    pair, mask, pw, gw, pb, gb, ob, ns, no, send, gate, turned, columns, keep, pair_in, mask_in, pw_in, gw_in, pb_in, gb_in, ob_in, ns_in, no_in, rows, arrived, mixed
):
    moves = [(pair, pair_in), (pb, pb_in), (gb, gb_in), (ob, ob_in), (ns, ns_in), (no, no_in)]
    moves += [(pw.at[0], pw_in), (gw.at[0], gw_in), (mask, mask_in)]
    moves = [pltpu.make_async_copy(a, b, arrived.at[n]) for n, (a, b) in enumerate(moves)]
    for n, move in enumerate(moves):
        move.start(priority=0 if n in (0, 6) else 1)
    for move in moves:
        move.wait()
    width = pair.shape[1]
    z = [pair_in[i].T for i in range(OWN)]
    for i in range(OWN):
        turned[:, i * width : (i + 1) * width] = z[i]
    h = pw.shape[2] // 4
    for u in range(2):
        found = [ns_in[u, 0:1, :], no_in[u, 0:1, :]] + [pb_in[u : u + 1, n * h : (n + 1) * h] for n in range(4)]
        found += [gb_in[u : u + 1, :], ns_in[u, 1:2, :], no_in[u, 1:2, :], ob_in[u : u + 1, :]]
        for n, row in enumerate(found):
            rows[u * EACH + n : u * EACH + n + 1, :] = row
    columns[...] = rows[...].T
    keep[0:OWN, :] = mask_in[...].astype(F32)
    project(0, [v.astype(F32) for v in z], keep, pw_in[...], gw_in[...], columns, send, gate, mixed)


def middle_kernel(summed, old, old_gate, columns, keep, pw, gw, ow, send, gate, turned, mixed, mixed_back):
    width = keep.shape[1]
    z = finish(0, [old[:, i * width : (i + 1) * width] for i in range(OWN)], summed, old_gate, ow[0], columns, mixed_back)
    for i in range(OWN):
        turned[:, i * width : (i + 1) * width] = z[i]
    project(1, [v.astype(F32) for v in z], keep, pw[1], gw[1], columns, send, gate, mixed)


def last_kernel(summed, old, old_gate, columns, ow, out, mixed_back):
    width = out.shape[1]
    z = finish(1, [old[:, i * width : (i + 1) * width] for i in range(OWN)], summed, old_gate, ow[1], columns, mixed_back)
    for i in range(OWN):
        out[i] = z[i].T


def reorder(values, have, want):
    tiles = values.reshape(len(have), 2 * OWN, values.shape[1])
    places = [have.index(chip) for chip in want]
    return jnp.concatenate([tiles[n : n + 1] for n in places]).reshape(values.shape)


def triangle_kernel(incoming, sides, out):
    come, go = ORDERS[1 if incoming else 0]
    in_mesh = tuple(range(len(come)))
    left, right = [unpack(sides[:, n : n + 16, :].astype(F32)) for n in (0, 16)]
    if incoming:
        summed = [over_rows(a.astype(BF16), b.astype(BF16)) for a, b in zip(left, right)]
        summed = [reorder(v, in_mesh, go) for v in summed]
    else:
        left = [reorder(v, come, go) for v in left]
        right = [reorder(v, come, in_mesh) for v in right]
        summed = [over_columns(a.astype(BF16), b.astype(BF16)) for a, b in zip(left, right)]
    out[...] = pack(summed).astype(BF16)


def call(kernel, outs, scratch, *args, place=pltpu.VMEM):
    in_vmem = pl.BlockSpec(memory_space=pltpu.VMEM)
    return pl.pallas_call(
        kernel,
        out_shape=[jax.ShapeDtypeStruct(*o) for o in outs],
        in_specs=[pl.BlockSpec(memory_space=place)] * len(args),
        out_specs=[in_vmem] * len(outs),
        scratch_shapes=scratch,
        compiler_params=pltpu.CompilerParams(vmem_limit_bytes=24 * 2**20),
    )(*args)


def exchange(blocks):
    return lax.all_to_all(blocks, PEERS, split_axis=0, concat_axis=0, tiled=True)


def exchange_in_order(blocks, chips):
    listed = [[2 * chip + core for chip in chips for core in range(2)]]
    return lax.all_to_all(blocks, "row", split_axis=0, concat_axis=0, axis_index_groups=listed, tiled=True)


def packed_updates(count, pair_rep, pair_mask, pw, pb, gw, gb, ow, ob, ns, no):
    rows_of, width, channels = pair_rep.shape
    flat = (channels, rows_of * width)
    projected = [((count, 32, width), BF16), (flat, F32), (flat, BF16)]
    summed = [((count, 16, width), BF16)]
    params = [pair_rep, pair_mask, pw, gw, pb, gb, ob, ns, no]
    params = [pltpu.with_memory_space_constraint(v, pltpu.HBM) for v in params]
    held = [pltpu.VMEM(v.shape[1:] if n in (2, 3) else v.shape, v.dtype) for n, v in enumerate(params)]
    held += [pltpu.VMEM((2 * EACH, channels), F32), pltpu.SemaphoreType.DMA((len(params),))]
    back = pltpu.VMEM((OWN * channels, width), F32)
    mixed = pltpu.VMEM((2, OWN * channels, width), F32)
    kept = [((channels, 2 * EACH), F32), ((2 * OWN, width), F32)]
    send, gate, turned, columns, keep = call(first_kernel, projected + kept, held + [mixed], *params, place=pltpu.HBM)
    (send,) = call(functools.partial(triangle_kernel, False), summed, [], exchange_in_order(send, ORDERS[0][0]))
    send, gate, turned = call(middle_kernel, projected, [mixed, back], exchange_in_order(send, ORDERS[0][1]), turned, gate, columns, keep, pw, gw, ow)
    (send,) = call(functools.partial(triangle_kernel, True), summed, [], exchange_in_order(send, ORDERS[1][0]))
    (out,) = call(last_kernel, [(pair_rep.shape, BF16)], [back], exchange_in_order(send, ORDERS[1][1]), turned, gate, columns, ow)
    return out


def update(pair_t, pair_mask, u, incoming, peers, rows_of, pw, pb, gw, gb, ow, ob, ns, no):
    channels, positions = pair_t.shape
    width = positions // rows_of
    h = pw.shape[2] // 4
    count = peers[0] * peers[1]
    own = h // count
    normed = layer_norm(pair_t, ns[u, 0][:, None], no[u, 0][:, None]).astype(BF16)
    projected = over_rows(jnp.concatenate([pw[u], gw[u]], 1), normed) + jnp.concatenate([pb[u], gb[u]], 0)[:, None]
    parts = [projected[n * h : (n + 1) * h] for n in range(4)]
    gating = jax.nn.sigmoid(projected[4 * h :])
    mask = pair_mask.astype(F32).reshape(1, positions)
    left = (mask * jax.nn.sigmoid(parts[1]) * parts[0]).astype(BF16)
    right = (mask * jax.nn.sigmoid(parts[3]) * parts[2]).astype(BF16)
    sides = exchange(jnp.stack([v.reshape(count, own, rows_of, width) for v in (left, right)], 1))
    sides = sides.reshape(peers[0], peers[1], 2, own, rows_of, width)
    sides = sides.transpose(2, 3, 0, 4, 1, 5).reshape(2, own, peers[0] * rows_of, peers[1] * width)
    form = "cki,ckj->cij" if incoming else "cik,cjk->cij"
    summed = jnp.einsum(form, sides[0], sides[1], preferred_element_type=F32).astype(BF16)
    summed = summed.reshape(own, peers[0], rows_of, peers[1], width).transpose(1, 3, 0, 2, 4)
    summed = exchange(summed.reshape(count, own, rows_of, width)).reshape(h, positions).astype(F32)
    hidden = layer_norm(summed, ns[u, 1][:, None], no[u, 1][:, None]).astype(BF16)
    change = over_rows(ow[u], hidden) + ob[u][:, None]
    return (pair_t + gating * change).astype(BF16)


def plain_updates(peers, pair_rep, pair_mask, *params):
    rows_of, width, channels = pair_rep.shape
    pair_t = pair_rep.reshape(rows_of * width, channels).T
    for u in range(2):
        pair_t = update(pair_t.astype(F32), pair_mask, u, u == 1, peers, rows_of, *params)
    return pair_t.T.reshape(rows_of, width, channels)


def solution(mesh):
    peers = (mesh.shape["row"], mesh.shape["ka"])
    count = peers[0] * peers[1]

    def on_device(pair_rep, pair_mask, *params):
        rows_of, width, channels = pair_rep.shape
        hidden = params[0].shape[2] // 4
        fits = peers[1] == 1 and rows_of == OWN and hidden == OWN * count and count == 2 * len(ORDERS[0][0])
        if fits and channels == hidden == 128 and width % 128 == 0:
            return packed_updates(count, pair_rep, pair_mask, *params)
        return plain_updates(peers, pair_rep, pair_mask, *params)

    split = P(("grp", "row"), "ka", None)
    in_specs = (split, P(("grp", "row"), "ka")) + (P(),) * 8
    return jax.shard_map(on_device, mesh=mesh, in_specs=in_specs, out_specs=split, check_vma=False)
```

```python
import functools

import jax
import jax.numpy as jnp
from jax import lax
from jax.experimental import pallas as pl
from jax.experimental.pallas import tpu as pltpu
from jax.sharding import PartitionSpec as P

PEERS = ("row", "ka")
OWN = 4
ORDERS = (
    ((0, 15, 11, 14, 13, 10, 9, 7, 12, 5, 8, 6, 4, 3, 2, 1), (0, 15, 11, 14, 13, 10, 9, 7, 12, 5, 8, 6, 4, 3, 2, 1)),
    ((0, 15, 11, 14, 13, 10, 9, 7, 12, 5, 8, 6, 4, 3, 2, 1), (0, 15, 11, 14, 13, 10, 9, 7, 12, 5, 8, 6, 4, 3, 2, 1)),
)
EACH = 16
BF16, F32 = jnp.bfloat16, jnp.float32


def over_rows(a, b):
    return lax.dot_general(a, b, (((0,), (0,)), ((), ())), preferred_element_type=F32)


def over_columns(a, b):
    return lax.dot_general(a, b, (((1,), (1,)), ((), ())), preferred_element_type=F32)


def layer_norm(values, norm_gain, norm_bias):
    average = jnp.mean(values, 0, keepdims=True)
    centred = values - average
    variance = jnp.mean(centred * centred, 0, keepdims=True)
    return centred * lax.rsqrt(variance + 1e-05) * norm_gain + norm_bias


def pack(blocks):
    channels, width = blocks[0].shape
    tiles = [b.reshape(channels // 8, 8, width) for b in blocks]
    turned = [pltpu.roll(b, 4, axis=0).reshape(channels // 8, 8, width) for b in blocks]
    low = lax.broadcasted_iota(jnp.int32, tiles[0].shape, 1) < 4
    back = [pltpu.roll(b, channels - 4, axis=0).reshape(channels // 8, 8, width) for b in blocks]
    even = [jnp.where(low, tiles[n], turned[n + 1]) for n in (0, 2)]
    odd = [jnp.where(low, back[n], tiles[n + 1]) for n in (0, 2)]
    return jnp.stack([jnp.stack(even, 1), jnp.stack(odd, 1)], 1).reshape(channels // 4, 16, width)


def unpack(packed):
    count, _, width = packed.shape
    tiles = packed.reshape(count // 2, 2, 2, 8, width)
    low = lax.broadcasted_iota(jnp.int32, (count // 2, 8, width), 1) < 4
    blocks = []
    for n in range(2):
        even, odd = tiles[:, 0, n], tiles[:, 1, n]
        down = pltpu.roll(odd.reshape(count * 4, width), 4, axis=0).reshape(even.shape)
        up = pltpu.roll(even.reshape(count * 4, width), count * 4 - 4, axis=0).reshape(even.shape)
        blocks.append(jnp.where(low, even, down).reshape(count * 4, width))
        blocks.append(jnp.where(low, up, odd).reshape(count * 4, width))
    return blocks


def broadcast_columns(columns, first, many, width):
    held = columns[...]
    return [jnp.broadcast_to(held[:, n : n + 1], (held.shape[0], width)) for n in range(first, first + many)]


def project(u, z, mask, proj_weight, gate_weight, columns, send, gate, mixed):
    width = z[0].shape[1]
    h = proj_weight.shape[1] // 4
    rows = mixed.shape[1]
    gain, offset, *biases = broadcast_columns(columns, u * EACH, 7, width)
    scales = (1.0, 0.5, 1.0, 0.5, 0.5)
    biases = [b * k for b, k in zip(biases, scales)]
    turned = [proj_weight[:, n * h : (n + 1) * h] for n in range(4)] + [gate_weight]
    turned = [(w * jnp.asarray(k, BF16)).T if k != 1.0 else w.T for w, k in zip(turned, scales)]
    pairs = []
    for pair in range(0, OWN, 2):
        normed = [layer_norm(z[i], gain, offset).astype(BF16) for i in (pair, pair + 1)]
        pairs.append(jnp.concatenate(normed, 1))
    for side in range(2):
        for pair, normed in enumerate(pairs):
            value, gating = [jnp.dot(turned[2 * side + n], normed, preferred_element_type=F32) for n in range(2)]
            for n in range(2):
                i, at = 2 * pair + n, slice(n * width, (n + 1) * width)
                half = mask[i : i + 1, :] * 0.5
                weight = jnp.tanh(gating[:, at] + biases[2 * side + 1]) * half + half
                mixed[side, pl.ds(i, h, stride=OWN), :] = weight * (value[:, at] + biases[2 * side])
    for side in range(2):
        send[:, side * 16 : (side + 1) * 16, :] = mixed[side].reshape(rows // 16, 16, width).astype(BF16)
    for pair, normed in enumerate(pairs):
        gating = jnp.dot(turned[4], normed, preferred_element_type=F32)
        for n in range(2):
            i = 2 * pair + n
            gate[:, i * width : (i + 1) * width] = 0.5 * jnp.tanh(gating[:, n * width : (n + 1) * width] + biases[4]) + 0.5


def finish(u, z, summed, gate, out_weight, columns, mixed):
    width = z[0].shape[1]
    gain, offset, bias = broadcast_columns(columns, u * EACH + 7, 3, width)
    turned = out_weight.T
    mixed[...] = summed[...].astype(F32).reshape(mixed.shape)
    for pair in range(0, OWN, 2):
        blocks = [mixed[pl.ds(i, mixed.shape[0] // OWN, stride=OWN), :] for i in (pair, pair + 1)]
        blocks = [reorder(v, ORDERS[u][1], ORDERS[u][0]) for v in blocks]
        hidden = jnp.concatenate([layer_norm(v, gain, offset).astype(BF16) for v in blocks], 1)
        both = jnp.dot(turned, hidden, preferred_element_type=F32)
        results = []
        for n in range(2):
            change = both[:, n * width : (n + 1) * width] + bias
            at = slice((pair + n) * width, (pair + n + 1) * width)
            results.append((z[pair + n].astype(F32) + gate[:, at] * change).astype(BF16))
        yield results


def first_kernel(
    pair, mask, pw, gw, pb, gb, ob, ns, no, send, gate, turned, columns, keep, pair_in, mask_in, pw_in, gw_in, pb_in, gb_in, ob_in, ns_in, no_in, rows, arrived, mixed
):
    moves = [(pair, pair_in), (pb, pb_in), (gb, gb_in), (ob, ob_in), (ns, ns_in), (no, no_in)]
    moves += [(pw.at[0], pw_in), (gw.at[0], gw_in), (mask, mask_in)]
    moves = [pltpu.make_async_copy(a, b, arrived.at[n]) for n, (a, b) in enumerate(moves)]
    for move in moves:
        move.start()
    for move in moves:
        move.wait()
    width = pair.shape[1]
    z = [pair_in[i].T for i in range(OWN)]
    for i in range(OWN):
        turned[:, i * width : (i + 1) * width] = z[i]
    h = pw.shape[2] // 4
    for u in range(2):
        found = [ns_in[u, 0:1, :], no_in[u, 0:1, :]] + [pb_in[u : u + 1, n * h : (n + 1) * h] for n in range(4)]
        found += [gb_in[u : u + 1, :], ns_in[u, 1:2, :], no_in[u, 1:2, :], ob_in[u : u + 1, :]]
        for n, row in enumerate(found):
            rows[u * EACH + n : u * EACH + n + 1, :] = row
    columns[...] = rows[...].T
    keep[0:OWN, :] = mask_in[...].astype(F32)
    project(0, [v.astype(F32) for v in z], keep, pw_in[...], gw_in[...], columns, send, gate, mixed)


def middle_kernel(summed, old, old_gate, columns, keep, pw, gw, ow, send, gate, turned, mixed, mixed_back):
    width = keep.shape[1]
    pairs = finish(0, [old[:, i * width : (i + 1) * width] for i in range(OWN)], summed, old_gate, ow[0], columns, mixed_back)
    z = [v for pair in pairs for v in pair]
    for i in range(OWN):
        turned[:, i * width : (i + 1) * width] = z[i]
    project(1, [v.astype(F32) for v in z], keep, pw[1], gw[1], columns, send, gate, mixed)


def last_kernel(summed, old, old_gate, columns, ow, out, ready, left, mixed_back):
    width = out.shape[1]
    z = [old[:, i * width : (i + 1) * width] for i in range(OWN)]
    moves = []
    for n, pair in enumerate(finish(1, z, summed, old_gate, ow[1], columns, mixed_back)):
        here = pl.ds(2 * n, 2)
        for i, v in enumerate(pair):
            ready[2 * n + i] = v.T
        moves.append(pltpu.make_async_copy(ready.at[here], out.at[here], left.at[n]))
        moves[n].start()
    for move in moves:
        move.wait()


def reorder(values, have, want):
    tiles = values.reshape(len(have), 2 * OWN, values.shape[1])
    places = [have.index(chip) for chip in want]
    return jnp.concatenate([tiles[n : n + 1] for n in places]).reshape(values.shape)


def triangle_kernel(incoming, sides, out):
    come, go = ORDERS[1 if incoming else 0]
    in_mesh = tuple(range(len(come)))
    left, right = [unpack(sides[:, n : n + 16, :].astype(F32)) for n in (0, 16)]
    if incoming:
        summed = [over_rows(a.astype(BF16), b.astype(BF16)) for a, b in zip(left, right)]
        summed = [reorder(v, in_mesh, go) for v in summed]
    else:
        left = [reorder(v, come, go) for v in left]
        right = [reorder(v, come, in_mesh) for v in right]
        summed = [over_columns(a.astype(BF16), b.astype(BF16)) for a, b in zip(left, right)]
    out[...] = pack(summed).astype(BF16)


def call(kernel, outs, scratch, *args, place=pltpu.VMEM, result=pltpu.VMEM):
    return pl.pallas_call(
        kernel,
        out_shape=[jax.ShapeDtypeStruct(*o) for o in outs],
        in_specs=[pl.BlockSpec(memory_space=place)] * len(args),
        out_specs=[pl.BlockSpec(memory_space=result)] * len(outs),
        scratch_shapes=scratch,
        compiler_params=pltpu.CompilerParams(vmem_limit_bytes=24 * 2**20),
    )(*args)


def exchange(blocks):
    return lax.all_to_all(blocks, PEERS, split_axis=0, concat_axis=0, tiled=True)


def exchange_in_order(blocks, chips):
    listed = [[2 * chip + core for chip in chips for core in range(2)]]
    return lax.all_to_all(blocks, "row", split_axis=0, concat_axis=0, axis_index_groups=listed, tiled=True)


def packed_updates(count, pair_rep, pair_mask, pw, pb, gw, gb, ow, ob, ns, no):
    rows_of, width, channels = pair_rep.shape
    flat = (channels, rows_of * width)
    projected = [((count, 32, width), BF16), (flat, F32), (flat, BF16)]
    summed = [((count, 16, width), BF16)]
    params = [pair_rep, pair_mask, pw, gw, pb, gb, ob, ns, no]
    params = [pltpu.with_memory_space_constraint(v, pltpu.HBM) for v in params]
    held = [pltpu.VMEM(v.shape[1:] if n in (2, 3) else v.shape, v.dtype) for n, v in enumerate(params)]
    held += [pltpu.VMEM((2 * EACH, channels), F32), pltpu.SemaphoreType.DMA((len(params),))]
    back = pltpu.VMEM((OWN * channels, width), F32)
    mixed = pltpu.VMEM((2, OWN * channels, width), F32)
    kept = [((channels, 2 * EACH), F32), ((2 * OWN, width), F32)]
    send, gate, turned, columns, keep = call(first_kernel, projected + kept, held + [mixed], *params, place=pltpu.HBM)
    (send,) = call(functools.partial(triangle_kernel, False), summed, [], exchange_in_order(send, ORDERS[0][0]))
    send, gate, turned = call(middle_kernel, projected, [mixed, back], exchange_in_order(send, ORDERS[0][1]), turned, gate, columns, keep, pw, gw, ow)
    (send,) = call(functools.partial(triangle_kernel, True), summed, [], exchange_in_order(send, ORDERS[1][0]))
    held = [pltpu.VMEM(pair_rep.shape, BF16), pltpu.SemaphoreType.DMA((rows_of // 2,)), back]
    send = exchange_in_order(send, ORDERS[1][1])
    (out,) = call(last_kernel, [(pair_rep.shape, BF16)], held, send, turned, gate, columns, ow, result=pltpu.HBM)
    return out


def update(pair_t, pair_mask, u, incoming, peers, rows_of, pw, pb, gw, gb, ow, ob, ns, no):
    channels, positions = pair_t.shape
    width = positions // rows_of
    h = pw.shape[2] // 4
    count = peers[0] * peers[1]
    own = h // count
    normed = layer_norm(pair_t, ns[u, 0][:, None], no[u, 0][:, None]).astype(BF16)
    projected = over_rows(jnp.concatenate([pw[u], gw[u]], 1), normed) + jnp.concatenate([pb[u], gb[u]], 0)[:, None]
    parts = [projected[n * h : (n + 1) * h] for n in range(4)]
    gating = jax.nn.sigmoid(projected[4 * h :])
    mask = pair_mask.astype(F32).reshape(1, positions)
    left = (mask * jax.nn.sigmoid(parts[1]) * parts[0]).astype(BF16)
    right = (mask * jax.nn.sigmoid(parts[3]) * parts[2]).astype(BF16)
    sides = exchange(jnp.stack([v.reshape(count, own, rows_of, width) for v in (left, right)], 1))
    sides = sides.reshape(peers[0], peers[1], 2, own, rows_of, width)
    sides = sides.transpose(2, 3, 0, 4, 1, 5).reshape(2, own, peers[0] * rows_of, peers[1] * width)
    form = "cki,ckj->cij" if incoming else "cik,cjk->cij"
    summed = jnp.einsum(form, sides[0], sides[1], preferred_element_type=F32).astype(BF16)
    summed = summed.reshape(own, peers[0], rows_of, peers[1], width).transpose(1, 3, 0, 2, 4)
    summed = exchange(summed.reshape(count, own, rows_of, width)).reshape(h, positions).astype(F32)
    hidden = layer_norm(summed, ns[u, 1][:, None], no[u, 1][:, None]).astype(BF16)
    change = over_rows(ow[u], hidden) + ob[u][:, None]
    return (pair_t + gating * change).astype(BF16)


def plain_updates(peers, pair_rep, pair_mask, *params):
    rows_of, width, channels = pair_rep.shape
    pair_t = pair_rep.reshape(rows_of * width, channels).T
    for u in range(2):
        pair_t = update(pair_t.astype(F32), pair_mask, u, u == 1, peers, rows_of, *params)
    return pair_t.T.reshape(rows_of, width, channels)


def solution(mesh):
    peers = (mesh.shape["row"], mesh.shape["ka"])
    count = peers[0] * peers[1]

    def on_device(pair_rep, pair_mask, *params):
        rows_of, width, channels = pair_rep.shape
        hidden = params[0].shape[2] // 4
        fits = peers[1] == 1 and rows_of == OWN and hidden == OWN * count and count == 2 * len(ORDERS[0][0])
        if fits and channels == hidden == 128 and width % 128 == 0:
            return packed_updates(count, pair_rep, pair_mask, *params)
        return plain_updates(peers, pair_rep, pair_mask, *params)

    split = P(("grp", "row"), "ka", None)
    in_specs = (split, P(("grp", "row"), "ka")) + (P(),) * 8
    return jax.shard_map(on_device, mesh=mesh, in_specs=in_specs, out_specs=split, check_vma=False)
```

```python
import functools

import jax
import jax.numpy as jnp
from jax import lax
from jax.experimental import pallas as pl
from jax.experimental.pallas import tpu as pltpu
from jax.sharding import PartitionSpec as P

PEERS = ("row", "ka")
OWN = 4
CHIPS = (0, 15, 11, 14, 13, 10, 9, 7, 12, 5, 8, 6, 4, 3, 2, 1)
EACH = 16
BF16, F32 = jnp.bfloat16, jnp.float32


def over_rows(a, b):
    return lax.dot_general(a, b, (((0,), (0,)), ((), ())), preferred_element_type=F32)


def over_columns(a, b):
    return lax.dot_general(a, b, (((1,), (1,)), ((), ())), preferred_element_type=F32)


def layer_norm(values, norm_gain, norm_bias):
    average = jnp.mean(values, 0, keepdims=True)
    centred = values - average
    variance = jnp.mean(centred * centred, 0, keepdims=True)
    return centred * lax.rsqrt(variance + 1e-05) * norm_gain + norm_bias


def pack(blocks):
    channels, width = blocks[0].shape
    tiles = [b.reshape(channels // 8, 8, width) for b in blocks]
    turned = [pltpu.roll(b, 4, axis=0).reshape(channels // 8, 8, width) for b in blocks]
    low = lax.broadcasted_iota(jnp.int32, tiles[0].shape, 1) < 4
    back = [pltpu.roll(b, channels - 4, axis=0).reshape(channels // 8, 8, width) for b in blocks]
    even = [jnp.where(low, tiles[n], turned[n + 1]) for n in (0, 2)]
    odd = [jnp.where(low, back[n], tiles[n + 1]) for n in (0, 2)]
    return jnp.stack([jnp.stack(even, 1), jnp.stack(odd, 1)], 1).reshape(channels // 4, 16, width)


def unpack(packed):
    count, _, width = packed.shape
    tiles = packed.reshape(count // 2, 2, 2, 8, width)
    low = lax.broadcasted_iota(jnp.int32, (count // 2, 8, width), 1) < 4
    blocks = []
    for n in range(2):
        even, odd = tiles[:, 0, n], tiles[:, 1, n]
        down = pltpu.roll(odd.reshape(count * 4, width), 4, axis=0).reshape(even.shape)
        up = pltpu.roll(even.reshape(count * 4, width), count * 4 - 4, axis=0).reshape(even.shape)
        blocks.append(jnp.where(low, even, down).reshape(count * 4, width))
        blocks.append(jnp.where(low, up, odd).reshape(count * 4, width))
    return blocks


def broadcast_columns(columns, first, many, width):
    held = columns[...]
    return [jnp.broadcast_to(held[:, n : n + 1], (held.shape[0], width)) for n in range(first, first + many)]


def both_columns(pair, width):
    return pl.ds(pl.multiple_of(pair * 2 * width, 2 * width), 2 * width)


def project(u, z, half_mask, proj_weight, gate_weight, columns, send, gate, mixed):
    width = z.shape[1] // OWN
    h = proj_weight.shape[1] // 4
    rows = mixed.shape[1]
    gain, offset, *biases = broadcast_columns(columns, u * EACH, 7, 2 * width)
    scales = (1.0, 0.5, 1.0, 0.5, 0.5)
    biases = [b * k for b, k in zip(biases, scales)]
    turned = [proj_weight[:, n * h : (n + 1) * h] for n in range(4)] + [gate_weight]
    turned = [(w * jnp.asarray(k, BF16)).T if k != 1.0 else w.T for w, k in zip(turned, scales)]

    @pl.loop(0, OWN // 2)
    def _(pair):
        at = both_columns(pair, width)
        normed = layer_norm(z[:, at].astype(F32), gain, offset).astype(BF16)
        half = half_mask[0:1, at]
        for side in range(2):
            value, gating = [
                jnp.dot(turned[m], normed, preferred_element_type=F32) + biases[m] for m in (2 * side, 2 * side + 1)
            ]
            value = (jnp.tanh(gating) * half + half) * value
            for n in range(2):
                mixed[side, pl.ds(2 * pair + n, h, stride=OWN), :] = value[:, n * width : (n + 1) * width]
        gate[:, at] = 0.5 * jnp.tanh(jnp.dot(turned[4], normed, preferred_element_type=F32) + biases[4]) + 0.5

    for side in range(2):
        send[:, side * 16 : (side + 1) * 16, :] = mixed[side].reshape(rows // 16, 16, width).astype(BF16)


def finish(u, z, summed, gate, out_weight, columns, mixed, use):
    width = z.shape[1] // OWN
    rows = mixed.shape[0]
    gain, offset, bias = broadcast_columns(columns, u * EACH + 7, 3, 2 * width)
    turned = out_weight.T
    mixed[...] = summed[...].astype(F32).reshape(mixed.shape)

    @pl.loop(0, OWN // 2)
    def _(pair):
        at = both_columns(pair, width)
        blocks = [mixed[pl.ds(2 * pair + n, rows // OWN, stride=OWN), :] for n in range(2)]
        hidden = layer_norm(jnp.concatenate(blocks, 1), gain, offset).astype(BF16)
        change = jnp.dot(turned, hidden, preferred_element_type=F32) + bias
        use(pair, (z[:, at].astype(F32) + gate[:, at] * change).astype(BF16))


def first_kernel(
    pair, mask, pw, gw, pb, gb, ob, ns, no, send, gate, turned, columns, keep, pair_in, mask_in, pw_in, gw_in, pb_in, gb_in, ob_in, ns_in, no_in, rows, arrived, mixed
):
    moves = [(pair, pair_in), (pb, pb_in), (gb, gb_in), (ob, ob_in), (ns, ns_in), (no, no_in)]
    moves += [(pw.at[0], pw_in), (gw.at[0], gw_in), (mask, mask_in)]
    moves = [pltpu.make_async_copy(a, b, arrived.at[n]) for n, (a, b) in enumerate(moves)]
    for move in moves:
        move.start()
    for move in moves:
        move.wait()
    width = pair.shape[1]
    for i in range(OWN):
        turned[:, i * width : (i + 1) * width] = pair_in[i].T
    h = pw.shape[2] // 4
    for u in range(2):
        found = [ns_in[u, 0:1, :], no_in[u, 0:1, :]] + [pb_in[u : u + 1, n * h : (n + 1) * h] for n in range(4)]
        found += [gb_in[u : u + 1, :], ns_in[u, 1:2, :], no_in[u, 1:2, :], ob_in[u : u + 1, :]]
        for n, row in enumerate(found):
            rows[u * EACH + n : u * EACH + n + 1, :] = row
    columns[...] = rows[...].T
    for i in range(OWN):
        keep[0:1, i * width : (i + 1) * width] = 0.5 * mask_in[i : i + 1, :].astype(F32)
    project(0, turned, keep, pw_in[...], gw_in[...], columns, send, gate, mixed)


def middle_kernel(summed, old, old_gate, columns, keep, pw, gw, ow, send, gate, turned, mixed, mixed_back):
    width = old.shape[1] // OWN

    def use(pair, result):
        turned[:, both_columns(pair, width)] = result

    finish(0, old, summed, old_gate, ow[0], columns, mixed_back, use)
    project(1, turned, keep, pw[1], gw[1], columns, send, gate, mixed)


def last_kernel(summed, old, old_gate, columns, ow, out, mixed_back):
    width = old.shape[1] // OWN

    def use(pair, result):
        for n in range(2):
            out[2 * pair + n] = result[:, n * width : (n + 1) * width].T

    finish(1, old, summed, old_gate, ow[1], columns, mixed_back, use)


def reorder(values, have, want):
    tiles = values.reshape(len(have), 2 * OWN, values.shape[1])
    places = [have.index(chip) for chip in want]
    return jnp.concatenate([tiles[n : n + 1] for n in places]).reshape(values.shape)


def triangle_kernel(incoming, sides, out):
    in_mesh = tuple(range(len(CHIPS)))
    left, right = [unpack(sides[:, n : n + 16, :].astype(F32)) for n in (0, 16)]
    if incoming:
        summed = [over_rows(a.astype(BF16), b.astype(BF16)) for a, b in zip(left, right)]
        summed = [reorder(v, in_mesh, CHIPS) for v in summed]
    else:
        right = [reorder(v, CHIPS, in_mesh) for v in right]
        summed = [over_columns(a.astype(BF16), b.astype(BF16)) for a, b in zip(left, right)]
    out[...] = pack(summed).astype(BF16)


def call(kernel, outs, scratch, *args, place=pltpu.VMEM):
    in_vmem = pl.BlockSpec(memory_space=pltpu.VMEM)
    return pl.pallas_call(
        kernel,
        out_shape=[jax.ShapeDtypeStruct(*o) for o in outs],
        in_specs=[pl.BlockSpec(memory_space=place)] * len(args),
        out_specs=[in_vmem] * len(outs),
        scratch_shapes=scratch,
        compiler_params=pltpu.CompilerParams(vmem_limit_bytes=24 * 2**20),
    )(*args)


def exchange(blocks):
    return lax.all_to_all(blocks, PEERS, split_axis=0, concat_axis=0, tiled=True)


def exchange_in_order(blocks):
    listed = [[2 * chip + core for chip in CHIPS for core in range(2)]]
    return lax.all_to_all(blocks, "row", split_axis=0, concat_axis=0, axis_index_groups=listed, tiled=True)


def packed_updates(count, pair_rep, pair_mask, pw, pb, gw, gb, ow, ob, ns, no):
    rows_of, width, channels = pair_rep.shape
    flat = (channels, rows_of * width)
    projected = [((count, 32, width), BF16), (flat, F32), (flat, BF16)]
    summed = [((count, 16, width), BF16)]
    params = [pair_rep, pair_mask, pw, gw, pb, gb, ob, ns, no]
    params = [pltpu.with_memory_space_constraint(v, pltpu.HBM) for v in params]
    held = [pltpu.VMEM(v.shape[1:] if n in (2, 3) else v.shape, v.dtype) for n, v in enumerate(params)]
    held += [pltpu.VMEM((2 * EACH, channels), F32), pltpu.SemaphoreType.DMA((len(params),))]
    back = pltpu.VMEM((OWN * channels, width), F32)
    mixed = pltpu.VMEM((2, OWN * channels, width), F32)
    kept = [((channels, 2 * EACH), F32), ((8, rows_of * width), F32)]
    send, gate, turned, columns, keep = call(first_kernel, projected + kept, held + [mixed], *params, place=pltpu.HBM)
    (send,) = call(functools.partial(triangle_kernel, False), summed, [], exchange_in_order(send))
    send, gate, turned = call(middle_kernel, projected, [mixed, back], exchange_in_order(send), turned, gate, columns, keep, pw, gw, ow)
    (send,) = call(functools.partial(triangle_kernel, True), summed, [], exchange_in_order(send))
    (out,) = call(last_kernel, [(pair_rep.shape, BF16)], [back], exchange_in_order(send), turned, gate, columns, ow)
    return out


def update(pair_t, pair_mask, u, incoming, peers, rows_of, pw, pb, gw, gb, ow, ob, ns, no):
    channels, positions = pair_t.shape
    width = positions // rows_of
    h = pw.shape[2] // 4
    count = peers[0] * peers[1]
    own = h // count
    normed = layer_norm(pair_t, ns[u, 0][:, None], no[u, 0][:, None]).astype(BF16)
    projected = over_rows(jnp.concatenate([pw[u], gw[u]], 1), normed) + jnp.concatenate([pb[u], gb[u]], 0)[:, None]
    parts = [projected[n * h : (n + 1) * h] for n in range(4)]
    gating = jax.nn.sigmoid(projected[4 * h :])
    mask = pair_mask.astype(F32).reshape(1, positions)
    left = (mask * jax.nn.sigmoid(parts[1]) * parts[0]).astype(BF16)
    right = (mask * jax.nn.sigmoid(parts[3]) * parts[2]).astype(BF16)
    sides = exchange(jnp.stack([v.reshape(count, own, rows_of, width) for v in (left, right)], 1))
    sides = sides.reshape(peers[0], peers[1], 2, own, rows_of, width)
    sides = sides.transpose(2, 3, 0, 4, 1, 5).reshape(2, own, peers[0] * rows_of, peers[1] * width)
    form = "cki,ckj->cij" if incoming else "cik,cjk->cij"
    summed = jnp.einsum(form, sides[0], sides[1], preferred_element_type=F32).astype(BF16)
    summed = summed.reshape(own, peers[0], rows_of, peers[1], width).transpose(1, 3, 0, 2, 4)
    summed = exchange(summed.reshape(count, own, rows_of, width)).reshape(h, positions).astype(F32)
    hidden = layer_norm(summed, ns[u, 1][:, None], no[u, 1][:, None]).astype(BF16)
    change = over_rows(ow[u], hidden) + ob[u][:, None]
    return (pair_t + gating * change).astype(BF16)


def plain_updates(peers, pair_rep, pair_mask, *params):
    rows_of, width, channels = pair_rep.shape
    pair_t = pair_rep.reshape(rows_of * width, channels).T
    for u in range(2):
        pair_t = update(pair_t.astype(F32), pair_mask, u, u == 1, peers, rows_of, *params)
    return pair_t.T.reshape(rows_of, width, channels)


def solution(mesh):
    peers = (mesh.shape["row"], mesh.shape["ka"])
    count = peers[0] * peers[1]

    def on_device(pair_rep, pair_mask, *params):
        rows_of, width, channels = pair_rep.shape
        hidden = params[0].shape[2] // 4
        fits = peers[1] == 1 and rows_of == OWN and hidden == OWN * count and count == 2 * len(CHIPS)
        if fits and channels == hidden == 128 and width % 128 == 0:
            return packed_updates(count, pair_rep, pair_mask, *params)
        return plain_updates(peers, pair_rep, pair_mask, *params)

    split = P(("grp", "row"), "ka", None)
    in_specs = (split, P(("grp", "row"), "ka")) + (P(),) * 8
    return jax.shard_map(on_device, mesh=mesh, in_specs=in_specs, out_specs=split, check_vma=False)
```

```python
import functools

import jax
import jax.numpy as jnp
from jax import lax
from jax.experimental import pallas as pl
from jax.experimental.pallas import tpu as pltpu
from jax.sharding import PartitionSpec as P

PEERS = ("row", "ka")
OWN = 4
ORDERS = (
    ((0, 15, 11, 14, 13, 10, 9, 7, 12, 5, 8, 6, 4, 3, 2, 1), (0, 15, 11, 14, 13, 10, 9, 7, 12, 5, 8, 6, 4, 3, 2, 1)),
    ((0, 15, 11, 14, 13, 10, 9, 7, 12, 5, 8, 6, 4, 3, 2, 1), (0, 15, 11, 14, 13, 10, 9, 7, 12, 5, 8, 6, 4, 3, 2, 1)),
)
EACH = 16
BF16, F32 = jnp.bfloat16, jnp.float32


def over_rows(a, b):
    return lax.dot_general(a, b, (((0,), (0,)), ((), ())), preferred_element_type=F32)


def over_columns(a, b):
    return lax.dot_general(a, b, (((1,), (1,)), ((), ())), preferred_element_type=F32)


def layer_norm(values, norm_gain, norm_bias):
    average = jnp.mean(values, 0, keepdims=True)
    centred = values - average
    variance = jnp.mean(centred * centred, 0, keepdims=True)
    return centred * lax.rsqrt(variance + 1e-05) * norm_gain + norm_bias


def short_norm(values, norm_gain, norm_bias):
    distance = values - values[0:1, :]
    average = jnp.mean(distance, 0, keepdims=True)
    variance = jnp.mean(distance * distance, 0, keepdims=True) - average * average
    return (distance - average) * lax.rsqrt(variance + 1e-05) * norm_gain + norm_bias


def pack(blocks):
    channels, width = blocks[0].shape
    tiles = [b.reshape(channels // 8, 8, width) for b in blocks]
    turned = [pltpu.roll(b, 4, axis=0).reshape(channels // 8, 8, width) for b in blocks]
    low = lax.broadcasted_iota(jnp.int32, tiles[0].shape, 1) < 4
    back = [pltpu.roll(b, channels - 4, axis=0).reshape(channels // 8, 8, width) for b in blocks]
    even = [jnp.where(low, tiles[n], turned[n + 1]) for n in (0, 2)]
    odd = [jnp.where(low, back[n], tiles[n + 1]) for n in (0, 2)]
    return jnp.stack([jnp.stack(even, 1), jnp.stack(odd, 1)], 1).reshape(channels // 4, 16, width)


def unpack(packed):
    count, _, width = packed.shape
    tiles = packed.reshape(count // 2, 2, 2, 8, width)
    low = lax.broadcasted_iota(jnp.int32, (count // 2, 8, width), 1) < 4
    blocks = []
    for n in range(2):
        even, odd = tiles[:, 0, n], tiles[:, 1, n]
        down = pltpu.roll(odd.reshape(count * 4, width), 4, axis=0).reshape(even.shape)
        up = pltpu.roll(even.reshape(count * 4, width), count * 4 - 4, axis=0).reshape(even.shape)
        blocks.append(jnp.where(low, even, down).reshape(count * 4, width))
        blocks.append(jnp.where(low, up, odd).reshape(count * 4, width))
    return blocks


def broadcast_columns(columns, first, many, width):
    held = columns[...]
    return [jnp.broadcast_to(held[:, n : n + 1], (held.shape[0], width)) for n in range(first, first + many)]


def project(u, z, mask, proj_weight, gate_weight, columns, send, gate, mixed):
    width = z[0].shape[1]
    h = proj_weight.shape[1] // 4
    rows = mixed.shape[1]
    gain, offset, *biases = broadcast_columns(columns, u * EACH, 7, width)
    scales = (1.0, 0.5, 1.0, 0.5, 0.5)
    biases = [b * k for b, k in zip(biases, scales)]
    turned = [proj_weight[:, n * h : (n + 1) * h] for n in range(4)] + [gate_weight]
    turned = [(w * jnp.asarray(k, BF16)).T if k != 1.0 else w.T for w, k in zip(turned, scales)]
    pairs = []
    for pair in range(0, OWN, 2):
        normed = [short_norm(z[i], gain, offset).astype(BF16) for i in (pair, pair + 1)]
        pairs.append(jnp.concatenate(normed, 1))
    for side in range(2):
        for pair, normed in enumerate(pairs):
            value, gating = [jnp.dot(turned[2 * side + n], normed, preferred_element_type=F32) for n in range(2)]
            for n in range(2):
                i, at = 2 * pair + n, slice(n * width, (n + 1) * width)
                half = mask[i : i + 1, :] * 0.5
                weight = jnp.tanh(gating[:, at] + biases[2 * side + 1]) * half + half
                mixed[side, pl.ds(i, h, stride=OWN), :] = weight * (value[:, at] + biases[2 * side])
    for side in range(2):
        send[:, side * 16 : (side + 1) * 16, :] = mixed[side].reshape(rows // 16, 16, width).astype(BF16)
    for pair, normed in enumerate(pairs):
        gating = jnp.dot(turned[4], normed, preferred_element_type=F32)
        for n in range(2):
            i = 2 * pair + n
            gate[:, i * width : (i + 1) * width] = 0.5 * jnp.tanh(gating[:, n * width : (n + 1) * width] + biases[4]) + 0.5


def finish(u, z, summed, gate, out_weight, columns, mixed):
    width = z[0].shape[1]
    gain, offset, bias = broadcast_columns(columns, u * EACH + 7, 3, width)
    turned = out_weight.T
    mixed[...] = summed[...].astype(F32).reshape(mixed.shape)
    results = []
    for pair in range(0, OWN, 2):
        blocks = [mixed[pl.ds(i, mixed.shape[0] // OWN, stride=OWN), :] for i in (pair, pair + 1)]
        blocks = [reorder(v, ORDERS[u][1], ORDERS[u][0]) for v in blocks]
        hidden = jnp.concatenate([short_norm(v, gain, offset).astype(BF16) for v in blocks], 1)
        both = jnp.dot(turned, hidden, preferred_element_type=F32)
        for n in range(2):
            change = both[:, n * width : (n + 1) * width] + bias
            at = slice((pair + n) * width, (pair + n + 1) * width)
            results.append((z[pair + n].astype(F32) + gate[:, at] * change).astype(BF16))
    return results


def first_kernel(
    pair, mask, pw, gw, pb, gb, ob, ns, no, send, gate, turned, columns, keep, pair_in, mask_in, pw_in, gw_in, pb_in, gb_in, ob_in, ns_in, no_in, rows, arrived, mixed
):
    moves = [(pair, pair_in), (pb, pb_in), (gb, gb_in), (ob, ob_in), (ns, ns_in), (no, no_in)]
    moves += [(pw.at[0], pw_in), (gw.at[0], gw_in), (mask, mask_in)]
    moves = [pltpu.make_async_copy(a, b, arrived.at[n]) for n, (a, b) in enumerate(moves)]
    for move in moves:
        move.start()
    for move in moves:
        move.wait()
    width = pair.shape[1]
    z = [pair_in[i].T for i in range(OWN)]
    for i in range(OWN):
        turned[:, i * width : (i + 1) * width] = z[i]
    h = pw.shape[2] // 4
    for u in range(2):
        found = [ns_in[u, 0:1, :], no_in[u, 0:1, :]] + [pb_in[u : u + 1, n * h : (n + 1) * h] for n in range(4)]
        found += [gb_in[u : u + 1, :], ns_in[u, 1:2, :], no_in[u, 1:2, :], ob_in[u : u + 1, :]]
        for n, row in enumerate(found):
            rows[u * EACH + n : u * EACH + n + 1, :] = row
    columns[...] = rows[...].T
    keep[0:OWN, :] = mask_in[...].astype(F32)
    project(0, [v.astype(F32) for v in z], keep, pw_in[...], gw_in[...], columns, send, gate, mixed)


def middle_kernel(summed, old, old_gate, columns, keep, pw, gw, ow, send, gate, turned, mixed, mixed_back):
    width = keep.shape[1]
    z = finish(0, [old[:, i * width : (i + 1) * width] for i in range(OWN)], summed, old_gate, ow[0], columns, mixed_back)
    for i in range(OWN):
        turned[:, i * width : (i + 1) * width] = z[i]
    project(1, [v.astype(F32) for v in z], keep, pw[1], gw[1], columns, send, gate, mixed)


def last_kernel(summed, old, old_gate, columns, ow, out, mixed_back):
    width = out.shape[1]
    z = finish(1, [old[:, i * width : (i + 1) * width] for i in range(OWN)], summed, old_gate, ow[1], columns, mixed_back)
    for i in range(OWN):
        out[i] = z[i].T


def reorder(values, have, want):
    tiles = values.reshape(len(have), 2 * OWN, values.shape[1])
    places = [have.index(chip) for chip in want]
    return jnp.concatenate([tiles[n : n + 1] for n in places]).reshape(values.shape)


def triangle_kernel(incoming, sides, out):
    come, go = ORDERS[1 if incoming else 0]
    in_mesh = tuple(range(len(come)))
    left, right = [unpack(sides[:, n : n + 16, :].astype(F32)) for n in (0, 16)]
    if incoming:
        summed = [over_rows(a.astype(BF16), b.astype(BF16)) for a, b in zip(left, right)]
        summed = [reorder(v, in_mesh, go) for v in summed]
    else:
        left = [reorder(v, come, go) for v in left]
        right = [reorder(v, come, in_mesh) for v in right]
        summed = [over_columns(a.astype(BF16), b.astype(BF16)) for a, b in zip(left, right)]
    out[...] = pack(summed).astype(BF16)


def call(kernel, outs, scratch, *args, place=pltpu.VMEM):
    in_vmem = pl.BlockSpec(memory_space=pltpu.VMEM)
    return pl.pallas_call(
        kernel,
        out_shape=[jax.ShapeDtypeStruct(*o) for o in outs],
        in_specs=[pl.BlockSpec(memory_space=place)] * len(args),
        out_specs=[in_vmem] * len(outs),
        scratch_shapes=scratch,
        compiler_params=pltpu.CompilerParams(vmem_limit_bytes=24 * 2**20),
    )(*args)


def exchange(blocks):
    return lax.all_to_all(blocks, PEERS, split_axis=0, concat_axis=0, tiled=True)


def exchange_in_order(blocks, chips):
    listed = [[2 * chip + core for chip in chips for core in range(2)]]
    return lax.all_to_all(blocks, "row", split_axis=0, concat_axis=0, axis_index_groups=listed, tiled=True)


def packed_updates(count, pair_rep, pair_mask, pw, pb, gw, gb, ow, ob, ns, no):
    rows_of, width, channels = pair_rep.shape
    flat = (channels, rows_of * width)
    projected = [((count, 32, width), BF16), (flat, F32), (flat, BF16)]
    summed = [((count, 16, width), BF16)]
    params = [pair_rep, pair_mask, pw, gw, pb, gb, ob, ns, no]
    params = [pltpu.with_memory_space_constraint(v, pltpu.HBM) for v in params]
    held = [pltpu.VMEM(v.shape[1:] if n in (2, 3) else v.shape, v.dtype) for n, v in enumerate(params)]
    held += [pltpu.VMEM((2 * EACH, channels), F32), pltpu.SemaphoreType.DMA((len(params),))]
    back = pltpu.VMEM((OWN * channels, width), F32)
    mixed = pltpu.VMEM((2, OWN * channels, width), F32)
    kept = [((channels, 2 * EACH), F32), ((2 * OWN, width), F32)]
    send, gate, turned, columns, keep = call(first_kernel, projected + kept, held + [mixed], *params, place=pltpu.HBM)
    (send,) = call(functools.partial(triangle_kernel, False), summed, [], exchange_in_order(send, ORDERS[0][0]))
    send, gate, turned = call(middle_kernel, projected, [mixed, back], exchange_in_order(send, ORDERS[0][1]), turned, gate, columns, keep, pw, gw, ow)
    (send,) = call(functools.partial(triangle_kernel, True), summed, [], exchange_in_order(send, ORDERS[1][0]))
    (out,) = call(last_kernel, [(pair_rep.shape, BF16)], [back], exchange_in_order(send, ORDERS[1][1]), turned, gate, columns, ow)
    return out


def update(pair_t, pair_mask, u, incoming, peers, rows_of, pw, pb, gw, gb, ow, ob, ns, no):
    channels, positions = pair_t.shape
    width = positions // rows_of
    h = pw.shape[2] // 4
    count = peers[0] * peers[1]
    own = h // count
    normed = layer_norm(pair_t, ns[u, 0][:, None], no[u, 0][:, None]).astype(BF16)
    projected = over_rows(jnp.concatenate([pw[u], gw[u]], 1), normed) + jnp.concatenate([pb[u], gb[u]], 0)[:, None]
    parts = [projected[n * h : (n + 1) * h] for n in range(4)]
    gating = jax.nn.sigmoid(projected[4 * h :])
    mask = pair_mask.astype(F32).reshape(1, positions)
    left = (mask * jax.nn.sigmoid(parts[1]) * parts[0]).astype(BF16)
    right = (mask * jax.nn.sigmoid(parts[3]) * parts[2]).astype(BF16)
    sides = exchange(jnp.stack([v.reshape(count, own, rows_of, width) for v in (left, right)], 1))
    sides = sides.reshape(peers[0], peers[1], 2, own, rows_of, width)
    sides = sides.transpose(2, 3, 0, 4, 1, 5).reshape(2, own, peers[0] * rows_of, peers[1] * width)
    form = "cki,ckj->cij" if incoming else "cik,cjk->cij"
    summed = jnp.einsum(form, sides[0], sides[1], preferred_element_type=F32).astype(BF16)
    summed = summed.reshape(own, peers[0], rows_of, peers[1], width).transpose(1, 3, 0, 2, 4)
    summed = exchange(summed.reshape(count, own, rows_of, width)).reshape(h, positions).astype(F32)
    hidden = layer_norm(summed, ns[u, 1][:, None], no[u, 1][:, None]).astype(BF16)
    change = over_rows(ow[u], hidden) + ob[u][:, None]
    return (pair_t + gating * change).astype(BF16)


def plain_updates(peers, pair_rep, pair_mask, *params):
    rows_of, width, channels = pair_rep.shape
    pair_t = pair_rep.reshape(rows_of * width, channels).T
    for u in range(2):
        pair_t = update(pair_t.astype(F32), pair_mask, u, u == 1, peers, rows_of, *params)
    return pair_t.T.reshape(rows_of, width, channels)


def solution(mesh):
    peers = (mesh.shape["row"], mesh.shape["ka"])
    count = peers[0] * peers[1]

    def on_device(pair_rep, pair_mask, *params):
        rows_of, width, channels = pair_rep.shape
        hidden = params[0].shape[2] // 4
        fits = peers[1] == 1 and rows_of == OWN and hidden == OWN * count and count == 2 * len(ORDERS[0][0])
        if fits and channels == hidden == 128 and width % 128 == 0:
            return packed_updates(count, pair_rep, pair_mask, *params)
        return plain_updates(peers, pair_rep, pair_mask, *params)

    split = P(("grp", "row"), "ka", None)
    in_specs = (split, P(("grp", "row"), "ka")) + (P(),) * 8
    return jax.shard_map(on_device, mesh=mesh, in_specs=in_specs, out_specs=split, check_vma=False)
```

```python
import functools

import jax
import jax.numpy as jnp
from jax import lax
from jax.experimental import pallas as pl
from jax.experimental.pallas import tpu as pltpu
from jax.sharding import PartitionSpec as P

PEERS = ("row", "ka")
OWN = 4
CHIPS = (0, 15, 11, 14, 13, 10, 9, 7, 12, 5, 8, 6, 4, 3, 2, 1)
EACH = 16
BF16, F32 = jnp.bfloat16, jnp.float32


def over_rows(a, b):
    return lax.dot_general(a, b, (((0,), (0,)), ((), ())), preferred_element_type=F32)


def over_columns(a, b):
    return lax.dot_general(a, b, (((1,), (1,)), ((), ())), preferred_element_type=F32)


def layer_norm(values, norm_gain, norm_bias):
    average = jnp.mean(values, 0, keepdims=True)
    centred = values - average
    variance = jnp.mean(centred * centred, 0, keepdims=True)
    return centred * lax.rsqrt(variance + 1e-05) * norm_gain + norm_bias


def pack(blocks):
    channels, width = blocks[0].shape
    tiles = [b.reshape(channels // 8, 8, width) for b in blocks]
    turned = [pltpu.roll(b, 4, axis=0).reshape(channels // 8, 8, width) for b in blocks]
    low = lax.broadcasted_iota(jnp.int32, tiles[0].shape, 1) < 4
    back = [pltpu.roll(b, channels - 4, axis=0).reshape(channels // 8, 8, width) for b in blocks]
    even = [jnp.where(low, tiles[n], turned[n + 1]) for n in (0, 2)]
    odd = [jnp.where(low, back[n], tiles[n + 1]) for n in (0, 2)]
    return jnp.stack([jnp.stack(even, 1), jnp.stack(odd, 1)], 1).reshape(channels // 4, 16, width)


def unpack(packed):
    count, _, width = packed.shape
    tiles = packed.reshape(count // 2, 2, 2, 8, width)
    low = lax.broadcasted_iota(jnp.int32, (count // 2, 8, width), 1) < 4
    blocks = []
    for n in range(2):
        even, odd = tiles[:, 0, n], tiles[:, 1, n]
        down = pltpu.roll(odd.reshape(count * 4, width), 4, axis=0).reshape(even.shape)
        up = pltpu.roll(even.reshape(count * 4, width), count * 4 - 4, axis=0).reshape(even.shape)
        blocks.append(jnp.where(low, even, down).reshape(count * 4, width))
        blocks.append(jnp.where(low, up, odd).reshape(count * 4, width))
    return blocks


def broadcast_columns(columns, first, many, width):
    held = columns[...]
    return [jnp.broadcast_to(held[:, n : n + 1], (held.shape[0], width)) for n in range(first, first + many)]


def project(u, z, half_mask, proj_weight, gate_weight, columns, send, gate, mixed):
    width = z.shape[1] // OWN
    h = proj_weight.shape[1] // 4
    rows = mixed.shape[1]
    gain, offset, *biases = broadcast_columns(columns, u * EACH, 7, z.shape[1])
    scales = (1.0, 0.5, 1.0, 0.5, 0.5)
    biases = [b * k for b, k in zip(biases, scales)]
    turned = [proj_weight[:, n * h : (n + 1) * h] for n in range(4)] + [gate_weight]
    turned = [(w * jnp.asarray(k, BF16)).T if k != 1.0 else w.T for w, k in zip(turned, scales)]
    normed = layer_norm(z.astype(F32), gain, offset).astype(BF16)
    half = half_mask[0:1, :]
    for side in range(2):
        value, gating = [jnp.dot(turned[m], normed, preferred_element_type=F32) + biases[m] for m in (2 * side, 2 * side + 1)]
        value = (jnp.tanh(gating) * half + half) * value
        for i in range(OWN):
            mixed[side, pl.ds(i, h, stride=OWN), :] = value[:, i * width : (i + 1) * width]
        send[:, side * 16 : (side + 1) * 16, :] = mixed[side].reshape(rows // 16, 16, width).astype(BF16)
    gate[...] = 0.5 * jnp.tanh(jnp.dot(turned[4], normed, preferred_element_type=F32) + biases[4]) + 0.5


def finish(u, z, summed, gate, out_weight, columns, mixed):
    rows = mixed.shape[0]
    gain, offset, bias = broadcast_columns(columns, u * EACH + 7, 3, z.shape[1])
    mixed[...] = summed[...].astype(F32).reshape(mixed.shape)
    blocks = [mixed[pl.ds(i, rows // OWN, stride=OWN), :] for i in range(OWN)]
    hidden = layer_norm(jnp.concatenate(blocks, 1), gain, offset).astype(BF16)
    change = jnp.dot(out_weight.T, hidden, preferred_element_type=F32) + bias
    return (z[...].astype(F32) + gate[...] * change).astype(BF16)


def first_kernel(
    pair, mask, pw, gw, pb, gb, ob, ns, no, send, gate, turned, columns, keep, pair_in, mask_in, pw_in, gw_in, pb_in, gb_in, ob_in, ns_in, no_in, rows, arrived, mixed
):
    moves = [(pair, pair_in), (pb, pb_in), (gb, gb_in), (ob, ob_in), (ns, ns_in), (no, no_in)]
    moves += [(pw.at[0], pw_in), (gw.at[0], gw_in), (mask, mask_in)]
    moves = [pltpu.make_async_copy(a, b, arrived.at[n]) for n, (a, b) in enumerate(moves)]
    for move in moves:
        move.start()
    for move in moves:
        move.wait()
    width = pair.shape[1]
    for i in range(OWN):
        turned[:, i * width : (i + 1) * width] = pair_in[i].T
    h = pw.shape[2] // 4
    for u in range(2):
        found = [ns_in[u, 0:1, :], no_in[u, 0:1, :]] + [pb_in[u : u + 1, n * h : (n + 1) * h] for n in range(4)]
        found += [gb_in[u : u + 1, :], ns_in[u, 1:2, :], no_in[u, 1:2, :], ob_in[u : u + 1, :]]
        for n, row in enumerate(found):
            rows[u * EACH + n : u * EACH + n + 1, :] = row
    columns[...] = rows[...].T
    for i in range(OWN):
        keep[0:1, i * width : (i + 1) * width] = 0.5 * mask_in[i : i + 1, :].astype(F32)
    project(0, turned[...], keep, pw_in[...], gw_in[...], columns, send, gate, mixed)


def middle_kernel(summed, old, old_gate, columns, keep, pw, gw, ow, send, gate, turned, mixed, mixed_back):
    z = finish(0, old, summed, old_gate, ow[0], columns, mixed_back)
    turned[...] = z
    project(1, z, keep, pw[1], gw[1], columns, send, gate, mixed)


def last_kernel(summed, old, old_gate, columns, ow, out, mixed_back):
    width = out.shape[1]
    z = finish(1, old, summed, old_gate, ow[1], columns, mixed_back)
    for i in range(OWN):
        out[i] = z[:, i * width : (i + 1) * width].T


def reorder(values, have, want):
    tiles = values.reshape(len(have), 2 * OWN, values.shape[1])
    places = [have.index(chip) for chip in want]
    return jnp.concatenate([tiles[n : n + 1] for n in places]).reshape(values.shape)


def triangle_kernel(incoming, sides, out):
    in_mesh = tuple(range(len(CHIPS)))
    left, right = [unpack(sides[:, n : n + 16, :].astype(F32)) for n in (0, 16)]
    if incoming:
        summed = [over_rows(a.astype(BF16), b.astype(BF16)) for a, b in zip(left, right)]
        summed = [reorder(v, in_mesh, CHIPS) for v in summed]
    else:
        right = [reorder(v, CHIPS, in_mesh) for v in right]
        summed = [over_columns(a.astype(BF16), b.astype(BF16)) for a, b in zip(left, right)]
    out[...] = pack(summed).astype(BF16)


def call(kernel, outs, scratch, *args, place=pltpu.VMEM):
    in_vmem = pl.BlockSpec(memory_space=pltpu.VMEM)
    return pl.pallas_call(
        kernel,
        out_shape=[jax.ShapeDtypeStruct(*o) for o in outs],
        in_specs=[pl.BlockSpec(memory_space=place)] * len(args),
        out_specs=[in_vmem] * len(outs),
        scratch_shapes=scratch,
        compiler_params=pltpu.CompilerParams(vmem_limit_bytes=24 * 2**20),
    )(*args)


def exchange(blocks):
    return lax.all_to_all(blocks, PEERS, split_axis=0, concat_axis=0, tiled=True)


def exchange_in_order(blocks):
    listed = [[2 * chip + core for chip in CHIPS for core in range(2)]]
    return lax.all_to_all(blocks, "row", split_axis=0, concat_axis=0, axis_index_groups=listed, tiled=True)


def packed_updates(count, pair_rep, pair_mask, pw, pb, gw, gb, ow, ob, ns, no):
    rows_of, width, channels = pair_rep.shape
    flat = (channels, rows_of * width)
    projected = [((count, 32, width), BF16), (flat, F32), (flat, BF16)]
    summed = [((count, 16, width), BF16)]
    params = [pair_rep, pair_mask, pw, gw, pb, gb, ob, ns, no]
    params = [pltpu.with_memory_space_constraint(v, pltpu.HBM) for v in params]
    held = [pltpu.VMEM(v.shape[1:] if n in (2, 3) else v.shape, v.dtype) for n, v in enumerate(params)]
    held += [pltpu.VMEM((2 * EACH, channels), F32), pltpu.SemaphoreType.DMA((len(params),))]
    back = pltpu.VMEM((OWN * channels, width), F32)
    mixed = pltpu.VMEM((2, OWN * channels, width), F32)
    kept = [((channels, 2 * EACH), F32), ((8, rows_of * width), F32)]
    send, gate, turned, columns, keep = call(first_kernel, projected + kept, held + [mixed], *params, place=pltpu.HBM)
    (send,) = call(functools.partial(triangle_kernel, False), summed, [], exchange_in_order(send))
    send, gate, turned = call(middle_kernel, projected, [mixed, back], exchange_in_order(send), turned, gate, columns, keep, pw, gw, ow)
    (send,) = call(functools.partial(triangle_kernel, True), summed, [], exchange_in_order(send))
    (out,) = call(last_kernel, [(pair_rep.shape, BF16)], [back], exchange_in_order(send), turned, gate, columns, ow)
    return out


def update(pair_t, pair_mask, u, incoming, peers, rows_of, pw, pb, gw, gb, ow, ob, ns, no):
    channels, positions = pair_t.shape
    width = positions // rows_of
    h = pw.shape[2] // 4
    count = peers[0] * peers[1]
    own = h // count
    normed = layer_norm(pair_t, ns[u, 0][:, None], no[u, 0][:, None]).astype(BF16)
    projected = over_rows(jnp.concatenate([pw[u], gw[u]], 1), normed) + jnp.concatenate([pb[u], gb[u]], 0)[:, None]
    parts = [projected[n * h : (n + 1) * h] for n in range(4)]
    gating = jax.nn.sigmoid(projected[4 * h :])
    mask = pair_mask.astype(F32).reshape(1, positions)
    left = (mask * jax.nn.sigmoid(parts[1]) * parts[0]).astype(BF16)
    right = (mask * jax.nn.sigmoid(parts[3]) * parts[2]).astype(BF16)
    sides = exchange(jnp.stack([v.reshape(count, own, rows_of, width) for v in (left, right)], 1))
    sides = sides.reshape(peers[0], peers[1], 2, own, rows_of, width)
    sides = sides.transpose(2, 3, 0, 4, 1, 5).reshape(2, own, peers[0] * rows_of, peers[1] * width)
    form = "cki,ckj->cij" if incoming else "cik,cjk->cij"
    summed = jnp.einsum(form, sides[0], sides[1], preferred_element_type=F32).astype(BF16)
    summed = summed.reshape(own, peers[0], rows_of, peers[1], width).transpose(1, 3, 0, 2, 4)
    summed = exchange(summed.reshape(count, own, rows_of, width)).reshape(h, positions).astype(F32)
    hidden = layer_norm(summed, ns[u, 1][:, None], no[u, 1][:, None]).astype(BF16)
    change = over_rows(ow[u], hidden) + ob[u][:, None]
    return (pair_t + gating * change).astype(BF16)


def plain_updates(peers, pair_rep, pair_mask, *params):
    rows_of, width, channels = pair_rep.shape
    pair_t = pair_rep.reshape(rows_of * width, channels).T
    for u in range(2):
        pair_t = update(pair_t.astype(F32), pair_mask, u, u == 1, peers, rows_of, *params)
    return pair_t.T.reshape(rows_of, width, channels)


def solution(mesh):
    peers = (mesh.shape["row"], mesh.shape["ka"])
    count = peers[0] * peers[1]

    def on_device(pair_rep, pair_mask, *params):
        rows_of, width, channels = pair_rep.shape
        hidden = params[0].shape[2] // 4
        fits = peers[1] == 1 and rows_of == OWN and hidden == OWN * count and count == 2 * len(CHIPS)
        if fits and channels == hidden == 128 and width % 128 == 0:
            return packed_updates(count, pair_rep, pair_mask, *params)
        return plain_updates(peers, pair_rep, pair_mask, *params)

    split = P(("grp", "row"), "ka", None)
    in_specs = (split, P(("grp", "row"), "ka")) + (P(),) * 8
    return jax.shard_map(on_device, mesh=mesh, in_specs=in_specs, out_specs=split, check_vma=False)
```

```python
import functools

import jax
import jax.numpy as jnp
from jax import lax
from jax.experimental import pallas as pl
from jax.experimental.pallas import tpu as pltpu
from jax.sharding import PartitionSpec as P

PEERS = ("row", "ka")
OWN = 4
ORDERS = (
    ((0, 15, 11, 14, 13, 10, 9, 7, 12, 5, 8, 6, 4, 3, 2, 1), (0, 15, 11, 14, 13, 10, 9, 7, 12, 5, 8, 6, 4, 3, 2, 1)),
    ((0, 15, 11, 14, 13, 10, 9, 7, 12, 5, 8, 6, 4, 3, 2, 1), (0, 15, 11, 14, 13, 10, 9, 7, 12, 5, 8, 6, 4, 3, 2, 1)),
)
EACH = 16
BF16, F32 = jnp.bfloat16, jnp.float32


def over_rows(a, b):
    return lax.dot_general(a, b, (((0,), (0,)), ((), ())), preferred_element_type=F32)


def over_columns(a, b):
    return lax.dot_general(a, b, (((1,), (1,)), ((), ())), preferred_element_type=F32)


def layer_norm(values, norm_gain, norm_bias):
    average = jnp.mean(values, 0, keepdims=True)
    centred = values - average
    variance = jnp.mean(centred * centred, 0, keepdims=True)
    return centred * lax.rsqrt(variance + 1e-05) * norm_gain + norm_bias


def pack(blocks):
    channels, width = blocks[0].shape
    tiles = [b.reshape(channels // 8, 8, width) for b in blocks]
    turned = [pltpu.roll(b, 4, axis=0).reshape(channels // 8, 8, width) for b in blocks]
    low = lax.broadcasted_iota(jnp.int32, tiles[0].shape, 1) < 4
    back = [pltpu.roll(b, channels - 4, axis=0).reshape(channels // 8, 8, width) for b in blocks]
    even = [jnp.where(low, tiles[n], turned[n + 1]) for n in (0, 2)]
    odd = [jnp.where(low, back[n], tiles[n + 1]) for n in (0, 2)]
    return jnp.stack([jnp.stack(even, 1), jnp.stack(odd, 1)], 1).reshape(channels // 4, 16, width)


def unpack(packed):
    count, _, width = packed.shape
    tiles = packed.reshape(count // 2, 2, 2, 8, width)
    low = lax.broadcasted_iota(jnp.int32, (count // 2, 8, width), 1) < 4
    blocks = []
    for n in range(2):
        even, odd = tiles[:, 0, n], tiles[:, 1, n]
        down = pltpu.roll(odd.reshape(count * 4, width), 4, axis=0).reshape(even.shape)
        up = pltpu.roll(even.reshape(count * 4, width), count * 4 - 4, axis=0).reshape(even.shape)
        blocks.append(jnp.where(low, even, down).reshape(count * 4, width))
        blocks.append(jnp.where(low, up, odd).reshape(count * 4, width))
    return blocks


def broadcast_columns(columns, first, many, width):
    held = columns[...]
    return [jnp.broadcast_to(held[:, n : n + 1], (held.shape[0], width)) for n in range(first, first + many)]


def project(u, z, mask, proj_weight, columns, send, norm, mixed):
    width = z[0].shape[1]
    h = proj_weight.shape[1] // 4
    rows = mixed.shape[1]
    gain, offset, *biases = broadcast_columns(columns, u * EACH, 6, width)
    scales = (1.0, 0.5, 1.0, 0.5)
    biases = [b * k for b, k in zip(biases, scales)]
    turned = [proj_weight[:, n * h : (n + 1) * h] for n in range(4)]
    turned = [(w * jnp.asarray(k, BF16)).T if k != 1.0 else w.T for w, k in zip(turned, scales)]
    pairs = []
    for pair in range(0, OWN, 2):
        normed = [layer_norm(z[i], gain, offset).astype(BF16) for i in (pair, pair + 1)]
        pairs.append(jnp.concatenate(normed, 1))
    for side in range(2):
        for pair, normed in enumerate(pairs):
            value, gating = [jnp.dot(turned[2 * side + n], normed, preferred_element_type=F32) for n in range(2)]
            for n in range(2):
                i, at = 2 * pair + n, slice(n * width, (n + 1) * width)
                half = mask[i : i + 1, :] * 0.5
                weight = jnp.tanh(gating[:, at] + biases[2 * side + 1]) * half + half
                mixed[side, pl.ds(i, h, stride=OWN), :] = weight * (value[:, at] + biases[2 * side])
    for side in range(2):
        send[:, side * 16 : (side + 1) * 16, :] = mixed[side].reshape(rows // 16, 16, width).astype(BF16)
    for pair, normed in enumerate(pairs):
        norm[:, 2 * pair * width : 2 * (pair + 1) * width] = normed


def output_gate(u, norm, gate_weight, columns):
    width = norm.shape[1] // OWN
    turned = (gate_weight * jnp.asarray(0.5, BF16)).T
    (bias,) = broadcast_columns(columns, u * EACH + 6, 1, 2 * width)
    gates = []
    for pair in range(OWN // 2):
        gating = jnp.dot(turned, norm[:, 2 * pair * width : 2 * (pair + 1) * width], preferred_element_type=F32)
        gate = 0.5 * jnp.tanh(gating + 0.5 * bias) + 0.5
        gates += [gate[:, :width], gate[:, width:]]
    return gates


def finish(u, z, summed, gate, out_weight, columns, mixed):
    width = z[0].shape[1]
    gain, offset, bias = broadcast_columns(columns, u * EACH + 7, 3, width)
    turned = out_weight.T
    mixed[...] = summed[...].astype(F32).reshape(mixed.shape)
    results = []
    for pair in range(0, OWN, 2):
        blocks = [mixed[pl.ds(i, mixed.shape[0] // OWN, stride=OWN), :] for i in (pair, pair + 1)]
        blocks = [reorder(v, ORDERS[u][1], ORDERS[u][0]) for v in blocks]
        hidden = jnp.concatenate([layer_norm(v, gain, offset).astype(BF16) for v in blocks], 1)
        both = jnp.dot(turned, hidden, preferred_element_type=F32)
        for n in range(2):
            change = both[:, n * width : (n + 1) * width] + bias
            results.append((z[pair + n].astype(F32) + gate[pair + n] * change).astype(BF16))
    return results


def first_kernel(
    pair, mask, pw, pb, gb, ob, ns, no, send, norm, turned, columns, keep, pair_in, mask_in, pw_in, pb_in, gb_in, ob_in, ns_in, no_in, rows, arrived, mixed
):
    moves = [(pair, pair_in), (pb, pb_in), (gb, gb_in), (ob, ob_in), (ns, ns_in), (no, no_in)]
    moves += [(pw.at[0], pw_in), (mask, mask_in)]
    moves = [pltpu.make_async_copy(a, b, arrived.at[n]) for n, (a, b) in enumerate(moves)]
    for move in moves:
        move.start()
    for move in moves:
        move.wait()
    width = pair.shape[1]
    z = [pair_in[i].T for i in range(OWN)]
    for i in range(OWN):
        turned[:, i * width : (i + 1) * width] = z[i]
    h = pw.shape[2] // 4
    for u in range(2):
        found = [ns_in[u, 0:1, :], no_in[u, 0:1, :]] + [pb_in[u : u + 1, n * h : (n + 1) * h] for n in range(4)]
        found += [gb_in[u : u + 1, :], ns_in[u, 1:2, :], no_in[u, 1:2, :], ob_in[u : u + 1, :]]
        for n, row in enumerate(found):
            rows[u * EACH + n : u * EACH + n + 1, :] = row
    columns[...] = rows[...].T
    keep[0:OWN, :] = mask_in[...].astype(F32)
    project(0, [v.astype(F32) for v in z], keep, pw_in[...], columns, send, norm, mixed)


def middle_kernel(summed, old, old_norm, columns, keep, pw, gw, ow, send, norm, turned, mixed, mixed_back):
    width = keep.shape[1]
    gate = output_gate(0, old_norm, gw[0], columns)
    z = finish(0, [old[:, i * width : (i + 1) * width] for i in range(OWN)], summed, gate, ow[0], columns, mixed_back)
    for i in range(OWN):
        turned[:, i * width : (i + 1) * width] = z[i]
    project(1, [v.astype(F32) for v in z], keep, pw[1], columns, send, norm, mixed)


def last_kernel(summed, old, old_norm, columns, gw, ow, out, mixed_back):
    width = out.shape[1]
    gate = output_gate(1, old_norm, gw[1], columns)
    z = finish(1, [old[:, i * width : (i + 1) * width] for i in range(OWN)], summed, gate, ow[1], columns, mixed_back)
    for i in range(OWN):
        out[i] = z[i].T


def reorder(values, have, want):
    tiles = values.reshape(len(have), 2 * OWN, values.shape[1])
    places = [have.index(chip) for chip in want]
    return jnp.concatenate([tiles[n : n + 1] for n in places]).reshape(values.shape)


def triangle_kernel(incoming, sides, out):
    come, go = ORDERS[1 if incoming else 0]
    in_mesh = tuple(range(len(come)))
    left, right = [unpack(sides[:, n : n + 16, :].astype(F32)) for n in (0, 16)]
    if incoming:
        summed = [over_rows(a.astype(BF16), b.astype(BF16)) for a, b in zip(left, right)]
        summed = [reorder(v, in_mesh, go) for v in summed]
    else:
        left = [reorder(v, come, go) for v in left]
        right = [reorder(v, come, in_mesh) for v in right]
        summed = [over_columns(a.astype(BF16), b.astype(BF16)) for a, b in zip(left, right)]
    out[...] = pack(summed).astype(BF16)


def call(kernel, outs, scratch, *args, place=pltpu.VMEM):
    in_vmem = pl.BlockSpec(memory_space=pltpu.VMEM)
    return pl.pallas_call(
        kernel,
        out_shape=[jax.ShapeDtypeStruct(*o) for o in outs],
        in_specs=[pl.BlockSpec(memory_space=place)] * len(args),
        out_specs=[in_vmem] * len(outs),
        scratch_shapes=scratch,
        compiler_params=pltpu.CompilerParams(vmem_limit_bytes=24 * 2**20),
    )(*args)


def exchange(blocks):
    return lax.all_to_all(blocks, PEERS, split_axis=0, concat_axis=0, tiled=True)


def exchange_in_order(blocks, chips):
    listed = [[2 * chip + core for chip in chips for core in range(2)]]
    return lax.all_to_all(blocks, "row", split_axis=0, concat_axis=0, axis_index_groups=listed, tiled=True)


def packed_updates(count, pair_rep, pair_mask, pw, pb, gw, gb, ow, ob, ns, no):
    rows_of, width, channels = pair_rep.shape
    flat = (channels, rows_of * width)
    projected = [((count, 32, width), BF16), (flat, BF16), (flat, BF16)]
    summed = [((count, 16, width), BF16)]
    params = [pair_rep, pair_mask, pw, pb, gb, ob, ns, no]
    params = [pltpu.with_memory_space_constraint(v, pltpu.HBM) for v in params]
    held = [pltpu.VMEM(v.shape[1:] if n == 2 else v.shape, v.dtype) for n, v in enumerate(params)]
    held += [pltpu.VMEM((2 * EACH, channels), F32), pltpu.SemaphoreType.DMA((len(params),))]
    back = pltpu.VMEM((OWN * channels, width), F32)
    mixed = pltpu.VMEM((2, OWN * channels, width), F32)
    kept = [((channels, 2 * EACH), F32), ((2 * OWN, width), F32)]
    send, norm, turned, columns, keep = call(first_kernel, projected + kept, held + [mixed], *params, place=pltpu.HBM)
    (send,) = call(functools.partial(triangle_kernel, False), summed, [], exchange_in_order(send, ORDERS[0][0]))
    send, norm, turned = call(middle_kernel, projected, [mixed, back], exchange_in_order(send, ORDERS[0][1]), turned, norm, columns, keep, pw, gw, ow)
    (send,) = call(functools.partial(triangle_kernel, True), summed, [], exchange_in_order(send, ORDERS[1][0]))
    (out,) = call(last_kernel, [(pair_rep.shape, BF16)], [back], exchange_in_order(send, ORDERS[1][1]), turned, norm, columns, gw, ow)
    return out


def update(pair_t, pair_mask, u, incoming, peers, rows_of, pw, pb, gw, gb, ow, ob, ns, no):
    channels, positions = pair_t.shape
    width = positions // rows_of
    h = pw.shape[2] // 4
    count = peers[0] * peers[1]
    own = h // count
    normed = layer_norm(pair_t, ns[u, 0][:, None], no[u, 0][:, None]).astype(BF16)
    projected = over_rows(jnp.concatenate([pw[u], gw[u]], 1), normed) + jnp.concatenate([pb[u], gb[u]], 0)[:, None]
    parts = [projected[n * h : (n + 1) * h] for n in range(4)]
    gating = jax.nn.sigmoid(projected[4 * h :])
    mask = pair_mask.astype(F32).reshape(1, positions)
    left = (mask * jax.nn.sigmoid(parts[1]) * parts[0]).astype(BF16)
    right = (mask * jax.nn.sigmoid(parts[3]) * parts[2]).astype(BF16)
    sides = exchange(jnp.stack([v.reshape(count, own, rows_of, width) for v in (left, right)], 1))
    sides = sides.reshape(peers[0], peers[1], 2, own, rows_of, width)
    sides = sides.transpose(2, 3, 0, 4, 1, 5).reshape(2, own, peers[0] * rows_of, peers[1] * width)
    form = "cki,ckj->cij" if incoming else "cik,cjk->cij"
    summed = jnp.einsum(form, sides[0], sides[1], preferred_element_type=F32).astype(BF16)
    summed = summed.reshape(own, peers[0], rows_of, peers[1], width).transpose(1, 3, 0, 2, 4)
    summed = exchange(summed.reshape(count, own, rows_of, width)).reshape(h, positions).astype(F32)
    hidden = layer_norm(summed, ns[u, 1][:, None], no[u, 1][:, None]).astype(BF16)
    change = over_rows(ow[u], hidden) + ob[u][:, None]
    return (pair_t + gating * change).astype(BF16)


def plain_updates(peers, pair_rep, pair_mask, *params):
    rows_of, width, channels = pair_rep.shape
    pair_t = pair_rep.reshape(rows_of * width, channels).T
    for u in range(2):
        pair_t = update(pair_t.astype(F32), pair_mask, u, u == 1, peers, rows_of, *params)
    return pair_t.T.reshape(rows_of, width, channels)


def solution(mesh):
    peers = (mesh.shape["row"], mesh.shape["ka"])
    count = peers[0] * peers[1]

    def on_device(pair_rep, pair_mask, *params):
        rows_of, width, channels = pair_rep.shape
        hidden = params[0].shape[2] // 4
        fits = peers[1] == 1 and rows_of == OWN and hidden == OWN * count and count == 2 * len(ORDERS[0][0])
        if fits and channels == hidden == 128 and width % 128 == 0:
            return packed_updates(count, pair_rep, pair_mask, *params)
        return plain_updates(peers, pair_rep, pair_mask, *params)

    split = P(("grp", "row"), "ka", None)
    in_specs = (split, P(("grp", "row"), "ka")) + (P(),) * 8
    return jax.shard_map(on_device, mesh=mesh, in_specs=in_specs, out_specs=split, check_vma=False)
```

```python
import functools

import jax
import jax.numpy as jnp
from jax import lax
from jax.experimental import pallas as pl
from jax.experimental.pallas import tpu as pltpu
from jax.sharding import PartitionSpec as P

PEERS = ("row", "ka")
OWN = 4
ORDERS = (
    ((0, 4, 8, 12, 1, 5, 9, 13, 2, 6, 10, 14, 3, 7, 11, 15), (0, 15, 11, 14, 13, 10, 9, 7, 12, 5, 8, 6, 4, 3, 2, 1)),
    ((0, 4, 8, 12, 1, 5, 9, 13, 2, 6, 10, 14, 3, 7, 11, 15), (0, 15, 11, 14, 13, 10, 9, 7, 12, 5, 8, 6, 4, 3, 2, 1)),
)
EACH = 16
BF16, F32 = jnp.bfloat16, jnp.float32


def over_rows(a, b):
    return lax.dot_general(a, b, (((0,), (0,)), ((), ())), preferred_element_type=F32)


def over_columns(a, b):
    return lax.dot_general(a, b, (((1,), (1,)), ((), ())), preferred_element_type=F32)


def layer_norm(values, norm_gain, norm_bias):
    average = jnp.mean(values, 0, keepdims=True)
    centred = values - average
    variance = jnp.mean(centred * centred, 0, keepdims=True)
    return centred * lax.rsqrt(variance + 1e-05) * norm_gain + norm_bias


def pack(blocks):
    channels, width = blocks[0].shape
    tiles = [b.reshape(channels // 8, 8, width) for b in blocks]
    turned = [pltpu.roll(b, 4, axis=0).reshape(channels // 8, 8, width) for b in blocks]
    low = lax.broadcasted_iota(jnp.int32, tiles[0].shape, 1) < 4
    back = [pltpu.roll(b, channels - 4, axis=0).reshape(channels // 8, 8, width) for b in blocks]
    even = [jnp.where(low, tiles[n], turned[n + 1]) for n in (0, 2)]
    odd = [jnp.where(low, back[n], tiles[n + 1]) for n in (0, 2)]
    return jnp.stack([jnp.stack(even, 1), jnp.stack(odd, 1)], 1).reshape(channels // 4, 16, width)


def unpack(packed):
    count, _, width = packed.shape
    tiles = packed.reshape(count // 2, 2, 2, 8, width)
    low = lax.broadcasted_iota(jnp.int32, (count // 2, 8, width), 1) < 4
    blocks = []
    for n in range(2):
        even, odd = tiles[:, 0, n], tiles[:, 1, n]
        down = pltpu.roll(odd.reshape(count * 4, width), 4, axis=0).reshape(even.shape)
        up = pltpu.roll(even.reshape(count * 4, width), count * 4 - 4, axis=0).reshape(even.shape)
        blocks.append(jnp.where(low, even, down).reshape(count * 4, width))
        blocks.append(jnp.where(low, up, odd).reshape(count * 4, width))
    return blocks


def broadcast_columns(columns, first, many, width):
    held = columns[...]
    return [jnp.broadcast_to(held[:, n : n + 1], (held.shape[0], width)) for n in range(first, first + many)]


def project(u, z, mask, proj_weight, gate_weight, columns, send, gate, mixed):
    width = z[0].shape[1]
    h = proj_weight.shape[1] // 4
    rows = mixed.shape[1]
    gain, offset, *biases = broadcast_columns(columns, u * EACH, 7, width)
    scales = (1.0, 0.5, 1.0, 0.5, 0.5)
    biases = [b * k for b, k in zip(biases, scales)]
    turned = [proj_weight[:, n * h : (n + 1) * h] for n in range(4)] + [gate_weight]
    turned = [(w * jnp.asarray(k, BF16)).T if k != 1.0 else w.T for w, k in zip(turned, scales)]
    pairs = []
    for pair in range(0, OWN, 2):
        normed = [layer_norm(z[i], gain, offset).astype(BF16) for i in (pair, pair + 1)]
        pairs.append(jnp.concatenate(normed, 1))
    for side in range(2):
        for pair, normed in enumerate(pairs):
            value, gating = [jnp.dot(turned[2 * side + n], normed, preferred_element_type=F32) for n in range(2)]
            for n in range(2):
                i, at = 2 * pair + n, slice(n * width, (n + 1) * width)
                half = mask[i : i + 1, :] * 0.5
                weight = jnp.tanh(gating[:, at] + biases[2 * side + 1]) * half + half
                mixed[side, pl.ds(i, h, stride=OWN), :] = weight * (value[:, at] + biases[2 * side])
    for side in range(2):
        send[:, side * 16 : (side + 1) * 16, :] = mixed[side].reshape(rows // 16, 16, width).astype(BF16)
    for pair, normed in enumerate(pairs):
        gating = jnp.dot(turned[4], normed, preferred_element_type=F32)
        for n in range(2):
            i = 2 * pair + n
            gate[:, i * width : (i + 1) * width] = 0.5 * jnp.tanh(gating[:, n * width : (n + 1) * width] + biases[4]) + 0.5


def finish(u, z, summed, gate, out_weight, columns, mixed):
    width = z[0].shape[1]
    gain, offset, bias = broadcast_columns(columns, u * EACH + 7, 3, width)
    turned = out_weight.T
    mixed[...] = summed[...].astype(F32).reshape(mixed.shape)
    results = []
    for pair in range(0, OWN, 2):
        blocks = [mixed[pl.ds(i, mixed.shape[0] // OWN, stride=OWN), :] for i in (pair, pair + 1)]
        blocks = [reorder(v, ORDERS[u][1], ORDERS[u][0]) for v in blocks]
        hidden = jnp.concatenate([layer_norm(v, gain, offset).astype(BF16) for v in blocks], 1)
        both = jnp.dot(turned, hidden, preferred_element_type=F32)
        for n in range(2):
            change = both[:, n * width : (n + 1) * width] + bias
            at = slice((pair + n) * width, (pair + n + 1) * width)
            results.append((z[pair + n].astype(F32) + gate[:, at] * change).astype(BF16))
    return results


def first_kernel(
    pair, mask, pw, gw, pb, gb, ob, ns, no, send, gate, turned, columns, keep, pair_in, mask_in, pw_in, gw_in, pb_in, gb_in, ob_in, ns_in, no_in, rows, arrived, mixed
):
    moves = [(pair, pair_in), (pb, pb_in), (gb, gb_in), (ob, ob_in), (ns, ns_in), (no, no_in)]
    moves += [(pw.at[0], pw_in), (gw.at[0], gw_in), (mask, mask_in)]
    moves = [pltpu.make_async_copy(a, b, arrived.at[n]) for n, (a, b) in enumerate(moves)]
    for move in moves:
        move.start()
    for move in moves:
        move.wait()
    width = pair.shape[1]
    z = [pair_in[i].T for i in range(OWN)]
    for i in range(OWN):
        turned[:, i * width : (i + 1) * width] = z[i]
    h = pw.shape[2] // 4
    for u in range(2):
        found = [ns_in[u, 0:1, :], no_in[u, 0:1, :]] + [pb_in[u : u + 1, n * h : (n + 1) * h] for n in range(4)]
        found += [gb_in[u : u + 1, :], ns_in[u, 1:2, :], no_in[u, 1:2, :], ob_in[u : u + 1, :]]
        for n, row in enumerate(found):
            rows[u * EACH + n : u * EACH + n + 1, :] = row
    columns[...] = rows[...].T
    keep[0:OWN, :] = mask_in[...].astype(F32)
    project(0, [v.astype(F32) for v in z], keep, pw_in[...], gw_in[...], columns, send, gate, mixed)


def middle_kernel(summed, old, old_gate, columns, keep, pw, gw, ow, send, gate, turned, mixed, mixed_back):
    width = keep.shape[1]
    z = finish(0, [old[:, i * width : (i + 1) * width] for i in range(OWN)], summed, old_gate, ow[0], columns, mixed_back)
    for i in range(OWN):
        turned[:, i * width : (i + 1) * width] = z[i]
    project(1, [v.astype(F32) for v in z], keep, pw[1], gw[1], columns, send, gate, mixed)


def last_kernel(summed, old, old_gate, columns, ow, out, mixed_back):
    width = out.shape[1]
    z = finish(1, [old[:, i * width : (i + 1) * width] for i in range(OWN)], summed, old_gate, ow[1], columns, mixed_back)
    for i in range(OWN):
        out[i] = z[i].T


def reorder(values, have, want):
    tiles = values.reshape(len(have), 2 * OWN, values.shape[1])
    places = [have.index(chip) for chip in want]
    return jnp.concatenate([tiles[n : n + 1] for n in places]).reshape(values.shape)


def triangle_kernel(incoming, sides, out):
    come, go = ORDERS[1 if incoming else 0]
    in_mesh = tuple(range(len(come)))
    left, right = [unpack(sides[:, n : n + 16, :].astype(F32)) for n in (0, 16)]
    if incoming:
        summed = [over_rows(a.astype(BF16), b.astype(BF16)) for a, b in zip(left, right)]
        summed = [reorder(v, in_mesh, go) for v in summed]
    else:
        left = [reorder(v, come, go) for v in left]
        right = [reorder(v, come, in_mesh) for v in right]
        summed = [over_columns(a.astype(BF16), b.astype(BF16)) for a, b in zip(left, right)]
    out[...] = pack(summed).astype(BF16)


def call(kernel, outs, scratch, *args, place=pltpu.VMEM):
    in_vmem = pl.BlockSpec(memory_space=pltpu.VMEM)
    return pl.pallas_call(
        kernel,
        out_shape=[jax.ShapeDtypeStruct(*o) for o in outs],
        in_specs=[pl.BlockSpec(memory_space=place)] * len(args),
        out_specs=[in_vmem] * len(outs),
        scratch_shapes=scratch,
        compiler_params=pltpu.CompilerParams(vmem_limit_bytes=24 * 2**20),
    )(*args)


def exchange(blocks):
    return lax.all_to_all(blocks, PEERS, split_axis=0, concat_axis=0, tiled=True)


def exchange_in_order(blocks, chips):
    listed = [[2 * chip + core for chip in chips for core in range(2)]]
    return lax.all_to_all(blocks, "row", split_axis=0, concat_axis=0, axis_index_groups=listed, tiled=True)


def packed_updates(count, pair_rep, pair_mask, pw, pb, gw, gb, ow, ob, ns, no):
    rows_of, width, channels = pair_rep.shape
    flat = (channels, rows_of * width)
    projected = [((count, 32, width), BF16), (flat, F32), (flat, BF16)]
    summed = [((count, 16, width), BF16)]
    params = [pair_rep, pair_mask, pw, gw, pb, gb, ob, ns, no]
    params = [pltpu.with_memory_space_constraint(v, pltpu.HBM) for v in params]
    held = [pltpu.VMEM(v.shape[1:] if n in (2, 3) else v.shape, v.dtype) for n, v in enumerate(params)]
    held += [pltpu.VMEM((2 * EACH, channels), F32), pltpu.SemaphoreType.DMA((len(params),))]
    back = pltpu.VMEM((OWN * channels, width), F32)
    mixed = pltpu.VMEM((2, OWN * channels, width), F32)
    kept = [((channels, 2 * EACH), F32), ((2 * OWN, width), F32)]
    send, gate, turned, columns, keep = call(first_kernel, projected + kept, held + [mixed], *params, place=pltpu.HBM)
    (send,) = call(functools.partial(triangle_kernel, False), summed, [], exchange_in_order(send, ORDERS[0][0]))
    send, gate, turned = call(middle_kernel, projected, [mixed, back], exchange_in_order(send, ORDERS[0][1]), turned, gate, columns, keep, pw, gw, ow)
    (send,) = call(functools.partial(triangle_kernel, True), summed, [], exchange_in_order(send, ORDERS[1][0]))
    (out,) = call(last_kernel, [(pair_rep.shape, BF16)], [back], exchange_in_order(send, ORDERS[1][1]), turned, gate, columns, ow)
    return out


def update(pair_t, pair_mask, u, incoming, peers, rows_of, pw, pb, gw, gb, ow, ob, ns, no):
    channels, positions = pair_t.shape
    width = positions // rows_of
    h = pw.shape[2] // 4
    count = peers[0] * peers[1]
    own = h // count
    normed = layer_norm(pair_t, ns[u, 0][:, None], no[u, 0][:, None]).astype(BF16)
    projected = over_rows(jnp.concatenate([pw[u], gw[u]], 1), normed) + jnp.concatenate([pb[u], gb[u]], 0)[:, None]
    parts = [projected[n * h : (n + 1) * h] for n in range(4)]
    gating = jax.nn.sigmoid(projected[4 * h :])
    mask = pair_mask.astype(F32).reshape(1, positions)
    left = (mask * jax.nn.sigmoid(parts[1]) * parts[0]).astype(BF16)
    right = (mask * jax.nn.sigmoid(parts[3]) * parts[2]).astype(BF16)
    sides = exchange(jnp.stack([v.reshape(count, own, rows_of, width) for v in (left, right)], 1))
    sides = sides.reshape(peers[0], peers[1], 2, own, rows_of, width)
    sides = sides.transpose(2, 3, 0, 4, 1, 5).reshape(2, own, peers[0] * rows_of, peers[1] * width)
    form = "cki,ckj->cij" if incoming else "cik,cjk->cij"
    summed = jnp.einsum(form, sides[0], sides[1], preferred_element_type=F32).astype(BF16)
    summed = summed.reshape(own, peers[0], rows_of, peers[1], width).transpose(1, 3, 0, 2, 4)
    summed = exchange(summed.reshape(count, own, rows_of, width)).reshape(h, positions).astype(F32)
    hidden = layer_norm(summed, ns[u, 1][:, None], no[u, 1][:, None]).astype(BF16)
    change = over_rows(ow[u], hidden) + ob[u][:, None]
    return (pair_t + gating * change).astype(BF16)


def plain_updates(peers, pair_rep, pair_mask, *params):
    rows_of, width, channels = pair_rep.shape
    pair_t = pair_rep.reshape(rows_of * width, channels).T
    for u in range(2):
        pair_t = update(pair_t.astype(F32), pair_mask, u, u == 1, peers, rows_of, *params)
    return pair_t.T.reshape(rows_of, width, channels)


def solution(mesh):
    peers = (mesh.shape["row"], mesh.shape["ka"])
    count = peers[0] * peers[1]

    def on_device(pair_rep, pair_mask, *params):
        rows_of, width, channels = pair_rep.shape
        hidden = params[0].shape[2] // 4
        fits = peers[1] == 1 and rows_of == OWN and hidden == OWN * count and count == 2 * len(ORDERS[0][0])
        if fits and channels == hidden == 128 and width % 128 == 0:
            return packed_updates(count, pair_rep, pair_mask, *params)
        return plain_updates(peers, pair_rep, pair_mask, *params)

    split = P(("grp", "row"), "ka", None)
    in_specs = (split, P(("grp", "row"), "ka")) + (P(),) * 8
    return jax.shard_map(on_device, mesh=mesh, in_specs=in_specs, out_specs=split, check_vma=False)
```

```python
import functools

import jax
import jax.numpy as jnp
from jax import lax
from jax.experimental import pallas as pl
from jax.experimental.pallas import tpu as pltpu
from jax.sharding import PartitionSpec as P

PEERS = ("row", "ka")
OWN = 4
ORDERS = (
    ((0, 4, 8, 12, 1, 5, 9, 13, 2, 6, 10, 14, 3, 7, 11, 15), (0, 15, 11, 7, 3, 14, 10, 6, 2, 13, 9, 5, 1, 12, 8, 4)),
    ((0, 15, 11, 7, 3, 14, 10, 6, 2, 13, 9, 5, 1, 12, 8, 4), (0, 15, 11, 7, 3, 14, 10, 6, 2, 13, 9, 5, 1, 12, 8, 4)),
)
EACH = 16
BF16, F32 = jnp.bfloat16, jnp.float32


def over_rows(a, b):
    return lax.dot_general(a, b, (((0,), (0,)), ((), ())), preferred_element_type=F32)


def over_columns(a, b):
    return lax.dot_general(a, b, (((1,), (1,)), ((), ())), preferred_element_type=F32)


def layer_norm(values, norm_gain, norm_bias):
    average = jnp.mean(values, 0, keepdims=True)
    centred = values - average
    variance = jnp.mean(centred * centred, 0, keepdims=True)
    return centred * lax.rsqrt(variance + 1e-05) * norm_gain + norm_bias


def pack(blocks):
    channels, width = blocks[0].shape
    tiles = [b.reshape(channels // 8, 8, width) for b in blocks]
    turned = [pltpu.roll(b, 4, axis=0).reshape(channels // 8, 8, width) for b in blocks]
    low = lax.broadcasted_iota(jnp.int32, tiles[0].shape, 1) < 4
    back = [pltpu.roll(b, channels - 4, axis=0).reshape(channels // 8, 8, width) for b in blocks]
    even = [jnp.where(low, tiles[n], turned[n + 1]) for n in (0, 2)]
    odd = [jnp.where(low, back[n], tiles[n + 1]) for n in (0, 2)]
    return jnp.stack([jnp.stack(even, 1), jnp.stack(odd, 1)], 1).reshape(channels // 4, 16, width)


def unpack(packed):
    count, _, width = packed.shape
    tiles = packed.reshape(count // 2, 2, 2, 8, width)
    low = lax.broadcasted_iota(jnp.int32, (count // 2, 8, width), 1) < 4
    blocks = []
    for n in range(2):
        even, odd = tiles[:, 0, n], tiles[:, 1, n]
        down = pltpu.roll(odd.reshape(count * 4, width), 4, axis=0).reshape(even.shape)
        up = pltpu.roll(even.reshape(count * 4, width), count * 4 - 4, axis=0).reshape(even.shape)
        blocks.append(jnp.where(low, even, down).reshape(count * 4, width))
        blocks.append(jnp.where(low, up, odd).reshape(count * 4, width))
    return blocks


def broadcast_columns(columns, first, many, width):
    held = columns[...]
    return [jnp.broadcast_to(held[:, n : n + 1], (held.shape[0], width)) for n in range(first, first + many)]


def project(u, z, mask, proj_weight, gate_weight, columns, send, gate, mixed):
    width = z[0].shape[1]
    h = proj_weight.shape[1] // 4
    rows = mixed.shape[1]
    gain, offset, *biases = broadcast_columns(columns, u * EACH, 7, width)
    scales = (1.0, 0.5, 1.0, 0.5, 0.5)
    biases = [b * k for b, k in zip(biases, scales)]
    turned = [proj_weight[:, n * h : (n + 1) * h] for n in range(4)] + [gate_weight]
    turned = [(w * jnp.asarray(k, BF16)).T if k != 1.0 else w.T for w, k in zip(turned, scales)]
    pairs = []
    for pair in range(0, OWN, 2):
        normed = [layer_norm(z[i], gain, offset).astype(BF16) for i in (pair, pair + 1)]
        pairs.append(jnp.concatenate(normed, 1))
    for side in range(2):
        for pair, normed in enumerate(pairs):
            value, gating = [jnp.dot(turned[2 * side + n], normed, preferred_element_type=F32) for n in range(2)]
            for n in range(2):
                i, at = 2 * pair + n, slice(n * width, (n + 1) * width)
                half = mask[i : i + 1, :] * 0.5
                weight = jnp.tanh(gating[:, at] + biases[2 * side + 1]) * half + half
                mixed[side, pl.ds(i, h, stride=OWN), :] = weight * (value[:, at] + biases[2 * side])
    for side in range(2):
        send[:, side * 16 : (side + 1) * 16, :] = mixed[side].reshape(rows // 16, 16, width).astype(BF16)
    for pair, normed in enumerate(pairs):
        gating = jnp.dot(turned[4], normed, preferred_element_type=F32)
        for n in range(2):
            i = 2 * pair + n
            gate[:, i * width : (i + 1) * width] = 0.5 * jnp.tanh(gating[:, n * width : (n + 1) * width] + biases[4]) + 0.5


def finish(u, z, summed, gate, out_weight, columns, mixed):
    width = z[0].shape[1]
    gain, offset, bias = broadcast_columns(columns, u * EACH + 7, 3, width)
    turned = out_weight.T
    mixed[...] = summed[...].astype(F32).reshape(mixed.shape)
    results = []
    for pair in range(0, OWN, 2):
        blocks = [mixed[pl.ds(i, mixed.shape[0] // OWN, stride=OWN), :] for i in (pair, pair + 1)]
        blocks = [reorder(v, ORDERS[u][1], ORDERS[u][0]) for v in blocks]
        hidden = jnp.concatenate([layer_norm(v, gain, offset).astype(BF16) for v in blocks], 1)
        both = jnp.dot(turned, hidden, preferred_element_type=F32)
        for n in range(2):
            change = both[:, n * width : (n + 1) * width] + bias
            at = slice((pair + n) * width, (pair + n + 1) * width)
            results.append((z[pair + n].astype(F32) + gate[:, at] * change).astype(BF16))
    return results


def first_kernel(
    pair, mask, pw, gw, pb, gb, ob, ns, no, send, gate, turned, columns, keep, pair_in, mask_in, pw_in, gw_in, pb_in, gb_in, ob_in, ns_in, no_in, rows, arrived, mixed
):
    moves = [(pair, pair_in), (pb, pb_in), (gb, gb_in), (ob, ob_in), (ns, ns_in), (no, no_in)]
    moves += [(pw.at[0], pw_in), (gw.at[0], gw_in), (mask, mask_in)]
    moves = [pltpu.make_async_copy(a, b, arrived.at[n]) for n, (a, b) in enumerate(moves)]
    for move in moves:
        move.start()
    for move in moves:
        move.wait()
    width = pair.shape[1]
    z = [pair_in[i].T for i in range(OWN)]
    for i in range(OWN):
        turned[:, i * width : (i + 1) * width] = z[i]
    h = pw.shape[2] // 4
    for u in range(2):
        found = [ns_in[u, 0:1, :], no_in[u, 0:1, :]] + [pb_in[u : u + 1, n * h : (n + 1) * h] for n in range(4)]
        found += [gb_in[u : u + 1, :], ns_in[u, 1:2, :], no_in[u, 1:2, :], ob_in[u : u + 1, :]]
        for n, row in enumerate(found):
            rows[u * EACH + n : u * EACH + n + 1, :] = row
    columns[...] = rows[...].T
    keep[0:OWN, :] = mask_in[...].astype(F32)
    project(0, [v.astype(F32) for v in z], keep, pw_in[...], gw_in[...], columns, send, gate, mixed)


def middle_kernel(summed, old, old_gate, columns, keep, pw, gw, ow, send, gate, turned, mixed, mixed_back):
    width = keep.shape[1]
    z = finish(0, [old[:, i * width : (i + 1) * width] for i in range(OWN)], summed, old_gate, ow[0], columns, mixed_back)
    for i in range(OWN):
        turned[:, i * width : (i + 1) * width] = z[i]
    project(1, [v.astype(F32) for v in z], keep, pw[1], gw[1], columns, send, gate, mixed)


def last_kernel(summed, old, old_gate, columns, ow, out, mixed_back):
    width = out.shape[1]
    z = finish(1, [old[:, i * width : (i + 1) * width] for i in range(OWN)], summed, old_gate, ow[1], columns, mixed_back)
    for i in range(OWN):
        out[i] = z[i].T


def reorder(values, have, want):
    tiles = values.reshape(len(have), 2 * OWN, values.shape[1])
    places = [have.index(chip) for chip in want]
    return jnp.concatenate([tiles[n : n + 1] for n in places]).reshape(values.shape)


def triangle_kernel(incoming, sides, out):
    come, go = ORDERS[1 if incoming else 0]
    in_mesh = tuple(range(len(come)))
    left, right = [unpack(sides[:, n : n + 16, :].astype(F32)) for n in (0, 16)]
    if incoming:
        summed = [over_rows(a.astype(BF16), b.astype(BF16)) for a, b in zip(left, right)]
        summed = [reorder(v, in_mesh, go) for v in summed]
    else:
        left = [reorder(v, come, go) for v in left]
        right = [reorder(v, come, in_mesh) for v in right]
        summed = [over_columns(a.astype(BF16), b.astype(BF16)) for a, b in zip(left, right)]
    out[...] = pack(summed).astype(BF16)


def call(kernel, outs, scratch, *args, place=pltpu.VMEM):
    in_vmem = pl.BlockSpec(memory_space=pltpu.VMEM)
    return pl.pallas_call(
        kernel,
        out_shape=[jax.ShapeDtypeStruct(*o) for o in outs],
        in_specs=[pl.BlockSpec(memory_space=place)] * len(args),
        out_specs=[in_vmem] * len(outs),
        scratch_shapes=scratch,
        compiler_params=pltpu.CompilerParams(vmem_limit_bytes=24 * 2**20),
    )(*args)


def exchange(blocks):
    return lax.all_to_all(blocks, PEERS, split_axis=0, concat_axis=0, tiled=True)


def exchange_in_order(blocks, chips):
    listed = [[2 * chip + core for chip in chips for core in range(2)]]
    return lax.all_to_all(blocks, "row", split_axis=0, concat_axis=0, axis_index_groups=listed, tiled=True)


def packed_updates(count, pair_rep, pair_mask, pw, pb, gw, gb, ow, ob, ns, no):
    rows_of, width, channels = pair_rep.shape
    flat = (channels, rows_of * width)
    projected = [((count, 32, width), BF16), (flat, F32), (flat, BF16)]
    summed = [((count, 16, width), BF16)]
    params = [pair_rep, pair_mask, pw, gw, pb, gb, ob, ns, no]
    params = [pltpu.with_memory_space_constraint(v, pltpu.HBM) for v in params]
    held = [pltpu.VMEM(v.shape[1:] if n in (2, 3) else v.shape, v.dtype) for n, v in enumerate(params)]
    held += [pltpu.VMEM((2 * EACH, channels), F32), pltpu.SemaphoreType.DMA((len(params),))]
    back = pltpu.VMEM((OWN * channels, width), F32)
    mixed = pltpu.VMEM((2, OWN * channels, width), F32)
    kept = [((channels, 2 * EACH), F32), ((2 * OWN, width), F32)]
    send, gate, turned, columns, keep = call(first_kernel, projected + kept, held + [mixed], *params, place=pltpu.HBM)
    (send,) = call(functools.partial(triangle_kernel, False), summed, [], exchange_in_order(send, ORDERS[0][0]))
    send, gate, turned = call(middle_kernel, projected, [mixed, back], exchange_in_order(send, ORDERS[0][1]), turned, gate, columns, keep, pw, gw, ow)
    (send,) = call(functools.partial(triangle_kernel, True), summed, [], exchange_in_order(send, ORDERS[1][0]))
    (out,) = call(last_kernel, [(pair_rep.shape, BF16)], [back], exchange_in_order(send, ORDERS[1][1]), turned, gate, columns, ow)
    return out


def update(pair_t, pair_mask, u, incoming, peers, rows_of, pw, pb, gw, gb, ow, ob, ns, no):
    channels, positions = pair_t.shape
    width = positions // rows_of
    h = pw.shape[2] // 4
    count = peers[0] * peers[1]
    own = h // count
    normed = layer_norm(pair_t, ns[u, 0][:, None], no[u, 0][:, None]).astype(BF16)
    projected = over_rows(jnp.concatenate([pw[u], gw[u]], 1), normed) + jnp.concatenate([pb[u], gb[u]], 0)[:, None]
    parts = [projected[n * h : (n + 1) * h] for n in range(4)]
    gating = jax.nn.sigmoid(projected[4 * h :])
    mask = pair_mask.astype(F32).reshape(1, positions)
    left = (mask * jax.nn.sigmoid(parts[1]) * parts[0]).astype(BF16)
    right = (mask * jax.nn.sigmoid(parts[3]) * parts[2]).astype(BF16)
    sides = exchange(jnp.stack([v.reshape(count, own, rows_of, width) for v in (left, right)], 1))
    sides = sides.reshape(peers[0], peers[1], 2, own, rows_of, width)
    sides = sides.transpose(2, 3, 0, 4, 1, 5).reshape(2, own, peers[0] * rows_of, peers[1] * width)
    form = "cki,ckj->cij" if incoming else "cik,cjk->cij"
    summed = jnp.einsum(form, sides[0], sides[1], preferred_element_type=F32).astype(BF16)
    summed = summed.reshape(own, peers[0], rows_of, peers[1], width).transpose(1, 3, 0, 2, 4)
    summed = exchange(summed.reshape(count, own, rows_of, width)).reshape(h, positions).astype(F32)
    hidden = layer_norm(summed, ns[u, 1][:, None], no[u, 1][:, None]).astype(BF16)
    change = over_rows(ow[u], hidden) + ob[u][:, None]
    return (pair_t + gating * change).astype(BF16)


def plain_updates(peers, pair_rep, pair_mask, *params):
    rows_of, width, channels = pair_rep.shape
    pair_t = pair_rep.reshape(rows_of * width, channels).T
    for u in range(2):
        pair_t = update(pair_t.astype(F32), pair_mask, u, u == 1, peers, rows_of, *params)
    return pair_t.T.reshape(rows_of, width, channels)


def solution(mesh):
    peers = (mesh.shape["row"], mesh.shape["ka"])
    count = peers[0] * peers[1]

    def on_device(pair_rep, pair_mask, *params):
        rows_of, width, channels = pair_rep.shape
        hidden = params[0].shape[2] // 4
        fits = peers[1] == 1 and rows_of == OWN and hidden == OWN * count and count == 2 * len(ORDERS[0][0])
        if fits and channels == hidden == 128 and width % 128 == 0:
            return packed_updates(count, pair_rep, pair_mask, *params)
        return plain_updates(peers, pair_rep, pair_mask, *params)

    split = P(("grp", "row"), "ka", None)
    in_specs = (split, P(("grp", "row"), "ka")) + (P(),) * 8
    return jax.shard_map(on_device, mesh=mesh, in_specs=in_specs, out_specs=split, check_vma=False)
```

```python
import functools

import jax
import jax.numpy as jnp
from jax import lax
from jax.experimental import pallas as pl
from jax.experimental.pallas import tpu as pltpu
from jax.sharding import PartitionSpec as P

PEERS = ("row", "ka")
OWN = 4
ORDERS = (
    ((0, 15, 11, 7, 3, 14, 10, 6, 2, 13, 9, 5, 1, 12, 8, 4), (0, 15, 11, 7, 3, 14, 10, 6, 2, 13, 9, 5, 1, 12, 8, 4)),
    ((0, 15, 11, 7, 3, 14, 10, 6, 2, 13, 9, 5, 1, 12, 8, 4), (0, 15, 11, 7, 3, 14, 10, 6, 2, 13, 9, 5, 1, 12, 8, 4)),
)
EACH = 16
BF16, F32 = jnp.bfloat16, jnp.float32


def over_rows(a, b):
    return lax.dot_general(a, b, (((0,), (0,)), ((), ())), preferred_element_type=F32)


def over_columns(a, b):
    return lax.dot_general(a, b, (((1,), (1,)), ((), ())), preferred_element_type=F32)


def layer_norm(values, norm_gain, norm_bias):
    average = jnp.mean(values, 0, keepdims=True)
    centred = values - average
    variance = jnp.mean(centred * centred, 0, keepdims=True)
    return centred * lax.rsqrt(variance + 1e-05) * norm_gain + norm_bias


def pack(blocks):
    channels, width = blocks[0].shape
    tiles = [b.reshape(channels // 8, 8, width) for b in blocks]
    turned = [pltpu.roll(b, 4, axis=0).reshape(channels // 8, 8, width) for b in blocks]
    low = lax.broadcasted_iota(jnp.int32, tiles[0].shape, 1) < 4
    back = [pltpu.roll(b, channels - 4, axis=0).reshape(channels // 8, 8, width) for b in blocks]
    even = [jnp.where(low, tiles[n], turned[n + 1]) for n in (0, 2)]
    odd = [jnp.where(low, back[n], tiles[n + 1]) for n in (0, 2)]
    return jnp.stack([jnp.stack(even, 1), jnp.stack(odd, 1)], 1).reshape(channels // 4, 16, width)


def unpack(packed):
    count, _, width = packed.shape
    tiles = packed.reshape(count // 2, 2, 2, 8, width)
    low = lax.broadcasted_iota(jnp.int32, (count // 2, 8, width), 1) < 4
    blocks = []
    for n in range(2):
        even, odd = tiles[:, 0, n], tiles[:, 1, n]
        down = pltpu.roll(odd.reshape(count * 4, width), 4, axis=0).reshape(even.shape)
        up = pltpu.roll(even.reshape(count * 4, width), count * 4 - 4, axis=0).reshape(even.shape)
        blocks.append(jnp.where(low, even, down).reshape(count * 4, width))
        blocks.append(jnp.where(low, up, odd).reshape(count * 4, width))
    return blocks


def broadcast_columns(columns, first, many, width):
    held = columns[...]
    return [jnp.broadcast_to(held[:, n : n + 1], (held.shape[0], width)) for n in range(first, first + many)]


def project(u, z, mask, proj_weight, gate_weight, columns, send, gate, mixed):
    width = z[0].shape[1]
    h = proj_weight.shape[1] // 4
    rows = mixed.shape[1]
    gain, offset, *biases = broadcast_columns(columns, u * EACH, 7, width)
    scales = (1.0, 0.5, 1.0, 0.5, 0.5)
    biases = [b * k for b, k in zip(biases, scales)]
    turned = [proj_weight[:, n * h : (n + 1) * h] for n in range(4)] + [gate_weight]
    turned = [(w * jnp.asarray(k, BF16)).T if k != 1.0 else w.T for w, k in zip(turned, scales)]
    pairs = []
    for pair in range(0, OWN, 2):
        normed = [layer_norm(z[i], gain, offset).astype(BF16) for i in (pair, pair + 1)]
        pairs.append(jnp.concatenate(normed, 1))
    for side in range(2):
        for pair, normed in enumerate(pairs):
            value, gating = [jnp.dot(turned[2 * side + n], normed, preferred_element_type=F32) for n in range(2)]
            for n in range(2):
                i, at = 2 * pair + n, slice(n * width, (n + 1) * width)
                half = mask[i : i + 1, :] * 0.5
                weight = jnp.tanh(gating[:, at] + biases[2 * side + 1]) * half + half
                mixed[side, pl.ds(i, h, stride=OWN), :] = weight * (value[:, at] + biases[2 * side])
    for side in range(2):
        send[:, side * 16 : (side + 1) * 16, :] = mixed[side].reshape(rows // 16, 16, width).astype(BF16)
    for pair, normed in enumerate(pairs):
        gating = jnp.dot(turned[4], normed, preferred_element_type=F32)
        for n in range(2):
            i = 2 * pair + n
            gate[:, i * width : (i + 1) * width] = 0.5 * jnp.tanh(gating[:, n * width : (n + 1) * width] + biases[4]) + 0.5


def finish(u, z, summed, gate, out_weight, columns, mixed):
    width = z[0].shape[1]
    gain, offset, bias = broadcast_columns(columns, u * EACH + 7, 3, width)
    turned = out_weight.T
    mixed[...] = summed[...].astype(F32).reshape(mixed.shape)
    results = []
    for pair in range(0, OWN, 2):
        blocks = [mixed[pl.ds(i, mixed.shape[0] // OWN, stride=OWN), :] for i in (pair, pair + 1)]
        blocks = [reorder(v, ORDERS[u][1], ORDERS[u][0]) for v in blocks]
        hidden = jnp.concatenate([layer_norm(v, gain, offset).astype(BF16) for v in blocks], 1)
        both = jnp.dot(turned, hidden, preferred_element_type=F32)
        for n in range(2):
            change = both[:, n * width : (n + 1) * width] + bias
            at = slice((pair + n) * width, (pair + n + 1) * width)
            results.append((z[pair + n].astype(F32) + gate[:, at] * change).astype(BF16))
    return results


def first_kernel(
    pair, mask, pw, gw, pb, gb, ob, ns, no, send, gate, turned, columns, keep, pair_in, mask_in, pw_in, gw_in, pb_in, gb_in, ob_in, ns_in, no_in, rows, arrived, mixed
):
    moves = [(pair, pair_in), (pb, pb_in), (gb, gb_in), (ob, ob_in), (ns, ns_in), (no, no_in)]
    moves += [(pw.at[0], pw_in), (gw.at[0], gw_in), (mask, mask_in)]
    moves = [pltpu.make_async_copy(a, b, arrived.at[n]) for n, (a, b) in enumerate(moves)]
    for move in moves:
        move.start()
    for move in moves:
        move.wait()
    width = pair.shape[1]
    z = [pair_in[i].T for i in range(OWN)]
    for i in range(OWN):
        turned[:, i * width : (i + 1) * width] = z[i]
    h = pw.shape[2] // 4
    for u in range(2):
        found = [ns_in[u, 0:1, :], no_in[u, 0:1, :]] + [pb_in[u : u + 1, n * h : (n + 1) * h] for n in range(4)]
        found += [gb_in[u : u + 1, :], ns_in[u, 1:2, :], no_in[u, 1:2, :], ob_in[u : u + 1, :]]
        for n, row in enumerate(found):
            rows[u * EACH + n : u * EACH + n + 1, :] = row
    columns[...] = rows[...].T
    keep[0:OWN, :] = mask_in[...].astype(F32)
    project(0, [v.astype(F32) for v in z], keep, pw_in[...], gw_in[...], columns, send, gate, mixed)


def middle_kernel(summed, old, old_gate, columns, keep, pw, gw, ow, send, gate, turned, mixed, mixed_back):
    width = keep.shape[1]
    z = finish(0, [old[:, i * width : (i + 1) * width] for i in range(OWN)], summed, old_gate, ow[0], columns, mixed_back)
    for i in range(OWN):
        turned[:, i * width : (i + 1) * width] = z[i]
    project(1, [v.astype(F32) for v in z], keep, pw[1], gw[1], columns, send, gate, mixed)


def last_kernel(summed, old, old_gate, columns, ow, out, mixed_back):
    width = out.shape[1]
    z = finish(1, [old[:, i * width : (i + 1) * width] for i in range(OWN)], summed, old_gate, ow[1], columns, mixed_back)
    for i in range(OWN):
        out[i] = z[i].T


def reorder(values, have, want):
    tiles = values.reshape(len(have), 2 * OWN, values.shape[1])
    places = [have.index(chip) for chip in want]
    return jnp.concatenate([tiles[n : n + 1] for n in places]).reshape(values.shape)


def triangle_kernel(incoming, sides, out):
    come, go = ORDERS[1 if incoming else 0]
    in_mesh = tuple(range(len(come)))
    left, right = [unpack(sides[:, n : n + 16, :].astype(F32)) for n in (0, 16)]
    if incoming:
        summed = [over_rows(a.astype(BF16), b.astype(BF16)) for a, b in zip(left, right)]
        summed = [reorder(v, in_mesh, go) for v in summed]
    else:
        left = [reorder(v, come, go) for v in left]
        right = [reorder(v, come, in_mesh) for v in right]
        summed = [over_columns(a.astype(BF16), b.astype(BF16)) for a, b in zip(left, right)]
    out[...] = pack(summed).astype(BF16)


def call(kernel, outs, scratch, *args, place=pltpu.VMEM):
    in_vmem = pl.BlockSpec(memory_space=pltpu.VMEM)
    return pl.pallas_call(
        kernel,
        out_shape=[jax.ShapeDtypeStruct(*o) for o in outs],
        in_specs=[pl.BlockSpec(memory_space=place)] * len(args),
        out_specs=[in_vmem] * len(outs),
        scratch_shapes=scratch,
        compiler_params=pltpu.CompilerParams(vmem_limit_bytes=24 * 2**20),
    )(*args)


def exchange(blocks):
    return lax.all_to_all(blocks, PEERS, split_axis=0, concat_axis=0, tiled=True)


def exchange_in_order(blocks, chips):
    listed = [[2 * chip + core for chip in chips for core in range(2)]]
    return lax.all_to_all(blocks, "row", split_axis=0, concat_axis=0, axis_index_groups=listed, tiled=True)


def packed_updates(count, pair_rep, pair_mask, pw, pb, gw, gb, ow, ob, ns, no):
    rows_of, width, channels = pair_rep.shape
    flat = (channels, rows_of * width)
    projected = [((count, 32, width), BF16), (flat, F32), (flat, BF16)]
    summed = [((count, 16, width), BF16)]
    params = [pair_rep, pair_mask, pw, gw, pb, gb, ob, ns, no]
    params = [pltpu.with_memory_space_constraint(v, pltpu.HBM) for v in params]
    held = [pltpu.VMEM(v.shape[1:] if n in (2, 3) else v.shape, v.dtype) for n, v in enumerate(params)]
    held += [pltpu.VMEM((2 * EACH, channels), F32), pltpu.SemaphoreType.DMA((len(params),))]
    back = pltpu.VMEM((OWN * channels, width), F32)
    mixed = pltpu.VMEM((2, OWN * channels, width), F32)
    kept = [((channels, 2 * EACH), F32), ((2 * OWN, width), F32)]
    send, gate, turned, columns, keep = call(first_kernel, projected + kept, held + [mixed], *params, place=pltpu.HBM)
    (send,) = call(functools.partial(triangle_kernel, False), summed, [], exchange_in_order(send, ORDERS[0][0]))
    send, gate, turned = call(middle_kernel, projected, [mixed, back], exchange_in_order(send, ORDERS[0][1]), turned, gate, columns, keep, pw, gw, ow)
    (send,) = call(functools.partial(triangle_kernel, True), summed, [], exchange_in_order(send, ORDERS[1][0]))
    (out,) = call(last_kernel, [(pair_rep.shape, BF16)], [back], exchange_in_order(send, ORDERS[1][1]), turned, gate, columns, ow)
    return out


def update(pair_t, pair_mask, u, incoming, peers, rows_of, pw, pb, gw, gb, ow, ob, ns, no):
    channels, positions = pair_t.shape
    width = positions // rows_of
    h = pw.shape[2] // 4
    count = peers[0] * peers[1]
    own = h // count
    normed = layer_norm(pair_t, ns[u, 0][:, None], no[u, 0][:, None]).astype(BF16)
    projected = over_rows(jnp.concatenate([pw[u], gw[u]], 1), normed) + jnp.concatenate([pb[u], gb[u]], 0)[:, None]
    parts = [projected[n * h : (n + 1) * h] for n in range(4)]
    gating = jax.nn.sigmoid(projected[4 * h :])
    mask = pair_mask.astype(F32).reshape(1, positions)
    left = (mask * jax.nn.sigmoid(parts[1]) * parts[0]).astype(BF16)
    right = (mask * jax.nn.sigmoid(parts[3]) * parts[2]).astype(BF16)
    sides = exchange(jnp.stack([v.reshape(count, own, rows_of, width) for v in (left, right)], 1))
    sides = sides.reshape(peers[0], peers[1], 2, own, rows_of, width)
    sides = sides.transpose(2, 3, 0, 4, 1, 5).reshape(2, own, peers[0] * rows_of, peers[1] * width)
    form = "cki,ckj->cij" if incoming else "cik,cjk->cij"
    summed = jnp.einsum(form, sides[0], sides[1], preferred_element_type=F32).astype(BF16)
    summed = summed.reshape(own, peers[0], rows_of, peers[1], width).transpose(1, 3, 0, 2, 4)
    summed = exchange(summed.reshape(count, own, rows_of, width)).reshape(h, positions).astype(F32)
    hidden = layer_norm(summed, ns[u, 1][:, None], no[u, 1][:, None]).astype(BF16)
    change = over_rows(ow[u], hidden) + ob[u][:, None]
    return (pair_t + gating * change).astype(BF16)


def plain_updates(peers, pair_rep, pair_mask, *params):
    rows_of, width, channels = pair_rep.shape
    pair_t = pair_rep.reshape(rows_of * width, channels).T
    for u in range(2):
        pair_t = update(pair_t.astype(F32), pair_mask, u, u == 1, peers, rows_of, *params)
    return pair_t.T.reshape(rows_of, width, channels)


def solution(mesh):
    peers = (mesh.shape["row"], mesh.shape["ka"])
    count = peers[0] * peers[1]

    def on_device(pair_rep, pair_mask, *params):
        rows_of, width, channels = pair_rep.shape
        hidden = params[0].shape[2] // 4
        fits = peers[1] == 1 and rows_of == OWN and hidden == OWN * count and count == 2 * len(ORDERS[0][0])
        if fits and channels == hidden == 128 and width % 128 == 0:
            return packed_updates(count, pair_rep, pair_mask, *params)
        return plain_updates(peers, pair_rep, pair_mask, *params)

    split = P(("grp", "row"), "ka", None)
    in_specs = (split, P(("grp", "row"), "ka")) + (P(),) * 8
    return jax.shard_map(on_device, mesh=mesh, in_specs=in_specs, out_specs=split, check_vma=False)
```

```python
import functools

import jax
import jax.numpy as jnp
from jax import lax
from jax.experimental import pallas as pl
from jax.experimental.pallas import tpu as pltpu
from jax.sharding import PartitionSpec as P

PEERS = ("row", "ka")
OWN = 4
ORDERS = (
    ((0, 15, 11, 7, 3, 14, 10, 6, 2, 13, 9, 5, 1, 12, 8, 4), (0, 15, 11, 7, 3, 14, 10, 6, 2, 13, 9, 5, 1, 12, 8, 4)),
    ((0, 15, 11, 7, 3, 14, 10, 6, 2, 13, 9, 5, 1, 12, 8, 4), (0, 15, 11, 14, 13, 10, 9, 7, 12, 5, 8, 6, 4, 3, 2, 1)),
)
EACH = 16
BF16, F32 = jnp.bfloat16, jnp.float32


def over_rows(a, b):
    return lax.dot_general(a, b, (((0,), (0,)), ((), ())), preferred_element_type=F32)


def over_columns(a, b):
    return lax.dot_general(a, b, (((1,), (1,)), ((), ())), preferred_element_type=F32)


def layer_norm(values, norm_gain, norm_bias):
    average = jnp.mean(values, 0, keepdims=True)
    centred = values - average
    variance = jnp.mean(centred * centred, 0, keepdims=True)
    return centred * lax.rsqrt(variance + 1e-05) * norm_gain + norm_bias


def pack(blocks):
    channels, width = blocks[0].shape
    tiles = [b.reshape(channels // 8, 8, width) for b in blocks]
    turned = [pltpu.roll(b, 4, axis=0).reshape(channels // 8, 8, width) for b in blocks]
    low = lax.broadcasted_iota(jnp.int32, tiles[0].shape, 1) < 4
    back = [pltpu.roll(b, channels - 4, axis=0).reshape(channels // 8, 8, width) for b in blocks]
    even = [jnp.where(low, tiles[n], turned[n + 1]) for n in (0, 2)]
    odd = [jnp.where(low, back[n], tiles[n + 1]) for n in (0, 2)]
    return jnp.stack([jnp.stack(even, 1), jnp.stack(odd, 1)], 1).reshape(channels // 4, 16, width)


def unpack(packed):
    count, _, width = packed.shape
    tiles = packed.reshape(count // 2, 2, 2, 8, width)
    low = lax.broadcasted_iota(jnp.int32, (count // 2, 8, width), 1) < 4
    blocks = []
    for n in range(2):
        even, odd = tiles[:, 0, n], tiles[:, 1, n]
        down = pltpu.roll(odd.reshape(count * 4, width), 4, axis=0).reshape(even.shape)
        up = pltpu.roll(even.reshape(count * 4, width), count * 4 - 4, axis=0).reshape(even.shape)
        blocks.append(jnp.where(low, even, down).reshape(count * 4, width))
        blocks.append(jnp.where(low, up, odd).reshape(count * 4, width))
    return blocks


def broadcast_columns(columns, first, many, width):
    held = columns[...]
    return [jnp.broadcast_to(held[:, n : n + 1], (held.shape[0], width)) for n in range(first, first + many)]


def project(u, z, mask, proj_weight, gate_weight, columns, send, gate, mixed):
    width = z[0].shape[1]
    h = proj_weight.shape[1] // 4
    rows = mixed.shape[1]
    gain, offset, *biases = broadcast_columns(columns, u * EACH, 7, width)
    scales = (1.0, 0.5, 1.0, 0.5, 0.5)
    biases = [b * k for b, k in zip(biases, scales)]
    turned = [proj_weight[:, n * h : (n + 1) * h] for n in range(4)] + [gate_weight]
    turned = [(w * jnp.asarray(k, BF16)).T if k != 1.0 else w.T for w, k in zip(turned, scales)]
    pairs = []
    for pair in range(0, OWN, 2):
        normed = [layer_norm(z[i], gain, offset).astype(BF16) for i in (pair, pair + 1)]
        pairs.append(jnp.concatenate(normed, 1))
    for side in range(2):
        for pair, normed in enumerate(pairs):
            value, gating = [jnp.dot(turned[2 * side + n], normed, preferred_element_type=F32) for n in range(2)]
            for n in range(2):
                i, at = 2 * pair + n, slice(n * width, (n + 1) * width)
                half = mask[i : i + 1, :] * 0.5
                weight = jnp.tanh(gating[:, at] + biases[2 * side + 1]) * half + half
                mixed[side, pl.ds(i, h, stride=OWN), :] = weight * (value[:, at] + biases[2 * side])
    for side in range(2):
        send[:, side * 16 : (side + 1) * 16, :] = mixed[side].reshape(rows // 16, 16, width).astype(BF16)
    for pair, normed in enumerate(pairs):
        gating = jnp.dot(turned[4], normed, preferred_element_type=F32)
        for n in range(2):
            i = 2 * pair + n
            gate[:, i * width : (i + 1) * width] = 0.5 * jnp.tanh(gating[:, n * width : (n + 1) * width] + biases[4]) + 0.5


def finish(u, z, summed, gate, out_weight, columns, mixed):
    width = z[0].shape[1]
    gain, offset, bias = broadcast_columns(columns, u * EACH + 7, 3, width)
    turned = out_weight.T
    mixed[...] = summed[...].astype(F32).reshape(mixed.shape)
    results = []
    for pair in range(0, OWN, 2):
        blocks = [mixed[pl.ds(i, mixed.shape[0] // OWN, stride=OWN), :] for i in (pair, pair + 1)]
        blocks = [reorder(v, ORDERS[u][1], ORDERS[u][0]) for v in blocks]
        hidden = jnp.concatenate([layer_norm(v, gain, offset).astype(BF16) for v in blocks], 1)
        both = jnp.dot(turned, hidden, preferred_element_type=F32)
        for n in range(2):
            change = both[:, n * width : (n + 1) * width] + bias
            at = slice((pair + n) * width, (pair + n + 1) * width)
            results.append((z[pair + n].astype(F32) + gate[:, at] * change).astype(BF16))
    return results


def first_kernel(
    pair, mask, pw, gw, pb, gb, ob, ns, no, send, gate, turned, columns, keep, pair_in, mask_in, pw_in, gw_in, pb_in, gb_in, ob_in, ns_in, no_in, rows, arrived, mixed
):
    moves = [(pair, pair_in), (pb, pb_in), (gb, gb_in), (ob, ob_in), (ns, ns_in), (no, no_in)]
    moves += [(pw.at[0], pw_in), (gw.at[0], gw_in), (mask, mask_in)]
    moves = [pltpu.make_async_copy(a, b, arrived.at[n]) for n, (a, b) in enumerate(moves)]
    for move in moves:
        move.start()
    for move in moves:
        move.wait()
    width = pair.shape[1]
    z = [pair_in[i].T for i in range(OWN)]
    for i in range(OWN):
        turned[:, i * width : (i + 1) * width] = z[i]
    h = pw.shape[2] // 4
    for u in range(2):
        found = [ns_in[u, 0:1, :], no_in[u, 0:1, :]] + [pb_in[u : u + 1, n * h : (n + 1) * h] for n in range(4)]
        found += [gb_in[u : u + 1, :], ns_in[u, 1:2, :], no_in[u, 1:2, :], ob_in[u : u + 1, :]]
        for n, row in enumerate(found):
            rows[u * EACH + n : u * EACH + n + 1, :] = row
    columns[...] = rows[...].T
    keep[0:OWN, :] = mask_in[...].astype(F32)
    project(0, [v.astype(F32) for v in z], keep, pw_in[...], gw_in[...], columns, send, gate, mixed)


def middle_kernel(summed, old, old_gate, columns, keep, pw, gw, ow, send, gate, turned, mixed, mixed_back):
    width = keep.shape[1]
    z = finish(0, [old[:, i * width : (i + 1) * width] for i in range(OWN)], summed, old_gate, ow[0], columns, mixed_back)
    for i in range(OWN):
        turned[:, i * width : (i + 1) * width] = z[i]
    project(1, [v.astype(F32) for v in z], keep, pw[1], gw[1], columns, send, gate, mixed)


def last_kernel(summed, old, old_gate, columns, ow, out, mixed_back):
    width = out.shape[1]
    z = finish(1, [old[:, i * width : (i + 1) * width] for i in range(OWN)], summed, old_gate, ow[1], columns, mixed_back)
    for i in range(OWN):
        out[i] = z[i].T


def reorder(values, have, want):
    tiles = values.reshape(len(have), 2 * OWN, values.shape[1])
    places = [have.index(chip) for chip in want]
    return jnp.concatenate([tiles[n : n + 1] for n in places]).reshape(values.shape)


def triangle_kernel(incoming, sides, out):
    come, go = ORDERS[1 if incoming else 0]
    in_mesh = tuple(range(len(come)))
    left, right = [unpack(sides[:, n : n + 16, :].astype(F32)) for n in (0, 16)]
    if incoming:
        summed = [over_rows(a.astype(BF16), b.astype(BF16)) for a, b in zip(left, right)]
        summed = [reorder(v, in_mesh, go) for v in summed]
    else:
        left = [reorder(v, come, go) for v in left]
        right = [reorder(v, come, in_mesh) for v in right]
        summed = [over_columns(a.astype(BF16), b.astype(BF16)) for a, b in zip(left, right)]
    out[...] = pack(summed).astype(BF16)


def call(kernel, outs, scratch, *args, place=pltpu.VMEM):
    in_vmem = pl.BlockSpec(memory_space=pltpu.VMEM)
    return pl.pallas_call(
        kernel,
        out_shape=[jax.ShapeDtypeStruct(*o) for o in outs],
        in_specs=[pl.BlockSpec(memory_space=place)] * len(args),
        out_specs=[in_vmem] * len(outs),
        scratch_shapes=scratch,
        compiler_params=pltpu.CompilerParams(vmem_limit_bytes=24 * 2**20),
    )(*args)


def exchange(blocks):
    return lax.all_to_all(blocks, PEERS, split_axis=0, concat_axis=0, tiled=True)


def exchange_in_order(blocks, chips):
    listed = [[2 * chip + core for chip in chips for core in range(2)]]
    return lax.all_to_all(blocks, "row", split_axis=0, concat_axis=0, axis_index_groups=listed, tiled=True)


def packed_updates(count, pair_rep, pair_mask, pw, pb, gw, gb, ow, ob, ns, no):
    rows_of, width, channels = pair_rep.shape
    flat = (channels, rows_of * width)
    projected = [((count, 32, width), BF16), (flat, F32), (flat, BF16)]
    summed = [((count, 16, width), BF16)]
    params = [pair_rep, pair_mask, pw, gw, pb, gb, ob, ns, no]
    params = [pltpu.with_memory_space_constraint(v, pltpu.HBM) for v in params]
    held = [pltpu.VMEM(v.shape[1:] if n in (2, 3) else v.shape, v.dtype) for n, v in enumerate(params)]
    held += [pltpu.VMEM((2 * EACH, channels), F32), pltpu.SemaphoreType.DMA((len(params),))]
    back = pltpu.VMEM((OWN * channels, width), F32)
    mixed = pltpu.VMEM((2, OWN * channels, width), F32)
    kept = [((channels, 2 * EACH), F32), ((2 * OWN, width), F32)]
    send, gate, turned, columns, keep = call(first_kernel, projected + kept, held + [mixed], *params, place=pltpu.HBM)
    (send,) = call(functools.partial(triangle_kernel, False), summed, [], exchange_in_order(send, ORDERS[0][0]))
    send, gate, turned = call(middle_kernel, projected, [mixed, back], exchange_in_order(send, ORDERS[0][1]), turned, gate, columns, keep, pw, gw, ow)
    (send,) = call(functools.partial(triangle_kernel, True), summed, [], exchange_in_order(send, ORDERS[1][0]))
    (out,) = call(last_kernel, [(pair_rep.shape, BF16)], [back], exchange_in_order(send, ORDERS[1][1]), turned, gate, columns, ow)
    return out


def update(pair_t, pair_mask, u, incoming, peers, rows_of, pw, pb, gw, gb, ow, ob, ns, no):
    channels, positions = pair_t.shape
    width = positions // rows_of
    h = pw.shape[2] // 4
    count = peers[0] * peers[1]
    own = h // count
    normed = layer_norm(pair_t, ns[u, 0][:, None], no[u, 0][:, None]).astype(BF16)
    projected = over_rows(jnp.concatenate([pw[u], gw[u]], 1), normed) + jnp.concatenate([pb[u], gb[u]], 0)[:, None]
    parts = [projected[n * h : (n + 1) * h] for n in range(4)]
    gating = jax.nn.sigmoid(projected[4 * h :])
    mask = pair_mask.astype(F32).reshape(1, positions)
    left = (mask * jax.nn.sigmoid(parts[1]) * parts[0]).astype(BF16)
    right = (mask * jax.nn.sigmoid(parts[3]) * parts[2]).astype(BF16)
    sides = exchange(jnp.stack([v.reshape(count, own, rows_of, width) for v in (left, right)], 1))
    sides = sides.reshape(peers[0], peers[1], 2, own, rows_of, width)
    sides = sides.transpose(2, 3, 0, 4, 1, 5).reshape(2, own, peers[0] * rows_of, peers[1] * width)
    form = "cki,ckj->cij" if incoming else "cik,cjk->cij"
    summed = jnp.einsum(form, sides[0], sides[1], preferred_element_type=F32).astype(BF16)
    summed = summed.reshape(own, peers[0], rows_of, peers[1], width).transpose(1, 3, 0, 2, 4)
    summed = exchange(summed.reshape(count, own, rows_of, width)).reshape(h, positions).astype(F32)
    hidden = layer_norm(summed, ns[u, 1][:, None], no[u, 1][:, None]).astype(BF16)
    change = over_rows(ow[u], hidden) + ob[u][:, None]
    return (pair_t + gating * change).astype(BF16)


def plain_updates(peers, pair_rep, pair_mask, *params):
    rows_of, width, channels = pair_rep.shape
    pair_t = pair_rep.reshape(rows_of * width, channels).T
    for u in range(2):
        pair_t = update(pair_t.astype(F32), pair_mask, u, u == 1, peers, rows_of, *params)
    return pair_t.T.reshape(rows_of, width, channels)


def solution(mesh):
    peers = (mesh.shape["row"], mesh.shape["ka"])
    count = peers[0] * peers[1]

    def on_device(pair_rep, pair_mask, *params):
        rows_of, width, channels = pair_rep.shape
        hidden = params[0].shape[2] // 4
        fits = peers[1] == 1 and rows_of == OWN and hidden == OWN * count and count == 2 * len(ORDERS[0][0])
        if fits and channels == hidden == 128 and width % 128 == 0:
            return packed_updates(count, pair_rep, pair_mask, *params)
        return plain_updates(peers, pair_rep, pair_mask, *params)

    split = P(("grp", "row"), "ka", None)
    in_specs = (split, P(("grp", "row"), "ka")) + (P(),) * 8
    return jax.shard_map(on_device, mesh=mesh, in_specs=in_specs, out_specs=split, check_vma=False)
```

```python
import functools

import jax
import jax.numpy as jnp
from jax import lax
from jax.experimental import pallas as pl
from jax.experimental.pallas import tpu as pltpu
from jax.sharding import PartitionSpec as P

PEERS = ("row", "ka")
OWN = 4
ORDERS = (
    ((0, 13, 9, 5, 1, 15, 11, 7, 3, 14, 10, 6, 2, 12, 8, 4), (0, 13, 9, 5, 1, 15, 11, 7, 3, 14, 10, 6, 2, 12, 8, 4)),
    ((0, 13, 9, 5, 1, 15, 11, 7, 3, 14, 10, 6, 2, 12, 8, 4), (0, 15, 11, 14, 13, 10, 9, 7, 12, 5, 8, 6, 4, 3, 2, 1)),
)
EACH = 16
BF16, F32 = jnp.bfloat16, jnp.float32


def over_rows(a, b):
    return lax.dot_general(a, b, (((0,), (0,)), ((), ())), preferred_element_type=F32)


def over_columns(a, b):
    return lax.dot_general(a, b, (((1,), (1,)), ((), ())), preferred_element_type=F32)


def layer_norm(values, norm_gain, norm_bias):
    average = jnp.mean(values, 0, keepdims=True)
    centred = values - average
    variance = jnp.mean(centred * centred, 0, keepdims=True)
    return centred * lax.rsqrt(variance + 1e-05) * norm_gain + norm_bias


def pack(blocks):
    channels, width = blocks[0].shape
    tiles = [b.reshape(channels // 8, 8, width) for b in blocks]
    turned = [pltpu.roll(b, 4, axis=0).reshape(channels // 8, 8, width) for b in blocks]
    low = lax.broadcasted_iota(jnp.int32, tiles[0].shape, 1) < 4
    back = [pltpu.roll(b, channels - 4, axis=0).reshape(channels // 8, 8, width) for b in blocks]
    even = [jnp.where(low, tiles[n], turned[n + 1]) for n in (0, 2)]
    odd = [jnp.where(low, back[n], tiles[n + 1]) for n in (0, 2)]
    return jnp.stack([jnp.stack(even, 1), jnp.stack(odd, 1)], 1).reshape(channels // 4, 16, width)


def unpack(packed):
    count, _, width = packed.shape
    tiles = packed.reshape(count // 2, 2, 2, 8, width)
    low = lax.broadcasted_iota(jnp.int32, (count // 2, 8, width), 1) < 4
    blocks = []
    for n in range(2):
        even, odd = tiles[:, 0, n], tiles[:, 1, n]
        down = pltpu.roll(odd.reshape(count * 4, width), 4, axis=0).reshape(even.shape)
        up = pltpu.roll(even.reshape(count * 4, width), count * 4 - 4, axis=0).reshape(even.shape)
        blocks.append(jnp.where(low, even, down).reshape(count * 4, width))
        blocks.append(jnp.where(low, up, odd).reshape(count * 4, width))
    return blocks


def broadcast_columns(columns, first, many, width):
    held = columns[...]
    return [jnp.broadcast_to(held[:, n : n + 1], (held.shape[0], width)) for n in range(first, first + many)]


def project(u, z, mask, proj_weight, gate_weight, columns, send, gate, mixed):
    width = z[0].shape[1]
    h = proj_weight.shape[1] // 4
    rows = mixed.shape[1]
    gain, offset, *biases = broadcast_columns(columns, u * EACH, 7, width)
    scales = (1.0, 0.5, 1.0, 0.5, 0.5)
    biases = [b * k for b, k in zip(biases, scales)]
    turned = [proj_weight[:, n * h : (n + 1) * h] for n in range(4)] + [gate_weight]
    turned = [(w * jnp.asarray(k, BF16)).T if k != 1.0 else w.T for w, k in zip(turned, scales)]
    pairs = []
    for pair in range(0, OWN, 2):
        normed = [layer_norm(z[i], gain, offset).astype(BF16) for i in (pair, pair + 1)]
        pairs.append(jnp.concatenate(normed, 1))
    for side in range(2):
        for pair, normed in enumerate(pairs):
            value, gating = [jnp.dot(turned[2 * side + n], normed, preferred_element_type=F32) for n in range(2)]
            for n in range(2):
                i, at = 2 * pair + n, slice(n * width, (n + 1) * width)
                half = mask[i : i + 1, :] * 0.5
                weight = jnp.tanh(gating[:, at] + biases[2 * side + 1]) * half + half
                mixed[side, pl.ds(i, h, stride=OWN), :] = weight * (value[:, at] + biases[2 * side])
    for side in range(2):
        send[:, side * 16 : (side + 1) * 16, :] = mixed[side].reshape(rows // 16, 16, width).astype(BF16)
    for pair, normed in enumerate(pairs):
        gating = jnp.dot(turned[4], normed, preferred_element_type=F32)
        for n in range(2):
            i = 2 * pair + n
            gate[:, i * width : (i + 1) * width] = 0.5 * jnp.tanh(gating[:, n * width : (n + 1) * width] + biases[4]) + 0.5


def finish(u, z, summed, gate, out_weight, columns, mixed):
    width = z[0].shape[1]
    gain, offset, bias = broadcast_columns(columns, u * EACH + 7, 3, width)
    turned = out_weight.T
    mixed[...] = summed[...].astype(F32).reshape(mixed.shape)
    results = []
    for pair in range(0, OWN, 2):
        blocks = [mixed[pl.ds(i, mixed.shape[0] // OWN, stride=OWN), :] for i in (pair, pair + 1)]
        blocks = [reorder(v, ORDERS[u][1], ORDERS[u][0]) for v in blocks]
        hidden = jnp.concatenate([layer_norm(v, gain, offset).astype(BF16) for v in blocks], 1)
        both = jnp.dot(turned, hidden, preferred_element_type=F32)
        for n in range(2):
            change = both[:, n * width : (n + 1) * width] + bias
            at = slice((pair + n) * width, (pair + n + 1) * width)
            results.append((z[pair + n].astype(F32) + gate[:, at] * change).astype(BF16))
    return results


def first_kernel(
    pair, mask, pw, gw, pb, gb, ob, ns, no, send, gate, turned, columns, keep, pair_in, mask_in, pw_in, gw_in, pb_in, gb_in, ob_in, ns_in, no_in, rows, arrived, mixed
):
    moves = [(pair, pair_in), (pb, pb_in), (gb, gb_in), (ob, ob_in), (ns, ns_in), (no, no_in)]
    moves += [(pw.at[0], pw_in), (gw.at[0], gw_in), (mask, mask_in)]
    moves = [pltpu.make_async_copy(a, b, arrived.at[n]) for n, (a, b) in enumerate(moves)]
    for move in moves:
        move.start()
    for move in moves:
        move.wait()
    width = pair.shape[1]
    z = [pair_in[i].T for i in range(OWN)]
    for i in range(OWN):
        turned[:, i * width : (i + 1) * width] = z[i]
    h = pw.shape[2] // 4
    for u in range(2):
        found = [ns_in[u, 0:1, :], no_in[u, 0:1, :]] + [pb_in[u : u + 1, n * h : (n + 1) * h] for n in range(4)]
        found += [gb_in[u : u + 1, :], ns_in[u, 1:2, :], no_in[u, 1:2, :], ob_in[u : u + 1, :]]
        for n, row in enumerate(found):
            rows[u * EACH + n : u * EACH + n + 1, :] = row
    columns[...] = rows[...].T
    keep[0:OWN, :] = mask_in[...].astype(F32)
    project(0, [v.astype(F32) for v in z], keep, pw_in[...], gw_in[...], columns, send, gate, mixed)


def middle_kernel(summed, old, old_gate, columns, keep, pw, gw, ow, send, gate, turned, mixed, mixed_back):
    width = keep.shape[1]
    z = finish(0, [old[:, i * width : (i + 1) * width] for i in range(OWN)], summed, old_gate, ow[0], columns, mixed_back)
    for i in range(OWN):
        turned[:, i * width : (i + 1) * width] = z[i]
    project(1, [v.astype(F32) for v in z], keep, pw[1], gw[1], columns, send, gate, mixed)


def last_kernel(summed, old, old_gate, columns, ow, out, mixed_back):
    width = out.shape[1]
    z = finish(1, [old[:, i * width : (i + 1) * width] for i in range(OWN)], summed, old_gate, ow[1], columns, mixed_back)
    for i in range(OWN):
        out[i] = z[i].T


def reorder(values, have, want):
    tiles = values.reshape(len(have), 2 * OWN, values.shape[1])
    places = [have.index(chip) for chip in want]
    return jnp.concatenate([tiles[n : n + 1] for n in places]).reshape(values.shape)


def triangle_kernel(incoming, sides, out):
    come, go = ORDERS[1 if incoming else 0]
    in_mesh = tuple(range(len(come)))
    left, right = [unpack(sides[:, n : n + 16, :].astype(F32)) for n in (0, 16)]
    if incoming:
        summed = [over_rows(a.astype(BF16), b.astype(BF16)) for a, b in zip(left, right)]
        summed = [reorder(v, in_mesh, go) for v in summed]
    else:
        left = [reorder(v, come, go) for v in left]
        right = [reorder(v, come, in_mesh) for v in right]
        summed = [over_columns(a.astype(BF16), b.astype(BF16)) for a, b in zip(left, right)]
    out[...] = pack(summed).astype(BF16)


def call(kernel, outs, scratch, *args, place=pltpu.VMEM):
    in_vmem = pl.BlockSpec(memory_space=pltpu.VMEM)
    return pl.pallas_call(
        kernel,
        out_shape=[jax.ShapeDtypeStruct(*o) for o in outs],
        in_specs=[pl.BlockSpec(memory_space=place)] * len(args),
        out_specs=[in_vmem] * len(outs),
        scratch_shapes=scratch,
        compiler_params=pltpu.CompilerParams(vmem_limit_bytes=24 * 2**20),
    )(*args)


def exchange(blocks):
    return lax.all_to_all(blocks, PEERS, split_axis=0, concat_axis=0, tiled=True)


def exchange_in_order(blocks, chips):
    listed = [[2 * chip + core for chip in chips for core in range(2)]]
    return lax.all_to_all(blocks, "row", split_axis=0, concat_axis=0, axis_index_groups=listed, tiled=True)


def packed_updates(count, pair_rep, pair_mask, pw, pb, gw, gb, ow, ob, ns, no):
    rows_of, width, channels = pair_rep.shape
    flat = (channels, rows_of * width)
    projected = [((count, 32, width), BF16), (flat, F32), (flat, BF16)]
    summed = [((count, 16, width), BF16)]
    params = [pair_rep, pair_mask, pw, gw, pb, gb, ob, ns, no]
    params = [pltpu.with_memory_space_constraint(v, pltpu.HBM) for v in params]
    held = [pltpu.VMEM(v.shape[1:] if n in (2, 3) else v.shape, v.dtype) for n, v in enumerate(params)]
    held += [pltpu.VMEM((2 * EACH, channels), F32), pltpu.SemaphoreType.DMA((len(params),))]
    back = pltpu.VMEM((OWN * channels, width), F32)
    mixed = pltpu.VMEM((2, OWN * channels, width), F32)
    kept = [((channels, 2 * EACH), F32), ((2 * OWN, width), F32)]
    send, gate, turned, columns, keep = call(first_kernel, projected + kept, held + [mixed], *params, place=pltpu.HBM)
    (send,) = call(functools.partial(triangle_kernel, False), summed, [], exchange_in_order(send, ORDERS[0][0]))
    send, gate, turned = call(middle_kernel, projected, [mixed, back], exchange_in_order(send, ORDERS[0][1]), turned, gate, columns, keep, pw, gw, ow)
    (send,) = call(functools.partial(triangle_kernel, True), summed, [], exchange_in_order(send, ORDERS[1][0]))
    (out,) = call(last_kernel, [(pair_rep.shape, BF16)], [back], exchange_in_order(send, ORDERS[1][1]), turned, gate, columns, ow)
    return out


def update(pair_t, pair_mask, u, incoming, peers, rows_of, pw, pb, gw, gb, ow, ob, ns, no):
    channels, positions = pair_t.shape
    width = positions // rows_of
    h = pw.shape[2] // 4
    count = peers[0] * peers[1]
    own = h // count
    normed = layer_norm(pair_t, ns[u, 0][:, None], no[u, 0][:, None]).astype(BF16)
    projected = over_rows(jnp.concatenate([pw[u], gw[u]], 1), normed) + jnp.concatenate([pb[u], gb[u]], 0)[:, None]
    parts = [projected[n * h : (n + 1) * h] for n in range(4)]
    gating = jax.nn.sigmoid(projected[4 * h :])
    mask = pair_mask.astype(F32).reshape(1, positions)
    left = (mask * jax.nn.sigmoid(parts[1]) * parts[0]).astype(BF16)
    right = (mask * jax.nn.sigmoid(parts[3]) * parts[2]).astype(BF16)
    sides = exchange(jnp.stack([v.reshape(count, own, rows_of, width) for v in (left, right)], 1))
    sides = sides.reshape(peers[0], peers[1], 2, own, rows_of, width)
    sides = sides.transpose(2, 3, 0, 4, 1, 5).reshape(2, own, peers[0] * rows_of, peers[1] * width)
    form = "cki,ckj->cij" if incoming else "cik,cjk->cij"
    summed = jnp.einsum(form, sides[0], sides[1], preferred_element_type=F32).astype(BF16)
    summed = summed.reshape(own, peers[0], rows_of, peers[1], width).transpose(1, 3, 0, 2, 4)
    summed = exchange(summed.reshape(count, own, rows_of, width)).reshape(h, positions).astype(F32)
    hidden = layer_norm(summed, ns[u, 1][:, None], no[u, 1][:, None]).astype(BF16)
    change = over_rows(ow[u], hidden) + ob[u][:, None]
    return (pair_t + gating * change).astype(BF16)


def plain_updates(peers, pair_rep, pair_mask, *params):
    rows_of, width, channels = pair_rep.shape
    pair_t = pair_rep.reshape(rows_of * width, channels).T
    for u in range(2):
        pair_t = update(pair_t.astype(F32), pair_mask, u, u == 1, peers, rows_of, *params)
    return pair_t.T.reshape(rows_of, width, channels)


def solution(mesh):
    peers = (mesh.shape["row"], mesh.shape["ka"])
    count = peers[0] * peers[1]

    def on_device(pair_rep, pair_mask, *params):
        rows_of, width, channels = pair_rep.shape
        hidden = params[0].shape[2] // 4
        fits = peers[1] == 1 and rows_of == OWN and hidden == OWN * count and count == 2 * len(ORDERS[0][0])
        if fits and channels == hidden == 128 and width % 128 == 0:
            return packed_updates(count, pair_rep, pair_mask, *params)
        return plain_updates(peers, pair_rep, pair_mask, *params)

    split = P(("grp", "row"), "ka", None)
    in_specs = (split, P(("grp", "row"), "ka")) + (P(),) * 8
    return jax.shard_map(on_device, mesh=mesh, in_specs=in_specs, out_specs=split, check_vma=False)
```

```python
import functools

import jax
import jax.numpy as jnp
from jax import lax
from jax.experimental import pallas as pl
from jax.experimental.pallas import tpu as pltpu
from jax.sharding import PartitionSpec as P

PEERS = ("row", "ka")
OWN = 4
ORDERS = (
    ((0, 15, 14, 11, 10, 7, 6, 3, 2, 13, 12, 9, 8, 5, 4, 1), (0, 15, 14, 11, 10, 7, 6, 3, 2, 13, 12, 9, 8, 5, 4, 1)),
    ((0, 15, 14, 11, 10, 7, 6, 3, 2, 13, 12, 9, 8, 5, 4, 1), (0, 15, 11, 14, 13, 10, 9, 7, 12, 5, 8, 6, 4, 3, 2, 1)),
)
EACH = 16
BF16, F32 = jnp.bfloat16, jnp.float32


def over_rows(a, b):
    return lax.dot_general(a, b, (((0,), (0,)), ((), ())), preferred_element_type=F32)


def over_columns(a, b):
    return lax.dot_general(a, b, (((1,), (1,)), ((), ())), preferred_element_type=F32)


def layer_norm(values, norm_gain, norm_bias):
    average = jnp.mean(values, 0, keepdims=True)
    centred = values - average
    variance = jnp.mean(centred * centred, 0, keepdims=True)
    return centred * lax.rsqrt(variance + 1e-05) * norm_gain + norm_bias


def pack(blocks):
    channels, width = blocks[0].shape
    tiles = [b.reshape(channels // 8, 8, width) for b in blocks]
    turned = [pltpu.roll(b, 4, axis=0).reshape(channels // 8, 8, width) for b in blocks]
    low = lax.broadcasted_iota(jnp.int32, tiles[0].shape, 1) < 4
    back = [pltpu.roll(b, channels - 4, axis=0).reshape(channels // 8, 8, width) for b in blocks]
    even = [jnp.where(low, tiles[n], turned[n + 1]) for n in (0, 2)]
    odd = [jnp.where(low, back[n], tiles[n + 1]) for n in (0, 2)]
    return jnp.stack([jnp.stack(even, 1), jnp.stack(odd, 1)], 1).reshape(channels // 4, 16, width)


def unpack(packed):
    count, _, width = packed.shape
    tiles = packed.reshape(count // 2, 2, 2, 8, width)
    low = lax.broadcasted_iota(jnp.int32, (count // 2, 8, width), 1) < 4
    blocks = []
    for n in range(2):
        even, odd = tiles[:, 0, n], tiles[:, 1, n]
        down = pltpu.roll(odd.reshape(count * 4, width), 4, axis=0).reshape(even.shape)
        up = pltpu.roll(even.reshape(count * 4, width), count * 4 - 4, axis=0).reshape(even.shape)
        blocks.append(jnp.where(low, even, down).reshape(count * 4, width))
        blocks.append(jnp.where(low, up, odd).reshape(count * 4, width))
    return blocks


def broadcast_columns(columns, first, many, width):
    held = columns[...]
    return [jnp.broadcast_to(held[:, n : n + 1], (held.shape[0], width)) for n in range(first, first + many)]


def project(u, z, mask, proj_weight, gate_weight, columns, send, gate, mixed):
    width = z[0].shape[1]
    h = proj_weight.shape[1] // 4
    rows = mixed.shape[1]
    gain, offset, *biases = broadcast_columns(columns, u * EACH, 7, width)
    scales = (1.0, 0.5, 1.0, 0.5, 0.5)
    biases = [b * k for b, k in zip(biases, scales)]
    turned = [proj_weight[:, n * h : (n + 1) * h] for n in range(4)] + [gate_weight]
    turned = [(w * jnp.asarray(k, BF16)).T if k != 1.0 else w.T for w, k in zip(turned, scales)]
    pairs = []
    for pair in range(0, OWN, 2):
        normed = [layer_norm(z[i], gain, offset).astype(BF16) for i in (pair, pair + 1)]
        pairs.append(jnp.concatenate(normed, 1))
    for side in range(2):
        for pair, normed in enumerate(pairs):
            value, gating = [jnp.dot(turned[2 * side + n], normed, preferred_element_type=F32) for n in range(2)]
            for n in range(2):
                i, at = 2 * pair + n, slice(n * width, (n + 1) * width)
                half = mask[i : i + 1, :] * 0.5
                weight = jnp.tanh(gating[:, at] + biases[2 * side + 1]) * half + half
                mixed[side, pl.ds(i, h, stride=OWN), :] = weight * (value[:, at] + biases[2 * side])
    for side in range(2):
        send[:, side * 16 : (side + 1) * 16, :] = mixed[side].reshape(rows // 16, 16, width).astype(BF16)
    for pair, normed in enumerate(pairs):
        gating = jnp.dot(turned[4], normed, preferred_element_type=F32)
        for n in range(2):
            i = 2 * pair + n
            gate[:, i * width : (i + 1) * width] = 0.5 * jnp.tanh(gating[:, n * width : (n + 1) * width] + biases[4]) + 0.5


def finish(u, z, summed, gate, out_weight, columns, mixed):
    width = z[0].shape[1]
    gain, offset, bias = broadcast_columns(columns, u * EACH + 7, 3, width)
    turned = out_weight.T
    mixed[...] = summed[...].astype(F32).reshape(mixed.shape)
    results = []
    for pair in range(0, OWN, 2):
        blocks = [mixed[pl.ds(i, mixed.shape[0] // OWN, stride=OWN), :] for i in (pair, pair + 1)]
        blocks = [reorder(v, ORDERS[u][1], ORDERS[u][0]) for v in blocks]
        hidden = jnp.concatenate([layer_norm(v, gain, offset).astype(BF16) for v in blocks], 1)
        both = jnp.dot(turned, hidden, preferred_element_type=F32)
        for n in range(2):
            change = both[:, n * width : (n + 1) * width] + bias
            at = slice((pair + n) * width, (pair + n + 1) * width)
            results.append((z[pair + n].astype(F32) + gate[:, at] * change).astype(BF16))
    return results


def first_kernel(
    pair, mask, pw, gw, pb, gb, ob, ns, no, send, gate, turned, columns, keep, pair_in, mask_in, pw_in, gw_in, pb_in, gb_in, ob_in, ns_in, no_in, rows, arrived, mixed
):
    moves = [(pair, pair_in), (pb, pb_in), (gb, gb_in), (ob, ob_in), (ns, ns_in), (no, no_in)]
    moves += [(pw.at[0], pw_in), (gw.at[0], gw_in), (mask, mask_in)]
    moves = [pltpu.make_async_copy(a, b, arrived.at[n]) for n, (a, b) in enumerate(moves)]
    for move in moves:
        move.start()
    for move in moves:
        move.wait()
    width = pair.shape[1]
    z = [pair_in[i].T for i in range(OWN)]
    for i in range(OWN):
        turned[:, i * width : (i + 1) * width] = z[i]
    h = pw.shape[2] // 4
    for u in range(2):
        found = [ns_in[u, 0:1, :], no_in[u, 0:1, :]] + [pb_in[u : u + 1, n * h : (n + 1) * h] for n in range(4)]
        found += [gb_in[u : u + 1, :], ns_in[u, 1:2, :], no_in[u, 1:2, :], ob_in[u : u + 1, :]]
        for n, row in enumerate(found):
            rows[u * EACH + n : u * EACH + n + 1, :] = row
    columns[...] = rows[...].T
    keep[0:OWN, :] = mask_in[...].astype(F32)
    project(0, [v.astype(F32) for v in z], keep, pw_in[...], gw_in[...], columns, send, gate, mixed)


def middle_kernel(summed, old, old_gate, columns, keep, pw, gw, ow, send, gate, turned, mixed, mixed_back):
    width = keep.shape[1]
    z = finish(0, [old[:, i * width : (i + 1) * width] for i in range(OWN)], summed, old_gate, ow[0], columns, mixed_back)
    for i in range(OWN):
        turned[:, i * width : (i + 1) * width] = z[i]
    project(1, [v.astype(F32) for v in z], keep, pw[1], gw[1], columns, send, gate, mixed)


def last_kernel(summed, old, old_gate, columns, ow, out, mixed_back):
    width = out.shape[1]
    z = finish(1, [old[:, i * width : (i + 1) * width] for i in range(OWN)], summed, old_gate, ow[1], columns, mixed_back)
    for i in range(OWN):
        out[i] = z[i].T


def reorder(values, have, want):
    tiles = values.reshape(len(have), 2 * OWN, values.shape[1])
    places = [have.index(chip) for chip in want]
    return jnp.concatenate([tiles[n : n + 1] for n in places]).reshape(values.shape)


def triangle_kernel(incoming, sides, out):
    come, go = ORDERS[1 if incoming else 0]
    in_mesh = tuple(range(len(come)))
    left, right = [unpack(sides[:, n : n + 16, :].astype(F32)) for n in (0, 16)]
    if incoming:
        summed = [over_rows(a.astype(BF16), b.astype(BF16)) for a, b in zip(left, right)]
        summed = [reorder(v, in_mesh, go) for v in summed]
    else:
        left = [reorder(v, come, go) for v in left]
        right = [reorder(v, come, in_mesh) for v in right]
        summed = [over_columns(a.astype(BF16), b.astype(BF16)) for a, b in zip(left, right)]
    out[...] = pack(summed).astype(BF16)


def call(kernel, outs, scratch, *args, place=pltpu.VMEM):
    in_vmem = pl.BlockSpec(memory_space=pltpu.VMEM)
    return pl.pallas_call(
        kernel,
        out_shape=[jax.ShapeDtypeStruct(*o) for o in outs],
        in_specs=[pl.BlockSpec(memory_space=place)] * len(args),
        out_specs=[in_vmem] * len(outs),
        scratch_shapes=scratch,
        compiler_params=pltpu.CompilerParams(vmem_limit_bytes=24 * 2**20),
    )(*args)


def exchange(blocks):
    return lax.all_to_all(blocks, PEERS, split_axis=0, concat_axis=0, tiled=True)


def exchange_in_order(blocks, chips):
    listed = [[2 * chip + core for chip in chips for core in range(2)]]
    return lax.all_to_all(blocks, "row", split_axis=0, concat_axis=0, axis_index_groups=listed, tiled=True)


def packed_updates(count, pair_rep, pair_mask, pw, pb, gw, gb, ow, ob, ns, no):
    rows_of, width, channels = pair_rep.shape
    flat = (channels, rows_of * width)
    projected = [((count, 32, width), BF16), (flat, F32), (flat, BF16)]
    summed = [((count, 16, width), BF16)]
    params = [pair_rep, pair_mask, pw, gw, pb, gb, ob, ns, no]
    params = [pltpu.with_memory_space_constraint(v, pltpu.HBM) for v in params]
    held = [pltpu.VMEM(v.shape[1:] if n in (2, 3) else v.shape, v.dtype) for n, v in enumerate(params)]
    held += [pltpu.VMEM((2 * EACH, channels), F32), pltpu.SemaphoreType.DMA((len(params),))]
    back = pltpu.VMEM((OWN * channels, width), F32)
    mixed = pltpu.VMEM((2, OWN * channels, width), F32)
    kept = [((channels, 2 * EACH), F32), ((2 * OWN, width), F32)]
    send, gate, turned, columns, keep = call(first_kernel, projected + kept, held + [mixed], *params, place=pltpu.HBM)
    (send,) = call(functools.partial(triangle_kernel, False), summed, [], exchange_in_order(send, ORDERS[0][0]))
    send, gate, turned = call(middle_kernel, projected, [mixed, back], exchange_in_order(send, ORDERS[0][1]), turned, gate, columns, keep, pw, gw, ow)
    (send,) = call(functools.partial(triangle_kernel, True), summed, [], exchange_in_order(send, ORDERS[1][0]))
    (out,) = call(last_kernel, [(pair_rep.shape, BF16)], [back], exchange_in_order(send, ORDERS[1][1]), turned, gate, columns, ow)
    return out


def update(pair_t, pair_mask, u, incoming, peers, rows_of, pw, pb, gw, gb, ow, ob, ns, no):
    channels, positions = pair_t.shape
    width = positions // rows_of
    h = pw.shape[2] // 4
    count = peers[0] * peers[1]
    own = h // count
    normed = layer_norm(pair_t, ns[u, 0][:, None], no[u, 0][:, None]).astype(BF16)
    projected = over_rows(jnp.concatenate([pw[u], gw[u]], 1), normed) + jnp.concatenate([pb[u], gb[u]], 0)[:, None]
    parts = [projected[n * h : (n + 1) * h] for n in range(4)]
    gating = jax.nn.sigmoid(projected[4 * h :])
    mask = pair_mask.astype(F32).reshape(1, positions)
    left = (mask * jax.nn.sigmoid(parts[1]) * parts[0]).astype(BF16)
    right = (mask * jax.nn.sigmoid(parts[3]) * parts[2]).astype(BF16)
    sides = exchange(jnp.stack([v.reshape(count, own, rows_of, width) for v in (left, right)], 1))
    sides = sides.reshape(peers[0], peers[1], 2, own, rows_of, width)
    sides = sides.transpose(2, 3, 0, 4, 1, 5).reshape(2, own, peers[0] * rows_of, peers[1] * width)
    form = "cki,ckj->cij" if incoming else "cik,cjk->cij"
    summed = jnp.einsum(form, sides[0], sides[1], preferred_element_type=F32).astype(BF16)
    summed = summed.reshape(own, peers[0], rows_of, peers[1], width).transpose(1, 3, 0, 2, 4)
    summed = exchange(summed.reshape(count, own, rows_of, width)).reshape(h, positions).astype(F32)
    hidden = layer_norm(summed, ns[u, 1][:, None], no[u, 1][:, None]).astype(BF16)
    change = over_rows(ow[u], hidden) + ob[u][:, None]
    return (pair_t + gating * change).astype(BF16)


def plain_updates(peers, pair_rep, pair_mask, *params):
    rows_of, width, channels = pair_rep.shape
    pair_t = pair_rep.reshape(rows_of * width, channels).T
    for u in range(2):
        pair_t = update(pair_t.astype(F32), pair_mask, u, u == 1, peers, rows_of, *params)
    return pair_t.T.reshape(rows_of, width, channels)


def solution(mesh):
    peers = (mesh.shape["row"], mesh.shape["ka"])
    count = peers[0] * peers[1]

    def on_device(pair_rep, pair_mask, *params):
        rows_of, width, channels = pair_rep.shape
        hidden = params[0].shape[2] // 4
        fits = peers[1] == 1 and rows_of == OWN and hidden == OWN * count and count == 2 * len(ORDERS[0][0])
        if fits and channels == hidden == 128 and width % 128 == 0:
            return packed_updates(count, pair_rep, pair_mask, *params)
        return plain_updates(peers, pair_rep, pair_mask, *params)

    split = P(("grp", "row"), "ka", None)
    in_specs = (split, P(("grp", "row"), "ka")) + (P(),) * 8
    return jax.shard_map(on_device, mesh=mesh, in_specs=in_specs, out_specs=split, check_vma=False)
```

```python
import functools

import jax
import jax.numpy as jnp
from jax import lax
from jax.experimental import pallas as pl
from jax.experimental.pallas import tpu as pltpu
from jax.sharding import PartitionSpec as P

PEERS = ("row", "ka")
OWN = 4
ORDERS = (
    ((15, 11, 7, 3, 14, 10, 6, 2, 13, 9, 5, 1, 12, 8, 4, 0), (15, 11, 7, 3, 14, 10, 6, 2, 13, 9, 5, 1, 12, 8, 4, 0)),
    ((15, 11, 7, 3, 14, 10, 6, 2, 13, 9, 5, 1, 12, 8, 4, 0), (15, 11, 7, 3, 14, 10, 6, 2, 13, 9, 5, 1, 12, 8, 4, 0)),
)
EACH = 16
BF16, F32 = jnp.bfloat16, jnp.float32


def over_rows(a, b):
    return lax.dot_general(a, b, (((0,), (0,)), ((), ())), preferred_element_type=F32)


def over_columns(a, b):
    return lax.dot_general(a, b, (((1,), (1,)), ((), ())), preferred_element_type=F32)


def layer_norm(values, norm_gain, norm_bias):
    average = jnp.mean(values, 0, keepdims=True)
    centred = values - average
    variance = jnp.mean(centred * centred, 0, keepdims=True)
    return centred * lax.rsqrt(variance + 1e-05) * norm_gain + norm_bias


def pack(blocks):
    rows, width = blocks[0].shape
    tiles = [b.reshape(rows // 8, 8, width) for b in blocks]
    turned = [pltpu.roll(b, 4, axis=0).reshape(rows // 8, 8, width) for b in blocks]
    low = lax.broadcasted_iota(jnp.int32, tiles[0].shape, 1) < 4
    back = [pltpu.roll(b, rows - 4, axis=0).reshape(rows // 8, 8, width) for b in blocks]
    first = [jnp.where(low, tiles[n], turned[n + 1]) for n in (0, 2)]
    second = [jnp.where(low, back[n], tiles[n + 1]) for n in (0, 2)]
    grouped = (rows // 32, 4, 2, 8, width)
    return jnp.stack([jnp.stack(v, 1).reshape(grouped) for v in (first, second)], 1).reshape(rows // 4, 16, width)


def unpack(packed):
    count, _, width = packed.shape
    tiles = packed.reshape(count // 8, 2, 4, 2, 8, width)
    low = lax.broadcasted_iota(jnp.int32, (count // 2, 8, width), 1) < 4
    blocks = []
    for n in range(2):
        first, second = [tiles[:, core, :, n].reshape(count // 2, 8, width) for core in range(2)]
        down = pltpu.roll(second.reshape(count * 4, width), 4, axis=0).reshape(first.shape)
        up = pltpu.roll(first.reshape(count * 4, width), count * 4 - 4, axis=0).reshape(first.shape)
        blocks.append(jnp.where(low, first, down).reshape(count * 4, width))
        blocks.append(jnp.where(low, up, second).reshape(count * 4, width))
    return blocks


def broadcast_columns(columns, first, many, width):
    held = columns[...]
    return [jnp.broadcast_to(held[:, n : n + 1], (held.shape[0], width)) for n in range(first, first + many)]


def project(u, z, mask, proj_weight, gate_weight, columns, send, gate, mixed):
    width = z[0].shape[1]
    h = proj_weight.shape[1] // 4
    rows = mixed.shape[1]
    gain, offset, *biases = broadcast_columns(columns, u * EACH, 7, width)
    scales = (1.0, 0.5, 1.0, 0.5, 0.5)
    biases = [b * k for b, k in zip(biases, scales)]
    turned = [proj_weight[:, n * h : (n + 1) * h] for n in range(4)] + [gate_weight]
    turned = [(w * jnp.asarray(k, BF16)).T if k != 1.0 else w.T for w, k in zip(turned, scales)]
    pairs = []
    for pair in range(0, OWN, 2):
        normed = [layer_norm(z[i], gain, offset).astype(BF16) for i in (pair, pair + 1)]
        pairs.append(jnp.concatenate(normed, 1))
    for side in range(2):
        for pair, normed in enumerate(pairs):
            value, gating = [jnp.dot(turned[2 * side + n], normed, preferred_element_type=F32) for n in range(2)]
            for n in range(2):
                i, at = 2 * pair + n, slice(n * width, (n + 1) * width)
                half = mask[i : i + 1, :] * 0.5
                weight = jnp.tanh(gating[:, at] + biases[2 * side + 1]) * half + half
                mixed[side, pl.ds(i, h, stride=OWN), :] = weight * (value[:, at] + biases[2 * side])
    for side in range(2):
        send[:, side * 16 : (side + 1) * 16, :] = mixed[side].reshape(rows // 16, 16, width).astype(BF16)
    for pair, normed in enumerate(pairs):
        gating = jnp.dot(turned[4], normed, preferred_element_type=F32)
        for n in range(2):
            i = 2 * pair + n
            gate[:, i * width : (i + 1) * width] = 0.5 * jnp.tanh(gating[:, n * width : (n + 1) * width] + biases[4]) + 0.5


def finish(u, z, summed, gate, out_weight, columns, mixed):
    width = z[0].shape[1]
    gain, offset, bias = broadcast_columns(columns, u * EACH + 7, 3, width)
    turned = out_weight.T
    mixed[...] = summed[...].astype(F32).reshape(mixed.shape)
    results = []
    for pair in range(0, OWN, 2):
        blocks = [mixed[pl.ds(i, mixed.shape[0] // OWN, stride=OWN), :] for i in (pair, pair + 1)]
        blocks = [reorder(v, ORDERS[u][1], ORDERS[u][0]) for v in blocks]
        hidden = jnp.concatenate([layer_norm(v, gain, offset).astype(BF16) for v in blocks], 1)
        both = jnp.dot(turned, hidden, preferred_element_type=F32)
        for n in range(2):
            change = both[:, n * width : (n + 1) * width] + bias
            at = slice((pair + n) * width, (pair + n + 1) * width)
            results.append((z[pair + n].astype(F32) + gate[:, at] * change).astype(BF16))
    return results


def first_kernel(
    pair, mask, pw, gw, pb, gb, ob, ns, no, send, gate, turned, columns, keep, pair_in, mask_in, pw_in, gw_in, pb_in, gb_in, ob_in, ns_in, no_in, rows, arrived, mixed
):
    moves = [(pair, pair_in), (pb, pb_in), (gb, gb_in), (ob, ob_in), (ns, ns_in), (no, no_in)]
    moves += [(pw.at[0], pw_in), (gw.at[0], gw_in), (mask, mask_in)]
    moves = [pltpu.make_async_copy(a, b, arrived.at[n]) for n, (a, b) in enumerate(moves)]
    for move in moves:
        move.start()
    for move in moves:
        move.wait()
    width = pair.shape[1]
    z = [pair_in[i].T for i in range(OWN)]
    for i in range(OWN):
        turned[:, i * width : (i + 1) * width] = z[i]
    h = pw.shape[2] // 4
    for u in range(2):
        found = [ns_in[u, 0:1, :], no_in[u, 0:1, :]] + [pb_in[u : u + 1, n * h : (n + 1) * h] for n in range(4)]
        found += [gb_in[u : u + 1, :], ns_in[u, 1:2, :], no_in[u, 1:2, :], ob_in[u : u + 1, :]]
        for n, row in enumerate(found):
            rows[u * EACH + n : u * EACH + n + 1, :] = row
    columns[...] = rows[...].T
    keep[0:OWN, :] = mask_in[...].astype(F32)
    project(0, [v.astype(F32) for v in z], keep, pw_in[...], gw_in[...], columns, send, gate, mixed)


def middle_kernel(summed, old, old_gate, columns, keep, pw, gw, ow, send, gate, turned, mixed, mixed_back):
    width = keep.shape[1]
    z = finish(0, [old[:, i * width : (i + 1) * width] for i in range(OWN)], summed, old_gate, ow[0], columns, mixed_back)
    for i in range(OWN):
        turned[:, i * width : (i + 1) * width] = z[i]
    project(1, [v.astype(F32) for v in z], keep, pw[1], gw[1], columns, send, gate, mixed)


def last_kernel(summed, old, old_gate, columns, ow, out, mixed_back):
    width = out.shape[1]
    z = finish(1, [old[:, i * width : (i + 1) * width] for i in range(OWN)], summed, old_gate, ow[1], columns, mixed_back)
    for i in range(OWN):
        out[i] = z[i].T


def reorder(values, have, want):
    tiles = values.reshape(len(have), 2 * OWN, values.shape[1])
    places = [have.index(chip) for chip in want]
    return jnp.concatenate([tiles[n : n + 1] for n in places]).reshape(values.shape)


def triangle_kernel(incoming, sides, out):
    come, go = ORDERS[1 if incoming else 0]
    in_mesh = tuple(range(len(come)))
    left, right = [unpack(sides[:, n : n + 16, :].astype(F32)) for n in (0, 16)]
    if incoming:
        summed = [over_rows(a.astype(BF16), b.astype(BF16)) for a, b in zip(left, right)]
        summed = [reorder(v, in_mesh, go) for v in summed]
    else:
        left = [reorder(v, come, go) for v in left]
        right = [reorder(v, come, in_mesh) for v in right]
        summed = [over_columns(a.astype(BF16), b.astype(BF16)) for a, b in zip(left, right)]
    out[...] = pack(summed).astype(BF16)


def call(kernel, outs, scratch, *args, place=pltpu.VMEM):
    in_vmem = pl.BlockSpec(memory_space=pltpu.VMEM)
    return pl.pallas_call(
        kernel,
        out_shape=[jax.ShapeDtypeStruct(*o) for o in outs],
        in_specs=[pl.BlockSpec(memory_space=place)] * len(args),
        out_specs=[in_vmem] * len(outs),
        scratch_shapes=scratch,
        compiler_params=pltpu.CompilerParams(vmem_limit_bytes=24 * 2**20),
    )(*args)


def exchange(blocks):
    return lax.all_to_all(blocks, PEERS, split_axis=0, concat_axis=0, tiled=True)


def exchange_in_order(blocks, chips):
    listed = [[2 * chip + core for n in range(0, len(chips), 4) for core in range(2) for chip in chips[n : n + 4]]]
    return lax.all_to_all(blocks, "row", split_axis=0, concat_axis=0, axis_index_groups=listed, tiled=True)


def packed_updates(count, pair_rep, pair_mask, pw, pb, gw, gb, ow, ob, ns, no):
    rows_of, width, channels = pair_rep.shape
    flat = (channels, rows_of * width)
    projected = [((count, 32, width), BF16), (flat, F32), (flat, BF16)]
    summed = [((count, 16, width), BF16)]
    params = [pair_rep, pair_mask, pw, gw, pb, gb, ob, ns, no]
    params = [pltpu.with_memory_space_constraint(v, pltpu.HBM) for v in params]
    held = [pltpu.VMEM(v.shape[1:] if n in (2, 3) else v.shape, v.dtype) for n, v in enumerate(params)]
    held += [pltpu.VMEM((2 * EACH, channels), F32), pltpu.SemaphoreType.DMA((len(params),))]
    back = pltpu.VMEM((OWN * channels, width), F32)
    mixed = pltpu.VMEM((2, OWN * channels, width), F32)
    kept = [((channels, 2 * EACH), F32), ((2 * OWN, width), F32)]
    send, gate, turned, columns, keep = call(first_kernel, projected + kept, held + [mixed], *params, place=pltpu.HBM)
    (send,) = call(functools.partial(triangle_kernel, False), summed, [], exchange_in_order(send, ORDERS[0][0]))
    send, gate, turned = call(middle_kernel, projected, [mixed, back], exchange_in_order(send, ORDERS[0][1]), turned, gate, columns, keep, pw, gw, ow)
    (send,) = call(functools.partial(triangle_kernel, True), summed, [], exchange_in_order(send, ORDERS[1][0]))
    (out,) = call(last_kernel, [(pair_rep.shape, BF16)], [back], exchange_in_order(send, ORDERS[1][1]), turned, gate, columns, ow)
    return out


def update(pair_t, pair_mask, u, incoming, peers, rows_of, pw, pb, gw, gb, ow, ob, ns, no):
    channels, positions = pair_t.shape
    width = positions // rows_of
    h = pw.shape[2] // 4
    count = peers[0] * peers[1]
    own = h // count
    normed = layer_norm(pair_t, ns[u, 0][:, None], no[u, 0][:, None]).astype(BF16)
    projected = over_rows(jnp.concatenate([pw[u], gw[u]], 1), normed) + jnp.concatenate([pb[u], gb[u]], 0)[:, None]
    parts = [projected[n * h : (n + 1) * h] for n in range(4)]
    gating = jax.nn.sigmoid(projected[4 * h :])
    mask = pair_mask.astype(F32).reshape(1, positions)
    left = (mask * jax.nn.sigmoid(parts[1]) * parts[0]).astype(BF16)
    right = (mask * jax.nn.sigmoid(parts[3]) * parts[2]).astype(BF16)
    sides = exchange(jnp.stack([v.reshape(count, own, rows_of, width) for v in (left, right)], 1))
    sides = sides.reshape(peers[0], peers[1], 2, own, rows_of, width)
    sides = sides.transpose(2, 3, 0, 4, 1, 5).reshape(2, own, peers[0] * rows_of, peers[1] * width)
    form = "cki,ckj->cij" if incoming else "cik,cjk->cij"
    summed = jnp.einsum(form, sides[0], sides[1], preferred_element_type=F32).astype(BF16)
    summed = summed.reshape(own, peers[0], rows_of, peers[1], width).transpose(1, 3, 0, 2, 4)
    summed = exchange(summed.reshape(count, own, rows_of, width)).reshape(h, positions).astype(F32)
    hidden = layer_norm(summed, ns[u, 1][:, None], no[u, 1][:, None]).astype(BF16)
    change = over_rows(ow[u], hidden) + ob[u][:, None]
    return (pair_t + gating * change).astype(BF16)


def plain_updates(peers, pair_rep, pair_mask, *params):
    rows_of, width, channels = pair_rep.shape
    pair_t = pair_rep.reshape(rows_of * width, channels).T
    for u in range(2):
        pair_t = update(pair_t.astype(F32), pair_mask, u, u == 1, peers, rows_of, *params)
    return pair_t.T.reshape(rows_of, width, channels)


def solution(mesh):
    peers = (mesh.shape["row"], mesh.shape["ka"])
    count = peers[0] * peers[1]

    def on_device(pair_rep, pair_mask, *params):
        rows_of, width, channels = pair_rep.shape
        hidden = params[0].shape[2] // 4
        fits = peers[1] == 1 and rows_of == OWN and hidden == OWN * count and count == 2 * len(ORDERS[0][0])
        if fits and channels == hidden == 128 and width % 128 == 0:
            return packed_updates(count, pair_rep, pair_mask, *params)
        return plain_updates(peers, pair_rep, pair_mask, *params)

    split = P(("grp", "row"), "ka", None)
    in_specs = (split, P(("grp", "row"), "ka")) + (P(),) * 8
    return jax.shard_map(on_device, mesh=mesh, in_specs=in_specs, out_specs=split, check_vma=False)
```

```python
import functools

import jax
import jax.numpy as jnp
from jax import lax
from jax.experimental import pallas as pl
from jax.experimental.pallas import tpu as pltpu
from jax.sharding import PartitionSpec as P

PEERS = ("row", "ka")
OWN = 4
ORDERS = (
    ((0, 13, 9, 5, 1, 15, 11, 7, 3, 14, 10, 6, 2, 12, 8, 4), (0, 13, 9, 5, 1, 15, 11, 7, 3, 14, 10, 6, 2, 12, 8, 4)),
    ((0, 13, 9, 5, 1, 15, 11, 7, 3, 14, 10, 6, 2, 12, 8, 4), (0, 15, 11, 14, 13, 10, 9, 7, 12, 5, 8, 6, 4, 3, 2, 1)),
)
COLUMNS = ((15, 11, 7, 3), (14, 10, 6, 2), (13, 9, 5, 1), (12, 8, 4, 0))
LAST = tuple(2 * chip + core for column in COLUMNS for core in range(2) for chip in column)
EACH = 16
BF16, F32 = jnp.bfloat16, jnp.float32


def over_rows(a, b):
    return lax.dot_general(a, b, (((0,), (0,)), ((), ())), preferred_element_type=F32)


def over_columns(a, b):
    return lax.dot_general(a, b, (((1,), (1,)), ((), ())), preferred_element_type=F32)


def layer_norm(values, norm_gain, norm_bias):
    average = jnp.mean(values, 0, keepdims=True)
    centred = values - average
    variance = jnp.mean(centred * centred, 0, keepdims=True)
    return centred * lax.rsqrt(variance + 1e-05) * norm_gain + norm_bias


def pack(blocks):
    channels, width = blocks[0].shape
    tiles = [b.reshape(channels // 8, 8, width) for b in blocks]
    turned = [pltpu.roll(b, 4, axis=0).reshape(channels // 8, 8, width) for b in blocks]
    low = lax.broadcasted_iota(jnp.int32, tiles[0].shape, 1) < 4
    back = [pltpu.roll(b, channels - 4, axis=0).reshape(channels // 8, 8, width) for b in blocks]
    even = [jnp.where(low, tiles[n], turned[n + 1]) for n in (0, 2)]
    odd = [jnp.where(low, back[n], tiles[n + 1]) for n in (0, 2)]
    return jnp.stack([jnp.stack(even, 1), jnp.stack(odd, 1)], 1).reshape(channels // 4, 16, width)


def unpack(packed):
    count, _, width = packed.shape
    tiles = packed.reshape(count // 2, 2, 2, 8, width)
    low = lax.broadcasted_iota(jnp.int32, (count // 2, 8, width), 1) < 4
    blocks = []
    for n in range(2):
        even, odd = tiles[:, 0, n], tiles[:, 1, n]
        down = pltpu.roll(odd.reshape(count * 4, width), 4, axis=0).reshape(even.shape)
        up = pltpu.roll(even.reshape(count * 4, width), count * 4 - 4, axis=0).reshape(even.shape)
        blocks.append(jnp.where(low, even, down).reshape(count * 4, width))
        blocks.append(jnp.where(low, up, odd).reshape(count * 4, width))
    return blocks


def broadcast_columns(columns, first, many, width):
    held = columns[...]
    return [jnp.broadcast_to(held[:, n : n + 1], (held.shape[0], width)) for n in range(first, first + many)]


def project(u, z, mask, proj_weight, gate_weight, columns, send, gate, mixed):
    width = z[0].shape[1]
    h = proj_weight.shape[1] // 4
    rows = mixed.shape[1]
    gain, offset, *biases = broadcast_columns(columns, u * EACH, 7, width)
    scales = (1.0, 0.5, 1.0, 0.5, 0.5)
    biases = [b * k for b, k in zip(biases, scales)]
    turned = [proj_weight[:, n * h : (n + 1) * h] for n in range(4)] + [gate_weight]
    turned = [(w * jnp.asarray(k, BF16)).T if k != 1.0 else w.T for w, k in zip(turned, scales)]
    pairs = []
    for pair in range(0, OWN, 2):
        normed = [layer_norm(z[i], gain, offset).astype(BF16) for i in (pair, pair + 1)]
        pairs.append(jnp.concatenate(normed, 1))
    for side in range(2):
        for pair, normed in enumerate(pairs):
            value, gating = [jnp.dot(turned[2 * side + n], normed, preferred_element_type=F32) for n in range(2)]
            for n in range(2):
                i, at = 2 * pair + n, slice(n * width, (n + 1) * width)
                half = mask[i : i + 1, :] * 0.5
                weight = jnp.tanh(gating[:, at] + biases[2 * side + 1]) * half + half
                mixed[side, pl.ds(i, h, stride=OWN), :] = weight * (value[:, at] + biases[2 * side])
    for side in range(2):
        send[:, side * 16 : (side + 1) * 16, :] = mixed[side].reshape(rows // 16, 16, width).astype(BF16)
    for pair, normed in enumerate(pairs):
        gating = jnp.dot(turned[4], normed, preferred_element_type=F32)
        for n in range(2):
            i = 2 * pair + n
            gate[:, i * width : (i + 1) * width] = 0.5 * jnp.tanh(gating[:, n * width : (n + 1) * width] + biases[4]) + 0.5


def finish(u, z, summed, gate, out_weight, columns, mixed):
    width = z[0].shape[1]
    gain, offset, bias = broadcast_columns(columns, u * EACH + 7, 3, width)
    turned = out_weight.T
    sums = summed[...].astype(F32)
    if u == 1:
        sums = rearrange(sums, LAST, devices(ORDERS[u][1]))
    mixed[...] = sums.reshape(mixed.shape)
    results = []
    for pair in range(0, OWN, 2):
        blocks = [mixed[pl.ds(i, mixed.shape[0] // OWN, stride=OWN), :] for i in (pair, pair + 1)]
        blocks = [reorder(v, ORDERS[u][1], ORDERS[u][0]) for v in blocks]
        hidden = jnp.concatenate([layer_norm(v, gain, offset).astype(BF16) for v in blocks], 1)
        both = jnp.dot(turned, hidden, preferred_element_type=F32)
        for n in range(2):
            change = both[:, n * width : (n + 1) * width] + bias
            at = slice((pair + n) * width, (pair + n + 1) * width)
            results.append((z[pair + n].astype(F32) + gate[:, at] * change).astype(BF16))
    return results


def first_kernel(
    pair, mask, pw, gw, pb, gb, ob, ns, no, send, gate, turned, columns, keep, pair_in, mask_in, pw_in, gw_in, pb_in, gb_in, ob_in, ns_in, no_in, rows, arrived, mixed
):
    moves = [(pair, pair_in), (pb, pb_in), (gb, gb_in), (ob, ob_in), (ns, ns_in), (no, no_in)]
    moves += [(pw.at[0], pw_in), (gw.at[0], gw_in), (mask, mask_in)]
    moves = [pltpu.make_async_copy(a, b, arrived.at[n]) for n, (a, b) in enumerate(moves)]
    for move in moves:
        move.start()
    for move in moves:
        move.wait()
    width = pair.shape[1]
    z = [pair_in[i].T for i in range(OWN)]
    for i in range(OWN):
        turned[:, i * width : (i + 1) * width] = z[i]
    h = pw.shape[2] // 4
    for u in range(2):
        found = [ns_in[u, 0:1, :], no_in[u, 0:1, :]] + [pb_in[u : u + 1, n * h : (n + 1) * h] for n in range(4)]
        found += [gb_in[u : u + 1, :], ns_in[u, 1:2, :], no_in[u, 1:2, :], ob_in[u : u + 1, :]]
        for n, row in enumerate(found):
            rows[u * EACH + n : u * EACH + n + 1, :] = row
    columns[...] = rows[...].T
    keep[0:OWN, :] = mask_in[...].astype(F32)
    project(0, [v.astype(F32) for v in z], keep, pw_in[...], gw_in[...], columns, send, gate, mixed)


def middle_kernel(summed, old, old_gate, columns, keep, pw, gw, ow, send, gate, turned, mixed, mixed_back):
    width = keep.shape[1]
    z = finish(0, [old[:, i * width : (i + 1) * width] for i in range(OWN)], summed, old_gate, ow[0], columns, mixed_back)
    for i in range(OWN):
        turned[:, i * width : (i + 1) * width] = z[i]
    project(1, [v.astype(F32) for v in z], keep, pw[1], gw[1], columns, send, gate, mixed)


def last_kernel(summed, old, old_gate, columns, ow, out, mixed_back):
    width = out.shape[1]
    z = finish(1, [old[:, i * width : (i + 1) * width] for i in range(OWN)], summed, old_gate, ow[1], columns, mixed_back)
    for i in range(OWN):
        out[i] = z[i].T


def reorder(values, have, want):
    tiles = values.reshape(len(have), 2 * OWN, values.shape[1])
    places = [have.index(chip) for chip in want]
    return jnp.concatenate([tiles[n : n + 1] for n in places]).reshape(values.shape)


def devices(chips):
    return tuple(2 * chip + core for chip in chips for core in range(2))


def rearrange(blocks, have, want):
    return jnp.concatenate([blocks[n : n + 1] for n in [have.index(device) for device in want]])


def triangle_kernel(incoming, sides, out):
    come, go = ORDERS[1 if incoming else 0]
    in_mesh = tuple(range(len(come)))
    left, right = [unpack(sides[:, n : n + 16, :].astype(F32)) for n in (0, 16)]
    if incoming:
        summed = [over_rows(a.astype(BF16), b.astype(BF16)) for a, b in zip(left, right)]
        summed = [reorder(v, in_mesh, go) for v in summed]
    else:
        left = [reorder(v, come, go) for v in left]
        right = [reorder(v, come, in_mesh) for v in right]
        summed = [over_columns(a.astype(BF16), b.astype(BF16)) for a, b in zip(left, right)]
    packed = pack(summed).astype(BF16)
    out[...] = rearrange(packed, devices(go), LAST) if incoming else packed


def call(kernel, outs, scratch, *args, place=pltpu.VMEM):
    in_vmem = pl.BlockSpec(memory_space=pltpu.VMEM)
    return pl.pallas_call(
        kernel,
        out_shape=[jax.ShapeDtypeStruct(*o) for o in outs],
        in_specs=[pl.BlockSpec(memory_space=place)] * len(args),
        out_specs=[in_vmem] * len(outs),
        scratch_shapes=scratch,
        compiler_params=pltpu.CompilerParams(vmem_limit_bytes=24 * 2**20),
    )(*args)


def exchange(blocks):
    return lax.all_to_all(blocks, PEERS, split_axis=0, concat_axis=0, tiled=True)


def exchange_in_order(blocks, listed):
    return lax.all_to_all(blocks, "row", split_axis=0, concat_axis=0, axis_index_groups=[list(listed)], tiled=True)


def packed_updates(count, pair_rep, pair_mask, pw, pb, gw, gb, ow, ob, ns, no):
    rows_of, width, channels = pair_rep.shape
    flat = (channels, rows_of * width)
    projected = [((count, 32, width), BF16), (flat, F32), (flat, BF16)]
    summed = [((count, 16, width), BF16)]
    params = [pair_rep, pair_mask, pw, gw, pb, gb, ob, ns, no]
    params = [pltpu.with_memory_space_constraint(v, pltpu.HBM) for v in params]
    held = [pltpu.VMEM(v.shape[1:] if n in (2, 3) else v.shape, v.dtype) for n, v in enumerate(params)]
    held += [pltpu.VMEM((2 * EACH, channels), F32), pltpu.SemaphoreType.DMA((len(params),))]
    back = pltpu.VMEM((OWN * channels, width), F32)
    mixed = pltpu.VMEM((2, OWN * channels, width), F32)
    kept = [((channels, 2 * EACH), F32), ((2 * OWN, width), F32)]
    send, gate, turned, columns, keep = call(first_kernel, projected + kept, held + [mixed], *params, place=pltpu.HBM)
    (send,) = call(functools.partial(triangle_kernel, False), summed, [], exchange_in_order(send, devices(ORDERS[0][0])))
    send, gate, turned = call(middle_kernel, projected, [mixed, back], exchange_in_order(send, devices(ORDERS[0][1])), turned, gate, columns, keep, pw, gw, ow)
    (send,) = call(functools.partial(triangle_kernel, True), summed, [], exchange_in_order(send, devices(ORDERS[1][0])))
    (out,) = call(last_kernel, [(pair_rep.shape, BF16)], [back], exchange_in_order(send, LAST), turned, gate, columns, ow)
    return out


def update(pair_t, pair_mask, u, incoming, peers, rows_of, pw, pb, gw, gb, ow, ob, ns, no):
    channels, positions = pair_t.shape
    width = positions // rows_of
    h = pw.shape[2] // 4
    count = peers[0] * peers[1]
    own = h // count
    normed = layer_norm(pair_t, ns[u, 0][:, None], no[u, 0][:, None]).astype(BF16)
    projected = over_rows(jnp.concatenate([pw[u], gw[u]], 1), normed) + jnp.concatenate([pb[u], gb[u]], 0)[:, None]
    parts = [projected[n * h : (n + 1) * h] for n in range(4)]
    gating = jax.nn.sigmoid(projected[4 * h :])
    mask = pair_mask.astype(F32).reshape(1, positions)
    left = (mask * jax.nn.sigmoid(parts[1]) * parts[0]).astype(BF16)
    right = (mask * jax.nn.sigmoid(parts[3]) * parts[2]).astype(BF16)
    sides = exchange(jnp.stack([v.reshape(count, own, rows_of, width) for v in (left, right)], 1))
    sides = sides.reshape(peers[0], peers[1], 2, own, rows_of, width)
    sides = sides.transpose(2, 3, 0, 4, 1, 5).reshape(2, own, peers[0] * rows_of, peers[1] * width)
    form = "cki,ckj->cij" if incoming else "cik,cjk->cij"
    summed = jnp.einsum(form, sides[0], sides[1], preferred_element_type=F32).astype(BF16)
    summed = summed.reshape(own, peers[0], rows_of, peers[1], width).transpose(1, 3, 0, 2, 4)
    summed = exchange(summed.reshape(count, own, rows_of, width)).reshape(h, positions).astype(F32)
    hidden = layer_norm(summed, ns[u, 1][:, None], no[u, 1][:, None]).astype(BF16)
    change = over_rows(ow[u], hidden) + ob[u][:, None]
    return (pair_t + gating * change).astype(BF16)


def plain_updates(peers, pair_rep, pair_mask, *params):
    rows_of, width, channels = pair_rep.shape
    pair_t = pair_rep.reshape(rows_of * width, channels).T
    for u in range(2):
        pair_t = update(pair_t.astype(F32), pair_mask, u, u == 1, peers, rows_of, *params)
    return pair_t.T.reshape(rows_of, width, channels)


def solution(mesh):
    peers = (mesh.shape["row"], mesh.shape["ka"])
    count = peers[0] * peers[1]

    def on_device(pair_rep, pair_mask, *params):
        rows_of, width, channels = pair_rep.shape
        hidden = params[0].shape[2] // 4
        fits = peers[1] == 1 and rows_of == OWN and hidden == OWN * count and count == 2 * len(ORDERS[0][0])
        if fits and channels == hidden == 128 and width % 128 == 0:
            return packed_updates(count, pair_rep, pair_mask, *params)
        return plain_updates(peers, pair_rep, pair_mask, *params)

    split = P(("grp", "row"), "ka", None)
    in_specs = (split, P(("grp", "row"), "ka")) + (P(),) * 8
    return jax.shard_map(on_device, mesh=mesh, in_specs=in_specs, out_specs=split, check_vma=False)
```

```python
import functools

import jax
import jax.numpy as jnp
from jax import lax
from jax.experimental import pallas as pl
from jax.experimental.pallas import tpu as pltpu
from jax.sharding import PartitionSpec as P

PEERS = ("row", "ka")
OWN = 4
ORDERS = (
    ((0, 15, 11, 7, 3, 14, 10, 6, 2, 13, 9, 5, 1, 12, 8, 4), (0, 15, 11, 7, 3, 14, 10, 6, 2, 13, 9, 5, 1, 12, 8, 4)),
    ((0, 13, 9, 5, 1, 15, 11, 7, 3, 14, 10, 6, 2, 12, 8, 4), (0, 15, 11, 14, 13, 10, 9, 7, 12, 5, 8, 6, 4, 3, 2, 1)),
)
EACH = 16
BF16, F32 = jnp.bfloat16, jnp.float32


def over_rows(a, b):
    return lax.dot_general(a, b, (((0,), (0,)), ((), ())), preferred_element_type=F32)


def over_columns(a, b):
    return lax.dot_general(a, b, (((1,), (1,)), ((), ())), preferred_element_type=F32)


def layer_norm(values, norm_gain, norm_bias):
    average = jnp.mean(values, 0, keepdims=True)
    centred = values - average
    variance = jnp.mean(centred * centred, 0, keepdims=True)
    return centred * lax.rsqrt(variance + 1e-05) * norm_gain + norm_bias


def pack(blocks):
    channels, width = blocks[0].shape
    tiles = [b.reshape(channels // 8, 8, width) for b in blocks]
    turned = [pltpu.roll(b, 4, axis=0).reshape(channels // 8, 8, width) for b in blocks]
    low = lax.broadcasted_iota(jnp.int32, tiles[0].shape, 1) < 4
    back = [pltpu.roll(b, channels - 4, axis=0).reshape(channels // 8, 8, width) for b in blocks]
    even = [jnp.where(low, tiles[n], turned[n + 1]) for n in (0, 2)]
    odd = [jnp.where(low, back[n], tiles[n + 1]) for n in (0, 2)]
    return jnp.stack([jnp.stack(even, 1), jnp.stack(odd, 1)], 1).reshape(channels // 4, 16, width)


def unpack(packed):
    count, _, width = packed.shape
    tiles = packed.reshape(count // 2, 2, 2, 8, width)
    low = lax.broadcasted_iota(jnp.int32, (count // 2, 8, width), 1) < 4
    blocks = []
    for n in range(2):
        even, odd = tiles[:, 0, n], tiles[:, 1, n]
        down = pltpu.roll(odd.reshape(count * 4, width), 4, axis=0).reshape(even.shape)
        up = pltpu.roll(even.reshape(count * 4, width), count * 4 - 4, axis=0).reshape(even.shape)
        blocks.append(jnp.where(low, even, down).reshape(count * 4, width))
        blocks.append(jnp.where(low, up, odd).reshape(count * 4, width))
    return blocks


def broadcast_columns(columns, first, many, width):
    held = columns[...]
    return [jnp.broadcast_to(held[:, n : n + 1], (held.shape[0], width)) for n in range(first, first + many)]


def project(u, z, mask, proj_weight, gate_weight, columns, send, gate, mixed):
    width = z[0].shape[1]
    h = proj_weight.shape[1] // 4
    rows = mixed.shape[1]
    gain, offset, *biases = broadcast_columns(columns, u * EACH, 7, width)
    scales = (1.0, 0.5, 1.0, 0.5, 0.5)
    biases = [b * k for b, k in zip(biases, scales)]
    turned = [proj_weight[:, n * h : (n + 1) * h] for n in range(4)] + [gate_weight]
    turned = [(w * jnp.asarray(k, BF16)).T if k != 1.0 else w.T for w, k in zip(turned, scales)]
    pairs = []
    for pair in range(0, OWN, 2):
        normed = [layer_norm(z[i], gain, offset).astype(BF16) for i in (pair, pair + 1)]
        pairs.append(jnp.concatenate(normed, 1))
    for side in range(2):
        for pair, normed in enumerate(pairs):
            value, gating = [jnp.dot(turned[2 * side + n], normed, preferred_element_type=F32) for n in range(2)]
            for n in range(2):
                i, at = 2 * pair + n, slice(n * width, (n + 1) * width)
                half = mask[i : i + 1, :] * 0.5
                weight = jnp.tanh(gating[:, at] + biases[2 * side + 1]) * half + half
                mixed[side, pl.ds(i, h, stride=OWN), :] = weight * (value[:, at] + biases[2 * side])
    for side in range(2):
        send[:, side * 16 : (side + 1) * 16, :] = mixed[side].reshape(rows // 16, 16, width).astype(BF16)
    for pair, normed in enumerate(pairs):
        gating = jnp.dot(turned[4], normed, preferred_element_type=F32)
        for n in range(2):
            i = 2 * pair + n
            gate[:, i * width : (i + 1) * width] = 0.5 * jnp.tanh(gating[:, n * width : (n + 1) * width] + biases[4]) + 0.5


def finish(u, z, summed, gate, out_weight, columns, mixed):
    width = z[0].shape[1]
    gain, offset, bias = broadcast_columns(columns, u * EACH + 7, 3, width)
    turned = out_weight.T
    mixed[...] = summed[...].astype(F32).reshape(mixed.shape)
    results = []
    for pair in range(0, OWN, 2):
        blocks = [mixed[pl.ds(i, mixed.shape[0] // OWN, stride=OWN), :] for i in (pair, pair + 1)]
        blocks = [reorder(v, ORDERS[u][1], ORDERS[u][0]) for v in blocks]
        hidden = jnp.concatenate([layer_norm(v, gain, offset).astype(BF16) for v in blocks], 1)
        both = jnp.dot(turned, hidden, preferred_element_type=F32)
        for n in range(2):
            change = both[:, n * width : (n + 1) * width] + bias
            at = slice((pair + n) * width, (pair + n + 1) * width)
            results.append((z[pair + n].astype(F32) + gate[:, at] * change).astype(BF16))
    return results


def first_kernel(
    pair, mask, pw, gw, pb, gb, ob, ns, no, send, gate, turned, columns, keep, pair_in, mask_in, pw_in, gw_in, pb_in, gb_in, ob_in, ns_in, no_in, rows, arrived, mixed
):
    moves = [(pair, pair_in), (pb, pb_in), (gb, gb_in), (ob, ob_in), (ns, ns_in), (no, no_in)]
    moves += [(pw.at[0], pw_in), (gw.at[0], gw_in), (mask, mask_in)]
    moves = [pltpu.make_async_copy(a, b, arrived.at[n]) for n, (a, b) in enumerate(moves)]
    for move in moves:
        move.start()
    for move in moves:
        move.wait()
    width = pair.shape[1]
    z = [pair_in[i].T for i in range(OWN)]
    for i in range(OWN):
        turned[:, i * width : (i + 1) * width] = z[i]
    h = pw.shape[2] // 4
    for u in range(2):
        found = [ns_in[u, 0:1, :], no_in[u, 0:1, :]] + [pb_in[u : u + 1, n * h : (n + 1) * h] for n in range(4)]
        found += [gb_in[u : u + 1, :], ns_in[u, 1:2, :], no_in[u, 1:2, :], ob_in[u : u + 1, :]]
        for n, row in enumerate(found):
            rows[u * EACH + n : u * EACH + n + 1, :] = row
    columns[...] = rows[...].T
    keep[0:OWN, :] = mask_in[...].astype(F32)
    project(0, [v.astype(F32) for v in z], keep, pw_in[...], gw_in[...], columns, send, gate, mixed)


def middle_kernel(summed, old, old_gate, columns, keep, pw, gw, ow, send, gate, turned, mixed, mixed_back):
    width = keep.shape[1]
    z = finish(0, [old[:, i * width : (i + 1) * width] for i in range(OWN)], summed, old_gate, ow[0], columns, mixed_back)
    for i in range(OWN):
        turned[:, i * width : (i + 1) * width] = z[i]
    project(1, [v.astype(F32) for v in z], keep, pw[1], gw[1], columns, send, gate, mixed)


def last_kernel(summed, old, old_gate, columns, ow, out, mixed_back):
    width = out.shape[1]
    z = finish(1, [old[:, i * width : (i + 1) * width] for i in range(OWN)], summed, old_gate, ow[1], columns, mixed_back)
    for i in range(OWN):
        out[i] = z[i].T


def reorder(values, have, want):
    tiles = values.reshape(len(have), 2 * OWN, values.shape[1])
    places = [have.index(chip) for chip in want]
    return jnp.concatenate([tiles[n : n + 1] for n in places]).reshape(values.shape)


def triangle_kernel(incoming, sides, out):
    come, go = ORDERS[1 if incoming else 0]
    in_mesh = tuple(range(len(come)))
    left, right = [unpack(sides[:, n : n + 16, :].astype(F32)) for n in (0, 16)]
    if incoming:
        summed = [over_rows(a.astype(BF16), b.astype(BF16)) for a, b in zip(left, right)]
        summed = [reorder(v, in_mesh, go) for v in summed]
    else:
        left = [reorder(v, come, go) for v in left]
        right = [reorder(v, come, in_mesh) for v in right]
        summed = [over_columns(a.astype(BF16), b.astype(BF16)) for a, b in zip(left, right)]
    out[...] = pack(summed).astype(BF16)


def call(kernel, outs, scratch, *args, place=pltpu.VMEM):
    in_vmem = pl.BlockSpec(memory_space=pltpu.VMEM)
    return pl.pallas_call(
        kernel,
        out_shape=[jax.ShapeDtypeStruct(*o) for o in outs],
        in_specs=[pl.BlockSpec(memory_space=place)] * len(args),
        out_specs=[in_vmem] * len(outs),
        scratch_shapes=scratch,
        compiler_params=pltpu.CompilerParams(vmem_limit_bytes=24 * 2**20),
    )(*args)


def exchange(blocks):
    return lax.all_to_all(blocks, PEERS, split_axis=0, concat_axis=0, tiled=True)


def exchange_in_order(blocks, chips):
    listed = [[2 * chip + core for chip in chips for core in range(2)]]
    return lax.all_to_all(blocks, "row", split_axis=0, concat_axis=0, axis_index_groups=listed, tiled=True)


def packed_updates(count, pair_rep, pair_mask, pw, pb, gw, gb, ow, ob, ns, no):
    rows_of, width, channels = pair_rep.shape
    flat = (channels, rows_of * width)
    projected = [((count, 32, width), BF16), (flat, F32), (flat, BF16)]
    summed = [((count, 16, width), BF16)]
    params = [pair_rep, pair_mask, pw, gw, pb, gb, ob, ns, no]
    params = [pltpu.with_memory_space_constraint(v, pltpu.HBM) for v in params]
    held = [pltpu.VMEM(v.shape[1:] if n in (2, 3) else v.shape, v.dtype) for n, v in enumerate(params)]
    held += [pltpu.VMEM((2 * EACH, channels), F32), pltpu.SemaphoreType.DMA((len(params),))]
    back = pltpu.VMEM((OWN * channels, width), F32)
    mixed = pltpu.VMEM((2, OWN * channels, width), F32)
    kept = [((channels, 2 * EACH), F32), ((2 * OWN, width), F32)]
    send, gate, turned, columns, keep = call(first_kernel, projected + kept, held + [mixed], *params, place=pltpu.HBM)
    (send,) = call(functools.partial(triangle_kernel, False), summed, [], exchange_in_order(send, ORDERS[0][0]))
    send, gate, turned = call(middle_kernel, projected, [mixed, back], exchange_in_order(send, ORDERS[0][1]), turned, gate, columns, keep, pw, gw, ow)
    (send,) = call(functools.partial(triangle_kernel, True), summed, [], exchange_in_order(send, ORDERS[1][0]))
    (out,) = call(last_kernel, [(pair_rep.shape, BF16)], [back], exchange_in_order(send, ORDERS[1][1]), turned, gate, columns, ow)
    return out


def update(pair_t, pair_mask, u, incoming, peers, rows_of, pw, pb, gw, gb, ow, ob, ns, no):
    channels, positions = pair_t.shape
    width = positions // rows_of
    h = pw.shape[2] // 4
    count = peers[0] * peers[1]
    own = h // count
    normed = layer_norm(pair_t, ns[u, 0][:, None], no[u, 0][:, None]).astype(BF16)
    projected = over_rows(jnp.concatenate([pw[u], gw[u]], 1), normed) + jnp.concatenate([pb[u], gb[u]], 0)[:, None]
    parts = [projected[n * h : (n + 1) * h] for n in range(4)]
    gating = jax.nn.sigmoid(projected[4 * h :])
    mask = pair_mask.astype(F32).reshape(1, positions)
    left = (mask * jax.nn.sigmoid(parts[1]) * parts[0]).astype(BF16)
    right = (mask * jax.nn.sigmoid(parts[3]) * parts[2]).astype(BF16)
    sides = exchange(jnp.stack([v.reshape(count, own, rows_of, width) for v in (left, right)], 1))
    sides = sides.reshape(peers[0], peers[1], 2, own, rows_of, width)
    sides = sides.transpose(2, 3, 0, 4, 1, 5).reshape(2, own, peers[0] * rows_of, peers[1] * width)
    form = "cki,ckj->cij" if incoming else "cik,cjk->cij"
    summed = jnp.einsum(form, sides[0], sides[1], preferred_element_type=F32).astype(BF16)
    summed = summed.reshape(own, peers[0], rows_of, peers[1], width).transpose(1, 3, 0, 2, 4)
    summed = exchange(summed.reshape(count, own, rows_of, width)).reshape(h, positions).astype(F32)
    hidden = layer_norm(summed, ns[u, 1][:, None], no[u, 1][:, None]).astype(BF16)
    change = over_rows(ow[u], hidden) + ob[u][:, None]
    return (pair_t + gating * change).astype(BF16)


def plain_updates(peers, pair_rep, pair_mask, *params):
    rows_of, width, channels = pair_rep.shape
    pair_t = pair_rep.reshape(rows_of * width, channels).T
    for u in range(2):
        pair_t = update(pair_t.astype(F32), pair_mask, u, u == 1, peers, rows_of, *params)
    return pair_t.T.reshape(rows_of, width, channels)


def solution(mesh):
    peers = (mesh.shape["row"], mesh.shape["ka"])
    count = peers[0] * peers[1]

    def on_device(pair_rep, pair_mask, *params):
        rows_of, width, channels = pair_rep.shape
        hidden = params[0].shape[2] // 4
        fits = peers[1] == 1 and rows_of == OWN and hidden == OWN * count and count == 2 * len(ORDERS[0][0])
        if fits and channels == hidden == 128 and width % 128 == 0:
            return packed_updates(count, pair_rep, pair_mask, *params)
        return plain_updates(peers, pair_rep, pair_mask, *params)

    split = P(("grp", "row"), "ka", None)
    in_specs = (split, P(("grp", "row"), "ka")) + (P(),) * 8
    return jax.shard_map(on_device, mesh=mesh, in_specs=in_specs, out_specs=split, check_vma=False)
```

```python
import functools

import jax
import jax.numpy as jnp
from jax import lax
from jax.experimental import pallas as pl
from jax.experimental.pallas import tpu as pltpu
from jax.sharding import PartitionSpec as P

PEERS = ("row", "ka")
OWN = 4
ORDERS = (
    ((0, 14, 10, 6, 2, 15, 11, 7, 3, 13, 9, 5, 1, 12, 8, 4), (0, 14, 10, 6, 2, 15, 11, 7, 3, 13, 9, 5, 1, 12, 8, 4)),
    ((0, 14, 10, 6, 2, 15, 11, 7, 3, 13, 9, 5, 1, 12, 8, 4), (0, 15, 11, 14, 13, 10, 9, 7, 12, 5, 8, 6, 4, 3, 2, 1)),
)
EACH = 16
BF16, F32 = jnp.bfloat16, jnp.float32


def over_rows(a, b):
    return lax.dot_general(a, b, (((0,), (0,)), ((), ())), preferred_element_type=F32)


def over_columns(a, b):
    return lax.dot_general(a, b, (((1,), (1,)), ((), ())), preferred_element_type=F32)


def layer_norm(values, norm_gain, norm_bias):
    average = jnp.mean(values, 0, keepdims=True)
    centred = values - average
    variance = jnp.mean(centred * centred, 0, keepdims=True)
    return centred * lax.rsqrt(variance + 1e-05) * norm_gain + norm_bias


def pack(blocks):
    channels, width = blocks[0].shape
    tiles = [b.reshape(channels // 8, 8, width) for b in blocks]
    turned = [pltpu.roll(b, 4, axis=0).reshape(channels // 8, 8, width) for b in blocks]
    low = lax.broadcasted_iota(jnp.int32, tiles[0].shape, 1) < 4
    back = [pltpu.roll(b, channels - 4, axis=0).reshape(channels // 8, 8, width) for b in blocks]
    even = [jnp.where(low, tiles[n], turned[n + 1]) for n in (0, 2)]
    odd = [jnp.where(low, back[n], tiles[n + 1]) for n in (0, 2)]
    return jnp.stack([jnp.stack(even, 1), jnp.stack(odd, 1)], 1).reshape(channels // 4, 16, width)


def unpack(packed):
    count, _, width = packed.shape
    tiles = packed.reshape(count // 2, 2, 2, 8, width)
    low = lax.broadcasted_iota(jnp.int32, (count // 2, 8, width), 1) < 4
    blocks = []
    for n in range(2):
        even, odd = tiles[:, 0, n], tiles[:, 1, n]
        down = pltpu.roll(odd.reshape(count * 4, width), 4, axis=0).reshape(even.shape)
        up = pltpu.roll(even.reshape(count * 4, width), count * 4 - 4, axis=0).reshape(even.shape)
        blocks.append(jnp.where(low, even, down).reshape(count * 4, width))
        blocks.append(jnp.where(low, up, odd).reshape(count * 4, width))
    return blocks


def broadcast_columns(columns, first, many, width):
    held = columns[...]
    return [jnp.broadcast_to(held[:, n : n + 1], (held.shape[0], width)) for n in range(first, first + many)]


def project(u, z, mask, proj_weight, gate_weight, columns, send, gate, mixed):
    width = z[0].shape[1]
    h = proj_weight.shape[1] // 4
    rows = mixed.shape[1]
    gain, offset, *biases = broadcast_columns(columns, u * EACH, 7, width)
    scales = (1.0, 0.5, 1.0, 0.5, 0.5)
    biases = [b * k for b, k in zip(biases, scales)]
    turned = [proj_weight[:, n * h : (n + 1) * h] for n in range(4)] + [gate_weight]
    turned = [(w * jnp.asarray(k, BF16)).T if k != 1.0 else w.T for w, k in zip(turned, scales)]
    pairs = []
    for pair in range(0, OWN, 2):
        normed = [layer_norm(z[i], gain, offset).astype(BF16) for i in (pair, pair + 1)]
        pairs.append(jnp.concatenate(normed, 1))
    for side in range(2):
        for pair, normed in enumerate(pairs):
            value, gating = [jnp.dot(turned[2 * side + n], normed, preferred_element_type=F32) for n in range(2)]
            for n in range(2):
                i, at = 2 * pair + n, slice(n * width, (n + 1) * width)
                half = mask[i : i + 1, :] * 0.5
                weight = jnp.tanh(gating[:, at] + biases[2 * side + 1]) * half + half
                mixed[side, pl.ds(i, h, stride=OWN), :] = weight * (value[:, at] + biases[2 * side])
    for side in range(2):
        send[:, side * 16 : (side + 1) * 16, :] = mixed[side].reshape(rows // 16, 16, width).astype(BF16)
    for pair, normed in enumerate(pairs):
        gating = jnp.dot(turned[4], normed, preferred_element_type=F32)
        for n in range(2):
            i = 2 * pair + n
            gate[:, i * width : (i + 1) * width] = 0.5 * jnp.tanh(gating[:, n * width : (n + 1) * width] + biases[4]) + 0.5


def finish(u, z, summed, gate, out_weight, columns, mixed):
    width = z[0].shape[1]
    gain, offset, bias = broadcast_columns(columns, u * EACH + 7, 3, width)
    turned = out_weight.T
    mixed[...] = summed[...].astype(F32).reshape(mixed.shape)
    results = []
    for pair in range(0, OWN, 2):
        blocks = [mixed[pl.ds(i, mixed.shape[0] // OWN, stride=OWN), :] for i in (pair, pair + 1)]
        blocks = [reorder(v, ORDERS[u][1], ORDERS[u][0]) for v in blocks]
        hidden = jnp.concatenate([layer_norm(v, gain, offset).astype(BF16) for v in blocks], 1)
        both = jnp.dot(turned, hidden, preferred_element_type=F32)
        for n in range(2):
            change = both[:, n * width : (n + 1) * width] + bias
            at = slice((pair + n) * width, (pair + n + 1) * width)
            results.append((z[pair + n].astype(F32) + gate[:, at] * change).astype(BF16))
    return results


def first_kernel(
    pair, mask, pw, gw, pb, gb, ob, ns, no, send, gate, turned, columns, keep, pair_in, mask_in, pw_in, gw_in, pb_in, gb_in, ob_in, ns_in, no_in, rows, arrived, mixed
):
    moves = [(pair, pair_in), (pb, pb_in), (gb, gb_in), (ob, ob_in), (ns, ns_in), (no, no_in)]
    moves += [(pw.at[0], pw_in), (gw.at[0], gw_in), (mask, mask_in)]
    moves = [pltpu.make_async_copy(a, b, arrived.at[n]) for n, (a, b) in enumerate(moves)]
    for move in moves:
        move.start()
    for move in moves:
        move.wait()
    width = pair.shape[1]
    z = [pair_in[i].T for i in range(OWN)]
    for i in range(OWN):
        turned[:, i * width : (i + 1) * width] = z[i]
    h = pw.shape[2] // 4
    for u in range(2):
        found = [ns_in[u, 0:1, :], no_in[u, 0:1, :]] + [pb_in[u : u + 1, n * h : (n + 1) * h] for n in range(4)]
        found += [gb_in[u : u + 1, :], ns_in[u, 1:2, :], no_in[u, 1:2, :], ob_in[u : u + 1, :]]
        for n, row in enumerate(found):
            rows[u * EACH + n : u * EACH + n + 1, :] = row
    columns[...] = rows[...].T
    keep[0:OWN, :] = mask_in[...].astype(F32)
    project(0, [v.astype(F32) for v in z], keep, pw_in[...], gw_in[...], columns, send, gate, mixed)


def middle_kernel(summed, old, old_gate, columns, keep, pw, gw, ow, send, gate, turned, mixed, mixed_back):
    width = keep.shape[1]
    z = finish(0, [old[:, i * width : (i + 1) * width] for i in range(OWN)], summed, old_gate, ow[0], columns, mixed_back)
    for i in range(OWN):
        turned[:, i * width : (i + 1) * width] = z[i]
    project(1, [v.astype(F32) for v in z], keep, pw[1], gw[1], columns, send, gate, mixed)


def last_kernel(summed, old, old_gate, columns, ow, out, mixed_back):
    width = out.shape[1]
    z = finish(1, [old[:, i * width : (i + 1) * width] for i in range(OWN)], summed, old_gate, ow[1], columns, mixed_back)
    for i in range(OWN):
        out[i] = z[i].T


def reorder(values, have, want):
    tiles = values.reshape(len(have), 2 * OWN, values.shape[1])
    places = [have.index(chip) for chip in want]
    return jnp.concatenate([tiles[n : n + 1] for n in places]).reshape(values.shape)


def triangle_kernel(incoming, sides, out):
    come, go = ORDERS[1 if incoming else 0]
    in_mesh = tuple(range(len(come)))
    left, right = [unpack(sides[:, n : n + 16, :].astype(F32)) for n in (0, 16)]
    if incoming:
        summed = [over_rows(a.astype(BF16), b.astype(BF16)) for a, b in zip(left, right)]
        summed = [reorder(v, in_mesh, go) for v in summed]
    else:
        left = [reorder(v, come, go) for v in left]
        right = [reorder(v, come, in_mesh) for v in right]
        summed = [over_columns(a.astype(BF16), b.astype(BF16)) for a, b in zip(left, right)]
    out[...] = pack(summed).astype(BF16)


def call(kernel, outs, scratch, *args, place=pltpu.VMEM):
    in_vmem = pl.BlockSpec(memory_space=pltpu.VMEM)
    return pl.pallas_call(
        kernel,
        out_shape=[jax.ShapeDtypeStruct(*o) for o in outs],
        in_specs=[pl.BlockSpec(memory_space=place)] * len(args),
        out_specs=[in_vmem] * len(outs),
        scratch_shapes=scratch,
        compiler_params=pltpu.CompilerParams(vmem_limit_bytes=24 * 2**20),
    )(*args)


def exchange(blocks):
    return lax.all_to_all(blocks, PEERS, split_axis=0, concat_axis=0, tiled=True)


def exchange_in_order(blocks, chips):
    listed = [[2 * chip + core for chip in chips for core in range(2)]]
    return lax.all_to_all(blocks, "row", split_axis=0, concat_axis=0, axis_index_groups=listed, tiled=True)


def packed_updates(count, pair_rep, pair_mask, pw, pb, gw, gb, ow, ob, ns, no):
    rows_of, width, channels = pair_rep.shape
    flat = (channels, rows_of * width)
    projected = [((count, 32, width), BF16), (flat, F32), (flat, BF16)]
    summed = [((count, 16, width), BF16)]
    params = [pair_rep, pair_mask, pw, gw, pb, gb, ob, ns, no]
    params = [pltpu.with_memory_space_constraint(v, pltpu.HBM) for v in params]
    held = [pltpu.VMEM(v.shape[1:] if n in (2, 3) else v.shape, v.dtype) for n, v in enumerate(params)]
    held += [pltpu.VMEM((2 * EACH, channels), F32), pltpu.SemaphoreType.DMA((len(params),))]
    back = pltpu.VMEM((OWN * channels, width), F32)
    mixed = pltpu.VMEM((2, OWN * channels, width), F32)
    kept = [((channels, 2 * EACH), F32), ((2 * OWN, width), F32)]
    send, gate, turned, columns, keep = call(first_kernel, projected + kept, held + [mixed], *params, place=pltpu.HBM)
    (send,) = call(functools.partial(triangle_kernel, False), summed, [], exchange_in_order(send, ORDERS[0][0]))
    send, gate, turned = call(middle_kernel, projected, [mixed, back], exchange_in_order(send, ORDERS[0][1]), turned, gate, columns, keep, pw, gw, ow)
    (send,) = call(functools.partial(triangle_kernel, True), summed, [], exchange_in_order(send, ORDERS[1][0]))
    (out,) = call(last_kernel, [(pair_rep.shape, BF16)], [back], exchange_in_order(send, ORDERS[1][1]), turned, gate, columns, ow)
    return out


def update(pair_t, pair_mask, u, incoming, peers, rows_of, pw, pb, gw, gb, ow, ob, ns, no):
    channels, positions = pair_t.shape
    width = positions // rows_of
    h = pw.shape[2] // 4
    count = peers[0] * peers[1]
    own = h // count
    normed = layer_norm(pair_t, ns[u, 0][:, None], no[u, 0][:, None]).astype(BF16)
    projected = over_rows(jnp.concatenate([pw[u], gw[u]], 1), normed) + jnp.concatenate([pb[u], gb[u]], 0)[:, None]
    parts = [projected[n * h : (n + 1) * h] for n in range(4)]
    gating = jax.nn.sigmoid(projected[4 * h :])
    mask = pair_mask.astype(F32).reshape(1, positions)
    left = (mask * jax.nn.sigmoid(parts[1]) * parts[0]).astype(BF16)
    right = (mask * jax.nn.sigmoid(parts[3]) * parts[2]).astype(BF16)
    sides = exchange(jnp.stack([v.reshape(count, own, rows_of, width) for v in (left, right)], 1))
    sides = sides.reshape(peers[0], peers[1], 2, own, rows_of, width)
    sides = sides.transpose(2, 3, 0, 4, 1, 5).reshape(2, own, peers[0] * rows_of, peers[1] * width)
    form = "cki,ckj->cij" if incoming else "cik,cjk->cij"
    summed = jnp.einsum(form, sides[0], sides[1], preferred_element_type=F32).astype(BF16)
    summed = summed.reshape(own, peers[0], rows_of, peers[1], width).transpose(1, 3, 0, 2, 4)
    summed = exchange(summed.reshape(count, own, rows_of, width)).reshape(h, positions).astype(F32)
    hidden = layer_norm(summed, ns[u, 1][:, None], no[u, 1][:, None]).astype(BF16)
    change = over_rows(ow[u], hidden) + ob[u][:, None]
    return (pair_t + gating * change).astype(BF16)


def plain_updates(peers, pair_rep, pair_mask, *params):
    rows_of, width, channels = pair_rep.shape
    pair_t = pair_rep.reshape(rows_of * width, channels).T
    for u in range(2):
        pair_t = update(pair_t.astype(F32), pair_mask, u, u == 1, peers, rows_of, *params)
    return pair_t.T.reshape(rows_of, width, channels)


def solution(mesh):
    peers = (mesh.shape["row"], mesh.shape["ka"])
    count = peers[0] * peers[1]

    def on_device(pair_rep, pair_mask, *params):
        rows_of, width, channels = pair_rep.shape
        hidden = params[0].shape[2] // 4
        fits = peers[1] == 1 and rows_of == OWN and hidden == OWN * count and count == 2 * len(ORDERS[0][0])
        if fits and channels == hidden == 128 and width % 128 == 0:
            return packed_updates(count, pair_rep, pair_mask, *params)
        return plain_updates(peers, pair_rep, pair_mask, *params)

    split = P(("grp", "row"), "ka", None)
    in_specs = (split, P(("grp", "row"), "ka")) + (P(),) * 8
    return jax.shard_map(on_device, mesh=mesh, in_specs=in_specs, out_specs=split, check_vma=False)
```

```python
import functools

import jax
import jax.numpy as jnp
from jax import lax
from jax.experimental import pallas as pl
from jax.experimental.pallas import tpu as pltpu
from jax.sharding import PartitionSpec as P

PEERS = ("row", "ka")
OWN = 4
ORDERS = (
    ((0, 13, 9, 5, 1, 15, 11, 7, 3, 14, 10, 6, 2, 12, 8, 4), (0, 13, 9, 5, 1, 15, 11, 7, 3, 14, 10, 6, 2, 12, 8, 4)),
    ((0, 13, 9, 5, 1, 15, 11, 7, 3, 14, 10, 6, 2, 12, 8, 4), (0, 13, 9, 5, 1, 15, 11, 7, 3, 14, 10, 6, 2, 12, 8, 4)),
)
EACH = 16
BF16, F32 = jnp.bfloat16, jnp.float32


def over_rows(a, b):
    return lax.dot_general(a, b, (((0,), (0,)), ((), ())), preferred_element_type=F32)


def over_columns(a, b):
    return lax.dot_general(a, b, (((1,), (1,)), ((), ())), preferred_element_type=F32)


def layer_norm(values, norm_gain, norm_bias):
    average = jnp.mean(values, 0, keepdims=True)
    centred = values - average
    variance = jnp.mean(centred * centred, 0, keepdims=True)
    return centred * lax.rsqrt(variance + 1e-05) * norm_gain + norm_bias


def pack(blocks):
    channels, width = blocks[0].shape
    tiles = [b.reshape(channels // 8, 8, width) for b in blocks]
    turned = [pltpu.roll(b, 4, axis=0).reshape(channels // 8, 8, width) for b in blocks]
    low = lax.broadcasted_iota(jnp.int32, tiles[0].shape, 1) < 4
    back = [pltpu.roll(b, channels - 4, axis=0).reshape(channels // 8, 8, width) for b in blocks]
    even = [jnp.where(low, tiles[n], turned[n + 1]) for n in (0, 2)]
    odd = [jnp.where(low, back[n], tiles[n + 1]) for n in (0, 2)]
    return jnp.stack([jnp.stack(even, 1), jnp.stack(odd, 1)], 1).reshape(channels // 4, 16, width)


def unpack(packed):
    count, _, width = packed.shape
    tiles = packed.reshape(count // 2, 2, 2, 8, width)
    low = lax.broadcasted_iota(jnp.int32, (count // 2, 8, width), 1) < 4
    blocks = []
    for n in range(2):
        even, odd = tiles[:, 0, n], tiles[:, 1, n]
        down = pltpu.roll(odd.reshape(count * 4, width), 4, axis=0).reshape(even.shape)
        up = pltpu.roll(even.reshape(count * 4, width), count * 4 - 4, axis=0).reshape(even.shape)
        blocks.append(jnp.where(low, even, down).reshape(count * 4, width))
        blocks.append(jnp.where(low, up, odd).reshape(count * 4, width))
    return blocks


def broadcast_columns(columns, first, many, width):
    held = columns[...]
    return [jnp.broadcast_to(held[:, n : n + 1], (held.shape[0], width)) for n in range(first, first + many)]


def project(u, z, mask, proj_weight, gate_weight, columns, send, gate, mixed):
    width = z[0].shape[1]
    h = proj_weight.shape[1] // 4
    rows = mixed.shape[1]
    gain, offset, *biases = broadcast_columns(columns, u * EACH, 7, width)
    scales = (1.0, 0.5, 1.0, 0.5, 0.5)
    biases = [b * k for b, k in zip(biases, scales)]
    turned = [proj_weight[:, n * h : (n + 1) * h] for n in range(4)] + [gate_weight]
    turned = [(w * jnp.asarray(k, BF16)).T if k != 1.0 else w.T for w, k in zip(turned, scales)]
    pairs = []
    for pair in range(0, OWN, 2):
        normed = [layer_norm(z[i], gain, offset).astype(BF16) for i in (pair, pair + 1)]
        pairs.append(jnp.concatenate(normed, 1))
    for side in range(2):
        for pair, normed in enumerate(pairs):
            value, gating = [jnp.dot(turned[2 * side + n], normed, preferred_element_type=F32) for n in range(2)]
            for n in range(2):
                i, at = 2 * pair + n, slice(n * width, (n + 1) * width)
                half = mask[i : i + 1, :] * 0.5
                weight = jnp.tanh(gating[:, at] + biases[2 * side + 1]) * half + half
                mixed[side, pl.ds(i, h, stride=OWN), :] = weight * (value[:, at] + biases[2 * side])
    for side in range(2):
        send[:, side * 16 : (side + 1) * 16, :] = mixed[side].reshape(rows // 16, 16, width).astype(BF16)
    for pair, normed in enumerate(pairs):
        gating = jnp.dot(turned[4], normed, preferred_element_type=F32)
        for n in range(2):
            i = 2 * pair + n
            gate[:, i * width : (i + 1) * width] = 0.5 * jnp.tanh(gating[:, n * width : (n + 1) * width] + biases[4]) + 0.5


def finish(u, z, summed, gate, out_weight, columns, mixed):
    width = z[0].shape[1]
    gain, offset, bias = broadcast_columns(columns, u * EACH + 7, 3, width)
    turned = out_weight.T
    mixed[...] = summed[...].astype(F32).reshape(mixed.shape)
    results = []
    for pair in range(0, OWN, 2):
        blocks = [mixed[pl.ds(i, mixed.shape[0] // OWN, stride=OWN), :] for i in (pair, pair + 1)]
        blocks = [reorder(v, ORDERS[u][1], ORDERS[u][0]) for v in blocks]
        hidden = jnp.concatenate([layer_norm(v, gain, offset).astype(BF16) for v in blocks], 1)
        both = jnp.dot(turned, hidden, preferred_element_type=F32)
        for n in range(2):
            change = both[:, n * width : (n + 1) * width] + bias
            at = slice((pair + n) * width, (pair + n + 1) * width)
            results.append((z[pair + n].astype(F32) + gate[:, at] * change).astype(BF16))
    return results


def first_kernel(
    pair, mask, pw, gw, pb, gb, ob, ns, no, send, gate, turned, columns, keep, pair_in, mask_in, pw_in, gw_in, pb_in, gb_in, ob_in, ns_in, no_in, rows, arrived, mixed
):
    moves = [(pair, pair_in), (pb, pb_in), (gb, gb_in), (ob, ob_in), (ns, ns_in), (no, no_in)]
    moves += [(pw.at[0], pw_in), (gw.at[0], gw_in), (mask, mask_in)]
    moves = [pltpu.make_async_copy(a, b, arrived.at[n]) for n, (a, b) in enumerate(moves)]
    for move in moves:
        move.start()
    for move in moves:
        move.wait()
    width = pair.shape[1]
    z = [pair_in[i].T for i in range(OWN)]
    for i in range(OWN):
        turned[:, i * width : (i + 1) * width] = z[i]
    h = pw.shape[2] // 4
    for u in range(2):
        found = [ns_in[u, 0:1, :], no_in[u, 0:1, :]] + [pb_in[u : u + 1, n * h : (n + 1) * h] for n in range(4)]
        found += [gb_in[u : u + 1, :], ns_in[u, 1:2, :], no_in[u, 1:2, :], ob_in[u : u + 1, :]]
        for n, row in enumerate(found):
            rows[u * EACH + n : u * EACH + n + 1, :] = row
    columns[...] = rows[...].T
    keep[0:OWN, :] = mask_in[...].astype(F32)
    project(0, [v.astype(F32) for v in z], keep, pw_in[...], gw_in[...], columns, send, gate, mixed)


def middle_kernel(summed, old, old_gate, columns, keep, pw, gw, ow, send, gate, turned, mixed, mixed_back):
    width = keep.shape[1]
    z = finish(0, [old[:, i * width : (i + 1) * width] for i in range(OWN)], summed, old_gate, ow[0], columns, mixed_back)
    for i in range(OWN):
        turned[:, i * width : (i + 1) * width] = z[i]
    project(1, [v.astype(F32) for v in z], keep, pw[1], gw[1], columns, send, gate, mixed)


def last_kernel(summed, old, old_gate, columns, ow, out, mixed_back):
    width = out.shape[1]
    z = finish(1, [old[:, i * width : (i + 1) * width] for i in range(OWN)], summed, old_gate, ow[1], columns, mixed_back)
    for i in range(OWN):
        out[i] = z[i].T


def reorder(values, have, want):
    tiles = values.reshape(len(have), 2 * OWN, values.shape[1])
    places = [have.index(chip) for chip in want]
    return jnp.concatenate([tiles[n : n + 1] for n in places]).reshape(values.shape)


def triangle_kernel(incoming, sides, out):
    come, go = ORDERS[1 if incoming else 0]
    in_mesh = tuple(range(len(come)))
    left, right = [unpack(sides[:, n : n + 16, :].astype(F32)) for n in (0, 16)]
    if incoming:
        summed = [over_rows(a.astype(BF16), b.astype(BF16)) for a, b in zip(left, right)]
        summed = [reorder(v, in_mesh, go) for v in summed]
    else:
        left = [reorder(v, come, go) for v in left]
        right = [reorder(v, come, in_mesh) for v in right]
        summed = [over_columns(a.astype(BF16), b.astype(BF16)) for a, b in zip(left, right)]
    out[...] = pack(summed).astype(BF16)


def call(kernel, outs, scratch, *args, place=pltpu.VMEM):
    in_vmem = pl.BlockSpec(memory_space=pltpu.VMEM)
    return pl.pallas_call(
        kernel,
        out_shape=[jax.ShapeDtypeStruct(*o) for o in outs],
        in_specs=[pl.BlockSpec(memory_space=place)] * len(args),
        out_specs=[in_vmem] * len(outs),
        scratch_shapes=scratch,
        compiler_params=pltpu.CompilerParams(vmem_limit_bytes=24 * 2**20),
    )(*args)


def exchange(blocks):
    return lax.all_to_all(blocks, PEERS, split_axis=0, concat_axis=0, tiled=True)


def exchange_in_order(blocks, chips):
    listed = [[2 * chip + core for chip in chips for core in range(2)]]
    return lax.all_to_all(blocks, "row", split_axis=0, concat_axis=0, axis_index_groups=listed, tiled=True)


def packed_updates(count, pair_rep, pair_mask, pw, pb, gw, gb, ow, ob, ns, no):
    rows_of, width, channels = pair_rep.shape
    flat = (channels, rows_of * width)
    projected = [((count, 32, width), BF16), (flat, F32), (flat, BF16)]
    summed = [((count, 16, width), BF16)]
    params = [pair_rep, pair_mask, pw, gw, pb, gb, ob, ns, no]
    params = [pltpu.with_memory_space_constraint(v, pltpu.HBM) for v in params]
    held = [pltpu.VMEM(v.shape[1:] if n in (2, 3) else v.shape, v.dtype) for n, v in enumerate(params)]
    held += [pltpu.VMEM((2 * EACH, channels), F32), pltpu.SemaphoreType.DMA((len(params),))]
    back = pltpu.VMEM((OWN * channels, width), F32)
    mixed = pltpu.VMEM((2, OWN * channels, width), F32)
    kept = [((channels, 2 * EACH), F32), ((2 * OWN, width), F32)]
    send, gate, turned, columns, keep = call(first_kernel, projected + kept, held + [mixed], *params, place=pltpu.HBM)
    (send,) = call(functools.partial(triangle_kernel, False), summed, [], exchange_in_order(send, ORDERS[0][0]))
    send, gate, turned = call(middle_kernel, projected, [mixed, back], exchange_in_order(send, ORDERS[0][1]), turned, gate, columns, keep, pw, gw, ow)
    (send,) = call(functools.partial(triangle_kernel, True), summed, [], exchange_in_order(send, ORDERS[1][0]))
    (out,) = call(last_kernel, [(pair_rep.shape, BF16)], [back], exchange_in_order(send, ORDERS[1][1]), turned, gate, columns, ow)
    return out


def update(pair_t, pair_mask, u, incoming, peers, rows_of, pw, pb, gw, gb, ow, ob, ns, no):
    channels, positions = pair_t.shape
    width = positions // rows_of
    h = pw.shape[2] // 4
    count = peers[0] * peers[1]
    own = h // count
    normed = layer_norm(pair_t, ns[u, 0][:, None], no[u, 0][:, None]).astype(BF16)
    projected = over_rows(jnp.concatenate([pw[u], gw[u]], 1), normed) + jnp.concatenate([pb[u], gb[u]], 0)[:, None]
    parts = [projected[n * h : (n + 1) * h] for n in range(4)]
    gating = jax.nn.sigmoid(projected[4 * h :])
    mask = pair_mask.astype(F32).reshape(1, positions)
    left = (mask * jax.nn.sigmoid(parts[1]) * parts[0]).astype(BF16)
    right = (mask * jax.nn.sigmoid(parts[3]) * parts[2]).astype(BF16)
    sides = exchange(jnp.stack([v.reshape(count, own, rows_of, width) for v in (left, right)], 1))
    sides = sides.reshape(peers[0], peers[1], 2, own, rows_of, width)
    sides = sides.transpose(2, 3, 0, 4, 1, 5).reshape(2, own, peers[0] * rows_of, peers[1] * width)
    form = "cki,ckj->cij" if incoming else "cik,cjk->cij"
    summed = jnp.einsum(form, sides[0], sides[1], preferred_element_type=F32).astype(BF16)
    summed = summed.reshape(own, peers[0], rows_of, peers[1], width).transpose(1, 3, 0, 2, 4)
    summed = exchange(summed.reshape(count, own, rows_of, width)).reshape(h, positions).astype(F32)
    hidden = layer_norm(summed, ns[u, 1][:, None], no[u, 1][:, None]).astype(BF16)
    change = over_rows(ow[u], hidden) + ob[u][:, None]
    return (pair_t + gating * change).astype(BF16)


def plain_updates(peers, pair_rep, pair_mask, *params):
    rows_of, width, channels = pair_rep.shape
    pair_t = pair_rep.reshape(rows_of * width, channels).T
    for u in range(2):
        pair_t = update(pair_t.astype(F32), pair_mask, u, u == 1, peers, rows_of, *params)
    return pair_t.T.reshape(rows_of, width, channels)


def solution(mesh):
    peers = (mesh.shape["row"], mesh.shape["ka"])
    count = peers[0] * peers[1]

    def on_device(pair_rep, pair_mask, *params):
        rows_of, width, channels = pair_rep.shape
        hidden = params[0].shape[2] // 4
        fits = peers[1] == 1 and rows_of == OWN and hidden == OWN * count and count == 2 * len(ORDERS[0][0])
        if fits and channels == hidden == 128 and width % 128 == 0:
            return packed_updates(count, pair_rep, pair_mask, *params)
        return plain_updates(peers, pair_rep, pair_mask, *params)

    split = P(("grp", "row"), "ka", None)
    in_specs = (split, P(("grp", "row"), "ka")) + (P(),) * 8
    return jax.shard_map(on_device, mesh=mesh, in_specs=in_specs, out_specs=split, check_vma=False)
```

```python
import functools

import jax
import jax.numpy as jnp
from jax import lax
from jax.experimental import pallas as pl
from jax.experimental.pallas import tpu as pltpu
from jax.sharding import PartitionSpec as P

PEERS = ("row", "ka")
OWN = 4
ORDERS = (
    ((0, 15, 11, 7, 3, 14, 10, 6, 2, 13, 9, 5, 1, 12, 8, 4), (0, 13, 9, 5, 1, 15, 11, 7, 3, 14, 10, 6, 2, 12, 8, 4)),
    ((0, 13, 9, 5, 1, 15, 11, 7, 3, 14, 10, 6, 2, 12, 8, 4), (0, 15, 11, 14, 13, 10, 9, 7, 12, 5, 8, 6, 4, 3, 2, 1)),
)
EACH = 16
BF16, F32 = jnp.bfloat16, jnp.float32


def over_rows(a, b):
    return lax.dot_general(a, b, (((0,), (0,)), ((), ())), preferred_element_type=F32)


def over_columns(a, b):
    return lax.dot_general(a, b, (((1,), (1,)), ((), ())), preferred_element_type=F32)


def layer_norm(values, norm_gain, norm_bias):
    average = jnp.mean(values, 0, keepdims=True)
    centred = values - average
    variance = jnp.mean(centred * centred, 0, keepdims=True)
    return centred * lax.rsqrt(variance + 1e-05) * norm_gain + norm_bias


def pack(blocks):
    channels, width = blocks[0].shape
    tiles = [b.reshape(channels // 8, 8, width) for b in blocks]
    turned = [pltpu.roll(b, 4, axis=0).reshape(channels // 8, 8, width) for b in blocks]
    low = lax.broadcasted_iota(jnp.int32, tiles[0].shape, 1) < 4
    back = [pltpu.roll(b, channels - 4, axis=0).reshape(channels // 8, 8, width) for b in blocks]
    even = [jnp.where(low, tiles[n], turned[n + 1]) for n in (0, 2)]
    odd = [jnp.where(low, back[n], tiles[n + 1]) for n in (0, 2)]
    return jnp.stack([jnp.stack(even, 1), jnp.stack(odd, 1)], 1).reshape(channels // 4, 16, width)


def unpack(packed):
    count, _, width = packed.shape
    tiles = packed.reshape(count // 2, 2, 2, 8, width)
    low = lax.broadcasted_iota(jnp.int32, (count // 2, 8, width), 1) < 4
    blocks = []
    for n in range(2):
        even, odd = tiles[:, 0, n], tiles[:, 1, n]
        down = pltpu.roll(odd.reshape(count * 4, width), 4, axis=0).reshape(even.shape)
        up = pltpu.roll(even.reshape(count * 4, width), count * 4 - 4, axis=0).reshape(even.shape)
        blocks.append(jnp.where(low, even, down).reshape(count * 4, width))
        blocks.append(jnp.where(low, up, odd).reshape(count * 4, width))
    return blocks


def broadcast_columns(columns, first, many, width):
    held = columns[...]
    return [jnp.broadcast_to(held[:, n : n + 1], (held.shape[0], width)) for n in range(first, first + many)]


def project(u, z, mask, proj_weight, gate_weight, columns, send, gate, mixed):
    width = z[0].shape[1]
    h = proj_weight.shape[1] // 4
    rows = mixed.shape[1]
    gain, offset, *biases = broadcast_columns(columns, u * EACH, 7, width)
    scales = (1.0, 0.5, 1.0, 0.5, 0.5)
    biases = [b * k for b, k in zip(biases, scales)]
    turned = [proj_weight[:, n * h : (n + 1) * h] for n in range(4)] + [gate_weight]
    turned = [(w * jnp.asarray(k, BF16)).T if k != 1.0 else w.T for w, k in zip(turned, scales)]
    pairs = []
    for pair in range(0, OWN, 2):
        normed = [layer_norm(z[i], gain, offset).astype(BF16) for i in (pair, pair + 1)]
        pairs.append(jnp.concatenate(normed, 1))
    for side in range(2):
        for pair, normed in enumerate(pairs):
            value, gating = [jnp.dot(turned[2 * side + n], normed, preferred_element_type=F32) for n in range(2)]
            for n in range(2):
                i, at = 2 * pair + n, slice(n * width, (n + 1) * width)
                half = mask[i : i + 1, :] * 0.5
                weight = jnp.tanh(gating[:, at] + biases[2 * side + 1]) * half + half
                mixed[side, pl.ds(i, h, stride=OWN), :] = weight * (value[:, at] + biases[2 * side])
    for side in range(2):
        send[:, side * 16 : (side + 1) * 16, :] = mixed[side].reshape(rows // 16, 16, width).astype(BF16)
    for pair, normed in enumerate(pairs):
        gating = jnp.dot(turned[4], normed, preferred_element_type=F32)
        for n in range(2):
            i = 2 * pair + n
            gate[:, i * width : (i + 1) * width] = 0.5 * jnp.tanh(gating[:, n * width : (n + 1) * width] + biases[4]) + 0.5


def finish(u, z, summed, gate, out_weight, columns, mixed):
    width = z[0].shape[1]
    gain, offset, bias = broadcast_columns(columns, u * EACH + 7, 3, width)
    turned = out_weight.T
    mixed[...] = summed[...].astype(F32).reshape(mixed.shape)
    results = []
    for pair in range(0, OWN, 2):
        blocks = [mixed[pl.ds(i, mixed.shape[0] // OWN, stride=OWN), :] for i in (pair, pair + 1)]
        blocks = [reorder(v, ORDERS[u][1], ORDERS[u][0]) for v in blocks]
        hidden = jnp.concatenate([layer_norm(v, gain, offset).astype(BF16) for v in blocks], 1)
        both = jnp.dot(turned, hidden, preferred_element_type=F32)
        for n in range(2):
            change = both[:, n * width : (n + 1) * width] + bias
            at = slice((pair + n) * width, (pair + n + 1) * width)
            results.append((z[pair + n].astype(F32) + gate[:, at] * change).astype(BF16))
    return results


def first_kernel(
    pair, mask, pw, gw, pb, gb, ob, ns, no, send, gate, turned, columns, keep, pair_in, mask_in, pw_in, gw_in, pb_in, gb_in, ob_in, ns_in, no_in, rows, arrived, mixed
):
    moves = [(pair, pair_in), (pb, pb_in), (gb, gb_in), (ob, ob_in), (ns, ns_in), (no, no_in)]
    moves += [(pw.at[0], pw_in), (gw.at[0], gw_in), (mask, mask_in)]
    moves = [pltpu.make_async_copy(a, b, arrived.at[n]) for n, (a, b) in enumerate(moves)]
    for move in moves:
        move.start()
    for move in moves:
        move.wait()
    width = pair.shape[1]
    z = [pair_in[i].T for i in range(OWN)]
    for i in range(OWN):
        turned[:, i * width : (i + 1) * width] = z[i]
    h = pw.shape[2] // 4
    for u in range(2):
        found = [ns_in[u, 0:1, :], no_in[u, 0:1, :]] + [pb_in[u : u + 1, n * h : (n + 1) * h] for n in range(4)]
        found += [gb_in[u : u + 1, :], ns_in[u, 1:2, :], no_in[u, 1:2, :], ob_in[u : u + 1, :]]
        for n, row in enumerate(found):
            rows[u * EACH + n : u * EACH + n + 1, :] = row
    columns[...] = rows[...].T
    keep[0:OWN, :] = mask_in[...].astype(F32)
    project(0, [v.astype(F32) for v in z], keep, pw_in[...], gw_in[...], columns, send, gate, mixed)


def middle_kernel(summed, old, old_gate, columns, keep, pw, gw, ow, send, gate, turned, mixed, mixed_back):
    width = keep.shape[1]
    z = finish(0, [old[:, i * width : (i + 1) * width] for i in range(OWN)], summed, old_gate, ow[0], columns, mixed_back)
    for i in range(OWN):
        turned[:, i * width : (i + 1) * width] = z[i]
    project(1, [v.astype(F32) for v in z], keep, pw[1], gw[1], columns, send, gate, mixed)


def last_kernel(summed, old, old_gate, columns, ow, out, mixed_back):
    width = out.shape[1]
    z = finish(1, [old[:, i * width : (i + 1) * width] for i in range(OWN)], summed, old_gate, ow[1], columns, mixed_back)
    for i in range(OWN):
        out[i] = z[i].T


def reorder(values, have, want):
    tiles = values.reshape(len(have), 2 * OWN, values.shape[1])
    places = [have.index(chip) for chip in want]
    return jnp.concatenate([tiles[n : n + 1] for n in places]).reshape(values.shape)


def triangle_kernel(incoming, sides, out):
    come, go = ORDERS[1 if incoming else 0]
    in_mesh = tuple(range(len(come)))
    left, right = [unpack(sides[:, n : n + 16, :].astype(F32)) for n in (0, 16)]
    if incoming:
        summed = [over_rows(a.astype(BF16), b.astype(BF16)) for a, b in zip(left, right)]
        summed = [reorder(v, in_mesh, go) for v in summed]
    else:
        left = [reorder(v, come, go) for v in left]
        right = [reorder(v, come, in_mesh) for v in right]
        summed = [over_columns(a.astype(BF16), b.astype(BF16)) for a, b in zip(left, right)]
    out[...] = pack(summed).astype(BF16)


def call(kernel, outs, scratch, *args, place=pltpu.VMEM):
    in_vmem = pl.BlockSpec(memory_space=pltpu.VMEM)
    return pl.pallas_call(
        kernel,
        out_shape=[jax.ShapeDtypeStruct(*o) for o in outs],
        in_specs=[pl.BlockSpec(memory_space=place)] * len(args),
        out_specs=[in_vmem] * len(outs),
        scratch_shapes=scratch,
        compiler_params=pltpu.CompilerParams(vmem_limit_bytes=24 * 2**20),
    )(*args)


def exchange(blocks):
    return lax.all_to_all(blocks, PEERS, split_axis=0, concat_axis=0, tiled=True)


def exchange_in_order(blocks, chips):
    listed = [[2 * chip + core for chip in chips for core in range(2)]]
    return lax.all_to_all(blocks, "row", split_axis=0, concat_axis=0, axis_index_groups=listed, tiled=True)


def packed_updates(count, pair_rep, pair_mask, pw, pb, gw, gb, ow, ob, ns, no):
    rows_of, width, channels = pair_rep.shape
    flat = (channels, rows_of * width)
    projected = [((count, 32, width), BF16), (flat, F32), (flat, BF16)]
    summed = [((count, 16, width), BF16)]
    params = [pair_rep, pair_mask, pw, gw, pb, gb, ob, ns, no]
    params = [pltpu.with_memory_space_constraint(v, pltpu.HBM) for v in params]
    held = [pltpu.VMEM(v.shape[1:] if n in (2, 3) else v.shape, v.dtype) for n, v in enumerate(params)]
    held += [pltpu.VMEM((2 * EACH, channels), F32), pltpu.SemaphoreType.DMA((len(params),))]
    back = pltpu.VMEM((OWN * channels, width), F32)
    mixed = pltpu.VMEM((2, OWN * channels, width), F32)
    kept = [((channels, 2 * EACH), F32), ((2 * OWN, width), F32)]
    send, gate, turned, columns, keep = call(first_kernel, projected + kept, held + [mixed], *params, place=pltpu.HBM)
    (send,) = call(functools.partial(triangle_kernel, False), summed, [], exchange_in_order(send, ORDERS[0][0]))
    send, gate, turned = call(middle_kernel, projected, [mixed, back], exchange_in_order(send, ORDERS[0][1]), turned, gate, columns, keep, pw, gw, ow)
    (send,) = call(functools.partial(triangle_kernel, True), summed, [], exchange_in_order(send, ORDERS[1][0]))
    (out,) = call(last_kernel, [(pair_rep.shape, BF16)], [back], exchange_in_order(send, ORDERS[1][1]), turned, gate, columns, ow)
    return out


def update(pair_t, pair_mask, u, incoming, peers, rows_of, pw, pb, gw, gb, ow, ob, ns, no):
    channels, positions = pair_t.shape
    width = positions // rows_of
    h = pw.shape[2] // 4
    count = peers[0] * peers[1]
    own = h // count
    normed = layer_norm(pair_t, ns[u, 0][:, None], no[u, 0][:, None]).astype(BF16)
    projected = over_rows(jnp.concatenate([pw[u], gw[u]], 1), normed) + jnp.concatenate([pb[u], gb[u]], 0)[:, None]
    parts = [projected[n * h : (n + 1) * h] for n in range(4)]
    gating = jax.nn.sigmoid(projected[4 * h :])
    mask = pair_mask.astype(F32).reshape(1, positions)
    left = (mask * jax.nn.sigmoid(parts[1]) * parts[0]).astype(BF16)
    right = (mask * jax.nn.sigmoid(parts[3]) * parts[2]).astype(BF16)
    sides = exchange(jnp.stack([v.reshape(count, own, rows_of, width) for v in (left, right)], 1))
    sides = sides.reshape(peers[0], peers[1], 2, own, rows_of, width)
    sides = sides.transpose(2, 3, 0, 4, 1, 5).reshape(2, own, peers[0] * rows_of, peers[1] * width)
    form = "cki,ckj->cij" if incoming else "cik,cjk->cij"
    summed = jnp.einsum(form, sides[0], sides[1], preferred_element_type=F32).astype(BF16)
    summed = summed.reshape(own, peers[0], rows_of, peers[1], width).transpose(1, 3, 0, 2, 4)
    summed = exchange(summed.reshape(count, own, rows_of, width)).reshape(h, positions).astype(F32)
    hidden = layer_norm(summed, ns[u, 1][:, None], no[u, 1][:, None]).astype(BF16)
    change = over_rows(ow[u], hidden) + ob[u][:, None]
    return (pair_t + gating * change).astype(BF16)


def plain_updates(peers, pair_rep, pair_mask, *params):
    rows_of, width, channels = pair_rep.shape
    pair_t = pair_rep.reshape(rows_of * width, channels).T
    for u in range(2):
        pair_t = update(pair_t.astype(F32), pair_mask, u, u == 1, peers, rows_of, *params)
    return pair_t.T.reshape(rows_of, width, channels)


def solution(mesh):
    peers = (mesh.shape["row"], mesh.shape["ka"])
    count = peers[0] * peers[1]

    def on_device(pair_rep, pair_mask, *params):
        rows_of, width, channels = pair_rep.shape
        hidden = params[0].shape[2] // 4
        fits = peers[1] == 1 and rows_of == OWN and hidden == OWN * count and count == 2 * len(ORDERS[0][0])
        if fits and channels == hidden == 128 and width % 128 == 0:
            return packed_updates(count, pair_rep, pair_mask, *params)
        return plain_updates(peers, pair_rep, pair_mask, *params)

    split = P(("grp", "row"), "ka", None)
    in_specs = (split, P(("grp", "row"), "ka")) + (P(),) * 8
    return jax.shard_map(on_device, mesh=mesh, in_specs=in_specs, out_specs=split, check_vma=False)
```
